32 devices in a mesh: wide: 8 (over z, y), narrow: 4 (over x, core).
Axes of the slice: x: 2, y: 2, z: 4, core: 2. Of those that a mesh axis runs over, the one named last changes fastest.
Arguments:
- tokens: bfloat16 [8, 1024, 1024], P('wide'), may hold values from -6 to 6
- conditions: float32 [8, 6, 1024], P('wide'), may hold values from -3 to 3
- item_live: int32 [8], P('wide'), may hold values from 0 to 1, as said below
- cotangent: bfloat16 [8, 1024, 1024], P('wide'), may hold values from -6 to 6
- modulation_table: float32 [6, 1024], replicated, may hold values from -3 to 3
- mixer_kernel: float32 [9, 1024], replicated, may hold values from -2 to 2
- hidden_kernel: float32 [9, 4096], P(None, 'narrow'), may hold values from -2 to 2
- attend_weight: float32 [1024, 3, 1024], P(None, None, 'narrow'), may hold values from -0.1875 to 0.1875
- output_weight: float32 [1024, 1024], P('narrow'), may hold values from -3 to 3
- expand_weight: float32 [1024, 4096], P(None, 'narrow'), may hold values from -0.1875 to 0.1875
- reduce_weight: float32 [4096, 1024], P('narrow'), may hold values from -0.15234375 to 0.15234375
- attend_moment: float32 [1024, 3, 1024], P(None, None, 'narrow'), may hold values from -0.0014095466 to 0.0014095466
- output_moment: float32 [1024, 1024], P('narrow'), may hold values from -0.0014095466 to 0.0014095466
- expand_moment: float32 [1024, 4096], P(None, 'narrow'), may hold values from -0.0014095466 to 0.0014095466
- reduce_moment: float32 [4096, 1024], P('narrow'), may hold values from -0.0014095466 to 0.0014095466
- table_first: float32 [6, 1024], replicated, may hold values from -0.00014095465 to 0.00014095465
- table_second: float32 [6, 1024], replicated, may hold values from 7.947286e-11 to 3.1789144e-10
- mixer_first: float32 [9, 1024], replicated, may hold values from -0.00014095465 to 0.00014095465
- mixer_second: float32 [9, 1024], replicated, may hold values from 7.947286e-11 to 3.1789144e-10
- hidden_first: float32 [9, 4096], P(None, 'narrow'), may hold values from -0.00014095465 to 0.00014095465
- hidden_second: float32 [9, 4096], P(None, 'narrow'), may hold values from 7.947286e-11 to 3.1789144e-10
Outputs:
- block_out: bfloat16 [8, 1024, 1024], P('wide')
- tokens_gradient: bfloat16 [8, 1024, 1024], P('wide')
- gradient_norm: float32 [], replicated
- attend_carried: float32 [1024, 3, 1024], P(None, None, 'narrow')
- output_carried: float32 [1024, 1024], P('narrow')
- expand_carried: float32 [1024, 4096], P(None, 'narrow')
- reduce_carried: float32 [4096, 1024], P('narrow')
- attend_result: float32 [1024, 3, 1024], P(None, None, 'narrow')
- output_result: float32 [1024, 1024], P('narrow')
- expand_result: float32 [1024, 4096], P(None, 'narrow')
- reduce_result: float32 [4096, 1024], P('narrow')
- table_moment: float32 [6, 1024], replicated
- table_square: float32 [6, 1024], replicated
- table_result: float32 [6, 1024], replicated
- mixer_moment: float32 [9, 1024], replicated
- mixer_square: float32 [9, 1024], replicated
- mixer_result: float32 [9, 1024], replicated
- hidden_moment: float32 [9, 4096], P(None, 'narrow')
- hidden_square: float32 [9, 4096], P(None, 'narrow')
- hidden_result: float32 [9, 4096], P(None, 'narrow')
The draws below stay inside these ranges and needn't reach their ends.
Inputs may be any that keep to these rules, and one draw needn't show every extreme that they name: `item_live`: in each aligned block of 1 items (the slots of one index of wide) the live items come first, and at least one block is wholly live.
All inputs are finite; a program needn't handle non-finite values.
Results may differ from the reference program's by a relative error of at most 0.014.
The reference program's roundings to bfloat16 on the way count: a program that leaves them out, or rounds other values in their place, can miss the bound.
Values sent between devices are 32-bit elements; how exact they have to be, the bound alone decides.
A program may use at most 320 MiB of HBM per device.

```python
import math
import jax
import jax.numpy as jnp
from jax import lax

D = 1024
HEADS = 16
HEAD = 64
FF = 4096
GRID = 32
SEQ = 1024
ITEMS_DEV = 1
ITEMS = 8
NEWTON = 5
STEP = 10
N_WIDE = 8


def draw_item_live(key, part):
    key = jax.random.fold_in(key, 11)
    count_key, full_key = jax.random.split(key)
    counts = jax.random.randint(count_key, (N_WIDE,), 0, ITEMS_DEV + 1)
    chosen = jax.random.randint(full_key, (), 0, N_WIDE)
    counts = jnp.where(jnp.arange(N_WIDE) == chosen, ITEMS_DEV, counts)
    slot_live = jnp.arange(ITEMS_DEV)[None, :] < counts[:, None]
    return slot_live.astype(jnp.int32).reshape(ITEMS)


def draw_output_weight(key, part):
    key = jax.random.fold_in(key, 23)
    position = jnp.arange(D, dtype=jnp.float32)[:, None] / (D - 1)
    noise = jax.random.truncated_normal(key, -5.0, 5.0, (D, D), jnp.float32)
    return noise * (1.0 + 2.0 * position) * 0.15


def draw_reduce_weight(key, part):
    key = jax.random.fold_in(key, 37)
    position = jnp.arange(FF, dtype=jnp.float32)[:, None] / (FF - 1)
    noise = jax.random.truncated_normal(key, -5.0, 5.0, (FF, D), jnp.float32)
    return noise * (1.0 + 2.0 * position) * (0.65 / FF ** 0.5)


def steps_of(key, shape, cuts, low, top_value):
    loudness = 1.0
    for dim, blocks in cuts:
        steps = jax.random.uniform(jax.random.fold_in(jax.random.fold_in(key, 6), dim), (blocks,), jnp.float32, low / len(cuts), top_value / len(cuts))
        loudness = loudness * jnp.repeat(jnp.exp(steps), shape[dim] // blocks).reshape((-1,) + (1,) * (len(shape) - 1 - dim))
    return loudness


def scatter_about(stream_key, extent, width, bound, cuts=(), kind=jnp.bfloat16):
    array = width * jax.random.normal(stream_key, extent, jnp.float32)
    if cuts:
        array = array * steps_of(stream_key, extent, cuts, -0.22, 0.18)
    return jnp.clip(array, -bound, bound).astype(kind)


def setup_inputs(seed: int = 0) -> dict:
    key_list = jax.random.split(jax.random.key(seed), 22)
    return {
        "tokens": scatter_about(key_list[0], (ITEMS, SEQ, D), 1.0, 6.0, ((0, 8),)),
        "conditions": scatter_about(key_list[1], (ITEMS, 6, D), 0.5, 3.0, ((0, 8),), jnp.float32),
        "item_live": draw_item_live(jax.random.fold_in(key_list[21], 71), 0),
        "cotangent": scatter_about(key_list[3], (ITEMS, SEQ, D), 1.0, 6.0, ((0, 8),)),
        "modulation_table": scatter_about(key_list[4], (6, D), 0.5, 3.0, (), jnp.float32),
        "mixer_kernel": scatter_about(key_list[5], (9, D), 9 ** -0.5, 2.0, (), jnp.float32),
        "hidden_kernel": scatter_about(key_list[6], (9, FF), 9 ** -0.5, 2.0, ((1, 4),), jnp.float32),
        "attend_weight": scatter_about(key_list[7], (D, 3, D), D ** -0.5, 0.1875, ((2, 4),), jnp.float32),
        "output_weight": draw_output_weight(jax.random.fold_in(key_list[21], 71), 0),
        "expand_weight": scatter_about(key_list[9], (D, FF), D ** -0.5, 0.1875, ((1, 4),), jnp.float32),
        "reduce_weight": draw_reduce_weight(jax.random.fold_in(key_list[21], 71), 0),
        "attend_moment": scatter_about(key_list[11], (D, 3, D), ((12 * D * D) ** -0.5), 0.0014095466, ((2, 4),), jnp.float32),
        "output_moment": scatter_about(key_list[12], (D, D), ((12 * D * D) ** -0.5), 0.0014095466, ((0, 4),), jnp.float32),
        "expand_moment": scatter_about(key_list[13], (D, FF), ((12 * D * D) ** -0.5), 0.0014095466, ((1, 4),), jnp.float32),
        "reduce_moment": scatter_about(key_list[14], (FF, D), ((12 * D * D) ** -0.5), 0.0014095466, ((0, 4),), jnp.float32),
        "table_first": scatter_about(key_list[15], (6, D), (0.11 * (12 * D * D) ** -0.5), 0.00014095465, (), jnp.float32),
        "table_second": jnp.clip(jnp.exp(jax.random.uniform(key_list[16], (6, D), jnp.float32, math.log(7.947285884934985e-11), math.log(3.178914353973994e-10))), 7.947285884934985e-11, 3.178914353973994e-10),
        "mixer_first": scatter_about(key_list[17], (9, D), (0.11 * (12 * D * D) ** -0.5), 0.00014095465, (), jnp.float32),
        "mixer_second": jnp.clip(jnp.exp(jax.random.uniform(key_list[18], (9, D), jnp.float32, math.log(7.947285884934985e-11), math.log(3.178914353973994e-10))), 7.947285884934985e-11, 3.178914353973994e-10),
        "hidden_first": scatter_about(key_list[19], (9, FF), (0.11 * (12 * D * D) ** -0.5), 0.00014095465, ((1, 4),), jnp.float32),
        "hidden_second": jnp.clip(jnp.exp(math.log(3.178914353973994e-10) - 1.3862944 * jax.random.uniform(key_list[20], (9, FF), jnp.float32) ** steps_of(key_list[20], (9, FF), ((1, 4),), -0.2, 0.2)), 7.947285884934985e-11, 3.178914353973994e-10),
    }


@jax.custom_vjp
def low(v):
    return lax.optimization_barrier(v.astype(jnp.bfloat16)).astype(jnp.float32)

@jax.custom_vjp
def low_back(v):
    return v

def low_keep(v):
    return (low(v), None)

def low_pass(kept, grad):
    return (grad,)

def back_keep(v):
    return (v, None)

def back_low(kept, grad):
    return (low(grad),)
low.defvjp(low_keep, low_pass)
low_back.defvjp(back_keep, back_low)
first_decay = 0.9
second_decay = 0.999
adam_rate = 0.3
muon_rate = 0.15
muon_momentum = 0.5
weight_decay = 0.01
newton_terms = (3.4445, -4.775, 2.0315)
gelu_slope = 0.7978845608
gelu_cubic = 0.044715

def exact_dot(left, right):
    return jnp.dot(left, right, precision=lax.Precision.HIGHEST, preferred_element_type=jnp.float32)

def layer_norm(values):
    average = lax.optimization_barrier(jnp.mean(values, axis=-1, keepdims=True))
    centred = values - average
    spread = lax.optimization_barrier(jnp.mean(centred * centred, axis=-1, keepdims=True))
    return centred * lax.rsqrt(spread + 1e-06)

def gelu_tanh(values):
    return 0.5 * values * (1.0 + jnp.tanh(gelu_slope * (values + gelu_cubic * values * values * values)))

def depthwise(values, kernel):
    grid_side = GRID
    shaped = values.reshape(grid_side, grid_side, values.shape[-1])
    padded = jnp.pad(shaped, ((1, 1), (1, 1), (0, 0)))
    summed = jnp.zeros_like(shaped)
    for tap_row in range(3):
        for tap_col in range(3):
            summed = summed + kernel[tap_row * 3 + tap_col] * padded[tap_row:tap_row + grid_side, tap_col:tap_col + grid_side]
    return summed.reshape(values.shape)

def item_forward(token_rows, cond_rows, modulation_table, mixer_kernel, hidden_kernel, attend_weight, output_weight, expand_weight, reduce_weight):
    modulation = modulation_table + cond_rows
    mixed_rows = low(depthwise(layer_norm(token_rows) * (1.0 + modulation[1]) + modulation[0], mixer_kernel))
    triple = low_back(low(exact_dot(mixed_rows, low(attend_weight).reshape(D, 3 * D))))
    triple = triple.reshape(SEQ, 3, HEADS, HEAD)
    queries = triple[:, 0]
    key_rows = triple[:, 1]
    value_rows = triple[:, 2]
    block_rows = min(512, SEQ)

    def attend_block(query_block):
        scores = low_back(jnp.einsum('qhe,khe->hqk', query_block, key_rows, precision=lax.Precision.HIGHEST) * HEAD ** (-0.5))
        row_peak = lax.optimization_barrier(jnp.max(scores, axis=-1, keepdims=True))
        weights = jnp.exp(scores - row_peak)
        soft = weights / lax.optimization_barrier(jnp.sum(weights, axis=-1, keepdims=True))
        return low_back(low(jnp.einsum('hqk,khe->qhe', low(soft), value_rows, precision=lax.Precision.HIGHEST)))
    context = lax.map(jax.checkpoint(attend_block), queries.reshape(SEQ // block_rows, block_rows, HEADS, HEAD))
    context = context.reshape(SEQ, D)
    branch = low_back(exact_dot(context, low(output_weight)))
    hidden = token_rows + modulation[2] * branch
    expand_entry = low(layer_norm(hidden) * (1.0 + modulation[4]) + modulation[3])
    upward = low_back(exact_dot(expand_entry, low(expand_weight)))
    activated = low(gelu_tanh(depthwise(upward, hidden_kernel)))
    ffn_branch = low_back(exact_dot(activated, low(reduce_weight)))
    return hidden + modulation[5] * ffn_branch

def orthogonalize(matrix):
    gramian = exact_dot(matrix, matrix.T)
    factor = 1.0 / (jnp.sqrt(jnp.trace(gramian)) + 1e-07)
    current = matrix * factor
    gramian = gramian * (factor * factor)
    for iteration in range(NEWTON):
        if iteration > 0:
            gramian = exact_dot(current, current.T)
        applied = exact_dot(gramian, current)
        twice_applied = exact_dot(gramian, applied)
        current = newton_terms[0] * current + newton_terms[1] * applied + newton_terms[2] * twice_applied
    return current

def adam_update(weight, moment, square, gradient):
    moment_new = first_decay * moment + (1.0 - first_decay) * gradient
    square_new = second_decay * square + (1.0 - second_decay) * gradient * gradient
    moment_hat = moment_new / (1.0 - first_decay ** STEP)
    square_hat = square_new / (1.0 - second_decay ** STEP)
    weight_new = weight * (1.0 - adam_rate * weight_decay) - adam_rate * moment_hat / (jnp.sqrt(square_hat) + 1e-08)
    return (moment_new, square_new, weight_new)

def muon_finish(weight, polar_part, longest):
    return weight * (1.0 - muon_rate * weight_decay) - muon_rate * 0.2 * math.sqrt(longest) * polar_part

def reference(tokens, conditions, item_live, cotangent, modulation_table, mixer_kernel, hidden_kernel, attend_weight, output_weight, expand_weight, reduce_weight, attend_moment, output_moment, expand_moment, reduce_moment, table_first, table_second, mixer_first, mixer_second, hidden_first, hidden_second):
    params = (modulation_table, mixer_kernel, hidden_kernel, attend_weight, output_weight, expand_weight, reduce_weight)
    zero_sums = jax.tree.map(lambda array_leaf: jnp.zeros(array_leaf.shape, jnp.float32), params)

    def per_item(running, inputs):
        token_rows, cond_rows, live_flag, cot_rows = inputs

        def forward(rows_in, weights):
            return item_forward(rows_in, cond_rows, *weights)
        result, pullback = jax.vjp(forward, token_rows.astype(jnp.float32), params)
        live_mask = live_flag.astype(jnp.float32)
        grad_rows, grad_params = pullback(cot_rows.astype(jnp.float32) * live_mask)
        running = jax.tree.map(jnp.add, running, grad_params)
        return (running, ((result * live_mask).astype(jnp.bfloat16), grad_rows.astype(jnp.bfloat16)))
    gradients, outputs = lax.scan(per_item, zero_sums, (tokens, conditions, item_live, cotangent))
    block_out, tokens_gradient = outputs
    squares = sum((jnp.sum(gradient * gradient) for gradient in gradients))
    gradient_norm = jnp.sqrt(squares)
    clip_factor = jnp.minimum(1.0, 1.0 / (gradient_norm + 1e-06))
    clipped = [gradient * clip_factor for gradient in gradients]
    table_moment, table_square, table_result = adam_update(modulation_table, table_first, table_second, clipped[0])
    mixer_moment, mixer_square, mixer_result = adam_update(mixer_kernel, mixer_first, mixer_second, clipped[1])
    hidden_moment, hidden_square, hidden_result = adam_update(hidden_kernel, hidden_first, hidden_second, clipped[2])
    moments = (attend_moment, output_moment, expand_moment, reduce_moment)
    carried = [muon_momentum * moment + gradient for moment, gradient in zip(moments, clipped[3:])]
    polar_attend = orthogonalize(carried[0].reshape(D, 3 * D)).reshape(D, 3, D)
    polar_output = orthogonalize(carried[1].T).T
    polar_expand = orthogonalize(carried[2])
    polar_reduce = orthogonalize(carried[3].T).T
    attend_result = muon_finish(attend_weight, polar_attend, 3 * D)
    output_result = muon_finish(output_weight, polar_output, D)
    expand_result = muon_finish(expand_weight, polar_expand, FF)
    reduce_result = muon_finish(reduce_weight, polar_reduce, FF)
    return (block_out, tokens_gradient, gradient_norm, carried[0], carried[1], carried[2], carried[3], attend_result, output_result, expand_result, reduce_result, table_moment, table_square, table_result, mixer_moment, mixer_square, mixer_result, hidden_moment, hidden_square, hidden_result)
```

```python
import functools
import math

import jax
import jax.numpy as jnp
from jax import lax
from jax.experimental import pallas as pl
from jax.experimental.pallas import tpu as pltpu
from jax.sharding import PartitionSpec as P

D = 1024
HEAD = 64
FF = 4096
GRID = 32
NEWTON = 5
STEP = 10


first_decay = 0.9
second_decay = 0.999
adam_rate = 0.3
muon_rate = 0.15
muon_momentum = 0.5
weight_decay = 0.01
newton_terms = (3.4445, -4.775, 2.0315)
gelu_slope = 0.7978845608
gelu_cubic = 0.044715


def layer_norm(values):
    average = jnp.mean(values, axis=-1, keepdims=True)
    centred = values - average
    spread = jnp.mean(centred * centred, axis=-1, keepdims=True)
    return centred * lax.rsqrt(spread + 1e-06)


def gelu_tanh(values):
    return (
        0.5
        * values
        * (1.0 + jnp.tanh(gelu_slope * (values + gelu_cubic * values * values * values)))
    )


def depthwise(values, kernel):
    grid_side = GRID
    shaped = values.reshape(values.shape[0], grid_side, grid_side, values.shape[-1])
    padded = jnp.pad(shaped, ((0, 0), (1, 1), (1, 1), (0, 0)))
    summed = jnp.zeros_like(shaped)
    for tap_row in range(3):
        for tap_col in range(3):
            summed = (
                summed
                + kernel[tap_row * 3 + tap_col]
                * padded[:, tap_row : tap_row + grid_side, tap_col : tap_col + grid_side]
            )
    return summed.reshape(values.shape)


def mixer_piece(token_rows, offset, stretch, kernel):
    return depthwise(layer_norm(token_rows) * (1.0 + stretch) + offset, kernel)


def entry_piece(hidden, offset, stretch):
    return layer_norm(hidden) * (1.0 + stretch) + offset


def middle_piece(upward, kernel):
    return gelu_tanh(depthwise(upward, kernel))


def attend_forward(queries, key_rows, value_rows):
    seq_len = queries.shape[0]
    block_rows = min(512, seq_len)
    blocks = queries.reshape(seq_len // block_rows, block_rows, queries.shape[1], queries.shape[2])
    scale_factor = HEAD ** (-0.5)

    def one_block(query_block):
        scores = (
            jnp.einsum("qhe,khe->hqk", query_block, key_rows, preferred_element_type=jnp.float32)
            * scale_factor
        )
        row_peak = jnp.max(scores, axis=-1, keepdims=True)
        weights = jnp.exp(scores - row_peak)
        summed = jnp.sum(weights, axis=-1, keepdims=True)
        soft_low = (weights / summed).astype(jnp.bfloat16)
        context = jnp.einsum(
            "hqk,khe->qhe", soft_low, value_rows, preferred_element_type=jnp.float32
        )
        return (context.astype(jnp.bfloat16), (row_peak + jnp.log(summed))[:, :, 0])

    context, logsum = lax.map(one_block, blocks)
    return (context.reshape(seq_len, -1), logsum)


def attend_backward(queries, key_rows, value_rows, logsum, grad_context):
    seq_len = queries.shape[0]
    block_rows = min(512, seq_len)
    block_count = seq_len // block_rows
    query_blocks = queries.reshape(block_count, block_rows, queries.shape[1], queries.shape[2])
    grad_blocks = grad_context.reshape(block_count, block_rows, queries.shape[1], queries.shape[2])
    scale_factor = HEAD ** (-0.5)

    def one_block(running, pieces):
        grad_keys, grad_values = running
        query_block, grad_block, logsum_block = pieces
        scores = (
            jnp.einsum("qhe,khe->hqk", query_block, key_rows, preferred_element_type=jnp.float32)
            * scale_factor
        )
        weights = jnp.exp(scores - logsum_block[:, :, None])
        soft_low = weights.astype(jnp.bfloat16)
        grad_values = grad_values + jnp.einsum(
            "hqk,qhe->khe", soft_low, grad_block, preferred_element_type=jnp.float32
        )
        grad_weights = jnp.einsum(
            "qhe,khe->hqk", grad_block, value_rows, preferred_element_type=jnp.float32
        )
        grad_scores = weights * (
            grad_weights - jnp.sum(weights * grad_weights, axis=-1, keepdims=True)
        )
        grad_low = grad_scores.astype(jnp.bfloat16)
        grad_query = (
            jnp.einsum("hqk,khe->qhe", grad_low, key_rows, preferred_element_type=jnp.float32)
            * scale_factor
        )
        grad_keys = (
            grad_keys
            + jnp.einsum("hqk,qhe->khe", grad_low, query_block, preferred_element_type=jnp.float32)
            * scale_factor
        )
        return ((grad_keys, grad_values), grad_query)

    start_sums = jnp.zeros(key_rows.shape, jnp.float32)
    finals, grad_queries = lax.scan(
        one_block, (start_sums, start_sums), (query_blocks, grad_blocks, logsum)
    )
    grad_queries = grad_queries.reshape(key_rows.shape)
    return jnp.stack([grad_queries, finals[0], finals[1]], axis=1)


MESH = pl.DeviceIdType.MESH
BLK = 256
LANES = 128
MATRICES = 4


def partner(index, bit):
    return index + (1 - 2 * ((index // bit) % 2)) * bit


def bits_of(count):
    found = []
    bit = 1
    while bit < count:
        found.append(bit)
        bit *= 2
    return found


def place_at(axis, bit):
    place = {"wide": lax.axis_index("wide"), "narrow": lax.axis_index("narrow")}
    place[axis] = partner(place[axis], bit)
    return (place["wide"], place["narrow"])


def greet(places):
    barrier = pltpu.get_barrier_semaphore()
    for place in places:
        pl.semaphore_signal(barrier, inc=1, device_id=place, device_id_type=MESH)
    pl.semaphore_wait(barrier, len(places))


def send(src, dst, sends, arrivals, slot, place):
    copy = pltpu.make_async_remote_copy(
        src_ref=src,
        dst_ref=dst,
        send_sem=sends.at[slot],
        recv_sem=arrivals.at[slot],
        device_id=place,
        device_id_type=MESH,
    )
    copy.start()
    return copy


def narrow_sum_kernel(far_bits, pieces, x_ref, o_ref, near, far, held, sends, arrivals, local):
    rows = x_ref.shape[0] // 2
    step = rows // pieces
    core = lax.axis_index("narrow") % 2
    mine, theirs = core * rows, (1 - core) * rows
    near_place = place_at("narrow", 1)
    far_places = [place_at("narrow", bit) for bit in far_bits]
    greet([near_place] + far_places)
    block = lambda base, p: pl.ds(pl.multiple_of(base + p * step, 8), step)
    count = len(far_bits)
    first = [
        send(x_ref.at[block(theirs, p)], near.at[p], sends, arrivals, p, near_place)
        for p in range(pieces)
    ]
    loads = [
        pltpu.make_async_copy(x_ref.at[block(mine, p)], held.at[0, p], local.at[p])
        for p in range(pieces)
    ]
    for load in loads:
        load.start()
    crossings = [[None] * pieces for _ in range(count)]
    last = []
    for p in range(pieces):
        loads[p].wait()
        first[p].wait_recv()
        held[0, p] = held[0, p] + near[p]
        crossings[0][p] = send(
            held.at[0, p], far.at[0, p], sends, arrivals, pieces + p, far_places[0]
        )
    for b in range(count):
        for p in range(pieces):
            crossings[b][p].wait_recv()
            held[b + 1, p] = held[b, p] + far[b, p]
            if b + 1 < count:
                crossings[b + 1][p] = send(
                    held.at[b + 1, p],
                    far.at[b + 1, p],
                    sends,
                    arrivals,
                    (b + 2) * pieces + p,
                    far_places[b + 1],
                )
            else:
                last.append(
                    send(
                        held.at[count, p],
                        o_ref.at[block(mine, p)],
                        sends,
                        arrivals,
                        (count + 1) * pieces + p,
                        near_place,
                    )
                )
    keeps = [
        pltpu.make_async_copy(held.at[count, p], o_ref.at[block(mine, p)], local.at[p])
        for p in range(pieces)
    ]
    for keep in keeps:
        keep.start()
    for copy in first:
        copy.wait_send()
    for row in crossings:
        for copy in row:
            copy.wait_send()
    for copy in last:
        copy.wait()
    for keep in keeps:
        keep.wait()


def narrow_sum(values, number):
    far_bits = bits_of(lax.axis_size("narrow"))[1:]
    count = len(far_bits)
    pieces = 4
    shape = values.shape
    flat = values.reshape(-1, shape[-1])
    step = flat.shape[0] // (2 * pieces)
    slots = (count + 2) * pieces
    total = pl.pallas_call(
        functools.partial(narrow_sum_kernel, far_bits, pieces),
        out_shape=jax.ShapeDtypeStruct(flat.shape, jnp.float32),
        in_specs=[pl.BlockSpec(memory_space=pl.ANY)],
        out_specs=pl.BlockSpec(memory_space=pl.ANY),
        scratch_shapes=[
            pltpu.VMEM((pieces, step, flat.shape[1]), jnp.float32),
            pltpu.VMEM((count, pieces, step, flat.shape[1]), jnp.float32),
            pltpu.VMEM((count + 1, pieces, step, flat.shape[1]), jnp.float32),
            pltpu.SemaphoreType.DMA((slots,)),
            pltpu.SemaphoreType.DMA((slots,)),
            pltpu.SemaphoreType.DMA((pieces,)),
        ],
        compiler_params=pltpu.CompilerParams(
            collective_id=number, has_side_effects=True, vmem_limit_bytes=32 * 2**20
        ),
        cost_estimate=pl.CostEstimate(
            flops=flat.size, bytes_accessed=flat.size * 32, transcendentals=0
        ),
    )(flat)
    return total.reshape(shape)


def narrow_sum_steps(values):
    shape = values.shape
    values = values.reshape(-1, shape[-1])
    rows = values.shape[0] // 2
    side = lax.axis_index("narrow") % 2
    give = lax.dynamic_slice_in_dim(values, (1 - side) * rows, rows, 0)
    keep = lax.dynamic_slice_in_dim(values, side * rows, rows, 0)
    values = keep + permute(give, "narrow", 1)
    for bit in bits_of(lax.axis_size("narrow"))[1:]:
        values = values + permute(values, "narrow", bit)
    other = permute(values, "narrow", 1)
    return jnp.where(
        side == 0,
        jnp.concatenate([values, other], axis=0),
        jnp.concatenate([other, values], axis=0),
    ).reshape(shape)


def small_kernel(
    wide_bits,
    narrow_bits,
    shared_rows,
    split_rows,
    x_ref,
    o_ref,
    norm_ref,
    slots,
    sends,
    arrivals,
    spare,
    spare_in,
):
    wide_places = [place_at("wide", bit) for bit in wide_bits]
    narrow_places = [place_at("narrow", bit) for bit in narrow_bits]
    greet(wide_places + narrow_places)
    count = len(wide_bits)
    copies = []
    slots[0] = x_ref[...]
    for b in range(count):
        copy = send(slots.at[b], slots.at[count + 1 + b], sends, arrivals, b, wide_places[b])
        copies.append(copy)
        copy.wait_recv()
        slots[b + 1] = slots[b] + slots[count + 1 + b]
    total = slots[count]
    o_ref[...] = total
    shared_part = total[:shared_rows]
    split_part = total[shared_rows : shared_rows + split_rows]
    shared = jnp.sum(shared_part * shared_part)
    split_sum = jnp.sum(split_part * split_part) + jnp.sum(
        total[shared_rows + split_rows : shared_rows + split_rows + 1]
    )
    spare[0] = jnp.full(spare.shape[1:], split_sum, jnp.float32)
    for b in range(len(narrow_bits)):
        copy = send(spare.at[b], spare_in.at[b], sends, arrivals, count + b, narrow_places[b])
        copies.append(copy)
        copy.wait_recv()
        spare[b + 1] = spare[b] + spare_in[b]
    norm_ref[...] = jnp.sqrt(spare[len(narrow_bits)] + shared)
    for copy in copies:
        copy.wait_send()


def small_sums(stacked, shared_rows, split_rows, number):
    wide_bits = bits_of(lax.axis_size("wide"))
    narrow_bits = bits_of(lax.axis_size("narrow"))
    vmem = pl.BlockSpec(memory_space=pltpu.VMEM)
    count = len(wide_bits)
    total = count + len(narrow_bits)
    return pl.pallas_call(
        functools.partial(small_kernel, wide_bits, narrow_bits, shared_rows, split_rows),
        out_shape=(
            jax.ShapeDtypeStruct(stacked.shape, jnp.float32),
            jax.ShapeDtypeStruct((8, LANES), jnp.float32),
        ),
        in_specs=[vmem],
        out_specs=(vmem, vmem),
        scratch_shapes=[
            pltpu.VMEM((2 * count + 1,) + stacked.shape, jnp.float32),
            pltpu.SemaphoreType.DMA((total,)),
            pltpu.SemaphoreType.DMA((total,)),
            pltpu.VMEM((len(narrow_bits) + 1, 8, LANES), jnp.float32),
            pltpu.VMEM((len(narrow_bits), 8, LANES), jnp.float32),
        ],
        compiler_params=pltpu.CompilerParams(
            collective_id=number, has_side_effects=True, vmem_limit_bytes=16 * 2**20
        ),
    )(stacked)


def permute(values, axis, bit):
    size = lax.axis_size(axis)
    return lax.ppermute(values, axis, [(index, index ^ bit) for index in range(size)])


def wide_scatter(values):
    for bit in bits_of(lax.axis_size("wide")):
        rows = values.shape[0] // 2
        side = (lax.axis_index("wide") // bit) % 2
        give = lax.dynamic_slice_in_dim(values, (1 - side) * rows, rows, 0)
        keep = lax.dynamic_slice_in_dim(values, side * rows, rows, 0)
        values = keep + permute(give, "wide", bit)
    return values


def wide_gather(values):
    for bit in reversed(bits_of(lax.axis_size("wide"))):
        side = (lax.axis_index("wide") // bit) % 2
        other = permute(values, "wide", bit)
        values = jnp.where(
            side == 0,
            jnp.concatenate([values, other], axis=0),
            jnp.concatenate([other, values], axis=0),
        )
    return values


def gram_kernel(narrow_bits, gathers, x_ref, o_ref, halves, inbox, sends, arrivals, local):
    parts, rows = x_ref.shape[0], x_ref.shape[1]
    sub = parts // MATRICES
    w, n = lax.axis_index("wide"), lax.axis_index("narrow")
    places = {}
    for axis, bit in [("narrow", bit) for bit in narrow_bits] + gathers:
        places[(axis, bit)] = place_at(axis, bit)
    greet(list(places.values()))
    load = pltpu.make_async_copy(x_ref, halves, local.at[0])
    load.start()
    load.wait()
    base = 0 * n
    size, at, slot = parts, 0, 0
    for bit in reversed(narrow_bits):
        size //= 2
        side = (n // bit) % 2
        copy = send(
            halves.at[pl.ds(base + (1 - side) * size, size)],
            inbox.at[pl.ds(at, size)],
            sends,
            arrivals,
            slot,
            places[("narrow", bit)],
        )
        base = base + side * size
        copy.wait()
        for s in range(size):
            halves[base + s] = halves[base + s] + inbox[at + s]
        at += size
        slot += 1

    def rows_of(item):
        big, small = w, n % sub
        for index, (axis, bit) in enumerate(gathers):
            if (item >> index) % 2:
                if axis == "wide":
                    big = partner(big, bit)
                else:
                    small = partner(small, bit)
        return pl.ds(pl.multiple_of((big * sub + small) * rows, 8), rows)

    keep = pltpu.make_async_copy(halves.at[n], o_ref.at[rows_of(0)], local.at[0])
    keep.start()
    copies = {}
    order = sorted(range(2 ** len(gathers)), key=lambda item: (bin(item).count("1"), item))
    for item in order:
        if item:
            copies[item].wait_recv()
        for index in reversed(range(item.bit_length(), len(gathers))):
            later = item + 2**index
            src = o_ref.at[rows_of(item)] if item else halves.at[n]
            copies[later] = send(
                src, o_ref.at[rows_of(item)], sends, arrivals, slot + later - 1, places[gathers[index]]
            )
    keep.wait()
    for copy in copies.values():
        copy.wait_send()


def gram_whole(partial, number):
    narrow_bits = bits_of(lax.axis_size("narrow"))
    wide_bits = bits_of(lax.axis_size("wide"))
    parts, rows, width = partial.shape
    sub = parts // MATRICES
    gathers = [("narrow", bit) for bit in bits_of(sub)]
    gathers += [("wide", bit) for bit in reversed(wide_bits)]
    slots = len(narrow_bits) + 2 ** len(gathers) - 1
    return pl.pallas_call(
        functools.partial(gram_kernel, narrow_bits, gathers),
        out_shape=jax.ShapeDtypeStruct((width, width), jnp.float32),
        in_specs=[pl.BlockSpec(memory_space=pl.ANY)],
        out_specs=pl.BlockSpec(memory_space=pl.ANY),
        scratch_shapes=[
            pltpu.VMEM(partial.shape, jnp.float32),
            pltpu.VMEM(partial.shape, jnp.float32),
            pltpu.SemaphoreType.DMA((slots,)),
            pltpu.SemaphoreType.DMA((slots,)),
            pltpu.SemaphoreType.DMA((1,)),
        ],
        compiler_params=pltpu.CompilerParams(
            collective_id=number, has_side_effects=True, vmem_limit_bytes=16 * 2**20
        ),
    )(partial)


def split(values):
    high = values.astype(jnp.bfloat16)
    return high, (values - high.astype(jnp.float32)).astype(jnp.bfloat16)


def product(left_high, left_low, right_high, right_low):
    dot = functools.partial(jnp.dot, preferred_element_type=jnp.float32)
    return dot(left_high, right_high) + (dot(left_high, right_low) + dot(left_low, right_high))


def polar_kernel(g_ref, q_ref, gh, gl, ph, pw, th, tl):
    size = g_ref.shape[0]
    blocks = size // BLK
    first, second, third = newton_terms
    rows = lambda block: pl.ds(block * BLK, BLK)
    square = (BLK, BLK)
    unit = (
        lax.broadcasted_iota(jnp.int32, square, 0) == lax.broadcasted_iota(jnp.int32, square, 1)
    ).astype(jnp.float32)
    trace = jnp.zeros((), jnp.float32)
    for i in range(blocks):
        trace = trace + jnp.sum(g_ref[rows(i), rows(i)] * unit)
    factor = 1.0 / (jnp.sqrt(trace) + 1e-07)
    for i in range(blocks):
        gh[rows(i), :], gl[rows(i), :] = split(g_ref[rows(i), :] * (factor * factor))

    def put(high, low, i, j, values):
        high[rows(i), rows(j)], low[rows(i), rows(j)] = split(values)
        if i != j:
            high[rows(j), rows(i)], low[rows(j), rows(i)] = split(values.T)

    def symmetric(left, right, emit):
        for i in range(blocks):
            columns = pl.ds(i * BLK, size - i * BLK)
            values = product(
                left[0][rows(i), :], left[1][rows(i), :], right[0][:, columns], right[1][:, columns]
            )
            for j in range(i, blocks):
                emit(i, j, values[:, (j - i) * BLK : (j - i + 1) * BLK])

    def emit_terms(i, j, values):
        gram = gh[rows(i), rows(j)].astype(jnp.float32) + gl[rows(i), rows(j)].astype(jnp.float32)
        terms = second * gram + third * values
        if i == j:
            terms = terms + first * unit
        put(ph, pw, i, j, terms)

    def emit_total(i, j, values):
        q_ref[rows(i), rows(j)] = values
        if i != j:
            q_ref[rows(j), rows(i)] = values.T

    symmetric((gh, gl), (gh, gl), emit_terms)
    for i in range(blocks):
        q_ref[rows(i), :] = (
            ph[rows(i), :].astype(jnp.float32) + pw[rows(i), :].astype(jnp.float32)
        ) * factor

    def one_step(step, carry):
        symmetric((ph, pw), (gh, gl), functools.partial(put, th, tl))
        symmetric((th, tl), (ph, pw), functools.partial(put, gh, gl))
        symmetric((gh, gl), (gh, gl), emit_terms)
        for i in range(blocks):
            th[rows(i), :], tl[rows(i), :] = split(q_ref[rows(i), :])
        symmetric((ph, pw), (th, tl), emit_total)
        return carry

    lax.fori_loop(0, NEWTON - 1, one_step, 0)


def polar_factor(gramian):
    size = gramian.shape[0]
    vmem = pl.BlockSpec(memory_space=pltpu.VMEM)
    return pl.pallas_call(
        polar_kernel,
        out_shape=jax.ShapeDtypeStruct((size, size), jnp.float32),
        in_specs=[vmem],
        out_specs=vmem,
        scratch_shapes=[pltpu.VMEM((size, size), jnp.bfloat16)] * 6,
        compiler_params=pltpu.CompilerParams(vmem_limit_bytes=48 * 2**20),
        cost_estimate=pl.CostEstimate(
            flops=17 * 6 * size**3, bytes_accessed=8 * size * size, transcendentals=0
        ),
    )(gramian)


def spread_kernel(sub, pieces, q_ref, o_ref, sends, arrivals, local):
    size = q_ref.shape[0]
    half = size // 2
    step = half // pieces
    w, n = lax.axis_index("wide"), lax.axis_index("narrow")
    own = n // sub
    across = partner(own, 2)
    near_place, far_place = place_at("narrow", sub), place_at("narrow", 2 * sub)
    side_place = place_at("wide", 1)
    greet([near_place, far_place, side_place])
    top = w % 2
    rows = lambda side, p: pl.ds(pl.multiple_of(side * half + p * step, 8), step)
    keep = pltpu.make_async_copy(q_ref, o_ref.at[own], local.at[0])
    keep.start()
    copies = []

    def push(src, dst, place):
        copies.append(send(src, dst, sends, arrivals, len(copies), place))
        return copies[-1]

    crossing = [
        push(q_ref.at[rows(top, p)], o_ref.at[own, rows(top, p)], far_place) for p in range(pieces)
    ]
    landing = [push(q_ref, o_ref.at[own], near_place)]
    aside = []
    for p in range(pieces):
        crossing[p].wait_recv()
        spot = o_ref.at[across, rows(top, p)]
        aside.append(push(spot, spot, side_place))
        landing.append(push(spot, spot, near_place))
    for p in range(pieces):
        aside[p].wait_recv()
        spot = o_ref.at[across, rows(1 - top, p)]
        landing.append(push(spot, spot, near_place))
    keep.wait()
    for copy in copies:
        copy.wait_send()
    for copy in landing:
        copy.wait_recv()


def spread(factor, number):
    size = factor.shape[0]
    pieces = 4
    slots = 1 + 4 * pieces
    sub = lax.axis_size("narrow") // MATRICES
    return pl.pallas_call(
        functools.partial(spread_kernel, sub, pieces),
        out_shape=jax.ShapeDtypeStruct((MATRICES, size, size), jnp.float32),
        in_specs=[pl.BlockSpec(memory_space=pl.ANY)],
        out_specs=pl.BlockSpec(memory_space=pl.ANY),
        scratch_shapes=[
            pltpu.SemaphoreType.DMA((slots,)),
            pltpu.SemaphoreType.DMA((slots,)),
            pltpu.SemaphoreType.DMA((1,)),
        ],
        compiler_params=pltpu.CompilerParams(collective_id=number, has_side_effects=True),
    )(factor)


def adam_update(weight, moment, square, gradient):
    moment_new = first_decay * moment + (1.0 - first_decay) * gradient
    square_new = second_decay * square + (1.0 - second_decay) * gradient * gradient
    moment_hat = moment_new / (1.0 - first_decay**STEP)
    square_hat = square_new / (1.0 - second_decay**STEP)
    weight_new = weight * (1.0 - adam_rate * weight_decay) - adam_rate * moment_hat / (
        jnp.sqrt(square_hat) + 1e-08
    )
    return (moment_new, square_new, weight_new)


def muon_finish(weight, polar_part, longest):
    return (
        weight * (1.0 - muon_rate * weight_decay)
        - muon_rate * 0.2 * math.sqrt(longest) * polar_part
    )


def row_block_gram(matrix, layout, start, count):
    axis = 0 if layout == "columns" else 1
    block = lax.dynamic_slice_in_dim(matrix, start, count, axis)
    return lax.dot_general(
        block,
        matrix,
        (((1 - axis,), (1 - axis,)), ((), ())),
        precision=lax.Precision.HIGH,
        preferred_element_type=jnp.float32,
    )


def apply_factor(factor, matrix, layout):
    left, right = (factor, matrix) if layout == "columns" else (matrix, factor)
    return jnp.dot(
        left, right, precision=lax.Precision.HIGH, preferred_element_type=jnp.float32
    )


def local(
    tokens,
    conditions,
    item_live,
    cotangent,
    modulation_table,
    mixer_kernel,
    hidden_kernel,
    attend_weight,
    output_weight,
    expand_weight,
    reduce_weight,
    attend_moment,
    output_moment,
    expand_moment,
    reduce_moment,
    table_first,
    table_second,
    mixer_first,
    mixer_second,
    hidden_first,
    hidden_second,
):
    item_count = tokens.shape[0]
    seq_len = tokens.shape[1]
    local_heads = attend_weight.shape[2] // HEAD
    live_mask = item_live.astype(jnp.float32)[:, None, None]
    token_rows = tokens.astype(jnp.float32)
    modulation = modulation_table[None] + conditions
    shift_one = modulation[:, 0:1]
    scale_one = modulation[:, 1:2]
    gate_one = modulation[:, 2:3]
    shift_two = modulation[:, 3:4]
    scale_two = modulation[:, 4:5]
    gate_two = modulation[:, 5:6]
    mixed_rows, mixer_pull = jax.vjp(mixer_piece, token_rows, shift_one, scale_one, mixer_kernel)
    mixed_low = mixed_rows.astype(jnp.bfloat16)
    attend_low = attend_weight.astype(jnp.bfloat16)
    triple = jnp.einsum(
        "isd,dkc->iskc", mixed_low, attend_low, preferred_element_type=jnp.float32
    ).astype(jnp.bfloat16)
    heads_split = triple.reshape(item_count, seq_len, 3, local_heads, HEAD)

    def attend_item(member):
        return attend_forward(member[:, 0], member[:, 1], member[:, 2])

    context, logsum = lax.map(attend_item, heads_split)
    output_low = output_weight.astype(jnp.bfloat16)
    branch = narrow_sum(
        jnp.einsum("isc,cd->isd", context, output_low, preferred_element_type=jnp.float32), 1
    )
    hidden = token_rows + gate_one * branch
    expand_entry, entry_pull = jax.vjp(entry_piece, hidden, shift_two, scale_two)
    entry_low = expand_entry.astype(jnp.bfloat16)
    expand_low = expand_weight.astype(jnp.bfloat16)
    upward = jnp.einsum("isd,df->isf", entry_low, expand_low, preferred_element_type=jnp.float32)
    activated, middle_pull = jax.vjp(middle_piece, upward, hidden_kernel)
    activated_low = activated.astype(jnp.bfloat16)
    reduce_low = reduce_weight.astype(jnp.bfloat16)
    ffn_branch = narrow_sum_steps(
        jnp.einsum("isf,fd->isd", activated_low, reduce_low, preferred_element_type=jnp.float32)
    )
    block_out = (live_mask * (hidden + gate_two * ffn_branch)).astype(jnp.bfloat16)
    grad_result = cotangent.astype(jnp.float32) * live_mask
    grad_gate_two = jnp.sum(ffn_branch * grad_result, axis=1)
    grad_ffn_low = (gate_two * grad_result).astype(jnp.bfloat16)
    grad_reduce = jnp.einsum(
        "isf,isd->fd", activated_low, grad_ffn_low, preferred_element_type=jnp.float32
    )
    grad_activated = jnp.einsum(
        "isd,fd->isf", grad_ffn_low, reduce_low, preferred_element_type=jnp.float32
    )
    grad_upward, grad_hidden_kernel = middle_pull(grad_activated)
    grad_up_low = grad_upward.astype(jnp.bfloat16)
    grad_expand = jnp.einsum(
        "isd,isf->df", entry_low, grad_up_low, preferred_element_type=jnp.float32
    )
    grad_entry = narrow_sum(
        jnp.einsum("isf,df->isd", grad_up_low, expand_low, preferred_element_type=jnp.float32), 2
    )
    grad_hidden, grad_shift_two, grad_scale_two = entry_pull(grad_entry)
    grad_hidden = grad_hidden + grad_result
    grad_gate_one = jnp.sum(branch * grad_hidden, axis=1)
    grad_branch_low = (gate_one * grad_hidden).astype(jnp.bfloat16)
    grad_output = jnp.einsum(
        "isc,isd->cd", context, grad_branch_low, preferred_element_type=jnp.float32
    )
    grad_context = jnp.einsum(
        "isd,cd->isc", grad_branch_low, output_low, preferred_element_type=jnp.float32
    ).astype(jnp.bfloat16)

    def attend_item_back(pieces):
        member, logsum_item, grad_item = pieces
        return attend_backward(
            member[:, 0],
            member[:, 1],
            member[:, 2],
            logsum_item,
            grad_item.reshape(seq_len, local_heads, HEAD),
        )

    grad_split = lax.map(attend_item_back, (heads_split, logsum, grad_context))
    grad_triple = grad_split.reshape(item_count, seq_len, 3, local_heads * HEAD).astype(
        jnp.bfloat16
    )
    grad_attend = jnp.einsum(
        "isd,iskc->dkc", mixed_low, grad_triple, preferred_element_type=jnp.float32
    )
    grad_mixed = narrow_sum(
        jnp.einsum("iskc,dkc->isd", grad_triple, attend_low, preferred_element_type=jnp.float32), 3
    )
    grad_tokens, grad_shift_one, grad_scale_one, grad_mixer_kernel = mixer_pull(grad_mixed)
    tokens_gradient = (grad_tokens + grad_hidden).astype(jnp.bfloat16)
    grad_table = jnp.sum(
        jnp.stack(
            [
                grad_shift_one[:, 0],
                grad_scale_one[:, 0],
                grad_gate_one,
                grad_shift_two[:, 0],
                grad_scale_two[:, 0],
                grad_gate_two,
            ],
            axis=1,
        ),
        axis=0,
    )
    width = tokens.shape[2]
    gradients = [grad_attend.reshape(width, -1), grad_output, grad_expand, grad_reduce]
    shares = [wide_scatter(gradient) for gradient in gradients]
    squares = sum(
        jnp.sum((share * share).reshape(-1, width), axis=0) for share in shares
    )
    shared_rows = grad_table.shape[0] + grad_mixer_kernel.shape[0]
    hidden_rows = -(-grad_hidden_kernel.size // width)
    padding = hidden_rows * width - grad_hidden_kernel.size
    hidden_flat = jnp.pad(grad_hidden_kernel.reshape(-1), (0, padding))
    stacked = jnp.concatenate(
        [grad_table, grad_mixer_kernel, hidden_flat.reshape(hidden_rows, width), squares[None]],
        axis=0,
    )
    stacked = jnp.pad(stacked, ((0, -stacked.shape[0] % 8), (0, 0)))
    small, norm = small_sums(stacked, shared_rows, hidden_rows, 4)
    gradient_norm = norm[0, 0]
    clip_factor = jnp.minimum(1.0, 1.0 / (gradient_norm + 1e-06))
    summed_table = small[: grad_table.shape[0]]
    summed_mixer = small[grad_table.shape[0] : shared_rows]
    summed_hidden = small[shared_rows : shared_rows + hidden_rows].reshape(-1)
    summed_hidden = summed_hidden[: hidden_kernel.size].reshape(hidden_kernel.shape)
    table_moment, table_square, table_result = adam_update(
        modulation_table, table_first, table_second, clip_factor * summed_table
    )
    mixer_moment, mixer_square, mixer_result = adam_update(
        mixer_kernel, mixer_first, mixer_second, clip_factor * summed_mixer
    )
    hidden_moment, hidden_square, hidden_result = adam_update(
        hidden_kernel, hidden_first, hidden_second, clip_factor * summed_hidden
    )
    moments = (attend_moment, output_moment, expand_moment, reduce_moment)
    carried = [
        muon_momentum * moment + clip_factor * wide_gather(share).reshape(moment.shape)
        for moment, share in zip(moments, shares)
    ]
    matrices = [carried[0].reshape(width, -1), carried[1], carried[2], carried[3]]
    layouts = ("columns", "rows", "columns", "rows")
    block_rows = width // lax.axis_size("wide")
    start = lax.axis_index("wide") * block_rows
    sub = lax.axis_size("narrow") // MATRICES
    partial = jnp.stack(
        [
            row_block_gram(matrix, layout, start, block_rows)
            for matrix, layout in zip(matrices, layouts)
        ]
    ).reshape(MATRICES * sub, block_rows // sub, width)
    factors = spread(polar_factor(gram_whole(partial, 5)), 6)
    polar_parts = [
        apply_factor(factors[position], matrix, layout)
        for position, (matrix, layout) in enumerate(zip(matrices, layouts))
    ]
    attend_result = muon_finish(attend_weight, polar_parts[0].reshape(attend_weight.shape), 3 * D)
    output_result = muon_finish(output_weight, polar_parts[1], D)
    expand_result = muon_finish(expand_weight, polar_parts[2], FF)
    reduce_result = muon_finish(reduce_weight, polar_parts[3], FF)
    return (
        block_out,
        tokens_gradient,
        gradient_norm,
        carried[0],
        carried[1],
        carried[2],
        carried[3],
        attend_result,
        output_result,
        expand_result,
        reduce_result,
        table_moment,
        table_square,
        table_result,
        mixer_moment,
        mixer_square,
        mixer_result,
        hidden_moment,
        hidden_square,
        hidden_result,
    )


def solution(mesh):
    placed = (
        P("wide", None, None),
        P("wide", None, None),
        P("wide"),
        P("wide", None, None),
        P(),
        P(),
        P(None, "narrow"),
        P(None, None, "narrow"),
        P("narrow", None),
        P(None, "narrow"),
        P("narrow", None),
        P(None, None, "narrow"),
        P("narrow", None),
        P(None, "narrow"),
        P("narrow", None),
        P(),
        P(),
        P(),
        P(),
        P(None, "narrow"),
        P(None, "narrow"),
    )
    return jax.shard_map(
        local,
        mesh=mesh,
        in_specs=placed,
        out_specs=(
            P("wide", None, None),
            P("wide", None, None),
            P(),
            P(None, None, "narrow"),
            P("narrow", None),
            P(None, "narrow"),
            P("narrow", None),
            P(None, None, "narrow"),
            P("narrow", None),
            P(None, "narrow"),
            P("narrow", None),
            P(),
            P(),
            P(),
            P(),
            P(),
            P(),
            P(None, "narrow"),
            P(None, "narrow"),
            P(None, "narrow"),
        ),
        check_vma=False,
    )
```

```python
import functools
import math

import jax
import jax.numpy as jnp
from jax import lax
from jax.experimental import pallas as pl
from jax.experimental.pallas import tpu as pltpu
from jax.sharding import PartitionSpec as P

D = 1024
HEAD = 64
FF = 4096
GRID = 32
NEWTON = 5
STEP = 10


first_decay = 0.9
second_decay = 0.999
adam_rate = 0.3
muon_rate = 0.15
muon_momentum = 0.5
weight_decay = 0.01
newton_terms = (3.4445, -4.775, 2.0315)
gelu_slope = 0.7978845608
gelu_cubic = 0.044715


def layer_norm(values):
    average = jnp.mean(values, axis=-1, keepdims=True)
    centred = values - average
    spread = jnp.mean(centred * centred, axis=-1, keepdims=True)
    return centred * lax.rsqrt(spread + 1e-06)


def gelu_tanh(values):
    return (
        0.5
        * values
        * (1.0 + jnp.tanh(gelu_slope * (values + gelu_cubic * values * values * values)))
    )


def depthwise(values, kernel):
    grid_side = GRID
    shaped = values.reshape(values.shape[0], grid_side, grid_side, values.shape[-1])
    padded = jnp.pad(shaped, ((0, 0), (1, 1), (1, 1), (0, 0)))
    summed = jnp.zeros_like(shaped)
    for tap_row in range(3):
        for tap_col in range(3):
            summed = (
                summed
                + kernel[tap_row * 3 + tap_col]
                * padded[:, tap_row : tap_row + grid_side, tap_col : tap_col + grid_side]
            )
    return summed.reshape(values.shape)


def mixer_piece(token_rows, offset, stretch, kernel):
    return depthwise(layer_norm(token_rows) * (1.0 + stretch) + offset, kernel)


def entry_piece(hidden, offset, stretch):
    return layer_norm(hidden) * (1.0 + stretch) + offset


def middle_piece(upward, kernel):
    return gelu_tanh(depthwise(upward, kernel))


def attend_forward(queries, key_rows, value_rows):
    seq_len = queries.shape[0]
    block_rows = min(512, seq_len)
    blocks = queries.reshape(seq_len // block_rows, block_rows, queries.shape[1], queries.shape[2])
    scale_factor = HEAD ** (-0.5)

    def one_block(query_block):
        scores = (
            jnp.einsum("qhe,khe->hqk", query_block, key_rows, preferred_element_type=jnp.float32)
            * scale_factor
        )
        row_peak = jnp.max(scores, axis=-1, keepdims=True)
        weights = jnp.exp(scores - row_peak)
        summed = jnp.sum(weights, axis=-1, keepdims=True)
        soft_low = (weights / summed).astype(jnp.bfloat16)
        context = jnp.einsum(
            "hqk,khe->qhe", soft_low, value_rows, preferred_element_type=jnp.float32
        )
        return (context.astype(jnp.bfloat16), (row_peak + jnp.log(summed))[:, :, 0])

    context, logsum = lax.map(one_block, blocks)
    return (context.reshape(seq_len, -1), logsum)


def attend_backward(queries, key_rows, value_rows, logsum, grad_context):
    seq_len = queries.shape[0]
    block_rows = min(512, seq_len)
    block_count = seq_len // block_rows
    query_blocks = queries.reshape(block_count, block_rows, queries.shape[1], queries.shape[2])
    grad_blocks = grad_context.reshape(block_count, block_rows, queries.shape[1], queries.shape[2])
    scale_factor = HEAD ** (-0.5)

    def one_block(running, pieces):
        grad_keys, grad_values = running
        query_block, grad_block, logsum_block = pieces
        scores = (
            jnp.einsum("qhe,khe->hqk", query_block, key_rows, preferred_element_type=jnp.float32)
            * scale_factor
        )
        weights = jnp.exp(scores - logsum_block[:, :, None])
        soft_low = weights.astype(jnp.bfloat16)
        grad_values = grad_values + jnp.einsum(
            "hqk,qhe->khe", soft_low, grad_block, preferred_element_type=jnp.float32
        )
        grad_weights = jnp.einsum(
            "qhe,khe->hqk", grad_block, value_rows, preferred_element_type=jnp.float32
        )
        grad_scores = weights * (
            grad_weights - jnp.sum(weights * grad_weights, axis=-1, keepdims=True)
        )
        grad_low = grad_scores.astype(jnp.bfloat16)
        grad_query = (
            jnp.einsum("hqk,khe->qhe", grad_low, key_rows, preferred_element_type=jnp.float32)
            * scale_factor
        )
        grad_keys = (
            grad_keys
            + jnp.einsum("hqk,qhe->khe", grad_low, query_block, preferred_element_type=jnp.float32)
            * scale_factor
        )
        return ((grad_keys, grad_values), grad_query)

    start_sums = jnp.zeros(key_rows.shape, jnp.float32)
    finals, grad_queries = lax.scan(
        one_block, (start_sums, start_sums), (query_blocks, grad_blocks, logsum)
    )
    grad_queries = grad_queries.reshape(key_rows.shape)
    return jnp.stack([grad_queries, finals[0], finals[1]], axis=1)


MESH = pl.DeviceIdType.MESH
BLK = 256
LANES = 128
MATRICES = 4


def partner(index, bit):
    return index + (1 - 2 * ((index // bit) % 2)) * bit


def bits_of(count):
    found = []
    bit = 1
    while bit < count:
        found.append(bit)
        bit *= 2
    return found


def place_at(axis, bit):
    place = {"wide": lax.axis_index("wide"), "narrow": lax.axis_index("narrow")}
    place[axis] = partner(place[axis], bit)
    return (place["wide"], place["narrow"])


def greet(places):
    barrier = pltpu.get_barrier_semaphore()
    for place in places:
        pl.semaphore_signal(barrier, inc=1, device_id=place, device_id_type=MESH)
    pl.semaphore_wait(barrier, len(places))


def send(src, dst, sends, arrivals, slot, place):
    copy = pltpu.make_async_remote_copy(
        src_ref=src,
        dst_ref=dst,
        send_sem=sends.at[slot],
        recv_sem=arrivals.at[slot],
        device_id=place,
        device_id_type=MESH,
    )
    copy.start()
    return copy


def narrow_sum_kernel(far_bits, pieces, x_ref, o_ref, near, far, held, sends, arrivals, local):
    rows = x_ref.shape[0] // 2
    step = rows // pieces
    core = lax.axis_index("narrow") % 2
    mine, theirs = core * rows, (1 - core) * rows
    near_place = place_at("narrow", 1)
    far_places = [place_at("narrow", bit) for bit in far_bits]
    greet([near_place] + far_places)
    block = lambda base, p: pl.ds(pl.multiple_of(base + p * step, 8), step)
    count = len(far_bits)
    first = [
        send(x_ref.at[block(theirs, p)], near.at[p], sends, arrivals, p, near_place)
        for p in range(pieces)
    ]
    loads = [
        pltpu.make_async_copy(x_ref.at[block(mine, p)], held.at[0, p], local.at[p])
        for p in range(pieces)
    ]
    for load in loads:
        load.start()
    crossings = [[None] * pieces for _ in range(count)]
    last = []
    for p in range(pieces):
        loads[p].wait()
        first[p].wait_recv()
        held[0, p] = held[0, p] + near[p]
        crossings[0][p] = send(
            held.at[0, p], far.at[0, p], sends, arrivals, pieces + p, far_places[0]
        )
    for b in range(count):
        for p in range(pieces):
            crossings[b][p].wait_recv()
            held[b + 1, p] = held[b, p] + far[b, p]
            if b + 1 < count:
                crossings[b + 1][p] = send(
                    held.at[b + 1, p],
                    far.at[b + 1, p],
                    sends,
                    arrivals,
                    (b + 2) * pieces + p,
                    far_places[b + 1],
                )
            else:
                last.append(
                    send(
                        held.at[count, p],
                        o_ref.at[block(mine, p)],
                        sends,
                        arrivals,
                        (count + 1) * pieces + p,
                        near_place,
                    )
                )
    keeps = [
        pltpu.make_async_copy(held.at[count, p], o_ref.at[block(mine, p)], local.at[p])
        for p in range(pieces)
    ]
    for keep in keeps:
        keep.start()
    for copy in first:
        copy.wait_send()
    for row in crossings:
        for copy in row:
            copy.wait_send()
    for copy in last:
        copy.wait()
    for keep in keeps:
        keep.wait()


def narrow_sum(values, number):
    far_bits = bits_of(lax.axis_size("narrow"))[1:]
    count = len(far_bits)
    pieces = 4
    shape = values.shape
    flat = values.reshape(-1, shape[-1])
    step = flat.shape[0] // (2 * pieces)
    slots = (count + 2) * pieces
    total = pl.pallas_call(
        functools.partial(narrow_sum_kernel, far_bits, pieces),
        out_shape=jax.ShapeDtypeStruct(flat.shape, jnp.float32),
        in_specs=[pl.BlockSpec(memory_space=pl.ANY)],
        out_specs=pl.BlockSpec(memory_space=pl.ANY),
        scratch_shapes=[
            pltpu.VMEM((pieces, step, flat.shape[1]), jnp.float32),
            pltpu.VMEM((count, pieces, step, flat.shape[1]), jnp.float32),
            pltpu.VMEM((count + 1, pieces, step, flat.shape[1]), jnp.float32),
            pltpu.SemaphoreType.DMA((slots,)),
            pltpu.SemaphoreType.DMA((slots,)),
            pltpu.SemaphoreType.DMA((pieces,)),
        ],
        compiler_params=pltpu.CompilerParams(
            collective_id=number, has_side_effects=True, vmem_limit_bytes=32 * 2**20
        ),
        cost_estimate=pl.CostEstimate(
            flops=flat.size, bytes_accessed=flat.size * 32, transcendentals=0
        ),
    )(flat)
    return total.reshape(shape)


def core_scatter(values):
    rows = values.shape[0] // 2
    side = lax.axis_index("narrow") % 2
    give = lax.dynamic_slice_in_dim(values, (1 - side) * rows, rows, 0)
    keep = lax.dynamic_slice_in_dim(values, side * rows, rows, 0)
    return keep, permute(give, "narrow", 1)


def core_place(half, other):
    side = lax.axis_index("narrow") % 2
    return jnp.where(
        side == 0,
        jnp.concatenate([half, other], axis=0),
        jnp.concatenate([other, half], axis=0),
    )


def small_kernel(
    wide_bits,
    narrow_bits,
    shared_rows,
    split_rows,
    x_ref,
    o_ref,
    norm_ref,
    slots,
    sends,
    arrivals,
    spare,
    spare_in,
):
    wide_places = [place_at("wide", bit) for bit in wide_bits]
    narrow_places = [place_at("narrow", bit) for bit in narrow_bits]
    greet(wide_places + narrow_places)
    count = len(wide_bits)
    copies = []
    slots[0] = x_ref[...]
    for b in range(count):
        copy = send(slots.at[b], slots.at[count + 1 + b], sends, arrivals, b, wide_places[b])
        copies.append(copy)
        copy.wait_recv()
        slots[b + 1] = slots[b] + slots[count + 1 + b]
    total = slots[count]
    o_ref[...] = total
    shared_part = total[:shared_rows]
    split_part = total[shared_rows : shared_rows + split_rows]
    shared = jnp.sum(shared_part * shared_part)
    split_sum = jnp.sum(split_part * split_part) + jnp.sum(
        total[shared_rows + split_rows : shared_rows + split_rows + 1]
    )
    spare[0] = jnp.full(spare.shape[1:], split_sum, jnp.float32)
    for b in range(len(narrow_bits)):
        copy = send(spare.at[b], spare_in.at[b], sends, arrivals, count + b, narrow_places[b])
        copies.append(copy)
        copy.wait_recv()
        spare[b + 1] = spare[b] + spare_in[b]
    norm_ref[...] = jnp.sqrt(spare[len(narrow_bits)] + shared)
    for copy in copies:
        copy.wait_send()


def small_sums(stacked, shared_rows, split_rows, number):
    wide_bits = bits_of(lax.axis_size("wide"))
    narrow_bits = bits_of(lax.axis_size("narrow"))
    vmem = pl.BlockSpec(memory_space=pltpu.VMEM)
    count = len(wide_bits)
    total = count + len(narrow_bits)
    return pl.pallas_call(
        functools.partial(small_kernel, wide_bits, narrow_bits, shared_rows, split_rows),
        out_shape=(
            jax.ShapeDtypeStruct(stacked.shape, jnp.float32),
            jax.ShapeDtypeStruct((8, LANES), jnp.float32),
        ),
        in_specs=[vmem],
        out_specs=(vmem, vmem),
        scratch_shapes=[
            pltpu.VMEM((2 * count + 1,) + stacked.shape, jnp.float32),
            pltpu.SemaphoreType.DMA((total,)),
            pltpu.SemaphoreType.DMA((total,)),
            pltpu.VMEM((len(narrow_bits) + 1, 8, LANES), jnp.float32),
            pltpu.VMEM((len(narrow_bits), 8, LANES), jnp.float32),
        ],
        compiler_params=pltpu.CompilerParams(
            collective_id=number, has_side_effects=True, vmem_limit_bytes=16 * 2**20
        ),
    )(stacked)


def permute(values, axis, bit):
    size = lax.axis_size(axis)
    return lax.ppermute(values, axis, [(index, index ^ bit) for index in range(size)])


def together(*values):
    return lax.optimization_barrier(values)


def pair_scatter(values):
    rows = values.shape[0] // 2
    side = lax.axis_index("wide") % 2
    give = lax.dynamic_slice_in_dim(values, (1 - side) * rows, rows, 0)
    keep = lax.dynamic_slice_in_dim(values, side * rows, rows, 0)
    return keep, permute(give, "wide", 1)


def line_scatter(values):
    count = lax.axis_size("wide") // 2
    rows = values.shape[0] // count
    place = lax.axis_index("wide") // 2
    keep = lax.dynamic_slice_in_dim(values, place * rows, rows, 0)
    arrived = []
    for offset in range(1, count):
        give = lax.dynamic_slice_in_dim(values, (place ^ offset) * rows, rows, 0)
        arrived.append(permute(give, "wide", 2 * offset))
    return keep, arrived


def line_gather(share):
    count = lax.axis_size("wide") // 2
    return [permute(share, "wide", 2 * offset) for offset in range(1, count)]


def line_place(share, arrived):
    count = lax.axis_size("wide") // 2
    rows = share.shape[0]
    place = lax.axis_index("wide") // 2
    whole = jnp.zeros((count * rows,) + share.shape[1:], share.dtype)
    whole = lax.dynamic_update_slice_in_dim(whole, share, place * rows, 0)
    for offset, piece in zip(range(1, count), arrived):
        whole = lax.dynamic_update_slice_in_dim(whole, piece, (place ^ offset) * rows, 0)
    return whole


def pair_place(half, other):
    side = lax.axis_index("wide") % 2
    return jnp.where(
        side == 0,
        jnp.concatenate([half, other], axis=0),
        jnp.concatenate([other, half], axis=0),
    )


def gram_kernel(narrow_bits, gathers, x_ref, o_ref, halves, inbox, sends, arrivals, local):
    parts, rows = x_ref.shape[0], x_ref.shape[1]
    sub = parts // MATRICES
    w, n = lax.axis_index("wide"), lax.axis_index("narrow")
    places = {}
    for axis, bit in [("narrow", bit) for bit in narrow_bits] + gathers:
        places[(axis, bit)] = place_at(axis, bit)
    greet(list(places.values()))
    load = pltpu.make_async_copy(x_ref, halves, local.at[0])
    load.start()
    load.wait()
    base = 0 * n
    size, at, slot = parts, 0, 0
    for bit in reversed(narrow_bits):
        size //= 2
        side = (n // bit) % 2
        copy = send(
            halves.at[pl.ds(base + (1 - side) * size, size)],
            inbox.at[pl.ds(at, size)],
            sends,
            arrivals,
            slot,
            places[("narrow", bit)],
        )
        base = base + side * size
        copy.wait()
        for s in range(size):
            halves[base + s] = halves[base + s] + inbox[at + s]
        at += size
        slot += 1

    def rows_of(item):
        big, small = w, n % sub
        for index, (axis, bit) in enumerate(gathers):
            if (item >> index) % 2:
                if axis == "wide":
                    big = partner(big, bit)
                else:
                    small = partner(small, bit)
        return pl.ds(pl.multiple_of((big * sub + small) * rows, 8), rows)

    keep = pltpu.make_async_copy(halves.at[n], o_ref.at[rows_of(0)], local.at[0])
    keep.start()
    copies = {}
    order = sorted(range(2 ** len(gathers)), key=lambda item: (bin(item).count("1"), item))
    for item in order:
        if item:
            copies[item].wait_recv()
        for index in reversed(range(item.bit_length(), len(gathers))):
            later = item + 2**index
            src = o_ref.at[rows_of(item)] if item else halves.at[n]
            copies[later] = send(
                src, o_ref.at[rows_of(item)], sends, arrivals, slot + later - 1, places[gathers[index]]
            )
    keep.wait()
    for copy in copies.values():
        copy.wait_send()


def gram_whole(partial, number):
    narrow_bits = bits_of(lax.axis_size("narrow"))
    wide_bits = bits_of(lax.axis_size("wide"))
    parts, rows, width = partial.shape
    sub = parts // MATRICES
    gathers = [("narrow", bit) for bit in bits_of(sub)]
    gathers += [("wide", bit) for bit in reversed(wide_bits)]
    slots = len(narrow_bits) + 2 ** len(gathers) - 1
    return pl.pallas_call(
        functools.partial(gram_kernel, narrow_bits, gathers),
        out_shape=jax.ShapeDtypeStruct((width, width), jnp.float32),
        in_specs=[pl.BlockSpec(memory_space=pl.ANY)],
        out_specs=pl.BlockSpec(memory_space=pl.ANY),
        scratch_shapes=[
            pltpu.VMEM(partial.shape, jnp.float32),
            pltpu.VMEM(partial.shape, jnp.float32),
            pltpu.SemaphoreType.DMA((slots,)),
            pltpu.SemaphoreType.DMA((slots,)),
            pltpu.SemaphoreType.DMA((1,)),
        ],
        compiler_params=pltpu.CompilerParams(
            collective_id=number, has_side_effects=True, vmem_limit_bytes=16 * 2**20
        ),
    )(partial)


def split(values):
    high = values.astype(jnp.bfloat16)
    return high, (values - high.astype(jnp.float32)).astype(jnp.bfloat16)


def product(left_high, left_low, right_high, right_low):
    dot = functools.partial(jnp.dot, preferred_element_type=jnp.float32)
    return dot(left_high, right_high) + (dot(left_high, right_low) + dot(left_low, right_high))


def polar_kernel(g_ref, q_ref, gh, gl, ph, pw, th, tl):
    size = g_ref.shape[0]
    blocks = size // BLK
    first, second, third = newton_terms
    rows = lambda block: pl.ds(block * BLK, BLK)
    square = (BLK, BLK)
    unit = (
        lax.broadcasted_iota(jnp.int32, square, 0) == lax.broadcasted_iota(jnp.int32, square, 1)
    ).astype(jnp.float32)
    trace = jnp.zeros((), jnp.float32)
    for i in range(blocks):
        trace = trace + jnp.sum(g_ref[rows(i), rows(i)] * unit)
    factor = 1.0 / (jnp.sqrt(trace) + 1e-07)
    for i in range(blocks):
        gh[rows(i), :], gl[rows(i), :] = split(g_ref[rows(i), :] * (factor * factor))

    def put(high, low, i, j, values):
        high[rows(i), rows(j)], low[rows(i), rows(j)] = split(values)
        if i != j:
            high[rows(j), rows(i)], low[rows(j), rows(i)] = split(values.T)

    def symmetric(left, right, emit):
        for i in range(blocks):
            columns = pl.ds(i * BLK, size - i * BLK)
            values = product(
                left[0][rows(i), :], left[1][rows(i), :], right[0][:, columns], right[1][:, columns]
            )
            for j in range(i, blocks):
                emit(i, j, values[:, (j - i) * BLK : (j - i + 1) * BLK])

    def emit_terms(i, j, values):
        gram = gh[rows(i), rows(j)].astype(jnp.float32) + gl[rows(i), rows(j)].astype(jnp.float32)
        terms = second * gram + third * values
        if i == j:
            terms = terms + first * unit
        put(ph, pw, i, j, terms)

    def emit_total(i, j, values):
        q_ref[rows(i), rows(j)] = values
        if i != j:
            q_ref[rows(j), rows(i)] = values.T

    symmetric((gh, gl), (gh, gl), emit_terms)
    for i in range(blocks):
        q_ref[rows(i), :] = (
            ph[rows(i), :].astype(jnp.float32) + pw[rows(i), :].astype(jnp.float32)
        ) * factor

    def one_step(step, carry):
        symmetric((ph, pw), (gh, gl), functools.partial(put, th, tl))
        symmetric((th, tl), (ph, pw), functools.partial(put, gh, gl))
        symmetric((gh, gl), (gh, gl), emit_terms)
        for i in range(blocks):
            th[rows(i), :], tl[rows(i), :] = split(q_ref[rows(i), :])
        symmetric((ph, pw), (th, tl), emit_total)
        return carry

    lax.fori_loop(0, NEWTON - 1, one_step, 0)


def polar_factor(gramian):
    size = gramian.shape[0]
    vmem = pl.BlockSpec(memory_space=pltpu.VMEM)
    return pl.pallas_call(
        polar_kernel,
        out_shape=jax.ShapeDtypeStruct((size, size), jnp.float32),
        in_specs=[vmem],
        out_specs=vmem,
        scratch_shapes=[pltpu.VMEM((size, size), jnp.bfloat16)] * 6,
        compiler_params=pltpu.CompilerParams(vmem_limit_bytes=48 * 2**20),
        cost_estimate=pl.CostEstimate(
            flops=17 * 6 * size**3, bytes_accessed=8 * size * size, transcendentals=0
        ),
    )(gramian)


def spread_kernel(sub, pieces, q_ref, o_ref, sends, arrivals, local):
    size = q_ref.shape[0]
    half = size // 2
    step = half // pieces
    w, n = lax.axis_index("wide"), lax.axis_index("narrow")
    own = n // sub
    across = partner(own, 2)
    near_place, far_place = place_at("narrow", sub), place_at("narrow", 2 * sub)
    side_place = place_at("wide", 1)
    greet([near_place, far_place, side_place])
    top = w % 2
    rows = lambda side, p: pl.ds(pl.multiple_of(side * half + p * step, 8), step)
    keep = pltpu.make_async_copy(q_ref, o_ref.at[own], local.at[0])
    keep.start()
    copies = []

    def push(src, dst, place):
        copies.append(send(src, dst, sends, arrivals, len(copies), place))
        return copies[-1]

    cross = lambda p: push(q_ref.at[rows(top, p)], o_ref.at[own, rows(top, p)], far_place)
    crossing = [cross(p) for p in range(2)]
    landing = [push(q_ref, o_ref.at[own], near_place)]
    aside = []
    for p in range(pieces):
        crossing[p].wait()
        if p + 2 < pieces:
            crossing.append(cross(p + 2))
        if p >= 2:
            aside[p - 2].wait()
        spot = o_ref.at[across, rows(top, p)]
        aside.append(push(spot, spot, side_place))
        landing.append(push(spot, spot, near_place))
        if p >= 2:
            spot = o_ref.at[across, rows(1 - top, p - 2)]
            landing.append(push(spot, spot, near_place))
    for p in range(pieces - 2, pieces):
        aside[p].wait()
        spot = o_ref.at[across, rows(1 - top, p)]
        landing.append(push(spot, spot, near_place))
    keep.wait()
    for copy in landing:
        copy.wait_send()
    for copy in landing:
        copy.wait_recv()


def spread(factor, number):
    size = factor.shape[0]
    pieces = 8
    slots = 1 + 4 * pieces
    sub = lax.axis_size("narrow") // MATRICES
    return pl.pallas_call(
        functools.partial(spread_kernel, sub, pieces),
        out_shape=jax.ShapeDtypeStruct((MATRICES, size, size), jnp.float32),
        in_specs=[pl.BlockSpec(memory_space=pltpu.VMEM)],
        out_specs=pl.BlockSpec(memory_space=pl.ANY),
        scratch_shapes=[
            pltpu.SemaphoreType.DMA((slots,)),
            pltpu.SemaphoreType.DMA((slots,)),
            pltpu.SemaphoreType.DMA((1,)),
        ],
        compiler_params=pltpu.CompilerParams(collective_id=number, has_side_effects=True),
    )(factor)


def adam_update(weight, moment, square, gradient):
    moment_new = first_decay * moment + (1.0 - first_decay) * gradient
    square_new = second_decay * square + (1.0 - second_decay) * gradient * gradient
    moment_hat = moment_new / (1.0 - first_decay**STEP)
    square_hat = square_new / (1.0 - second_decay**STEP)
    weight_new = weight * (1.0 - adam_rate * weight_decay) - adam_rate * moment_hat / (
        jnp.sqrt(square_hat) + 1e-08
    )
    return (moment_new, square_new, weight_new)


def muon_finish(weight, polar_part, longest):
    return (
        weight * (1.0 - muon_rate * weight_decay)
        - muon_rate * 0.2 * math.sqrt(longest) * polar_part
    )


def row_block_gram(matrix, layout, start, count):
    axis = 0 if layout == "columns" else 1
    block = lax.dynamic_slice_in_dim(matrix, start, count, axis)
    return lax.dot_general(
        block,
        matrix,
        (((1 - axis,), (1 - axis,)), ((), ())),
        precision=lax.Precision.HIGH,
        preferred_element_type=jnp.float32,
    )


def apply_factor(factor, matrix, layout):
    left, right = (factor, matrix) if layout == "columns" else (matrix, factor)
    return jnp.dot(
        left, right, precision=lax.Precision.HIGH, preferred_element_type=jnp.float32
    )


def local(
    tokens,
    conditions,
    item_live,
    cotangent,
    modulation_table,
    mixer_kernel,
    hidden_kernel,
    attend_weight,
    output_weight,
    expand_weight,
    reduce_weight,
    attend_moment,
    output_moment,
    expand_moment,
    reduce_moment,
    table_first,
    table_second,
    mixer_first,
    mixer_second,
    hidden_first,
    hidden_second,
):
    item_count = tokens.shape[0]
    seq_len = tokens.shape[1]
    local_heads = attend_weight.shape[2] // HEAD
    live_mask = item_live.astype(jnp.float32)[:, None, None]
    token_rows = tokens.astype(jnp.float32)
    modulation = modulation_table[None] + conditions
    shift_one = modulation[:, 0:1]
    scale_one = modulation[:, 1:2]
    gate_one = modulation[:, 2:3]
    shift_two = modulation[:, 3:4]
    scale_two = modulation[:, 4:5]
    gate_two = modulation[:, 5:6]
    mixed_rows, mixer_pull = jax.vjp(mixer_piece, token_rows, shift_one, scale_one, mixer_kernel)
    mixed_low = mixed_rows.astype(jnp.bfloat16)
    attend_low = attend_weight.astype(jnp.bfloat16)
    triple = jnp.einsum(
        "isd,dkc->iskc", mixed_low, attend_low, preferred_element_type=jnp.float32
    ).astype(jnp.bfloat16)
    heads_split = triple.reshape(item_count, seq_len, 3, local_heads, HEAD)

    def attend_item(member):
        return attend_forward(member[:, 0], member[:, 1], member[:, 2])

    context, logsum = lax.map(attend_item, heads_split)
    output_low = output_weight.astype(jnp.bfloat16)
    branch = narrow_sum(
        jnp.einsum("isc,cd->isd", context, output_low, preferred_element_type=jnp.float32), 1
    )
    hidden = token_rows + gate_one * branch
    expand_entry, entry_pull = jax.vjp(entry_piece, hidden, shift_two, scale_two)
    entry_low = expand_entry.astype(jnp.bfloat16)
    expand_low = expand_weight.astype(jnp.bfloat16)
    upward = jnp.einsum("isd,df->isf", entry_low, expand_low, preferred_element_type=jnp.float32)
    activated, middle_pull = jax.vjp(middle_piece, upward, hidden_kernel)
    activated_low = activated.astype(jnp.bfloat16)
    reduce_low = reduce_weight.astype(jnp.bfloat16)
    ffn_partial = jnp.einsum(
        "isf,fd->isd", activated_low, reduce_low, preferred_element_type=jnp.float32
    )
    ffn_keep, ffn_other = core_scatter(ffn_partial.reshape(-1, ffn_partial.shape[-1]))
    grad_result = cotangent.astype(jnp.float32) * live_mask
    grad_ffn_low = (gate_two * grad_result).astype(jnp.bfloat16)
    grad_reduce = jnp.einsum(
        "isf,isd->fd", activated_low, grad_ffn_low, preferred_element_type=jnp.float32
    )
    reduce_keep, reduce_other = pair_scatter(grad_reduce)
    grad_activated = jnp.einsum(
        "isd,fd->isf", grad_ffn_low, reduce_low, preferred_element_type=jnp.float32
    )
    grad_upward, grad_hidden_kernel = middle_pull(grad_activated)
    grad_up_low = grad_upward.astype(jnp.bfloat16)
    grad_expand = jnp.einsum(
        "isd,isf->df", entry_low, grad_up_low, preferred_element_type=jnp.float32
    )
    reduce_other, ffn_other, grad_up_low = together(reduce_other, ffn_other, grad_up_low)
    reduce_half = reduce_keep + reduce_other
    ffn_half = ffn_keep + ffn_other
    reduce_half, ffn_half, grad_up_low = together(reduce_half, ffn_half, grad_up_low)
    reduce_keep, reduce_pieces = line_scatter(reduce_half)
    expand_keep, expand_other = pair_scatter(grad_expand)
    grad_entry = narrow_sum(
        jnp.einsum("isf,df->isd", grad_up_low, expand_low, preferred_element_type=jnp.float32), 2
    )
    *reduce_pieces, expand_other, ffn_half, grad_entry = together(
        *reduce_pieces, expand_other, ffn_half, grad_entry
    )
    reduce_share = reduce_keep + sum(reduce_pieces)
    expand_half = expand_keep + expand_other
    reduce_share, expand_half, grad_entry = together(reduce_share, expand_half, grad_entry)
    reduce_pieces = line_gather(reduce_share)
    expand_keep, expand_pieces = line_scatter(expand_half)
    ffn_across = [permute(ffn_half, "narrow", bit) for bit in bits_of(lax.axis_size("narrow"))[1:2]]
    grad_hidden, grad_shift_two, grad_scale_two = entry_pull(grad_entry)
    grad_hidden = grad_hidden + grad_result
    grad_gate_one = jnp.sum(branch * grad_hidden, axis=1)
    grad_branch_low = (gate_one * grad_hidden).astype(jnp.bfloat16)
    grad_output = jnp.einsum(
        "isc,isd->cd", context, grad_branch_low, preferred_element_type=jnp.float32
    )
    grad_context = jnp.einsum(
        "isd,cd->isc", grad_branch_low, output_low, preferred_element_type=jnp.float32
    ).astype(jnp.bfloat16)

    def attend_item_back(pieces):
        member, logsum_item, grad_item = pieces
        return attend_backward(
            member[:, 0],
            member[:, 1],
            member[:, 2],
            logsum_item,
            grad_item.reshape(seq_len, local_heads, HEAD),
        )

    grad_split = lax.map(attend_item_back, (heads_split, logsum, grad_context))
    grad_triple = grad_split.reshape(item_count, seq_len, 3, local_heads * HEAD).astype(
        jnp.bfloat16
    )
    output_keep, output_other = pair_scatter(grad_output)
    *pieces, ffn_crossed, output_other, grad_triple = together(
        *reduce_pieces, *expand_pieces, ffn_across[0], output_other, grad_triple
    )
    reduce_pieces, expand_pieces = pieces[: len(reduce_pieces)], pieces[len(reduce_pieces) :]
    ffn_half = ffn_half + ffn_crossed
    for bit in bits_of(lax.axis_size("narrow"))[2:]:
        ffn_half = ffn_half + permute(ffn_half, "narrow", bit)
    reduce_line = line_place(reduce_share, reduce_pieces)
    expand_share = expand_keep + sum(expand_pieces)
    output_half = output_keep + output_other
    ffn_half, reduce_line, expand_share, output_half, grad_triple = together(
        ffn_half, reduce_line, expand_share, output_half, grad_triple
    )
    ffn_other = permute(ffn_half, "narrow", 1)
    reduce_other = permute(reduce_line, "wide", 1)
    expand_pieces = line_gather(expand_share)
    output_keep, output_pieces = line_scatter(output_half)
    grad_attend = jnp.einsum(
        "isd,iskc->dkc", mixed_low, grad_triple, preferred_element_type=jnp.float32
    )
    width = tokens.shape[2]
    attend_keep, attend_other = pair_scatter(grad_attend.reshape(width, -1))
    grad_mixed = narrow_sum(
        jnp.einsum("iskc,dkc->isd", grad_triple, attend_low, preferred_element_type=jnp.float32), 3
    )
    *expand_pieces, ffn_other, attend_other, grad_mixed = together(
        *expand_pieces, ffn_other, attend_other, grad_mixed
    )
    expand_line = line_place(expand_share, expand_pieces)
    attend_half = attend_keep + attend_other
    expand_line, attend_half, grad_mixed = together(expand_line, attend_half, grad_mixed)
    expand_other = permute(expand_line, "wide", 1)
    attend_keep, attend_pieces = line_scatter(attend_half)
    ffn_branch = core_place(ffn_half, ffn_other).reshape(ffn_partial.shape)
    block_out = (live_mask * (hidden + gate_two * ffn_branch)).astype(jnp.bfloat16)
    grad_gate_two = jnp.sum(ffn_branch * grad_result, axis=1)
    grad_tokens, grad_shift_one, grad_scale_one, grad_mixer_kernel = mixer_pull(grad_mixed)
    tokens_gradient = (grad_tokens + grad_hidden).astype(jnp.bfloat16)
    grad_table = jnp.sum(
        jnp.stack(
            [
                grad_shift_one[:, 0],
                grad_scale_one[:, 0],
                grad_gate_one,
                grad_shift_two[:, 0],
                grad_scale_two[:, 0],
                grad_gate_two,
            ],
            axis=1,
        ),
        axis=0,
    )
    *pieces, grad_table = together(*attend_pieces, *output_pieces, grad_table)
    attend_pieces, output_pieces = pieces[: len(attend_pieces)], pieces[len(attend_pieces) :]
    attend_share = attend_keep + sum(attend_pieces)
    output_share = output_keep + sum(output_pieces)
    attend_pieces = line_gather(attend_share)
    output_pieces = line_gather(output_share)
    shares = [attend_share, output_share, expand_share, reduce_share]
    squares = sum(
        jnp.sum((share * share).reshape(-1, width), axis=0) for share in shares
    )
    shared_rows = grad_table.shape[0] + grad_mixer_kernel.shape[0]
    hidden_rows = -(-grad_hidden_kernel.size // width)
    padding = hidden_rows * width - grad_hidden_kernel.size
    hidden_flat = jnp.pad(grad_hidden_kernel.reshape(-1), (0, padding))
    stacked = jnp.concatenate(
        [grad_table, grad_mixer_kernel, hidden_flat.reshape(hidden_rows, width), squares[None]],
        axis=0,
    )
    stacked = jnp.pad(stacked, ((0, -stacked.shape[0] % 8), (0, 0)))
    small, norm = small_sums(stacked, shared_rows, hidden_rows, 4)
    summed_table = small[: grad_table.shape[0]]
    summed_mixer = small[grad_table.shape[0] : shared_rows]
    summed_hidden = small[shared_rows : shared_rows + hidden_rows].reshape(-1)
    summed_hidden = summed_hidden[: hidden_kernel.size].reshape(hidden_kernel.shape)
    moments = (attend_moment, output_moment, expand_moment, reduce_moment)
    *pieces, reduce_other, expand_other, norm = together(
        *attend_pieces, *output_pieces, reduce_other, expand_other, norm
    )
    gradient_norm = norm[0, 0]
    clip_factor = jnp.minimum(1.0, 1.0 / (gradient_norm + 1e-06))
    attend_pieces, output_pieces = pieces[: len(attend_pieces)], pieces[len(attend_pieces) :]
    attend_line = line_place(attend_share, attend_pieces)
    output_line = line_place(output_share, output_pieces)
    gathered = [
        pair_place(attend_line, permute(attend_line, "wide", 1)),
        pair_place(output_line, permute(output_line, "wide", 1)),
        pair_place(expand_line, expand_other),
        pair_place(reduce_line, reduce_other),
    ]
    carried = [
        muon_momentum * moment + clip_factor * gradient.reshape(moment.shape)
        for moment, gradient in zip(moments, gathered)
    ]
    table_moment, table_square, table_result = adam_update(
        modulation_table, table_first, table_second, clip_factor * summed_table
    )
    mixer_moment, mixer_square, mixer_result = adam_update(
        mixer_kernel, mixer_first, mixer_second, clip_factor * summed_mixer
    )
    hidden_moment, hidden_square, hidden_result = adam_update(
        hidden_kernel, hidden_first, hidden_second, clip_factor * summed_hidden
    )
    matrices = [carried[0].reshape(width, -1), carried[1], carried[2], carried[3]]
    layouts = ("columns", "rows", "columns", "rows")
    block_rows = width // lax.axis_size("wide")
    start = lax.axis_index("wide") * block_rows
    sub = lax.axis_size("narrow") // MATRICES
    partial = jnp.stack(
        [
            row_block_gram(matrix, layout, start, block_rows)
            for matrix, layout in zip(matrices, layouts)
        ]
    ).reshape(MATRICES * sub, block_rows // sub, width)
    factors = spread(polar_factor(gram_whole(partial, 5)), 6)
    polar_parts = [
        apply_factor(factors[position], matrix, layout)
        for position, (matrix, layout) in enumerate(zip(matrices, layouts))
    ]
    attend_result = muon_finish(attend_weight, polar_parts[0].reshape(attend_weight.shape), 3 * D)
    output_result = muon_finish(output_weight, polar_parts[1], D)
    expand_result = muon_finish(expand_weight, polar_parts[2], FF)
    reduce_result = muon_finish(reduce_weight, polar_parts[3], FF)
    return (
        block_out,
        tokens_gradient,
        gradient_norm,
        carried[0],
        carried[1],
        carried[2],
        carried[3],
        attend_result,
        output_result,
        expand_result,
        reduce_result,
        table_moment,
        table_square,
        table_result,
        mixer_moment,
        mixer_square,
        mixer_result,
        hidden_moment,
        hidden_square,
        hidden_result,
    )


def solution(mesh):
    placed = (
        P("wide", None, None),
        P("wide", None, None),
        P("wide"),
        P("wide", None, None),
        P(),
        P(),
        P(None, "narrow"),
        P(None, None, "narrow"),
        P("narrow", None),
        P(None, "narrow"),
        P("narrow", None),
        P(None, None, "narrow"),
        P("narrow", None),
        P(None, "narrow"),
        P("narrow", None),
        P(),
        P(),
        P(),
        P(),
        P(None, "narrow"),
        P(None, "narrow"),
    )
    return jax.shard_map(
        local,
        mesh=mesh,
        in_specs=placed,
        out_specs=(
            P("wide", None, None),
            P("wide", None, None),
            P(),
            P(None, None, "narrow"),
            P("narrow", None),
            P(None, "narrow"),
            P("narrow", None),
            P(None, None, "narrow"),
            P("narrow", None),
            P(None, "narrow"),
            P("narrow", None),
            P(),
            P(),
            P(),
            P(),
            P(),
            P(),
            P(None, "narrow"),
            P(None, "narrow"),
            P(None, "narrow"),
        ),
        check_vma=False,
    )
```

```python
import functools
import math

import jax
import jax.numpy as jnp
from jax import lax
from jax.experimental import pallas as pl
from jax.experimental.pallas import tpu as pltpu
from jax.sharding import PartitionSpec as P

D = 1024
HEAD = 64
FF = 4096
GRID = 32
NEWTON = 5
STEP = 10


first_decay = 0.9
second_decay = 0.999
adam_rate = 0.3
muon_rate = 0.15
muon_momentum = 0.5
weight_decay = 0.01
newton_terms = (3.4445, -4.775, 2.0315)
gelu_slope = 0.7978845608
gelu_cubic = 0.044715


def layer_norm(values):
    average = jnp.mean(values, axis=-1, keepdims=True)
    centred = values - average
    spread = jnp.mean(centred * centred, axis=-1, keepdims=True)
    return centred * lax.rsqrt(spread + 1e-06)


def entry_piece(hidden, offset, stretch):
    return layer_norm(hidden) * (1.0 + stretch) + offset


def attend_forward(queries, key_rows, value_rows):
    seq_len = queries.shape[0]
    block_rows = min(512, seq_len)
    blocks = queries.reshape(seq_len // block_rows, block_rows, queries.shape[1], queries.shape[2])
    scale_factor = HEAD ** (-0.5)

    def one_block(query_block):
        scores = (
            jnp.einsum("qhe,khe->hqk", query_block, key_rows, preferred_element_type=jnp.float32)
            * scale_factor
        )
        row_peak = jnp.max(scores, axis=-1, keepdims=True)
        weights = jnp.exp(scores - row_peak)
        summed = jnp.sum(weights, axis=-1, keepdims=True)
        soft_low = (weights / summed).astype(jnp.bfloat16)
        context = jnp.einsum(
            "hqk,khe->qhe", soft_low, value_rows, preferred_element_type=jnp.float32
        )
        return (context.astype(jnp.bfloat16), (row_peak + jnp.log(summed))[:, :, 0])

    context, logsum = lax.map(one_block, blocks)
    return (context.reshape(seq_len, -1), logsum)


def attend_backward(queries, key_rows, value_rows, logsum, grad_context):
    seq_len = queries.shape[0]
    block_rows = min(512, seq_len)
    block_count = seq_len // block_rows
    query_blocks = queries.reshape(block_count, block_rows, queries.shape[1], queries.shape[2])
    grad_blocks = grad_context.reshape(block_count, block_rows, queries.shape[1], queries.shape[2])
    scale_factor = HEAD ** (-0.5)

    def one_block(running, pieces):
        grad_keys, grad_values = running
        query_block, grad_block, logsum_block = pieces
        scores = (
            jnp.einsum("qhe,khe->hqk", query_block, key_rows, preferred_element_type=jnp.float32)
            * scale_factor
        )
        weights = jnp.exp(scores - logsum_block[:, :, None])
        soft_low = weights.astype(jnp.bfloat16)
        grad_values = grad_values + jnp.einsum(
            "hqk,qhe->khe", soft_low, grad_block, preferred_element_type=jnp.float32
        )
        grad_weights = jnp.einsum(
            "qhe,khe->hqk", grad_block, value_rows, preferred_element_type=jnp.float32
        )
        grad_scores = weights * (
            grad_weights - jnp.sum(weights * grad_weights, axis=-1, keepdims=True)
        )
        grad_low = grad_scores.astype(jnp.bfloat16)
        grad_query = (
            jnp.einsum("hqk,khe->qhe", grad_low, key_rows, preferred_element_type=jnp.float32)
            * scale_factor
        )
        grad_keys = (
            grad_keys
            + jnp.einsum("hqk,qhe->khe", grad_low, query_block, preferred_element_type=jnp.float32)
            * scale_factor
        )
        return ((grad_keys, grad_values), grad_query)

    start_sums = jnp.zeros(key_rows.shape, jnp.float32)
    finals, grad_queries = lax.scan(
        one_block, (start_sums, start_sums), (query_blocks, grad_blocks, logsum)
    )
    grad_queries = grad_queries.reshape(key_rows.shape)
    return jnp.stack([grad_queries, finals[0], finals[1]], axis=1)


MESH = pl.DeviceIdType.MESH
BLK = 256
LANES = 128
SLAB = 16
UNROLL = 4
MATRICES = 4


def partner(index, bit):
    return index + (1 - 2 * ((index // bit) % 2)) * bit


def bits_of(count):
    found = []
    bit = 1
    while bit < count:
        found.append(bit)
        bit *= 2
    return found


def place_at(axis, bit):
    place = {"wide": lax.axis_index("wide"), "narrow": lax.axis_index("narrow")}
    place[axis] = partner(place[axis], bit)
    return (place["wide"], place["narrow"])


def greet(places):
    barrier = pltpu.get_barrier_semaphore()
    for place in places:
        pl.semaphore_signal(barrier, inc=1, device_id=place, device_id_type=MESH)
    pl.semaphore_wait(barrier, len(places))


def send(src, dst, sends, arrivals, slot, place):
    copy = pltpu.make_async_remote_copy(
        src_ref=src,
        dst_ref=dst,
        send_sem=sends.at[slot],
        recv_sem=arrivals.at[slot],
        device_id=place,
        device_id_type=MESH,
    )
    copy.start()
    return copy


def core_scatter(values):
    rows = values.shape[0] // 2
    side = lax.axis_index("narrow") % 2
    give = lax.dynamic_slice_in_dim(values, (1 - side) * rows, rows, 0)
    keep = lax.dynamic_slice_in_dim(values, side * rows, rows, 0)
    return keep, permute(give, "narrow", 1)


def core_place(half, other):
    side = lax.axis_index("narrow") % 2
    return jnp.where(
        side == 0,
        jnp.concatenate([half, other], axis=0),
        jnp.concatenate([other, half], axis=0),
    )


def permute(values, axis, bit):
    size = lax.axis_size(axis)
    return lax.ppermute(values, axis, [(index, index ^ bit) for index in range(size)])


def together(*values):
    return lax.optimization_barrier(values)


def pair_scatter(values, axis):
    extent = values.shape[axis] // 2
    side = lax.axis_index("wide") % 2
    give = lax.dynamic_slice_in_dim(values, (1 - side) * extent, extent, axis)
    keep = lax.dynamic_slice_in_dim(values, side * extent, extent, axis)
    return keep, permute(give, "wide", 1)


def line_gather(share):
    count = lax.axis_size("wide") // 2
    return [permute(share, "wide", 2 * offset) for offset in range(1, count)]


def line_place(share, arrived):
    count = lax.axis_size("wide") // 2
    rows = share.shape[0]
    place = lax.axis_index("wide") // 2
    whole = jnp.zeros((count * rows,) + share.shape[1:], share.dtype)
    whole = lax.dynamic_update_slice_in_dim(whole, share, place * rows, 0)
    for offset, piece in zip(range(1, count), arrived):
        whole = lax.dynamic_update_slice_in_dim(whole, piece, (place ^ offset) * rows, 0)
    return whole


def pair_place(half, other, axis):
    side = lax.axis_index("wide") % 2
    return jnp.where(
        side == 0,
        jnp.concatenate([half, other], axis=axis),
        jnp.concatenate([other, half], axis=axis),
    )


def own_half(values, axis):
    extent = values.shape[axis] // 2
    side = lax.axis_index("wide") % 2
    return lax.dynamic_slice_in_dim(values, side * extent, extent, axis)


def wide_parts():
    w = lax.axis_index("wide")
    return w % 2, w // 2


def line_partner(z, offset):
    for bit in bits_of(2 * offset):
        if (offset // bit) % 2:
            z = partner(z, bit)
    return z


def block_of(ref, kind, y, z):
    count = lax.axis_size("wide") // 2
    if kind == "rows":
        rows = ref.shape[0] // (2 * count)
        return ref.at[pl.ds(pl.multiple_of((y * count + z) * rows, 8), rows), :]
    rows = ref.shape[0] // count
    if kind == "half":
        return ref.at[pl.ds(pl.multiple_of(z * rows, 8), rows), :]
    columns = ref.shape[1] // 2
    return ref.at[
        pl.ds(pl.multiple_of(z * rows, 8), rows), pl.ds(pl.multiple_of(y * columns, 128), columns)
    ]


def block_shape(shape, kind):
    count = lax.axis_size("wide") // 2
    if kind == "rows":
        return (shape[0] // (2 * count), shape[1])
    if kind == "half":
        return (shape[0] // count, shape[1])
    return (shape[0] // count, shape[1] // 2)


class Scatter:
    def __init__(self, src, kind, held, beside, inbox, sends, arrivals, local, base):
        self.src, self.kind, self.held, self.beside, self.inbox = src, kind, held, beside, inbox
        self.sends, self.arrivals, self.local, self.base = sends, arrivals, local, base
        self.count = lax.axis_size("wide") // 2
        self.copies = {}
        self.loads = {}

    @staticmethod
    def slots():
        return lax.axis_size("wide") - 1

    def start(self):
        y, z = wide_parts()
        for e in reversed(range(self.count)):
            spot = line_partner(z, e)
            load = pltpu.make_async_copy(
                block_of(self.src, self.kind, y, spot), self.held.at[e], self.local.at[e]
            )
            load.start()
            self.loads[e] = load
            if self.kind != "half":
                self.copies[("y", e)] = send(
                    block_of(self.src, self.kind, 1 - y, spot),
                    self.beside.at[e],
                    self.sends,
                    self.arrivals,
                    self.base + e,
                    place_at("wide", 1),
                )

    def step(self, e):
        self.loads[e].wait()
        if self.kind != "half":
            self.copies[("y", e)].wait_recv()
            self.held[e] = self.held[e] + self.beside[e]
        bit = 1
        while bit < self.count and e % (2 * bit) == 0:
            self.copies[("z", e + bit)].wait_recv()
            self.held[e] = self.held[e] + self.inbox[e + bit - 1]
            bit *= 2
        if e:
            low = e & -e
            self.copies[("z", e)] = send(
                self.held.at[e],
                self.inbox.at[e - 1],
                self.sends,
                self.arrivals,
                self.base + self.count + e - 1,
                place_at("wide", 2 * low),
            )

    def finish(self):
        for copy in self.copies.values():
            copy.wait_send()


def scatter_scratch(shape, kind):
    count = lax.axis_size("wide") // 2
    block = block_shape(shape, kind)
    return [
        pltpu.VMEM((count,) + block, jnp.float32),
        pltpu.VMEM((count if kind != "half" else 1,) + block, jnp.float32),
        pltpu.VMEM((max(count - 1, 1),) + block, jnp.float32),
        pltpu.SemaphoreType.DMA((count,)),
    ]


class Gather:
    def __init__(self, own, spot_of, hops, sends, arrivals, base):
        self.own, self.spot_of, self.hops = own, spot_of, hops
        self.sends, self.arrivals, self.base = sends, arrivals, base
        self.copies = {}
        self.order = sorted(range(2 ** len(hops)), key=lambda item: (bin(item).count("1"), item))

    def step(self, item):
        if item:
            self.copies[item].wait_recv()
        for index in reversed(range(item.bit_length(), len(self.hops))):
            later = item + 2**index
            spot = self.spot_of(item)
            axis, bit = self.hops[index]
            self.copies[later] = send(
                spot if item else self.own,
                spot,
                self.sends,
                self.arrivals,
                self.base + later - 1,
                place_at(axis, bit),
            )

    def finish(self):
        for copy in self.copies.values():
            copy.wait_send()


def line_hops():
    return [("wide", bit) for bit in reversed(bits_of(lax.axis_size("wide"))) if bit > 1]


class NarrowSum:
    def __init__(self, far_bits, pieces, x, o, near, far, held, sends, arrivals, local, base):
        self.bits, self.pieces = far_bits, pieces
        self.x, self.o, self.near, self.far, self.held = x, o, near, far, held
        self.sends, self.arrivals, self.local, self.base = sends, arrivals, local, base
        self.rows = x.shape[0] // 2
        self.core = lax.axis_index("narrow") % 2
        self.copies = []
        self.cross = {}
        self.keeps = []

    def block(self, side, p):
        step = self.rows // self.pieces
        return pl.ds(pl.multiple_of(side * self.rows + p * step, 8), step)

    def push(self, src, dst, slot, bit):
        copy = send(
            src, dst, self.sends, self.arrivals, self.base + slot, place_at("narrow", bit)
        )
        self.copies.append(copy)
        return copy

    def start(self):
        self.first = [
            self.push(self.x.at[self.block(1 - self.core, p)], self.near.at[p], p, 1)
            for p in range(self.pieces)
        ]
        self.loads = [
            pltpu.make_async_copy(
                self.x.at[self.block(self.core, p)], self.held.at[0, p], self.local.at[p]
            )
            for p in range(self.pieces)
        ]
        for load in self.loads:
            load.start()

    def hop(self, b, p):
        slot = (b + 1) * self.pieces + p
        self.cross[(b, p)] = self.push(
            self.held.at[b, p], self.far.at[b, p], slot, self.bits[b]
        )

    def begin(self, p):
        self.loads[p].wait()
        self.first[p].wait_recv()
        self.held[0, p] = self.held[0, p] + self.near[p]
        self.hop(0, p)

    def step(self, b, p):
        self.cross[(b, p)].wait_recv()
        self.held[b + 1, p] = self.held[b, p] + self.far[b, p]
        if b + 1 < len(self.bits):
            self.hop(b + 1, p)
            return
        spot = self.o.at[self.block(self.core, p)]
        slot = (b + 2) * self.pieces + p
        self.keeps.append(self.push(self.held.at[b + 1, p], spot, slot, 1))
        keep = pltpu.make_async_copy(self.held.at[b + 1, p], spot, self.local.at[p])
        keep.start()
        self.loads[p] = keep

    def finish(self):
        for copy in self.keeps:
            copy.wait_recv()
        for keep in self.loads:
            keep.wait()
        for copy in self.copies:
            copy.wait_send()


def narrow_scratch(shape, pieces):
    count = len(bits_of(lax.axis_size("narrow"))) - 1
    step = shape[0] // (2 * pieces)
    return [
        pltpu.VMEM((pieces, step, shape[1]), jnp.float32),
        pltpu.VMEM((count, pieces, step, shape[1]), jnp.float32),
        pltpu.VMEM((count + 1, pieces, step, shape[1]), jnp.float32),
        pltpu.SemaphoreType.DMA((pieces,)),
    ]


def sum_scatter_kernel(kinds, pieces, x_ref, *refs):
    total = len(kinds)
    sources, refs = refs[:total], refs[total:]
    o_ref, shares, refs = refs[0], refs[1 : 1 + total], refs[1 + total :]
    near, far, held, local = refs[:4]
    refs = refs[4:]
    sends, arrivals = refs[-2:]
    far_bits = bits_of(lax.axis_size("narrow"))[1:]
    wide_bits = bits_of(lax.axis_size("wide")) if total else []
    if total and all(kind == "half" for kind in kinds):
        wide_bits = wide_bits[1:]
    greet(
        [place_at("narrow", bit) for bit in [1] + far_bits]
        + [place_at("wide", bit) for bit in wide_bits]
    )
    base = (len(far_bits) + 2) * pieces
    narrow = NarrowSum(far_bits, pieces, x_ref, o_ref, near, far, held, sends, arrivals, local, 0)
    scatters = []
    for index, kind in enumerate(kinds):
        block, beside, inbox, loads = refs[4 * index : 4 * index + 4]
        scatters.append(
            Scatter(sources[index], kind, block, beside, inbox, sends, arrivals, loads, base)
        )
        base += Scatter.slots()
    narrow.start()
    for scatter in scatters:
        scatter.start()
    for p in range(pieces):
        narrow.begin(p)
    count = lax.axis_size("wide") // 2
    for scatter in scatters:
        if scatter.kind == "half":
            for e in reversed(range(1, count)):
                if e % 2:
                    scatter.step(e)
    left = {
        index: [
            e for e in reversed(range(count)) if scatter.kind != "half" or e % 2 == 0
        ]
        for index, scatter in enumerate(scatters)
    }
    for b in range(len(far_bits)):
        for p in range(pieces):
            narrow.step(b, p)
            for index, scatter in enumerate(scatters):
                if len(left[index]) > 1:
                    scatter.step(left[index].pop(0))
    outs = []
    for index, scatter in enumerate(scatters):
        while left[index]:
            scatter.step(left[index].pop(0))
        out = pltpu.make_async_copy(scatter.held.at[0], shares[index], scatter.local.at[0])
        out.start()
        outs.append(out)
    narrow.finish()
    for scatter in scatters:
        scatter.finish()
    for out in outs:
        out.wait()


def sum_scatter(values, gradients, kinds, number):
    pieces = 4
    narrow_bits = bits_of(lax.axis_size("narrow"))
    slots = (len(narrow_bits) + 1) * pieces + len(kinds) * Scatter.slots()
    anywhere = pl.BlockSpec(memory_space=pl.ANY)
    scratch = narrow_scratch(values.shape, pieces)
    shapes = [jax.ShapeDtypeStruct(values.shape, jnp.float32)]
    for gradient, kind in zip(gradients, kinds):
        scratch += scatter_scratch(gradient.shape, kind)
        shapes.append(jax.ShapeDtypeStruct(block_shape(gradient.shape, kind), jnp.float32))
    scratch += [pltpu.SemaphoreType.DMA((slots,)), pltpu.SemaphoreType.DMA((slots,))]
    return pl.pallas_call(
        functools.partial(sum_scatter_kernel, kinds, pieces),
        out_shape=tuple(shapes),
        in_specs=[anywhere] * (1 + len(kinds)),
        out_specs=(anywhere,) * len(shapes),
        scratch_shapes=scratch,
        compiler_params=pltpu.CompilerParams(
            collective_id=number, has_side_effects=True, vmem_limit_bytes=40 * 2**20
        ),
        cost_estimate=pl.CostEstimate(
            flops=values.size, bytes_accessed=values.size * 32, transcendentals=0
        ),
    )(values, *gradients)


def small_kernel(shared_rows, split_rows, x_ref, share_ref, o_ref, norm_ref, half_ref, *refs):
    slots, spare, spare_in, sends, arrivals, local = refs
    wide_bits = bits_of(lax.axis_size("wide"))
    narrow_bits = bits_of(lax.axis_size("narrow"))
    greet(
        [place_at("wide", bit) for bit in wide_bits]
        + [place_at("narrow", bit) for bit in narrow_bits]
    )
    y, z = wide_parts()
    count = len(wide_bits)
    copies = []
    slots[0] = x_ref[...]
    hops = line_hops()

    def spot_of(item):
        spot = z
        for index, (_, bit) in enumerate(hops):
            if (item >> index) % 2:
                spot = partner(spot, bit // 2)
        return block_of(half_ref, "half", y, spot)

    gather = Gather(share_ref, spot_of, hops, sends, arrivals, count + len(narrow_bits))
    keep = pltpu.make_async_copy(share_ref, spot_of(0), local.at[0])
    keep.start()
    for b in range(count):
        copy = send(
            slots.at[b], slots.at[count + 1 + b], sends, arrivals, b, place_at("wide", wide_bits[b])
        )
        copies.append(copy)
        copy.wait_recv()
        slots[b + 1] = slots[b] + slots[count + 1 + b]
    gather.step(0)
    total = slots[count]
    o_ref[...] = total
    shared_part = total[:shared_rows]
    split_part = total[shared_rows : shared_rows + split_rows]
    shared = jnp.sum(shared_part * shared_part)
    split_sum = jnp.sum(split_part * split_part) + jnp.sum(
        total[shared_rows + split_rows : shared_rows + split_rows + 1]
    )
    spare[0] = jnp.full(spare.shape[1:], split_sum, jnp.float32)
    for b in range(len(narrow_bits)):
        copy = send(
            spare.at[b], spare_in.at[b], sends, arrivals, count + b, place_at("narrow", narrow_bits[b])
        )
        copies.append(copy)
        copy.wait_recv()
        spare[b + 1] = spare[b] + spare_in[b]
    norm_ref[...] = jnp.sqrt(spare[len(narrow_bits)] + shared)
    for item in gather.order[1:]:
        gather.step(item)
    keep.wait()
    gather.finish()
    for copy in copies:
        copy.wait_send()


def small_sums(stacked, share, shared_rows, split_rows, number):
    wide_bits = bits_of(lax.axis_size("wide"))
    narrow_bits = bits_of(lax.axis_size("narrow"))
    vmem = pl.BlockSpec(memory_space=pltpu.VMEM)
    anywhere = pl.BlockSpec(memory_space=pl.ANY)
    count = len(wide_bits)
    line = lax.axis_size("wide") // 2
    total = count + len(narrow_bits) + line - 1
    return pl.pallas_call(
        functools.partial(small_kernel, shared_rows, split_rows),
        out_shape=(
            jax.ShapeDtypeStruct(stacked.shape, jnp.float32),
            jax.ShapeDtypeStruct((8, LANES), jnp.float32),
            jax.ShapeDtypeStruct((line * share.shape[0], share.shape[1]), jnp.float32),
        ),
        in_specs=[vmem, vmem],
        out_specs=(vmem, vmem, anywhere),
        scratch_shapes=[
            pltpu.VMEM((2 * count + 1,) + stacked.shape, jnp.float32),
            pltpu.VMEM((len(narrow_bits) + 1, 8, LANES), jnp.float32),
            pltpu.VMEM((len(narrow_bits), 8, LANES), jnp.float32),
            pltpu.SemaphoreType.DMA((total,)),
            pltpu.SemaphoreType.DMA((total,)),
            pltpu.SemaphoreType.DMA((1,)),
        ],
        compiler_params=pltpu.CompilerParams(
            collective_id=number, has_side_effects=True, vmem_limit_bytes=16 * 2**20
        ),
    )(stacked, share)


def gram_kernel(narrow_bits, hops, x_ref, o_ref, halves, inbox, beside, sends, arrivals, local):
    parts, rows = x_ref.shape[0], x_ref.shape[1] // 2
    sub = parts // MATRICES
    w, n = lax.axis_index("wide"), lax.axis_index("narrow")
    y = w % 2
    greeted = {("narrow", bit) for bit in narrow_bits} | set(hops)
    greet([place_at(axis, bit) for axis, bit in sorted(greeted)])
    load = pltpu.make_async_copy(x_ref, halves, local.at[0])
    load.start()
    load.wait()
    base = 0 * n
    size, at, slot = parts, 0, 0
    for bit in reversed(narrow_bits):
        size //= 2
        side = (n // bit) % 2
        copy = send(
            halves.at[pl.ds(base + (1 - side) * size, size)],
            inbox.at[pl.ds(at, size)],
            sends,
            arrivals,
            slot,
            place_at("narrow", bit),
        )
        base = base + side * size
        copy.wait()
        for s in range(size):
            halves[base + s] = halves[base + s] + inbox[at + s]
        at += size
        slot += 1
    row_half = lambda side: pl.ds(pl.multiple_of(side * rows, 8), rows)
    copy = send(
        halves.at[n, row_half(1 - y)], beside.at[0], sends, arrivals, slot, place_at("wide", 1)
    )
    copy.wait()
    beside[1] = halves[n, row_half(y)] + beside[0]
    slot += 1

    def spot_of(item):
        big, small = w, n % sub
        for index, (axis, bit) in enumerate(hops):
            if (item >> index) % 2:
                if axis == "wide":
                    big = partner(big, bit)
                else:
                    small = partner(small, bit)
        start = ((big // 2) * (2 * sub) + small * 2 + big % 2) * rows
        return o_ref.at[pl.ds(pl.multiple_of(start, 8), rows), :]

    keep = pltpu.make_async_copy(beside.at[1], spot_of(0), local.at[0])
    keep.start()
    gather = Gather(beside.at[1], spot_of, hops, sends, arrivals, slot)
    for item in gather.order:
        gather.step(item)
    keep.wait()
    gather.finish()


def gram_whole(partial, number):
    narrow_bits = bits_of(lax.axis_size("narrow"))
    wide_bits = bits_of(lax.axis_size("wide"))
    parts, rows, band = partial.shape
    sub = parts // MATRICES
    hops = [("narrow", bit) for bit in bits_of(sub)]
    hops += [("wide", bit) for bit in reversed(wide_bits)]
    slots = len(narrow_bits) + 2 ** len(hops)
    return pl.pallas_call(
        functools.partial(gram_kernel, narrow_bits, hops),
        out_shape=jax.ShapeDtypeStruct((rows * sub * len_of_line(), band), jnp.float32),
        in_specs=[pl.BlockSpec(memory_space=pl.ANY)],
        out_specs=pl.BlockSpec(memory_space=pl.ANY),
        scratch_shapes=[
            pltpu.VMEM(partial.shape, jnp.float32),
            pltpu.VMEM(partial.shape, jnp.float32),
            pltpu.VMEM((2, rows // 2, band), jnp.float32),
            pltpu.SemaphoreType.DMA((slots,)),
            pltpu.SemaphoreType.DMA((slots,)),
            pltpu.SemaphoreType.DMA((1,)),
        ],
        compiler_params=pltpu.CompilerParams(
            collective_id=number, has_side_effects=True, vmem_limit_bytes=24 * 2**20
        ),
    )(partial)


def len_of_line():
    return lax.axis_size("wide") // 2


def split(values):
    high = values.astype(jnp.bfloat16)
    return high, (values - high.astype(jnp.float32)).astype(jnp.bfloat16)


def product(left_high, left_low, right_high, right_low):
    dot = functools.partial(jnp.dot, preferred_element_type=jnp.float32)
    return dot(left_high, right_high) + (dot(left_high, right_low) + dot(left_low, right_high))


def polar_kernel(g_ref, q_ref, gh, gl, ph, pw, th, tl):
    size = g_ref.shape[0]
    blocks = size // BLK
    first, second, third = newton_terms
    rows = lambda block: pl.ds(block * BLK, BLK)
    square = (BLK, BLK)
    unit = (
        lax.broadcasted_iota(jnp.int32, square, 0) == lax.broadcasted_iota(jnp.int32, square, 1)
    ).astype(jnp.float32)
    count = size // LANES
    lanes = lambda block: pl.ds((block % count) * LANES, LANES)
    trace = jnp.zeros((), jnp.float32)
    for i in range(count):
        trace = trace + jnp.sum(g_ref[lanes(i), lanes(0)] * unit[:LANES, :LANES])
    factor = 1.0 / (jnp.sqrt(trace) + 1e-07)
    for i in range(count):
        for j in range(count // 2 + 1):
            values = g_ref[lanes(i), lanes(j)] * (factor * factor)
            gh[lanes(i), lanes(i + j)], gl[lanes(i), lanes(i + j)] = split(values)
            if 0 < j < count // 2:
                values = values.T
                gh[lanes(i + j), lanes(i)], gl[lanes(i + j), lanes(i)] = split(values)

    def put(high, low, i, j, values):
        high[rows(i), rows(j)], low[rows(i), rows(j)] = split(values)
        if i != j:
            high[rows(j), rows(i)], low[rows(j), rows(i)] = split(values.T)

    def symmetric(left, right, emit):
        for i in range(blocks):
            columns = pl.ds(i * BLK, size - i * BLK)
            values = product(
                left[0][rows(i), :], left[1][rows(i), :], right[0][:, columns], right[1][:, columns]
            )
            for j in range(i, blocks):
                emit(i, j, values[:, (j - i) * BLK : (j - i + 1) * BLK])

    def emit_terms(i, j, values):
        gram = gh[rows(i), rows(j)].astype(jnp.float32) + gl[rows(i), rows(j)].astype(jnp.float32)
        terms = second * gram + third * values
        if i == j:
            terms = terms + first * unit
        put(ph, pw, i, j, terms)

    def emit_total(i, j, values):
        q_ref[rows(i), rows(j)] = values
        if i != j:
            q_ref[rows(j), rows(i)] = values.T

    symmetric((gh, gl), (gh, gl), emit_terms)
    for i in range(blocks):
        q_ref[rows(i), :] = (
            ph[rows(i), :].astype(jnp.float32) + pw[rows(i), :].astype(jnp.float32)
        ) * factor

    def one_step(step, carry):
        symmetric((ph, pw), (gh, gl), functools.partial(put, th, tl))
        symmetric((th, tl), (ph, pw), functools.partial(put, gh, gl))
        symmetric((gh, gl), (gh, gl), emit_terms)
        for i in range(blocks):
            th[rows(i), :], tl[rows(i), :] = split(q_ref[rows(i), :])
        symmetric((ph, pw), (th, tl), emit_total)
        return carry

    lax.fori_loop(0, NEWTON - 1, one_step, 0)


def polar_factor(gramian):
    size = gramian.shape[0]
    vmem = pl.BlockSpec(memory_space=pltpu.VMEM)
    return pl.pallas_call(
        polar_kernel,
        out_shape=jax.ShapeDtypeStruct((size, size), jnp.float32),
        in_specs=[vmem],
        out_specs=vmem,
        scratch_shapes=[pltpu.VMEM((size, size), jnp.bfloat16)] * 6,
        compiler_params=pltpu.CompilerParams(vmem_limit_bytes=48 * 2**20),
        cost_estimate=pl.CostEstimate(
            flops=17 * 6 * size**3, bytes_accessed=8 * size * size, transcendentals=0
        ),
    )(gramian)


def spread_kernel(sub, pieces, q_ref, o_ref, sends, arrivals, local):
    size = q_ref.shape[0]
    half = size // 2
    step = half // pieces
    w, n = lax.axis_index("wide"), lax.axis_index("narrow")
    own = n // sub
    across = partner(own, 2)
    near_place, far_place = place_at("narrow", sub), place_at("narrow", 2 * sub)
    side_place = place_at("wide", 1)
    greet([near_place, far_place, side_place])
    top = w % 2
    rows = lambda side, p: pl.ds(pl.multiple_of(side * half + p * step, 8), step)
    keep = pltpu.make_async_copy(q_ref, o_ref.at[own], local.at[0])
    keep.start()
    copies = []

    def push(src, dst, place):
        copies.append(send(src, dst, sends, arrivals, len(copies), place))
        return copies[-1]

    cross = lambda p: push(q_ref.at[rows(top, p)], o_ref.at[own, rows(top, p)], far_place)
    crossing = [cross(p) for p in range(2)]
    landing = [push(q_ref, o_ref.at[own], near_place)]
    aside = []
    for p in range(pieces):
        crossing[p].wait()
        if p + 2 < pieces:
            crossing.append(cross(p + 2))
        if p >= 2:
            aside[p - 2].wait()
        spot = o_ref.at[across, rows(top, p)]
        aside.append(push(spot, spot, side_place))
        landing.append(push(spot, spot, near_place))
        if p >= 2:
            spot = o_ref.at[across, rows(1 - top, p - 2)]
            landing.append(push(spot, spot, near_place))
    for p in range(pieces - 2, pieces):
        aside[p].wait()
        spot = o_ref.at[across, rows(1 - top, p)]
        landing.append(push(spot, spot, near_place))
    keep.wait()
    for copy in landing:
        copy.wait_send()
    for copy in landing:
        copy.wait_recv()


def spread(factor, number):
    size = factor.shape[0]
    pieces = 8
    slots = 1 + 4 * pieces
    sub = lax.axis_size("narrow") // MATRICES
    return pl.pallas_call(
        functools.partial(spread_kernel, sub, pieces),
        out_shape=jax.ShapeDtypeStruct((MATRICES, size, size), jnp.float32),
        in_specs=[pl.BlockSpec(memory_space=pltpu.VMEM)],
        out_specs=pl.BlockSpec(memory_space=pl.ANY),
        scratch_shapes=[
            pltpu.SemaphoreType.DMA((slots,)),
            pltpu.SemaphoreType.DMA((slots,)),
            pltpu.SemaphoreType.DMA((1,)),
        ],
        compiler_params=pltpu.CompilerParams(collective_id=number, has_side_effects=True),
    )(factor)


def adam_update(weight, moment, square, gradient):
    moment_new = first_decay * moment + (1.0 - first_decay) * gradient
    square_new = second_decay * square + (1.0 - second_decay) * gradient * gradient
    moment_hat = moment_new / (1.0 - first_decay**STEP)
    square_hat = square_new / (1.0 - second_decay**STEP)
    weight_new = weight * (1.0 - adam_rate * weight_decay) - adam_rate * moment_hat / (
        jnp.sqrt(square_hat) + 1e-08
    )
    return (moment_new, square_new, weight_new)


def muon_finish(weight, polar_part, longest):
    return (
        weight * (1.0 - muon_rate * weight_decay)
        - muon_rate * 0.2 * math.sqrt(longest) * polar_part
    )


def column_shifts(strip, column):
    rows = strip.shape[0]
    left = jnp.where(column == 0, 0.0, pltpu.roll(strip, 1, 0))
    right = jnp.where(column == rows - 1, 0.0, pltpu.roll(strip, rows - 1, 0))
    return (left, strip, right)


def tap_rows(shifts, taps):
    return [
        taps[3 * i] * shifts[0] + taps[3 * i + 1] * shifts[1] + taps[3 * i + 2] * shifts[2]
        for i in range(3)
    ]


def strip_at(index):
    return pl.ds(pl.multiple_of(index * GRID, GRID), GRID)


def convolve(load, taps, emit):
    shape = load(0).shape
    column = lax.broadcasted_iota(jnp.int32, shape, 0)

    def one(r, carry):
        above, here = carry
        upper, middle, lower = tap_rows(column_shifts(load(r), column), taps)
        emit(r - 1, here + lower)
        return (upper, above + middle)

    upper, middle, _ = tap_rows(column_shifts(load(0), column), taps)
    above, here = lax.fori_loop(1, GRID, one, (upper, middle))
    emit(GRID - 1, here)


def kernel_sums(load, weigh, width):
    column = lax.broadcasted_iota(jnp.int32, (GRID, width), 0)
    fold = lambda values: values.reshape(GRID // 8, 8, width).sum(axis=0)
    zero = jnp.zeros((8, width), jnp.float32)

    def one(r, carry):
        sums = carry
        shifts = column_shifts(load(r), column)
        later = weigh(jnp.minimum(r + 1, GRID - 1)) * jnp.where(r < GRID - 1, 1.0, 0.0)
        earlier = weigh(jnp.maximum(r - 1, 0)) * jnp.where(r > 0, 1.0, 0.0)
        terms = (later, weigh(r), earlier)
        return tuple(
            sums[3 * i + j] + fold(terms[i] * shifts[j]) for i in range(3) for j in range(3)
        )

    return lax.fori_loop(0, GRID, one, (zero,) * 9)


def middle_kernel(
    entry_ref,
    entry_t_ref,
    grad_ffn_ref,
    expand_ref,
    reduce_ref,
    taps_ref,
    ffn_ref,
    entry_grad_ref,
    grad_reduce_ref,
    grad_expand_ref,
    grad_taps_ref,
    upward,
    slope,
    weight,
    active,
    grad_up,
):
    width = expand_ref.shape[1]
    step = pl.program_id(0)

    def dot(left, right, dims):
        return lax.dot_general(left, right, (dims, ((), ())), preferred_element_type=jnp.float32)

    taps = [taps_ref[t : t + 1, :] for t in range(9)]
    upward[...] = dot(entry_ref[...], expand_ref[...], ((1,), (0,)))
    weight[...] = dot(grad_ffn_ref[...], reduce_ref[...], ((1,), (1,)))

    def emit_middle(r, z):
        inner = gelu_slope * (z + gelu_cubic * z * z * z)
        bent = jnp.tanh(inner)
        active[strip_at(r), :] = (0.5 * z * (1.0 + bent)).astype(jnp.bfloat16)
        turn = 0.5 * (1.0 + bent) + 0.5 * z * (1.0 - bent * bent) * (
            gelu_slope * (1.0 + 3.0 * gelu_cubic * z * z)
        )
        weight[strip_at(r), :] = weight[strip_at(r), :] * turn

    convolve(lambda r: upward[strip_at(r), :], taps, emit_middle)

    def emit_grad(r, values):
        grad_up[strip_at(r), :] = values.astype(jnp.bfloat16)

    convolve(lambda r: weight[strip_at(r), :], taps[::-1], emit_grad)
    sums = kernel_sums(lambda r: upward[strip_at(r), :], lambda r: weight[strip_at(r), :], width)
    for t in range(9):
        grad_taps_ref[t : t + 1, :] = jnp.sum(sums[t], axis=0, keepdims=True)
    grad_reduce_ref[...] = dot(active[...], grad_ffn_ref[...], ((0,), (0,)))
    grad_expand_ref[...] = dot(entry_t_ref[...], grad_up[...], ((1,), (0,)))
    ffn = dot(active[...], reduce_ref[...], ((1,), (0,)))
    back = dot(grad_up[...], expand_ref[...], ((1,), (1,)))

    @pl.when(step == 0)
    def _():
        ffn_ref[...] = ffn
        entry_grad_ref[...] = back

    @pl.when(step > 0)
    def _():
        ffn_ref[...] += ffn
        entry_grad_ref[...] += back


def middle(entry, grad_ffn, expand, reduce, taps):
    tokens, width = entry.shape
    hidden_units = expand.shape[1]
    block = min(256, hidden_units)
    whole = lambda shape: pl.BlockSpec(shape, lambda i: (0, 0))
    f32 = lambda *shape: jax.ShapeDtypeStruct(shape, jnp.float32)
    return pl.pallas_call(
        middle_kernel,
        grid=(hidden_units // block,),
        out_shape=(
            f32(tokens, width),
            f32(tokens, width),
            f32(hidden_units, width),
            f32(width, hidden_units),
            f32(9, hidden_units),
        ),
        in_specs=[
            whole((tokens, width)),
            whole((width, tokens)),
            whole((tokens, width)),
            pl.BlockSpec((width, block), lambda i: (0, i)),
            pl.BlockSpec((block, width), lambda i: (i, 0)),
            pl.BlockSpec((9, block), lambda i: (0, i)),
        ],
        out_specs=(
            whole((tokens, width)),
            whole((tokens, width)),
            pl.BlockSpec((block, width), lambda i: (i, 0)),
            pl.BlockSpec((width, block), lambda i: (0, i)),
            pl.BlockSpec((9, block), lambda i: (0, i)),
        ),
        scratch_shapes=[
            pltpu.VMEM((tokens, block), jnp.float32),
            pltpu.VMEM((tokens, block), jnp.float32),
            pltpu.VMEM((tokens, block), jnp.float32),
            pltpu.VMEM((tokens, block), jnp.bfloat16),
            pltpu.VMEM((tokens, block), jnp.bfloat16),
        ],
        compiler_params=pltpu.CompilerParams(vmem_limit_bytes=52 * 2**20),
        cost_estimate=pl.CostEstimate(
            flops=12 * tokens * width * hidden_units,
            bytes_accessed=32 * tokens * width,
            transcendentals=tokens * hidden_units,
        ),
    )(entry, entry.T, grad_ffn, expand, reduce, taps)


def norm_strip(values):
    average = jnp.mean(values, axis=-1, keepdims=True)
    centred = values - average
    spread_of = jnp.mean(centred * centred, axis=-1, keepdims=True)
    inverse = lax.rsqrt(spread_of + 1e-06)
    return centred * inverse, inverse


def slab_at(index):
    return pl.ds(pl.multiple_of(index * SLAB, SLAB), SLAB)


def fold_rows(values):
    return values.reshape(values.shape[0] // 8, 8, values.shape[1]).sum(axis=0)


def mixer_kernel_forward(tokens_ref, shift_ref, scale_ref, taps_ref, out_ref, entered):
    stretch = 1.0 + scale_ref[...]
    offset = shift_ref[...]

    def enter(r, carry):
        normed, _ = norm_strip(tokens_ref[slab_at(r), :].astype(jnp.float32))
        entered[slab_at(r), :] = normed * stretch + offset
        return carry

    rows, width = tokens_ref.shape
    lax.fori_loop(0, rows // SLAB, enter, 0, unroll=UNROLL)
    for start in range(0, width, BLK):
        lanes = pl.ds(start, BLK)

        def emit(r, values, lanes=lanes):
            out_ref[strip_at(r), lanes] = values.astype(jnp.bfloat16)

        taps = [taps_ref[t : t + 1, lanes] for t in range(9)]
        convolve(lambda r, lanes=lanes: entered[strip_at(r), lanes], taps, emit)


def mixer_forward(tokens, shift, scale, taps):
    rows, width = tokens.shape
    vmem = pl.BlockSpec(memory_space=pltpu.VMEM)
    return pl.pallas_call(
        mixer_kernel_forward,
        out_shape=jax.ShapeDtypeStruct((rows, width), jnp.bfloat16),
        in_specs=[vmem] * 4,
        out_specs=vmem,
        scratch_shapes=[pltpu.VMEM((rows, width), jnp.float32)],
        compiler_params=pltpu.CompilerParams(vmem_limit_bytes=40 * 2**20),
        cost_estimate=pl.CostEstimate(
            flops=40 * rows * width, bytes_accessed=4 * rows * width, transcendentals=0
        ),
    )(tokens, shift, scale, taps)


def mixer_kernel_backward(
    tokens_ref,
    shift_ref,
    scale_ref,
    taps_ref,
    grad_mixed_ref,
    grad_hidden_ref,
    out_ref,
    grad_taps_ref,
    grad_shift_ref,
    grad_scale_ref,
    normed_ref,
    back_ref,
    inverse_ref,
):
    width = tokens_ref.shape[1]
    stretch = 1.0 + scale_ref[...]

    def enter(r, carry):
        normed, inverse = norm_strip(tokens_ref[slab_at(r), :].astype(jnp.float32))
        normed_ref[slab_at(r), :] = normed
        inverse_ref[slab_at(r), :] = jnp.broadcast_to(inverse, (SLAB, LANES))
        return carry

    rows = tokens_ref.shape[0]
    lax.fori_loop(0, rows // SLAB, enter, 0, unroll=UNROLL)
    for start in range(0, width, BLK):
        lanes = pl.ds(start, BLK)
        taps = [taps_ref[t : t + 1, lanes] for t in range(9)]
        stretch_part = 1.0 + scale_ref[:, lanes]
        offset_part = shift_ref[:, lanes]

        def emit(r, values, lanes=lanes):
            back_ref[strip_at(r), lanes] = values

        def entered(r, lanes=lanes, stretch_part=stretch_part, offset_part=offset_part):
            return normed_ref[strip_at(r), lanes] * stretch_part + offset_part

        weigh = lambda r, lanes=lanes: grad_mixed_ref[strip_at(r), lanes]
        convolve(weigh, taps[::-1], emit)
        sums = kernel_sums(entered, weigh, BLK)
        for t in range(9):
            grad_taps_ref[t : t + 1, lanes] = jnp.sum(sums[t], axis=0, keepdims=True)

    def leave(r, carry):
        shifts, scales = carry
        normed = normed_ref[slab_at(r), :]
        back = back_ref[slab_at(r), :]
        stretched = back * stretch
        first = jnp.mean(stretched, axis=-1, keepdims=True)
        second = jnp.mean(stretched * normed, axis=-1, keepdims=True)
        inverse = inverse_ref[slab_at(r), :][:, :1]
        out = grad_hidden_ref[slab_at(r), :] + (stretched - first - normed * second) * inverse
        out_ref[slab_at(r), :] = out.astype(jnp.bfloat16)
        return shifts + fold_rows(back), scales + fold_rows(back * normed)

    zero = jnp.zeros((8, width), jnp.float32)
    shifts, scales = lax.fori_loop(0, rows // SLAB, leave, (zero, zero), unroll=UNROLL)
    grad_shift_ref[...] = jnp.sum(shifts, axis=0, keepdims=True)
    grad_scale_ref[...] = jnp.sum(scales, axis=0, keepdims=True)


def mixer_backward(tokens, shift, scale, taps, grad_mixed, grad_hidden):
    rows, width = tokens.shape
    vmem = pl.BlockSpec(memory_space=pltpu.VMEM)
    f32 = lambda *shape: jax.ShapeDtypeStruct(shape, jnp.float32)
    return pl.pallas_call(
        mixer_kernel_backward,
        out_shape=(
            jax.ShapeDtypeStruct((rows, width), jnp.bfloat16),
            f32(9, width),
            f32(1, width),
            f32(1, width),
        ),
        in_specs=[vmem] * 6,
        out_specs=(vmem,) * 4,
        scratch_shapes=[
            pltpu.VMEM((rows, width), jnp.float32),
            pltpu.VMEM((rows, width), jnp.float32),
            pltpu.VMEM((rows, LANES), jnp.float32),
        ],
        compiler_params=pltpu.CompilerParams(vmem_limit_bytes=48 * 2**20),
        cost_estimate=pl.CostEstimate(
            flops=100 * rows * width, bytes_accessed=12 * rows * width, transcendentals=0
        ),
    )(tokens, shift, scale, taps, grad_mixed, grad_hidden)


def hidden_kernel_backward(
    hidden_ref,
    branch_ref,
    grad_entry_ref,
    grad_ffn_ref,
    scale_ref,
    gate_ref,
    grad_hidden_ref,
    grad_branch_ref,
    grad_shift_ref,
    grad_scale_ref,
    grad_gate_ref,
):
    width = hidden_ref.shape[1]
    stretch = 1.0 + scale_ref[...]
    gate = gate_ref[...]

    def one(r, carry):
        shifts, scales, gates = carry
        normed, inverse = norm_strip(hidden_ref[slab_at(r), :])
        back = grad_entry_ref[slab_at(r), :]
        stretched = back * stretch
        first = jnp.mean(stretched, axis=-1, keepdims=True)
        second = jnp.mean(stretched * normed, axis=-1, keepdims=True)
        grad = grad_ffn_ref[slab_at(r), :].astype(jnp.float32) + (
            stretched - first - normed * second
        ) * inverse
        grad_hidden_ref[slab_at(r), :] = grad
        grad_branch_ref[slab_at(r), :] = (gate * grad).astype(jnp.bfloat16)
        return (
            shifts + fold_rows(back),
            scales + fold_rows(back * normed),
            gates + fold_rows(branch_ref[slab_at(r), :] * grad),
        )

    zero = jnp.zeros((8, width), jnp.float32)
    shifts, scales, gates = lax.fori_loop(
        0, hidden_ref.shape[0] // SLAB, one, (zero, zero, zero), unroll=UNROLL
    )
    grad_shift_ref[...] = jnp.sum(shifts, axis=0, keepdims=True)
    grad_scale_ref[...] = jnp.sum(scales, axis=0, keepdims=True)
    grad_gate_ref[...] = jnp.sum(gates, axis=0, keepdims=True)


def hidden_backward(hidden, branch, grad_entry, grad_result, scale, gate):
    rows, width = hidden.shape
    vmem = pl.BlockSpec(memory_space=pltpu.VMEM)
    f32 = lambda *shape: jax.ShapeDtypeStruct(shape, jnp.float32)
    return pl.pallas_call(
        hidden_kernel_backward,
        out_shape=(
            f32(rows, width),
            jax.ShapeDtypeStruct((rows, width), jnp.bfloat16),
            f32(1, width),
            f32(1, width),
            f32(1, width),
        ),
        in_specs=[vmem] * 6,
        out_specs=(vmem,) * 5,
        compiler_params=pltpu.CompilerParams(vmem_limit_bytes=48 * 2**20),
        cost_estimate=pl.CostEstimate(
            flops=30 * rows * width, bytes_accessed=22 * rows * width, transcendentals=0
        ),
    )(hidden, branch, grad_entry, grad_result, scale, gate)


def interleave(first, second):
    count = lax.axis_size("wide")
    width = first.shape[1]
    both = [first.reshape(count, -1, width), second.reshape(count, -1, width)]
    return jnp.concatenate(both, axis=1).reshape(-1, width)


def part(rows, second_rows):
    width = rows.shape[1]
    size = second_rows // lax.axis_size("wide")
    total = 4 * size
    blocks = rows.reshape(-1, total, width)
    return blocks[:, : total - size].reshape(-1, width), blocks[:, total - size :].reshape(-1, width)


def gram_band(matrix, layout):
    axis = 0 if layout == "columns" else 1
    width = matrix.shape[axis]
    count = 2 * width // lax.axis_size("wide")
    start = (lax.axis_index("wide") // 2) * count
    rows = lax.dynamic_slice_in_dim(matrix, start, count, axis)
    product_rows = lax.dot_general(
        rows,
        matrix,
        (((1 - axis,), (1 - axis,)), ((), ())),
        precision=lax.Precision.HIGH,
        preferred_element_type=jnp.float32,
    )
    band = width // 2 + LANES
    twice = jnp.concatenate([product_rows, product_rows[:, :band]], axis=1)
    return jnp.concatenate(
        [
            lax.dynamic_slice_in_dim(twice[at : at + LANES], start + at, band, 1)
            for at in range(0, count, LANES)
        ],
        axis=0,
    )


def apply_factor(factor, matrix, layout):
    left, right = (factor, matrix) if layout == "columns" else (matrix, factor)
    return jnp.dot(
        left, right, precision=lax.Precision.HIGH, preferred_element_type=jnp.float32
    )


def local(
    tokens,
    conditions,
    item_live,
    cotangent,
    modulation_table,
    mixer_kernel,
    hidden_kernel,
    attend_weight,
    output_weight,
    expand_weight,
    reduce_weight,
    attend_moment,
    output_moment,
    expand_moment,
    reduce_moment,
    table_first,
    table_second,
    mixer_first,
    mixer_second,
    hidden_first,
    hidden_second,
):
    item_count = tokens.shape[0]
    seq_len = tokens.shape[1]
    local_heads = attend_weight.shape[2] // HEAD
    live_mask = item_live.astype(jnp.float32)[:, None, None]
    token_rows = tokens.astype(jnp.float32)
    modulation = modulation_table[None] + conditions
    shift_one = modulation[:, 0:1]
    scale_one = modulation[:, 1:2]
    gate_one = modulation[:, 2:3]
    shift_two = modulation[:, 3:4]
    scale_two = modulation[:, 4:5]
    gate_two = modulation[:, 5:6]
    width = tokens.shape[2]
    flat_tokens = tokens.reshape(-1, width)
    mixed_low = mixer_forward(flat_tokens, shift_one[0], scale_one[0], mixer_kernel)[None]
    attend_low = attend_weight.astype(jnp.bfloat16)
    triple = jnp.einsum(
        "isd,dkc->iskc", mixed_low, attend_low, preferred_element_type=jnp.float32
    ).astype(jnp.bfloat16)
    heads_split = triple.reshape(item_count, seq_len, 3, local_heads, HEAD)

    def attend_item(member):
        return attend_forward(member[:, 0], member[:, 1], member[:, 2])

    context, logsum = lax.map(attend_item, heads_split)
    output_low = output_weight.astype(jnp.bfloat16)
    branch_partial = jnp.einsum(
        "isc,cd->isd", context, output_low, preferred_element_type=jnp.float32
    )
    (branch,) = sum_scatter(branch_partial.reshape(-1, width), [], [], 1)
    branch = branch.reshape(tokens.shape)
    hidden = token_rows + gate_one * branch
    entry_low = entry_piece(hidden, shift_two, scale_two).astype(jnp.bfloat16)
    expand_low = expand_weight.astype(jnp.bfloat16)
    reduce_low = reduce_weight.astype(jnp.bfloat16)
    grad_result = cotangent.astype(jnp.float32) * live_mask
    grad_ffn_low = (gate_two * grad_result).astype(jnp.bfloat16)
    ffn_partial, entry_partial, grad_reduce, grad_expand, grad_hidden_kernel = middle(
        entry_low.reshape(-1, width),
        grad_ffn_low.reshape(-1, width),
        expand_low,
        reduce_low,
        hidden_kernel,
    )
    ffn_keep, ffn_other = core_scatter(ffn_partial)
    grad_entry, reduce_share = sum_scatter(entry_partial, [grad_reduce], ["rows"], 2)
    grad_entry, reduce_share, ffn_other, grad_expand = together(
        grad_entry, reduce_share, ffn_other, grad_expand
    )
    expand_keep, expand_other = pair_scatter(grad_expand, 1)
    reduce_pieces = line_gather(reduce_share)
    ffn_half = ffn_keep + ffn_other
    ffn_across = permute(ffn_half, "narrow", 2)
    grad_hidden, grad_branch_low, grad_shift_two, grad_scale_two, grad_gate_one = hidden_backward(
        hidden.reshape(-1, width),
        branch.reshape(-1, width),
        grad_entry,
        grad_result.reshape(-1, width),
        scale_two[0],
        gate_one[0],
    )
    grad_branch_low = grad_branch_low.reshape(tokens.shape)
    grad_output = jnp.einsum(
        "isc,isd->cd", context, grad_branch_low, preferred_element_type=jnp.float32
    )
    grad_context = jnp.einsum(
        "isd,cd->isc", grad_branch_low, output_low, preferred_element_type=jnp.float32
    ).astype(jnp.bfloat16)

    def attend_item_back(pieces):
        member, logsum_item, grad_item = pieces
        return attend_backward(
            member[:, 0],
            member[:, 1],
            member[:, 2],
            logsum_item,
            grad_item.reshape(seq_len, local_heads, HEAD),
        )

    grad_split = lax.map(attend_item_back, (heads_split, logsum, grad_context))
    grad_triple = grad_split.reshape(item_count, seq_len, 3, local_heads * HEAD).astype(
        jnp.bfloat16
    )
    *reduce_pieces, ffn_across, expand_other, grad_triple = together(
        *reduce_pieces, ffn_across, expand_other, grad_triple
    )
    ffn_half = ffn_half + ffn_across
    for bit in bits_of(lax.axis_size("narrow"))[2:]:
        ffn_half = ffn_half + permute(ffn_half, "narrow", bit)
    expand_half = expand_keep + expand_other
    reduce_line = line_place(reduce_share, reduce_pieces)
    ffn_other = permute(ffn_half, "narrow", 1)
    grad_attend = jnp.einsum(
        "iskc,isd->kcd", grad_triple, mixed_low, preferred_element_type=jnp.float32
    )
    attend_out = interleave(grad_attend.reshape(-1, width), grad_output)
    mixed_partial = jnp.einsum(
        "iskc,dkc->isd", grad_triple, attend_low, preferred_element_type=jnp.float32
    )
    grad_mixed, expand_share, attend_out_share = sum_scatter(
        mixed_partial.reshape(-1, width), [expand_half, attend_out], ["half", "rows"], 3
    )
    ffn_other, grad_mixed, expand_share, reduce_line = together(
        ffn_other, grad_mixed, expand_share, reduce_line
    )
    expand_pieces = line_gather(expand_share)
    reduce_other = permute(reduce_line, "wide", 1)
    ffn_branch = core_place(ffn_half, ffn_other).reshape(tokens.shape)
    block_out = (live_mask * (hidden + gate_two * ffn_branch)).astype(jnp.bfloat16)
    grad_gate_two = jnp.sum(ffn_branch * grad_result, axis=1)
    tokens_gradient, grad_mixer_kernel, grad_shift_one, grad_scale_one = mixer_backward(
        flat_tokens,
        shift_one[0],
        scale_one[0],
        mixer_kernel,
        grad_mixed,
        grad_hidden,
    )
    tokens_gradient = tokens_gradient.reshape(tokens.shape)
    grad_table = jnp.concatenate(
        [
            grad_shift_one,
            grad_scale_one,
            grad_gate_one,
            grad_shift_two,
            grad_scale_two,
            grad_gate_two,
        ],
        axis=0,
    )
    shares = [attend_out_share, expand_share, reduce_share]
    squares = sum(
        jnp.sum((share * share).reshape(-1, width), axis=0) for share in shares
    )
    shared_rows = grad_table.shape[0] + grad_mixer_kernel.shape[0]
    hidden_rows = -(-grad_hidden_kernel.size // width)
    padding = hidden_rows * width - grad_hidden_kernel.size
    hidden_flat = jnp.pad(grad_hidden_kernel.reshape(-1), (0, padding))
    stacked = jnp.concatenate(
        [grad_table, grad_mixer_kernel, hidden_flat.reshape(hidden_rows, width), squares[None]],
        axis=0,
    )
    stacked = jnp.pad(stacked, ((0, -stacked.shape[0] % 8), (0, 0)))
    small, norm, attend_out_line = small_sums(
        stacked, attend_out_share, shared_rows, hidden_rows, 4
    )
    summed_table = small[: grad_table.shape[0]]
    summed_mixer = small[grad_table.shape[0] : shared_rows]
    summed_hidden = small[shared_rows : shared_rows + hidden_rows].reshape(-1)
    summed_hidden = summed_hidden[: hidden_kernel.size].reshape(hidden_kernel.shape)
    *expand_pieces, norm = together(*expand_pieces, norm)
    gradient_norm = norm[0, 0]
    clip_factor = jnp.minimum(1.0, 1.0 / (gradient_norm + 1e-06))
    expand_line = line_place(expand_share, expand_pieces)
    attend_line, output_line = part(attend_out_line, grad_output.shape[0])
    attend_turned = attend_moment.reshape(width, -1).T
    blend = lambda moment, gradient: muon_momentum * moment + clip_factor * gradient
    halves = [
        (blend(own_half(attend_turned, 0), attend_line), "rows"),
        (blend(own_half(output_moment, 0), output_line), "rows"),
        (blend(own_half(expand_moment, 1), expand_line), "columns"),
        (blend(own_half(reduce_moment, 0), reduce_line), "rows"),
    ]
    bands = jnp.stack([gram_band(matrix, layout) for matrix, layout in halves])
    sub = lax.axis_size("narrow") // MATRICES
    gramian = gram_whole(bands.reshape(MATRICES * sub, -1, bands.shape[2]), 5)
    gramian, expand_line, attend_out_line = together(gramian, expand_line, attend_out_line)
    expand_other = permute(expand_line, "wide", 1)
    attend_out_other = permute(attend_out_line, "wide", 1)
    factors = spread(polar_factor(gramian), 6)
    factors, expand_other, attend_out_other, reduce_other = together(
        factors, expand_other, attend_out_other, reduce_other
    )
    attend_whole, output_whole = part(
        pair_place(attend_out_line, attend_out_other, 0), grad_output.shape[0]
    )
    carried = [
        blend(attend_moment, attend_whole.T.reshape(attend_moment.shape)),
        blend(output_moment, output_whole),
        blend(expand_moment, pair_place(expand_line, expand_other, 1)),
        blend(reduce_moment, pair_place(reduce_line, reduce_other, 0)),
    ]
    table_moment, table_square, table_result = adam_update(
        modulation_table, table_first, table_second, clip_factor * summed_table
    )
    mixer_moment, mixer_square, mixer_result = adam_update(
        mixer_kernel, mixer_first, mixer_second, clip_factor * summed_mixer
    )
    hidden_moment, hidden_square, hidden_result = adam_update(
        hidden_kernel, hidden_first, hidden_second, clip_factor * summed_hidden
    )
    matrices = [carried[0].reshape(width, -1), carried[1], carried[2], carried[3]]
    layouts = ("columns", "rows", "columns", "rows")
    polar_parts = [
        apply_factor(factors[position], matrix, layout)
        for position, (matrix, layout) in enumerate(zip(matrices, layouts))
    ]
    attend_result = muon_finish(attend_weight, polar_parts[0].reshape(attend_weight.shape), 3 * D)
    output_result = muon_finish(output_weight, polar_parts[1], D)
    expand_result = muon_finish(expand_weight, polar_parts[2], FF)
    reduce_result = muon_finish(reduce_weight, polar_parts[3], FF)
    return (
        block_out,
        tokens_gradient,
        gradient_norm,
        carried[0],
        carried[1],
        carried[2],
        carried[3],
        attend_result,
        output_result,
        expand_result,
        reduce_result,
        table_moment,
        table_square,
        table_result,
        mixer_moment,
        mixer_square,
        mixer_result,
        hidden_moment,
        hidden_square,
        hidden_result,
    )


def solution(mesh):
    placed = (
        P("wide", None, None),
        P("wide", None, None),
        P("wide"),
        P("wide", None, None),
        P(),
        P(),
        P(None, "narrow"),
        P(None, None, "narrow"),
        P("narrow", None),
        P(None, "narrow"),
        P("narrow", None),
        P(None, None, "narrow"),
        P("narrow", None),
        P(None, "narrow"),
        P("narrow", None),
        P(),
        P(),
        P(),
        P(),
        P(None, "narrow"),
        P(None, "narrow"),
    )
    return jax.shard_map(
        local,
        mesh=mesh,
        in_specs=placed,
        out_specs=(
            P("wide", None, None),
            P("wide", None, None),
            P(),
            P(None, None, "narrow"),
            P("narrow", None),
            P(None, "narrow"),
            P("narrow", None),
            P(None, None, "narrow"),
            P("narrow", None),
            P(None, "narrow"),
            P("narrow", None),
            P(),
            P(),
            P(),
            P(),
            P(),
            P(),
            P(None, "narrow"),
            P(None, "narrow"),
            P(None, "narrow"),
        ),
        check_vma=False,
    )
```

```python
import functools
import math

import jax
import jax.numpy as jnp
from jax import lax
from jax.experimental import pallas as pl
from jax.experimental.pallas import tpu as pltpu
from jax.sharding import PartitionSpec as P

D = 1024
HEAD = 64
FF = 4096
GRID = 32
NEWTON = 5
STEP = 10


first_decay = 0.9
second_decay = 0.999
adam_rate = 0.3
muon_rate = 0.15
muon_momentum = 0.5
weight_decay = 0.01
newton_terms = (3.4445, -4.775, 2.0315)
gelu_slope = 0.7978845608
gelu_cubic = 0.044715


MESH = pl.DeviceIdType.MESH
BLK = 256
LANES = 128
SLAB = 16
QUERIES = 1024
UNROLL = 4
MATRICES = 4


def partner(index, bit):
    return index + (1 - 2 * ((index // bit) % 2)) * bit


def bits_of(count):
    found = []
    bit = 1
    while bit < count:
        found.append(bit)
        bit *= 2
    return found


def place_at(axis, bit):
    place = {"wide": lax.axis_index("wide"), "narrow": lax.axis_index("narrow")}
    place[axis] = partner(place[axis], bit)
    return (place["wide"], place["narrow"])


def greet(places):
    barrier = pltpu.get_barrier_semaphore()
    for place in places:
        pl.semaphore_signal(barrier, inc=1, device_id=place, device_id_type=MESH)
    pl.semaphore_wait(barrier, len(places))


def send(src, dst, sends, arrivals, slot, place):
    copy = pltpu.make_async_remote_copy(
        src_ref=src,
        dst_ref=dst,
        send_sem=sends.at[slot],
        recv_sem=arrivals.at[slot],
        device_id=place,
        device_id_type=MESH,
    )
    copy.start()
    return copy


def core_scatter(values):
    rows = values.shape[0] // 2
    side = lax.axis_index("narrow") % 2
    give = lax.dynamic_slice_in_dim(values, (1 - side) * rows, rows, 0)
    keep = lax.dynamic_slice_in_dim(values, side * rows, rows, 0)
    return keep, permute(give, "narrow", 1)


def core_place(half, other):
    side = lax.axis_index("narrow") % 2
    return jnp.where(
        side == 0,
        jnp.concatenate([half, other], axis=0),
        jnp.concatenate([other, half], axis=0),
    )


def permute(values, axis, bit):
    size = lax.axis_size(axis)
    return lax.ppermute(values, axis, [(index, index ^ bit) for index in range(size)])


def together(*values):
    return lax.optimization_barrier(values)


def pair_scatter(values, axis):
    extent = values.shape[axis] // 2
    side = lax.axis_index("wide") % 2
    give = lax.dynamic_slice_in_dim(values, (1 - side) * extent, extent, axis)
    keep = lax.dynamic_slice_in_dim(values, side * extent, extent, axis)
    return keep, permute(give, "wide", 1)


def line_gather(share):
    count = lax.axis_size("wide") // 2
    return [permute(share, "wide", 2 * offset) for offset in range(1, count)]


def line_place(share, arrived):
    count = lax.axis_size("wide") // 2
    rows = share.shape[0]
    place = lax.axis_index("wide") // 2
    whole = jnp.zeros((count * rows,) + share.shape[1:], share.dtype)
    whole = lax.dynamic_update_slice_in_dim(whole, share, place * rows, 0)
    for offset, piece in zip(range(1, count), arrived):
        whole = lax.dynamic_update_slice_in_dim(whole, piece, (place ^ offset) * rows, 0)
    return whole


def own_half(values, axis):
    extent = values.shape[axis] // 2
    side = lax.axis_index("wide") % 2
    return lax.dynamic_slice_in_dim(values, side * extent, extent, axis)


def wide_parts():
    w = lax.axis_index("wide")
    return w % 2, w // 2


def line_partner(z, offset):
    for bit in bits_of(2 * offset):
        if (offset // bit) % 2:
            z = partner(z, bit)
    return z


def block_of(ref, kind, y, z):
    count = lax.axis_size("wide") // 2
    if kind == "rows":
        rows = ref.shape[0] // (2 * count)
        return ref.at[pl.ds(pl.multiple_of((y * count + z) * rows, 8), rows), :]
    rows = ref.shape[0] // count
    if kind == "half":
        return ref.at[pl.ds(pl.multiple_of(z * rows, 8), rows), :]
    columns = ref.shape[1] // 2
    return ref.at[
        pl.ds(pl.multiple_of(z * rows, 8), rows), pl.ds(pl.multiple_of(y * columns, 128), columns)
    ]


def block_shape(shape, kind):
    count = lax.axis_size("wide") // 2
    if kind == "rows":
        return (shape[0] // (2 * count), shape[1])
    if kind == "half":
        return (shape[0] // count, shape[1])
    return (shape[0] // count, shape[1] // 2)


class Scatter:
    def __init__(self, src, kind, held, beside, inbox, sends, arrivals, local, base):
        self.src, self.kind, self.held, self.beside, self.inbox = src, kind, held, beside, inbox
        self.sends, self.arrivals, self.local, self.base = sends, arrivals, local, base
        self.count = lax.axis_size("wide") // 2
        self.copies = {}
        self.loads = {}

    @staticmethod
    def slots():
        return lax.axis_size("wide") - 1

    def start(self):
        y, z = wide_parts()
        for e in reversed(range(self.count)):
            spot = line_partner(z, e)
            load = pltpu.make_async_copy(
                block_of(self.src, self.kind, y, spot), self.held.at[e], self.local.at[e]
            )
            load.start()
            self.loads[e] = load
            if self.kind != "half":
                self.copies[("y", e)] = send(
                    block_of(self.src, self.kind, 1 - y, spot),
                    self.beside.at[e],
                    self.sends,
                    self.arrivals,
                    self.base + e,
                    place_at("wide", 1),
                )

    def step(self, e):
        self.loads[e].wait()
        if self.kind != "half":
            self.copies[("y", e)].wait_recv()
            self.held[e] = self.held[e] + self.beside[e]
        bit = 1
        while bit < self.count and e % (2 * bit) == 0:
            self.copies[("z", e + bit)].wait_recv()
            self.held[e] = self.held[e] + self.inbox[e + bit - 1]
            bit *= 2
        if e:
            low = e & -e
            self.copies[("z", e)] = send(
                self.held.at[e],
                self.inbox.at[e - 1],
                self.sends,
                self.arrivals,
                self.base + self.count + e - 1,
                place_at("wide", 2 * low),
            )

    def finish(self):
        for copy in self.copies.values():
            copy.wait_send()


def scatter_scratch(shape, kind):
    count = lax.axis_size("wide") // 2
    block = block_shape(shape, kind)
    return [
        pltpu.VMEM((count,) + block, jnp.float32),
        pltpu.VMEM((count if kind != "half" else 1,) + block, jnp.float32),
        pltpu.VMEM((max(count - 1, 1),) + block, jnp.float32),
        pltpu.SemaphoreType.DMA((count,)),
    ]


class Gather:
    def __init__(self, own, spot_of, hops, sends, arrivals, base):
        self.own, self.spot_of, self.hops = own, spot_of, hops
        self.sends, self.arrivals, self.base = sends, arrivals, base
        self.copies = {}
        self.order = sorted(range(2 ** len(hops)), key=lambda item: (bin(item).count("1"), item))

    def step(self, item):
        if item:
            self.copies[item].wait_recv()
        for index in reversed(range(item.bit_length(), len(self.hops))):
            later = item + 2**index
            spot = self.spot_of(item)
            axis, bit = self.hops[index]
            self.copies[later] = send(
                spot if item else self.own,
                spot,
                self.sends,
                self.arrivals,
                self.base + later - 1,
                place_at(axis, bit),
            )

    def finish(self):
        for copy in self.copies.values():
            copy.wait_send()


def line_hops():
    return [("wide", bit) for bit in reversed(bits_of(lax.axis_size("wide"))) if bit > 1]


class NarrowSum:
    def __init__(self, far_bits, pieces, x, o, near, far, held, sends, arrivals, local, base):
        self.bits, self.pieces = far_bits, pieces
        self.x, self.o, self.near, self.far, self.held = x, o, near, far, held
        self.sends, self.arrivals, self.local, self.base = sends, arrivals, local, base
        self.rows = x.shape[0] // 2
        self.core = lax.axis_index("narrow") % 2
        self.copies = []
        self.cross = {}
        self.keeps = []

    def block(self, side, p):
        step = self.rows // self.pieces
        return pl.ds(pl.multiple_of(side * self.rows + p * step, 8), step)

    def push(self, src, dst, slot, bit):
        copy = send(
            src, dst, self.sends, self.arrivals, self.base + slot, place_at("narrow", bit)
        )
        self.copies.append(copy)
        return copy

    def start(self):
        self.first = [
            self.push(self.x.at[self.block(1 - self.core, p)], self.near.at[p], p, 1)
            for p in range(self.pieces)
        ]
        self.loads = [
            pltpu.make_async_copy(
                self.x.at[self.block(self.core, p)], self.held.at[0, p], self.local.at[p]
            )
            for p in range(self.pieces)
        ]
        for load in self.loads:
            load.start()

    def hop(self, b, p):
        slot = (b + 1) * self.pieces + p
        self.cross[(b, p)] = self.push(
            self.held.at[b, p], self.far.at[b, p], slot, self.bits[b]
        )

    def begin(self, p):
        self.loads[p].wait()
        self.first[p].wait_recv()
        self.held[0, p] = self.held[0, p] + self.near[p]
        self.hop(0, p)

    def step(self, b, p):
        self.cross[(b, p)].wait_recv()
        self.held[b + 1, p] = self.held[b, p] + self.far[b, p]
        if b + 1 < len(self.bits):
            self.hop(b + 1, p)
            return
        spot = self.o.at[self.block(self.core, p)]
        slot = (b + 2) * self.pieces + p
        self.keeps.append(self.push(self.held.at[b + 1, p], spot, slot, 1))
        keep = pltpu.make_async_copy(self.held.at[b + 1, p], spot, self.local.at[p])
        keep.start()
        self.loads[p] = keep

    def finish(self):
        for copy in self.keeps:
            copy.wait_recv()
        for keep in self.loads:
            keep.wait()
        for copy in self.copies:
            copy.wait_send()


def narrow_scratch(shape, pieces):
    count = len(bits_of(lax.axis_size("narrow"))) - 1
    step = shape[0] // (2 * pieces)
    return [
        pltpu.VMEM((pieces, step, shape[1]), jnp.float32),
        pltpu.VMEM((count, pieces, step, shape[1]), jnp.float32),
        pltpu.VMEM((count + 1, pieces, step, shape[1]), jnp.float32),
        pltpu.SemaphoreType.DMA((pieces,)),
    ]


def sum_scatter_kernel(kinds, pieces, x_ref, *refs):
    total = len(kinds)
    sources, refs = refs[:total], refs[total:]
    o_ref, shares, refs = refs[0], refs[1 : 1 + total], refs[1 + total :]
    near, far, held, local = refs[:4]
    refs = refs[4:]
    sends, arrivals = refs[-2:]
    far_bits = bits_of(lax.axis_size("narrow"))[1:]
    wide_bits = bits_of(lax.axis_size("wide")) if total else []
    if total and all(kind == "half" for kind in kinds):
        wide_bits = wide_bits[1:]
    greet(
        [place_at("narrow", bit) for bit in [1] + far_bits]
        + [place_at("wide", bit) for bit in wide_bits]
    )
    base = (len(far_bits) + 2) * pieces
    narrow = NarrowSum(far_bits, pieces, x_ref, o_ref, near, far, held, sends, arrivals, local, 0)
    scatters = []
    for index, kind in enumerate(kinds):
        block, beside, inbox, loads = refs[4 * index : 4 * index + 4]
        scatters.append(
            Scatter(sources[index], kind, block, beside, inbox, sends, arrivals, loads, base)
        )
        base += Scatter.slots()
    narrow.start()
    for scatter in scatters:
        scatter.start()
    for p in range(pieces):
        narrow.begin(p)
    count = lax.axis_size("wide") // 2
    for scatter in scatters:
        if scatter.kind == "half":
            for e in reversed(range(1, count)):
                if e % 2:
                    scatter.step(e)
    left = {
        index: [
            e for e in reversed(range(count)) if scatter.kind != "half" or e % 2 == 0
        ]
        for index, scatter in enumerate(scatters)
    }
    for b in range(len(far_bits)):
        for p in range(pieces):
            narrow.step(b, p)
            for index, scatter in enumerate(scatters):
                if len(left[index]) > 1:
                    scatter.step(left[index].pop(0))
    outs = []
    for index, scatter in enumerate(scatters):
        while left[index]:
            scatter.step(left[index].pop(0))
        out = pltpu.make_async_copy(scatter.held.at[0], shares[index], scatter.local.at[0])
        out.start()
        outs.append(out)
    narrow.finish()
    for scatter in scatters:
        scatter.finish()
    for out in outs:
        out.wait()


def sum_scatter(values, gradients, kinds, number):
    pieces = 4
    narrow_bits = bits_of(lax.axis_size("narrow"))
    slots = (len(narrow_bits) + 1) * pieces + len(kinds) * Scatter.slots()
    anywhere = pl.BlockSpec(memory_space=pl.ANY)
    scratch = narrow_scratch(values.shape, pieces)
    shapes = [jax.ShapeDtypeStruct(values.shape, jnp.float32)]
    for gradient, kind in zip(gradients, kinds):
        scratch += scatter_scratch(gradient.shape, kind)
        shapes.append(jax.ShapeDtypeStruct(block_shape(gradient.shape, kind), jnp.float32))
    scratch += [pltpu.SemaphoreType.DMA((slots,)), pltpu.SemaphoreType.DMA((slots,))]
    return pl.pallas_call(
        functools.partial(sum_scatter_kernel, kinds, pieces),
        out_shape=tuple(shapes),
        in_specs=[anywhere] * (1 + len(kinds)),
        out_specs=(anywhere,) * len(shapes),
        scratch_shapes=scratch,
        compiler_params=pltpu.CompilerParams(
            collective_id=number, has_side_effects=True, vmem_limit_bytes=40 * 2**20
        ),
        cost_estimate=pl.CostEstimate(
            flops=values.size, bytes_accessed=values.size * 32, transcendentals=0
        ),
    )(values, *gradients)


def small_kernel(shared_rows, split_rows, x_ref, share_ref, o_ref, norm_ref, half_ref, *refs):
    slots, spare, spare_in, sends, arrivals, local = refs
    wide_bits = bits_of(lax.axis_size("wide"))
    narrow_bits = bits_of(lax.axis_size("narrow"))
    greet(
        [place_at("wide", bit) for bit in wide_bits]
        + [place_at("narrow", bit) for bit in narrow_bits]
    )
    y, z = wide_parts()
    count = len(wide_bits)
    copies = []
    slots[0] = x_ref[...]
    hops = line_hops()

    def spot_of(item):
        spot = z
        for index, (_, bit) in enumerate(hops):
            if (item >> index) % 2:
                spot = partner(spot, bit // 2)
        return block_of(half_ref, "half", y, spot)

    gather = Gather(share_ref, spot_of, hops, sends, arrivals, count + len(narrow_bits))
    keep = pltpu.make_async_copy(share_ref, spot_of(0), local.at[0])
    keep.start()
    for b in range(count):
        copy = send(
            slots.at[b], slots.at[count + 1 + b], sends, arrivals, b, place_at("wide", wide_bits[b])
        )
        copies.append(copy)
        copy.wait_recv()
        slots[b + 1] = slots[b] + slots[count + 1 + b]
    gather.step(0)
    total = slots[count]
    o_ref[...] = total
    shared_part = total[:shared_rows]
    split_part = total[shared_rows : shared_rows + split_rows]
    shared = jnp.sum(shared_part * shared_part)
    split_sum = jnp.sum(split_part * split_part) + jnp.sum(
        total[shared_rows + split_rows : shared_rows + split_rows + 1]
    )
    spare[0] = jnp.full(spare.shape[1:], split_sum, jnp.float32)
    for b in range(len(narrow_bits)):
        copy = send(
            spare.at[b], spare_in.at[b], sends, arrivals, count + b, place_at("narrow", narrow_bits[b])
        )
        copies.append(copy)
        copy.wait_recv()
        spare[b + 1] = spare[b] + spare_in[b]
    norm_ref[...] = jnp.sqrt(spare[len(narrow_bits)] + shared)
    for item in gather.order[1:]:
        gather.step(item)
    keep.wait()
    gather.finish()
    for copy in copies:
        copy.wait_send()


def small_sums(stacked, share, shared_rows, split_rows, number):
    wide_bits = bits_of(lax.axis_size("wide"))
    narrow_bits = bits_of(lax.axis_size("narrow"))
    vmem = pl.BlockSpec(memory_space=pltpu.VMEM)
    anywhere = pl.BlockSpec(memory_space=pl.ANY)
    count = len(wide_bits)
    line = lax.axis_size("wide") // 2
    total = count + len(narrow_bits) + line - 1
    return pl.pallas_call(
        functools.partial(small_kernel, shared_rows, split_rows),
        out_shape=(
            jax.ShapeDtypeStruct(stacked.shape, jnp.float32),
            jax.ShapeDtypeStruct((8, LANES), jnp.float32),
            jax.ShapeDtypeStruct((line * share.shape[0], share.shape[1]), jnp.float32),
        ),
        in_specs=[vmem, vmem],
        out_specs=(vmem, vmem, anywhere),
        scratch_shapes=[
            pltpu.VMEM((2 * count + 1,) + stacked.shape, jnp.float32),
            pltpu.VMEM((len(narrow_bits) + 1, 8, LANES), jnp.float32),
            pltpu.VMEM((len(narrow_bits), 8, LANES), jnp.float32),
            pltpu.SemaphoreType.DMA((total,)),
            pltpu.SemaphoreType.DMA((total,)),
            pltpu.SemaphoreType.DMA((1,)),
        ],
        compiler_params=pltpu.CompilerParams(
            collective_id=number, has_side_effects=True, vmem_limit_bytes=16 * 2**20
        ),
    )(stacked, share)


def gram_kernel(narrow_bits, hops, x_ref, o_ref, halves, inbox, beside, sends, arrivals, local):
    parts, rows = x_ref.shape[0], x_ref.shape[1] // 2
    sub = parts // MATRICES
    w, n = lax.axis_index("wide"), lax.axis_index("narrow")
    y = w % 2
    greeted = {("narrow", bit) for bit in narrow_bits} | set(hops)
    greet([place_at(axis, bit) for axis, bit in sorted(greeted)])
    load = pltpu.make_async_copy(x_ref, halves, local.at[0])
    load.start()
    load.wait()
    base = 0 * n
    size, at, slot = parts, 0, 0
    for bit in reversed(narrow_bits):
        size //= 2
        side = (n // bit) % 2
        copy = send(
            halves.at[pl.ds(base + (1 - side) * size, size)],
            inbox.at[pl.ds(at, size)],
            sends,
            arrivals,
            slot,
            place_at("narrow", bit),
        )
        base = base + side * size
        copy.wait()
        for s in range(size):
            halves[base + s] = halves[base + s] + inbox[at + s]
        at += size
        slot += 1
    row_half = lambda side: pl.ds(pl.multiple_of(side * rows, 8), rows)
    copy = send(
        halves.at[n, row_half(1 - y)], beside.at[0], sends, arrivals, slot, place_at("wide", 1)
    )
    copy.wait()
    beside[1] = halves[n, row_half(y)] + beside[0]
    slot += 1

    def spot_of(item):
        big, small = w, n % sub
        for index, (axis, bit) in enumerate(hops):
            if (item >> index) % 2:
                if axis == "wide":
                    big = partner(big, bit)
                else:
                    small = partner(small, bit)
        start = ((big // 2) * (2 * sub) + small * 2 + big % 2) * rows
        return o_ref.at[pl.ds(pl.multiple_of(start, 8), rows), :]

    keep = pltpu.make_async_copy(beside.at[1], spot_of(0), local.at[0])
    keep.start()
    gather = Gather(beside.at[1], spot_of, hops, sends, arrivals, slot)
    for item in gather.order:
        gather.step(item)
    keep.wait()
    gather.finish()


def gram_whole(partial, number):
    narrow_bits = bits_of(lax.axis_size("narrow"))
    wide_bits = bits_of(lax.axis_size("wide"))
    parts, rows, band = partial.shape
    sub = parts // MATRICES
    hops = [("narrow", bit) for bit in bits_of(sub)]
    hops += [("wide", bit) for bit in reversed(wide_bits)]
    slots = len(narrow_bits) + 2 ** len(hops)
    return pl.pallas_call(
        functools.partial(gram_kernel, narrow_bits, hops),
        out_shape=jax.ShapeDtypeStruct((rows * sub * len_of_line(), band), jnp.float32),
        in_specs=[pl.BlockSpec(memory_space=pl.ANY)],
        out_specs=pl.BlockSpec(memory_space=pl.ANY),
        scratch_shapes=[
            pltpu.VMEM(partial.shape, jnp.float32),
            pltpu.VMEM(partial.shape, jnp.float32),
            pltpu.VMEM((2, rows // 2, band), jnp.float32),
            pltpu.SemaphoreType.DMA((slots,)),
            pltpu.SemaphoreType.DMA((slots,)),
            pltpu.SemaphoreType.DMA((1,)),
        ],
        compiler_params=pltpu.CompilerParams(
            collective_id=number, has_side_effects=True, vmem_limit_bytes=24 * 2**20
        ),
    )(partial)


def len_of_line():
    return lax.axis_size("wide") // 2


def split(values):
    high = values.astype(jnp.bfloat16)
    return high, (values - high.astype(jnp.float32)).astype(jnp.bfloat16)


def product(left_high, left_low, right_high, right_low):
    dot = functools.partial(jnp.dot, preferred_element_type=jnp.float32)
    return dot(left_high, right_high) + (dot(left_high, right_low) + dot(left_low, right_high))


def polar_kernel(g_ref, q_ref, gh, gl, ph, pw, th, tl):
    size = g_ref.shape[0]
    blocks = size // BLK
    first, second, third = newton_terms
    rows = lambda block: pl.ds(block * BLK, BLK)
    square = (BLK, BLK)
    unit = (
        lax.broadcasted_iota(jnp.int32, square, 0) == lax.broadcasted_iota(jnp.int32, square, 1)
    ).astype(jnp.float32)
    count = size // LANES
    lanes = lambda block: pl.ds((block % count) * LANES, LANES)
    trace = jnp.zeros((), jnp.float32)
    for i in range(count):
        trace = trace + jnp.sum(g_ref[lanes(i), lanes(0)] * unit[:LANES, :LANES])
    factor = 1.0 / (jnp.sqrt(trace) + 1e-07)
    for i in range(count):
        for j in range(count // 2 + 1):
            values = g_ref[lanes(i), lanes(j)] * (factor * factor)
            gh[lanes(i), lanes(i + j)], gl[lanes(i), lanes(i + j)] = split(values)
            if 0 < j < count // 2:
                values = values.T
                gh[lanes(i + j), lanes(i)], gl[lanes(i + j), lanes(i)] = split(values)

    def put(high, low, i, j, values):
        high[rows(i), rows(j)], low[rows(i), rows(j)] = split(values)
        if i != j:
            high[rows(j), rows(i)], low[rows(j), rows(i)] = split(values.T)

    def symmetric(left, right, emit):
        for i in range(blocks):
            columns = pl.ds(i * BLK, size - i * BLK)
            values = product(
                left[0][rows(i), :], left[1][rows(i), :], right[0][:, columns], right[1][:, columns]
            )
            for j in range(i, blocks):
                emit(i, j, values[:, (j - i) * BLK : (j - i + 1) * BLK])

    def emit_terms(i, j, values):
        gram = gh[rows(i), rows(j)].astype(jnp.float32) + gl[rows(i), rows(j)].astype(jnp.float32)
        terms = second * gram + third * values
        if i == j:
            terms = terms + first * unit
        put(ph, pw, i, j, terms)

    def emit_total(i, j, values):
        q_ref[rows(i), rows(j)] = values
        if i != j:
            q_ref[rows(j), rows(i)] = values.T

    symmetric((gh, gl), (gh, gl), emit_terms)
    for i in range(blocks):
        q_ref[rows(i), :] = (
            ph[rows(i), :].astype(jnp.float32) + pw[rows(i), :].astype(jnp.float32)
        ) * factor

    def one_step(step, carry):
        symmetric((ph, pw), (gh, gl), functools.partial(put, th, tl))
        symmetric((th, tl), (ph, pw), functools.partial(put, gh, gl))
        symmetric((gh, gl), (gh, gl), emit_terms)
        for i in range(blocks):
            th[rows(i), :], tl[rows(i), :] = split(q_ref[rows(i), :])
        symmetric((ph, pw), (th, tl), emit_total)
        return carry

    lax.fori_loop(0, NEWTON - 1, one_step, 0)


def polar_factor(gramian):
    size = gramian.shape[0]
    vmem = pl.BlockSpec(memory_space=pltpu.VMEM)
    return pl.pallas_call(
        polar_kernel,
        out_shape=jax.ShapeDtypeStruct((size, size), jnp.float32),
        in_specs=[vmem],
        out_specs=vmem,
        scratch_shapes=[pltpu.VMEM((size, size), jnp.bfloat16)] * 6,
        compiler_params=pltpu.CompilerParams(vmem_limit_bytes=48 * 2**20),
        cost_estimate=pl.CostEstimate(
            flops=17 * 6 * size**3, bytes_accessed=8 * size * size, transcendentals=0
        ),
    )(gramian)


def finish_kernel(sub, pieces, norm_ref, q_ref, *refs):
    lines, others, refs = refs[0:6:2], refs[1:6:2], refs[6:]
    moments, weights, refs = refs[:4], refs[4:8], refs[8:]
    carried, results, refs = refs[:4], refs[4:8], refs[8:]
    qs, refs = refs[0], refs[1:]
    staged, values, highs, lows = refs[:3], refs[3:7], refs[7:11], refs[11:15]
    sends, arrivals, near_sems, load_sems, value_sems, out_sems = refs[15:]
    size = q_ref.shape[0]
    half = size // 2
    step = half // pieces
    w, n = lax.axis_index("wide"), lax.axis_index("narrow")
    own = n // sub
    across = partner(own, 2)
    far = own // 2
    near_place, far_place = place_at("narrow", sub), place_at("narrow", 2 * sub)
    side_place = place_at("wide", 1)
    greet([near_place, far_place, side_place])
    y = w % 2
    rows = lambda side, p: pl.ds(pl.multiple_of(side * half + p * step, 8), step)
    slot = iter(range(1 + 4 * pieces))
    copies = []

    def push(src, dst, place):
        copies.append(send(src, dst, sends, arrivals, next(slot), place))
        return copies[-1]

    crossing = [
        push(q_ref.at[rows(y, p)], qs.at[own, rows(y, p)], far_place) for p in range(pieces)
    ]
    near_own = push(q_ref, qs.at[own], near_place)
    keep = pltpu.make_async_copy(q_ref, qs.at[own], near_sems.at[0])
    keep.start()
    loads = []
    for index, (line, other, stage) in enumerate(zip(lines, others, staged)):
        for side, part_ref in ((y, line), (1 - y, other)):
            if index == 1:
                extent = stage.shape[1] // 2
                spot = stage.at[:, pl.ds(pl.multiple_of(side * extent, 128), extent)]
            else:
                extent = stage.shape[0] // 2
                spot = stage.at[pl.ds(pl.multiple_of(side * extent, 8), extent), :]
            loads.append(
                pltpu.make_async_copy(part_ref, spot, load_sems.at[len(loads)])
            )
            loads[-1].start()
    fills = []
    for k in range(MATRICES):
        fills.append(pltpu.make_async_copy(moments[k], values[k], value_sems.at[k]))
        fills[-1].start()
    norm = norm_ref[0:1, 0:1]
    clip = jnp.minimum(1.0, 1.0 / (norm + 1e-06))

    def blend(value, start, stage, stage_start, count):
        slab = 16 if count % 16 == 0 else 8

        def one(i, carry):
            spot = pl.ds(pl.multiple_of(start + i * slab, 8), slab)
            source = pl.ds(pl.multiple_of(stage_start + i * slab, 8), slab)
            value[spot, :] = muon_momentum * value[spot, :] + clip * stage[source, :]
            return carry

        lax.fori_loop(0, count // slab, one, 0, unroll=min(4, count // slab))

    blocks = lax.axis_size("wide")
    shares = [values[k].shape[0] // blocks for k in range(2)]
    outs = []
    for load in loads[:2]:
        load.wait()
    for k in range(2):
        fills[k].wait()

    def one_block(b, carry):
        stage_start = b * (shares[0] + shares[1])
        blend(values[0], b * shares[0], staged[0], stage_start, shares[0])
        blend(values[1], b * shares[1], staged[0], stage_start + shares[0], shares[1])
        return carry

    lax.fori_loop(0, blocks, one_block, 0)
    for k in (2, 3):
        loads[2 * k - 2].wait()
        loads[2 * k - 1].wait()
        fills[k].wait()
        blend(values[k], 0, staged[k - 1], 0, values[k].shape[0])
    for k in range(MATRICES):
        outs.append(pltpu.make_async_copy(values[k], carried[k], out_sems.at[k]))
        outs[-1].start()
    for k in range(MATRICES):

        def cut(i, carry, k=k):
            spot = pl.ds(pl.multiple_of(i * SLAB, SLAB), SLAB)
            highs[k][spot, :], lows[k][spot, :] = split(values[k][spot, :])
            return carry

        lax.fori_loop(0, values[k].shape[0] // SLAB, cut, 0, unroll=UNROLL)
    for k in range(MATRICES):
        outs[k].wait()
        fills[k] = pltpu.make_async_copy(weights[k], values[k], value_sems.at[k])
        fills[k].start()

    dot = lambda left, right, dims: lax.dot_general(
        left, right, (dims, ((), ())), preferred_element_type=jnp.float32
    )
    lengths = (3 * D, D, FF, FF)

    def process(k, start):
        spot = pl.ds(pl.multiple_of(start, BLK), BLK)
        q_high, q_low = split(qs[k, spot, :])
        high, low = highs[k], lows[k]
        scale = muon_rate * 0.2 * math.sqrt(lengths[k])
        if k == 2:
            dims = ((1,), (0,))
            polar = dot(q_high, high[...], dims) + (
                dot(q_high, low[...], dims) + dot(q_low, high[...], dims)
            )
            where = (spot, slice(None))
        else:
            dims = ((1,), (1,))
            polar = dot(high[...], q_high, dims) + (
                dot(low[...], q_high, dims) + dot(high[...], q_low, dims)
            )
            where = (slice(None), spot)
        values[k][where] = values[k][where] * (1.0 - muon_rate * weight_decay) - scale * polar
        pltpu.make_async_copy(
            values[k].at[where], results[k].at[where], out_sems.at[k]
        ).start()

    def pair(first, starts):
        for side in range(2):
            matrices = (0, 1) if first == (side == 0) else (2, 3)

            @pl.when(far == side)
            def _(matrices=matrices):
                for k in matrices:
                    lax.fori_loop(
                        0, len(starts), lambda i, c, k=k: (process(k, starts[0] + i * BLK), c)[1], 0
                    )

    aside, near_across, near_side = [], [], []

    def forward(p):
        crossing[p].wait_recv()
        spot = qs.at[across, rows(y, p)]
        aside.append(push(spot, spot, side_place))
        near_across.append(push(spot, spot, near_place))

    def forward_side(p):
        aside[p].wait_recv()
        spot = qs.at[across, rows(1 - y, p)]
        near_side.append(push(spot, spot, near_place))

    forward(0)
    keep.wait()
    near_own.wait_recv()
    for k in range(MATRICES):
        fills[k].wait()
    pair(True, [0, BLK])
    forward(1)
    pair(True, [2 * BLK, 3 * BLK])
    forward_side(0)
    for p in range(2, pieces):
        forward(p)
        forward_side(p - 1)
    group = BLK // step
    for copy in near_across:
        copy.wait_recv()
    pair(False, [y * half + i * BLK for i in range(half // BLK)])
    for copy in near_side[:group]:
        copy.wait_recv()
    pair(False, [(1 - y) * half])
    forward_side(pieces - 1)
    for copy in near_side[group:]:
        copy.wait_recv()
    pair(False, [(1 - y) * half + BLK])
    for copy in copies:
        copy.wait_send()
    for k in range(MATRICES):
        pltpu.make_async_copy(values[k], results[k], out_sems.at[k]).wait()


def finish(norm, factor, lines, others, moments, weights, number):
    pieces = 4
    size = factor.shape[0]
    sub = lax.axis_size("narrow") // MATRICES
    anywhere = pl.BlockSpec(memory_space=pl.ANY)
    operands = [part for both in zip(lines, others) for part in both]
    shapes = [jax.ShapeDtypeStruct(moment.shape, jnp.float32) for moment in moments]
    staged = [(moments[0].shape[0] + moments[1].shape[0], size), moments[2].shape, moments[3].shape]
    slots = 1 + 4 * pieces
    outs = pl.pallas_call(
        functools.partial(finish_kernel, sub, pieces),
        out_shape=tuple(shapes + shapes),
        in_specs=[pl.BlockSpec(memory_space=pltpu.VMEM)] + [anywhere] * (1 + len(operands) + 8),
        out_specs=(anywhere,) * 8,
        scratch_shapes=[pltpu.VMEM((MATRICES, size, size), jnp.float32)]
        + [pltpu.VMEM(shape, jnp.float32) for shape in staged]
        + [pltpu.VMEM(moment.shape, jnp.float32) for moment in moments]
        + [pltpu.VMEM(moment.shape, jnp.bfloat16) for moment in moments]
        + [pltpu.VMEM(moment.shape, jnp.bfloat16) for moment in moments]
        + [
            pltpu.SemaphoreType.DMA((slots,)),
            pltpu.SemaphoreType.DMA((slots,)),
            pltpu.SemaphoreType.DMA((1,)),
            pltpu.SemaphoreType.DMA((6,)),
            pltpu.SemaphoreType.DMA((MATRICES,)),
            pltpu.SemaphoreType.DMA((MATRICES,)),
        ],
        compiler_params=pltpu.CompilerParams(
            collective_id=number, has_side_effects=True, vmem_limit_bytes=60 * 2**20
        ),
        cost_estimate=pl.CostEstimate(
            flops=18 * size * size * size, bytes_accessed=80 * size * size, transcendentals=0
        ),
    )(norm, factor, *operands, *moments, *weights)
    return outs[:4], outs[4:]


def adam_update(weight, moment, square, gradient):
    moment_new = first_decay * moment + (1.0 - first_decay) * gradient
    square_new = second_decay * square + (1.0 - second_decay) * gradient * gradient
    moment_hat = moment_new / (1.0 - first_decay**STEP)
    square_hat = square_new / (1.0 - second_decay**STEP)
    weight_new = weight * (1.0 - adam_rate * weight_decay) - adam_rate * moment_hat / (
        jnp.sqrt(square_hat) + 1e-08
    )
    return (moment_new, square_new, weight_new)


def column_shifts(strip, column):
    rows = strip.shape[0]
    left = jnp.where(column == 0, 0.0, pltpu.roll(strip, 1, 0))
    right = jnp.where(column == rows - 1, 0.0, pltpu.roll(strip, rows - 1, 0))
    return (left, strip, right)


def tap_rows(shifts, taps):
    return [
        taps[3 * i] * shifts[0] + taps[3 * i + 1] * shifts[1] + taps[3 * i + 2] * shifts[2]
        for i in range(3)
    ]


def strip_at(index):
    return pl.ds(pl.multiple_of(index * GRID, GRID), GRID)


def convolve(load, taps, emit):
    shape = load(0).shape
    column = lax.broadcasted_iota(jnp.int32, shape, 0)

    def one(r, carry):
        above, here = carry
        upper, middle, lower = tap_rows(column_shifts(load(r), column), taps)
        emit(r - 1, here + lower)
        return (upper, above + middle)

    upper, middle, _ = tap_rows(column_shifts(load(0), column), taps)
    above, here = lax.fori_loop(1, GRID, one, (upper, middle))
    emit(GRID - 1, here)


def kernel_sums(load, weigh, width):
    column = lax.broadcasted_iota(jnp.int32, (GRID, width), 0)
    fold = lambda values: values.reshape(GRID // 8, 8, width).sum(axis=0)
    zero = jnp.zeros((8, width), jnp.float32)

    def one(r, carry):
        sums = carry
        shifts = column_shifts(load(r), column)
        later = weigh(jnp.minimum(r + 1, GRID - 1)) * jnp.where(r < GRID - 1, 1.0, 0.0)
        earlier = weigh(jnp.maximum(r - 1, 0)) * jnp.where(r > 0, 1.0, 0.0)
        terms = (later, weigh(r), earlier)
        return tuple(
            sums[3 * i + j] + fold(terms[i] * shifts[j]) for i in range(3) for j in range(3)
        )

    return lax.fori_loop(0, GRID, one, (zero,) * 9)


def middle_kernel(
    entry_ref,
    entry_t_ref,
    grad_ffn_ref,
    expand_ref,
    reduce_ref,
    taps_ref,
    ffn_ref,
    entry_grad_ref,
    grad_reduce_ref,
    grad_expand_ref,
    grad_taps_ref,
    upward,
    slope,
    weight,
    active,
    grad_up,
):
    width = expand_ref.shape[1]
    step = pl.program_id(0)

    def dot(left, right, dims):
        return lax.dot_general(left, right, (dims, ((), ())), preferred_element_type=jnp.float32)

    taps = [taps_ref[t : t + 1, :] for t in range(9)]
    upward[...] = dot(entry_ref[...], expand_ref[...], ((1,), (0,)))
    weight[...] = dot(grad_ffn_ref[...], reduce_ref[...], ((1,), (1,)))

    def emit_middle(r, z):
        inner = gelu_slope * (z + gelu_cubic * z * z * z)
        bent = jnp.tanh(inner)
        active[strip_at(r), :] = (0.5 * z * (1.0 + bent)).astype(jnp.bfloat16)
        turn = 0.5 * (1.0 + bent) + 0.5 * z * (1.0 - bent * bent) * (
            gelu_slope * (1.0 + 3.0 * gelu_cubic * z * z)
        )
        weight[strip_at(r), :] = weight[strip_at(r), :] * turn

    convolve(lambda r: upward[strip_at(r), :], taps, emit_middle)

    def emit_grad(r, values):
        grad_up[strip_at(r), :] = values.astype(jnp.bfloat16)

    convolve(lambda r: weight[strip_at(r), :], taps[::-1], emit_grad)
    sums = kernel_sums(lambda r: upward[strip_at(r), :], lambda r: weight[strip_at(r), :], width)
    for t in range(9):
        grad_taps_ref[t : t + 1, :] = jnp.sum(sums[t], axis=0, keepdims=True)
    grad_reduce_ref[...] = dot(active[...], grad_ffn_ref[...], ((0,), (0,)))
    grad_expand_ref[...] = dot(entry_t_ref[...], grad_up[...], ((1,), (0,)))
    ffn = dot(active[...], reduce_ref[...], ((1,), (0,)))
    back = dot(grad_up[...], expand_ref[...], ((1,), (1,)))

    @pl.when(step == 0)
    def _():
        ffn_ref[...] = ffn
        entry_grad_ref[...] = back

    @pl.when(step > 0)
    def _():
        ffn_ref[...] += ffn
        entry_grad_ref[...] += back


def middle(entry, entry_t, grad_ffn, expand, reduce, taps):
    tokens, width = entry.shape
    hidden_units = expand.shape[1]
    block = min(256, hidden_units)
    whole = lambda shape: pl.BlockSpec(shape, lambda i: (0, 0))
    f32 = lambda *shape: jax.ShapeDtypeStruct(shape, jnp.float32)
    return pl.pallas_call(
        middle_kernel,
        grid=(hidden_units // block,),
        out_shape=(
            f32(tokens, width),
            f32(tokens, width),
            f32(hidden_units, width),
            f32(width, hidden_units),
            f32(9, hidden_units),
        ),
        in_specs=[
            whole((tokens, width)),
            whole((width, tokens)),
            whole((tokens, width)),
            pl.BlockSpec((width, block), lambda i: (0, i)),
            pl.BlockSpec((block, width), lambda i: (i, 0)),
            pl.BlockSpec((9, block), lambda i: (0, i)),
        ],
        out_specs=(
            whole((tokens, width)),
            whole((tokens, width)),
            pl.BlockSpec((block, width), lambda i: (i, 0)),
            pl.BlockSpec((width, block), lambda i: (0, i)),
            pl.BlockSpec((9, block), lambda i: (0, i)),
        ),
        scratch_shapes=[
            pltpu.VMEM((tokens, block), jnp.float32),
            pltpu.VMEM((tokens, block), jnp.float32),
            pltpu.VMEM((tokens, block), jnp.float32),
            pltpu.VMEM((tokens, block), jnp.bfloat16),
            pltpu.VMEM((tokens, block), jnp.bfloat16),
        ],
        compiler_params=pltpu.CompilerParams(vmem_limit_bytes=52 * 2**20),
        cost_estimate=pl.CostEstimate(
            flops=12 * tokens * width * hidden_units,
            bytes_accessed=32 * tokens * width,
            transcendentals=tokens * hidden_units,
        ),
    )(entry, entry_t, grad_ffn, expand, reduce, taps)


def norm_strip(values):
    average = jnp.mean(values, axis=-1, keepdims=True)
    centred = values - average
    spread_of = jnp.mean(centred * centred, axis=-1, keepdims=True)
    inverse = lax.rsqrt(spread_of + 1e-06)
    return centred * inverse, inverse


def slab_at(index):
    return pl.ds(pl.multiple_of(index * SLAB, SLAB), SLAB)


def fold_rows(values):
    return values.reshape(values.shape[0] // 8, 8, values.shape[1]).sum(axis=0)


def mixer_kernel_forward(tokens_ref, shift_ref, scale_ref, taps_ref, out_ref, entered):
    stretch = 1.0 + scale_ref[...]
    offset = shift_ref[...]

    def enter(r, carry):
        normed, _ = norm_strip(tokens_ref[slab_at(r), :].astype(jnp.float32))
        entered[slab_at(r), :] = normed * stretch + offset
        return carry

    rows, width = tokens_ref.shape
    lax.fori_loop(0, rows // SLAB, enter, 0, unroll=UNROLL)
    for start in range(0, width, BLK):
        lanes = pl.ds(start, BLK)

        def emit(r, values, lanes=lanes):
            out_ref[strip_at(r), lanes] = values.astype(jnp.bfloat16)

        taps = [taps_ref[t : t + 1, lanes] for t in range(9)]
        convolve(lambda r, lanes=lanes: entered[strip_at(r), lanes], taps, emit)


def mixer_forward(tokens, shift, scale, taps):
    rows, width = tokens.shape
    vmem = pl.BlockSpec(memory_space=pltpu.VMEM)
    return pl.pallas_call(
        mixer_kernel_forward,
        out_shape=jax.ShapeDtypeStruct((rows, width), jnp.bfloat16),
        in_specs=[vmem] * 4,
        out_specs=vmem,
        scratch_shapes=[pltpu.VMEM((rows, width), jnp.float32)],
        compiler_params=pltpu.CompilerParams(vmem_limit_bytes=40 * 2**20),
        cost_estimate=pl.CostEstimate(
            flops=40 * rows * width, bytes_accessed=4 * rows * width, transcendentals=0
        ),
    )(tokens, shift, scale, taps)


def mixer_kernel_backward(
    tokens_ref,
    shift_ref,
    scale_ref,
    taps_ref,
    grad_mixed_ref,
    grad_hidden_ref,
    out_ref,
    grad_taps_ref,
    grad_shift_ref,
    grad_scale_ref,
    normed_ref,
    back_ref,
    inverse_ref,
):
    width = tokens_ref.shape[1]
    stretch = 1.0 + scale_ref[...]

    def enter(r, carry):
        normed, inverse = norm_strip(tokens_ref[slab_at(r), :].astype(jnp.float32))
        normed_ref[slab_at(r), :] = normed
        inverse_ref[slab_at(r), :] = jnp.broadcast_to(inverse, (SLAB, LANES))
        return carry

    rows = tokens_ref.shape[0]
    lax.fori_loop(0, rows // SLAB, enter, 0, unroll=UNROLL)
    for start in range(0, width, BLK):
        lanes = pl.ds(start, BLK)
        taps = [taps_ref[t : t + 1, lanes] for t in range(9)]
        stretch_part = 1.0 + scale_ref[:, lanes]
        offset_part = shift_ref[:, lanes]

        def emit(r, values, lanes=lanes):
            back_ref[strip_at(r), lanes] = values

        def entered(r, lanes=lanes, stretch_part=stretch_part, offset_part=offset_part):
            return normed_ref[strip_at(r), lanes] * stretch_part + offset_part

        weigh = lambda r, lanes=lanes: grad_mixed_ref[strip_at(r), lanes]
        convolve(weigh, taps[::-1], emit)
        sums = kernel_sums(entered, weigh, BLK)
        for t in range(9):
            grad_taps_ref[t : t + 1, lanes] = jnp.sum(sums[t], axis=0, keepdims=True)

    def leave(r, carry):
        shifts, scales = carry
        normed = normed_ref[slab_at(r), :]
        back = back_ref[slab_at(r), :]
        stretched = back * stretch
        first = jnp.mean(stretched, axis=-1, keepdims=True)
        second = jnp.mean(stretched * normed, axis=-1, keepdims=True)
        inverse = inverse_ref[slab_at(r), :][:, :1]
        out = grad_hidden_ref[slab_at(r), :] + (stretched - first - normed * second) * inverse
        out_ref[slab_at(r), :] = out.astype(jnp.bfloat16)
        return shifts + fold_rows(back), scales + fold_rows(back * normed)

    zero = jnp.zeros((8, width), jnp.float32)
    shifts, scales = lax.fori_loop(0, rows // SLAB, leave, (zero, zero), unroll=UNROLL)
    grad_shift_ref[...] = jnp.sum(shifts, axis=0, keepdims=True)
    grad_scale_ref[...] = jnp.sum(scales, axis=0, keepdims=True)


def mixer_backward(tokens, shift, scale, taps, grad_mixed, grad_hidden):
    rows, width = tokens.shape
    vmem = pl.BlockSpec(memory_space=pltpu.VMEM)
    f32 = lambda *shape: jax.ShapeDtypeStruct(shape, jnp.float32)
    return pl.pallas_call(
        mixer_kernel_backward,
        out_shape=(
            jax.ShapeDtypeStruct((rows, width), jnp.bfloat16),
            f32(9, width),
            f32(1, width),
            f32(1, width),
        ),
        in_specs=[vmem] * 6,
        out_specs=(vmem,) * 4,
        scratch_shapes=[
            pltpu.VMEM((rows, width), jnp.float32),
            pltpu.VMEM((rows, width), jnp.float32),
            pltpu.VMEM((rows, LANES), jnp.float32),
        ],
        compiler_params=pltpu.CompilerParams(vmem_limit_bytes=48 * 2**20),
        cost_estimate=pl.CostEstimate(
            flops=100 * rows * width, bytes_accessed=12 * rows * width, transcendentals=0
        ),
    )(tokens, shift, scale, taps, grad_mixed, grad_hidden)


def hidden_kernel_backward(
    hidden_ref,
    branch_ref,
    grad_entry_ref,
    grad_ffn_ref,
    scale_ref,
    gate_ref,
    grad_hidden_ref,
    grad_branch_ref,
    grad_shift_ref,
    grad_scale_ref,
    grad_gate_ref,
):
    width = hidden_ref.shape[1]
    stretch = 1.0 + scale_ref[...]
    gate = gate_ref[...]

    def one(r, carry):
        shifts, scales, gates = carry
        normed, inverse = norm_strip(hidden_ref[slab_at(r), :])
        back = grad_entry_ref[slab_at(r), :]
        stretched = back * stretch
        first = jnp.mean(stretched, axis=-1, keepdims=True)
        second = jnp.mean(stretched * normed, axis=-1, keepdims=True)
        grad = grad_ffn_ref[slab_at(r), :].astype(jnp.float32) + (
            stretched - first - normed * second
        ) * inverse
        grad_hidden_ref[slab_at(r), :] = grad
        grad_branch_ref[slab_at(r), :] = (gate * grad).astype(jnp.bfloat16)
        return (
            shifts + fold_rows(back),
            scales + fold_rows(back * normed),
            gates + fold_rows(branch_ref[slab_at(r), :] * grad),
        )

    zero = jnp.zeros((8, width), jnp.float32)
    shifts, scales, gates = lax.fori_loop(
        0, hidden_ref.shape[0] // SLAB, one, (zero, zero, zero), unroll=UNROLL
    )
    grad_shift_ref[...] = jnp.sum(shifts, axis=0, keepdims=True)
    grad_scale_ref[...] = jnp.sum(scales, axis=0, keepdims=True)
    grad_gate_ref[...] = jnp.sum(gates, axis=0, keepdims=True)


def hidden_backward(hidden, branch, grad_entry, grad_result, scale, gate):
    rows, width = hidden.shape
    vmem = pl.BlockSpec(memory_space=pltpu.VMEM)
    f32 = lambda *shape: jax.ShapeDtypeStruct(shape, jnp.float32)
    return pl.pallas_call(
        hidden_kernel_backward,
        out_shape=(
            f32(rows, width),
            jax.ShapeDtypeStruct((rows, width), jnp.bfloat16),
            f32(1, width),
            f32(1, width),
            f32(1, width),
        ),
        in_specs=[vmem] * 6,
        out_specs=(vmem,) * 5,
        compiler_params=pltpu.CompilerParams(vmem_limit_bytes=48 * 2**20),
        cost_estimate=pl.CostEstimate(
            flops=30 * rows * width, bytes_accessed=22 * rows * width, transcendentals=0
        ),
    )(hidden, branch, grad_entry, grad_result, scale, gate)


def dot_of(left, right, left_axis, right_axis):
    return lax.dot_general(
        left,
        right,
        (((left_axis,), (right_axis,)), ((), ())),
        preferred_element_type=jnp.float32,
    )


def head_only(values, head):
    lane = lax.broadcasted_iota(jnp.int32, values.shape, 1)
    return jnp.where(lane // HEAD == head, values, jnp.zeros_like(values))


def attend_kernel(
    mixed_ref, attend_ref, triple_ref, context_ref, logsum_ref, turned, values_t
):
    tokens = mixed_ref.shape[0]
    width = context_ref.shape[1]
    step = min(BLK, width)
    for start in range(0, 3 * width, step):
        columns = pl.ds(start, step)
        triple_ref[:, columns] = dot_of(mixed_ref[...], attend_ref[:, columns], 1, 0).astype(
            jnp.bfloat16
        )
    values_t[...] = triple_ref[:, pl.ds(2 * width, width)].T
    scale = jnp.bfloat16(HEAD ** (-0.5))
    for head in range(width // HEAD):
        pair = head * HEAD // LANES * LANES
        inside = head % (LANES // HEAD)

        def one(block, carry, head=head, pair=pair, inside=inside):
            spot = pl.ds(pl.multiple_of(block * QUERIES, QUERIES), QUERIES)
            queries = head_only(triple_ref[spot, pl.ds(pair, LANES)], inside) * scale
            scores = dot_of(triple_ref[:, pl.ds(width + pair, LANES)], queries, 1, 1)
            peak = jnp.max(scores, axis=0, keepdims=True)
            weights = jnp.exp(scores - peak)
            total = jnp.sum(weights, axis=0, keepdims=True)
            soft_low = (weights * (1.0 / total)).astype(jnp.bfloat16)
            turned[pl.ds(head * HEAD, HEAD), spot] = dot_of(
                values_t[pl.ds(head * HEAD, HEAD), :], soft_low, 1, 0
            )
            logsum_ref[pl.ds(head, 1), spot] = peak + jnp.log(total)
            return carry

        lax.fori_loop(0, tokens // QUERIES, one, 0)
    context_ref[...] = turned[...].T.astype(jnp.bfloat16)


def attend(mixed, attend_low):
    tokens, width = mixed.shape
    own = attend_low.shape[1] // 3
    vmem = pl.BlockSpec(memory_space=pltpu.VMEM)
    return pl.pallas_call(
        attend_kernel,
        out_shape=(
            jax.ShapeDtypeStruct((tokens, 3 * own), jnp.bfloat16),
            jax.ShapeDtypeStruct((tokens, own), jnp.bfloat16),
            jax.ShapeDtypeStruct((8, tokens), jnp.float32),
        ),
        in_specs=[vmem] * 2,
        out_specs=(vmem,) * 3,
        scratch_shapes=[
            pltpu.VMEM((own, tokens), jnp.float32),
            pltpu.VMEM((own, tokens), jnp.bfloat16),
        ],
        compiler_params=pltpu.CompilerParams(vmem_limit_bytes=40 * 2**20),
        cost_estimate=pl.CostEstimate(
            flops=16 * tokens * tokens * own,
            bytes_accessed=12 * tokens * width,
            transcendentals=tokens * tokens * own // HEAD,
        ),
    )(mixed, attend_low)


def attend_back_kernel(
    mixed_ref,
    attend_ref,
    output_ref,
    triple_ref,
    context_ref,
    logsum_ref,
    grad_branch_ref,
    grad_output_ref,
    grad_attend_ref,
    grad_mixed_ref,
    grad_context,
    keys_t,
    grad_queries_t,
    grad_keys,
    grad_values,
    grad_triple,
):
    tokens = mixed_ref.shape[0]
    width = output_ref.shape[0]
    grad_context[...] = dot_of(grad_branch_ref[...], output_ref[...], 1, 1).astype(jnp.bfloat16)
    keys_t[...] = triple_ref[:, pl.ds(width, width)].T
    grad_keys[...] = jnp.zeros_like(grad_keys)
    grad_values[...] = jnp.zeros_like(grad_values)
    scale = HEAD ** (-0.5)
    low_scale = jnp.bfloat16(scale)
    for head in range(width // HEAD):
        pair = head * HEAD // LANES * LANES
        inside = head % (LANES // HEAD)
        lanes = pl.ds(pair, LANES)

        def one(block, carry, head=head, pair=pair, inside=inside, lanes=lanes):
            spot = pl.ds(pl.multiple_of(block * QUERIES, QUERIES), QUERIES)
            queries = head_only(triple_ref[spot, lanes], inside)
            back = head_only(grad_context[spot, lanes], inside)
            scores = dot_of(triple_ref[:, pl.ds(width + pair, LANES)], queries * low_scale, 1, 1)
            weights = jnp.exp(scores - logsum_ref[pl.ds(head, 1), spot])
            grad_weights = dot_of(triple_ref[:, pl.ds(2 * width + pair, LANES)], back, 1, 1)
            grad_values[:, lanes] += dot_of(weights.astype(jnp.bfloat16), back, 1, 0)
            inner = jnp.sum(weights * grad_weights, axis=0, keepdims=True)
            grad_low = (weights * (grad_weights - inner)).astype(jnp.bfloat16)
            grad_keys[:, lanes] += dot_of(grad_low, queries, 1, 0)
            grad_queries_t[pl.ds(head * HEAD, HEAD), spot] = dot_of(
                keys_t[pl.ds(head * HEAD, HEAD), :], grad_low, 1, 0
            )
            return carry

        lax.fori_loop(0, tokens // QUERIES, one, 0)
    grad_triple[:, pl.ds(0, width)] = (grad_queries_t[...].T * scale).astype(jnp.bfloat16)
    grad_triple[:, pl.ds(width, width)] = (grad_keys[...] * scale).astype(jnp.bfloat16)
    grad_triple[:, pl.ds(2 * width, width)] = grad_values[...].astype(jnp.bfloat16)
    grad_output_ref[...] = dot_of(context_ref[...], grad_branch_ref[...], 0, 0)
    grad_attend_ref[...] = dot_of(grad_triple[...], mixed_ref[...], 0, 0)
    grad_mixed_ref[...] = dot_of(grad_triple[...], attend_ref[...], 1, 1)


def attend_back(mixed, attend_low, output_low, triple, context, logsum, grad_branch):
    tokens, width = mixed.shape
    own = output_low.shape[0]
    vmem = pl.BlockSpec(memory_space=pltpu.VMEM)
    f32 = lambda *shape: jax.ShapeDtypeStruct(shape, jnp.float32)
    return pl.pallas_call(
        attend_back_kernel,
        out_shape=(f32(own, width), f32(3 * own, width), f32(tokens, width)),
        in_specs=[vmem] * 7,
        out_specs=(vmem,) * 3,
        scratch_shapes=[
            pltpu.VMEM((tokens, own), jnp.bfloat16),
            pltpu.VMEM((own, tokens), jnp.bfloat16),
            pltpu.VMEM((own, tokens), jnp.float32),
            pltpu.VMEM((tokens, own), jnp.float32),
            pltpu.VMEM((tokens, own), jnp.float32),
            pltpu.VMEM((tokens, 3 * own), jnp.bfloat16),
        ],
        compiler_params=pltpu.CompilerParams(vmem_limit_bytes=52 * 2**20),
        cost_estimate=pl.CostEstimate(
            flops=40 * tokens * tokens * own,
            bytes_accessed=20 * tokens * width,
            transcendentals=tokens * tokens * own // HEAD,
        ),
    )(mixed, attend_low, output_low, triple, context, logsum, grad_branch)


def narrow_hops():
    return [("narrow", bit) for bit in reversed(bits_of(lax.axis_size("narrow")))]


def narrow_position(item):
    n = lax.axis_index("narrow")
    position = 0
    for index, (_, bit) in enumerate(narrow_hops()):
        value = (n // bit) % 2
        if (item >> index) % 2:
            value = 1 - value
        position = position + value * 2**index
    return position


def entry_kernel(
    pieces,
    context_ref,
    tokens_ref,
    output_ref,
    gate_ref,
    shift_ref,
    scale_ref,
    branch_ref,
    hidden_ref,
    entry_ref,
    entry_t_ref,
    slots,
    output_low,
    sends,
    arrivals,
):
    rows, own = context_ref.shape
    step = rows // pieces
    hops = narrow_hops()
    count = 2 ** len(hops)
    greet([place_at(axis, bit) for axis, bit in hops])
    chunk = lambda p: pl.ds(p * step, step)
    slots[narrow_position(0)] = context_ref[...].astype(jnp.float32)
    gathers = []
    for p in range(pieces):
        spot_of = lambda item, p=p: slots.at[narrow_position(item), chunk(p)]
        gathers.append(Gather(spot_of(0), spot_of, hops, sends, arrivals, p * (count - 1)))
        gathers[p].step(0)
    output_low[...] = output_ref[...].astype(jnp.bfloat16)
    gate, offset, stretch = gate_ref[...], shift_ref[...], 1.0 + scale_ref[...]
    for p in range(pieces):
        for item in gathers[p].order[1:]:
            gathers[p].step(item)
        branch = jnp.zeros((step, output_ref.shape[1]), jnp.float32)
        for position in range(count):
            branch = branch + dot_of(
                slots[position, chunk(p)].astype(jnp.bfloat16),
                output_low[pl.ds(position * own, own), :],
                1,
                0,
            )
        branch_ref[chunk(p), :] = branch

        def one(i, carry, p=p):
            spot = pl.ds(pl.multiple_of(p * step + i * SLAB, SLAB), SLAB)
            hidden = tokens_ref[spot, :].astype(jnp.float32) + gate * branch_ref[spot, :]
            hidden_ref[spot, :] = hidden
            normed, _ = norm_strip(hidden)
            entry_ref[spot, :] = (normed * stretch + offset).astype(jnp.bfloat16)
            return carry

        lax.fori_loop(0, step // SLAB, one, 0, unroll=UNROLL)
        entry_t_ref[:, chunk(p)] = entry_ref[chunk(p), :].T
    for gather in gathers:
        gather.finish()


def enter(context, tokens, output_all, gate, shift, scale, number):
    pieces = 4
    rows, own = context.shape
    width = tokens.shape[1]
    count = lax.axis_size("narrow")
    vmem = pl.BlockSpec(memory_space=pltpu.VMEM)
    slots = pieces * (count - 1)
    return pl.pallas_call(
        functools.partial(entry_kernel, pieces),
        out_shape=(
            jax.ShapeDtypeStruct((rows, width), jnp.float32),
            jax.ShapeDtypeStruct((rows, width), jnp.float32),
            jax.ShapeDtypeStruct((rows, width), jnp.bfloat16),
            jax.ShapeDtypeStruct((width, rows), jnp.bfloat16),
        ),
        in_specs=[vmem] * 6,
        out_specs=(vmem,) * 4,
        scratch_shapes=[
            pltpu.VMEM((count, rows, own), jnp.float32),
            pltpu.VMEM(output_all.shape, jnp.bfloat16),
            pltpu.SemaphoreType.DMA((slots,)),
            pltpu.SemaphoreType.DMA((slots,)),
        ],
        compiler_params=pltpu.CompilerParams(
            collective_id=number, has_side_effects=True, vmem_limit_bytes=40 * 2**20
        ),
        cost_estimate=pl.CostEstimate(
            flops=2 * rows * width * width, bytes_accessed=100 * rows * width, transcendentals=0
        ),
    )(context, tokens, output_all, gate, shift, scale)


def all_rows(values):
    for _, bit in narrow_hops():
        side = (lax.axis_index("narrow") // bit) % 2
        other = permute(values, "narrow", bit)
        values = jnp.where(
            side == 0,
            jnp.concatenate([values, other], axis=0),
            jnp.concatenate([other, values], axis=0),
        )
    return values


def interleave(first, second):
    count = lax.axis_size("wide")
    width = first.shape[1]
    both = [first.reshape(count, -1, width), second.reshape(count, -1, width)]
    return jnp.concatenate(both, axis=1).reshape(-1, width)


def part(rows, second_rows):
    width = rows.shape[1]
    size = second_rows // lax.axis_size("wide")
    total = 4 * size
    blocks = rows.reshape(-1, total, width)
    return blocks[:, : total - size].reshape(-1, width), blocks[:, total - size :].reshape(-1, width)


def gram_band(matrix, layout):
    axis = 0 if layout == "columns" else 1
    width = matrix.shape[axis]
    count = 2 * width // lax.axis_size("wide")
    start = (lax.axis_index("wide") // 2) * count
    rows = lax.dynamic_slice_in_dim(matrix, start, count, axis)
    product_rows = lax.dot_general(
        rows,
        matrix,
        (((1 - axis,), (1 - axis,)), ((), ())),
        precision=lax.Precision.HIGH,
        preferred_element_type=jnp.float32,
    )
    band = width // 2 + LANES
    twice = jnp.concatenate([product_rows, product_rows[:, :band]], axis=1)
    return jnp.concatenate(
        [
            lax.dynamic_slice_in_dim(twice[at : at + LANES], start + at, band, 1)
            for at in range(0, count, LANES)
        ],
        axis=0,
    )


def local(
    tokens,
    conditions,
    item_live,
    cotangent,
    modulation_table,
    mixer_kernel,
    hidden_kernel,
    attend_weight,
    output_weight,
    expand_weight,
    reduce_weight,
    attend_moment,
    output_moment,
    expand_moment,
    reduce_moment,
    table_first,
    table_second,
    mixer_first,
    mixer_second,
    hidden_first,
    hidden_second,
):
    live_mask = item_live.astype(jnp.float32)[:, None, None]
    modulation = modulation_table[None] + conditions
    shift_one = modulation[:, 0:1]
    scale_one = modulation[:, 1:2]
    gate_one = modulation[:, 2:3]
    shift_two = modulation[:, 3:4]
    scale_two = modulation[:, 4:5]
    gate_two = modulation[:, 5:6]
    width = tokens.shape[2]
    flat_tokens = tokens.reshape(-1, width)
    mixed_low = mixer_forward(flat_tokens, shift_one[0], scale_one[0], mixer_kernel)
    output_all = all_rows(output_weight)
    output_low = output_weight.astype(jnp.bfloat16)
    attend_low = attend_weight.astype(jnp.bfloat16).reshape(width, -1)
    triple, context, logsum = attend(mixed_low, attend_low)
    branch, hidden, entry_low, entry_turned = enter(
        context, flat_tokens, output_all, gate_one[0], shift_two[0], scale_two[0], 1
    )
    expand_low = expand_weight.astype(jnp.bfloat16)
    reduce_low = reduce_weight.astype(jnp.bfloat16)
    grad_result = cotangent.astype(jnp.float32) * live_mask
    grad_ffn_low = (gate_two * grad_result).astype(jnp.bfloat16)
    ffn_partial, entry_partial, grad_reduce, grad_expand, grad_hidden_kernel = middle(
        entry_low,
        entry_turned,
        grad_ffn_low.reshape(-1, width),
        expand_low,
        reduce_low,
        hidden_kernel,
    )
    ffn_keep, ffn_other = core_scatter(ffn_partial)
    grad_entry, reduce_share = sum_scatter(entry_partial, [grad_reduce], ["rows"], 2)
    grad_entry, reduce_share, ffn_other, grad_expand = together(
        grad_entry, reduce_share, ffn_other, grad_expand
    )
    expand_keep, expand_other = pair_scatter(grad_expand, 1)
    reduce_pieces = line_gather(reduce_share)
    ffn_half = ffn_keep + ffn_other
    ffn_across = permute(ffn_half, "narrow", 2)
    grad_hidden, grad_branch_low, grad_shift_two, grad_scale_two, grad_gate_one = hidden_backward(
        hidden,
        branch,
        grad_entry,
        grad_result.reshape(-1, width),
        scale_two[0],
        gate_one[0],
    )
    grad_output, grad_attend, mixed_partial = attend_back(
        mixed_low, attend_low, output_low, triple, context, logsum, grad_branch_low
    )
    *reduce_pieces, ffn_across, expand_other, mixed_partial = together(
        *reduce_pieces, ffn_across, expand_other, mixed_partial
    )
    ffn_half = ffn_half + ffn_across
    for bit in bits_of(lax.axis_size("narrow"))[2:]:
        ffn_half = ffn_half + permute(ffn_half, "narrow", bit)
    expand_half = expand_keep + expand_other
    reduce_line = line_place(reduce_share, reduce_pieces)
    ffn_other = permute(ffn_half, "narrow", 1)
    attend_out = interleave(grad_attend, grad_output)
    grad_mixed, expand_share, attend_out_share = sum_scatter(
        mixed_partial, [expand_half, attend_out], ["half", "rows"], 3
    )
    ffn_other, grad_mixed, expand_share, reduce_line = together(
        ffn_other, grad_mixed, expand_share, reduce_line
    )
    expand_pieces = line_gather(expand_share)
    reduce_other = permute(reduce_line, "wide", 1)
    ffn_branch = core_place(ffn_half, ffn_other).reshape(tokens.shape)
    block_out = (live_mask * (hidden[None] + gate_two * ffn_branch)).astype(jnp.bfloat16)
    grad_gate_two = jnp.sum(ffn_branch * grad_result, axis=1)
    tokens_gradient, grad_mixer_kernel, grad_shift_one, grad_scale_one = mixer_backward(
        flat_tokens,
        shift_one[0],
        scale_one[0],
        mixer_kernel,
        grad_mixed,
        grad_hidden,
    )
    tokens_gradient = tokens_gradient.reshape(tokens.shape)
    grad_table = jnp.concatenate(
        [
            grad_shift_one,
            grad_scale_one,
            grad_gate_one,
            grad_shift_two,
            grad_scale_two,
            grad_gate_two,
        ],
        axis=0,
    )
    shares = [attend_out_share, expand_share, reduce_share]
    squares = sum(
        jnp.sum((share * share).reshape(-1, width), axis=0) for share in shares
    )
    shared_rows = grad_table.shape[0] + grad_mixer_kernel.shape[0]
    hidden_rows = -(-grad_hidden_kernel.size // width)
    padding = hidden_rows * width - grad_hidden_kernel.size
    hidden_flat = jnp.pad(grad_hidden_kernel.reshape(-1), (0, padding))
    stacked = jnp.concatenate(
        [grad_table, grad_mixer_kernel, hidden_flat.reshape(hidden_rows, width), squares[None]],
        axis=0,
    )
    stacked = jnp.pad(stacked, ((0, -stacked.shape[0] % 8), (0, 0)))
    small, norm, attend_out_line = small_sums(
        stacked, attend_out_share, shared_rows, hidden_rows, 4
    )
    summed_table = small[: grad_table.shape[0]]
    summed_mixer = small[grad_table.shape[0] : shared_rows]
    summed_hidden = small[shared_rows : shared_rows + hidden_rows].reshape(-1)
    summed_hidden = summed_hidden[: hidden_kernel.size].reshape(hidden_kernel.shape)
    *expand_pieces, norm = together(*expand_pieces, norm)
    gradient_norm = norm[0, 0]
    clip_factor = jnp.minimum(1.0, 1.0 / (gradient_norm + 1e-06))
    expand_line = line_place(expand_share, expand_pieces)
    attend_line, output_line = part(attend_out_line, grad_output.shape[0])
    attend_turned = attend_moment.reshape(width, -1).T
    blend = lambda moment, gradient: muon_momentum * moment + clip_factor * gradient
    halves = [
        (blend(own_half(attend_turned, 0), attend_line), "rows"),
        (blend(own_half(output_moment, 0), output_line), "rows"),
        (blend(own_half(expand_moment, 1), expand_line), "columns"),
        (blend(own_half(reduce_moment, 0), reduce_line), "rows"),
    ]
    bands = jnp.stack([gram_band(matrix, layout) for matrix, layout in halves])
    sub = lax.axis_size("narrow") // MATRICES
    gramian = gram_whole(bands.reshape(MATRICES * sub, -1, bands.shape[2]), 5)
    gramian, expand_line, attend_out_line = together(gramian, expand_line, attend_out_line)
    expand_other = permute(expand_line, "wide", 1)
    attend_out_other = permute(attend_out_line, "wide", 1)
    factor = polar_factor(gramian)
    factor, expand_other, attend_out_other, reduce_other = together(
        factor, expand_other, attend_out_other, reduce_other
    )
    turn = lambda matrix: matrix.reshape(width, -1).T
    carried, results = finish(
        norm,
        factor,
        [attend_out_line, expand_line, reduce_line],
        [attend_out_other, expand_other, reduce_other],
        [attend_turned, output_moment, expand_moment, reduce_moment],
        [turn(attend_weight), output_weight, expand_weight, reduce_weight],
        6,
    )
    attend_carried = carried[0].T.reshape(attend_weight.shape)
    attend_result = results[0].T.reshape(attend_weight.shape)
    table_moment, table_square, table_result = adam_update(
        modulation_table, table_first, table_second, clip_factor * summed_table
    )
    mixer_moment, mixer_square, mixer_result = adam_update(
        mixer_kernel, mixer_first, mixer_second, clip_factor * summed_mixer
    )
    hidden_moment, hidden_square, hidden_result = adam_update(
        hidden_kernel, hidden_first, hidden_second, clip_factor * summed_hidden
    )
    return (
        block_out,
        tokens_gradient,
        gradient_norm,
        attend_carried,
        carried[1],
        carried[2],
        carried[3],
        attend_result,
        results[1],
        results[2],
        results[3],
        table_moment,
        table_square,
        table_result,
        mixer_moment,
        mixer_square,
        mixer_result,
        hidden_moment,
        hidden_square,
        hidden_result,
    )


def solution(mesh):
    placed = (
        P("wide", None, None),
        P("wide", None, None),
        P("wide"),
        P("wide", None, None),
        P(),
        P(),
        P(None, "narrow"),
        P(None, None, "narrow"),
        P("narrow", None),
        P(None, "narrow"),
        P("narrow", None),
        P(None, None, "narrow"),
        P("narrow", None),
        P(None, "narrow"),
        P("narrow", None),
        P(),
        P(),
        P(),
        P(),
        P(None, "narrow"),
        P(None, "narrow"),
    )
    return jax.shard_map(
        local,
        mesh=mesh,
        in_specs=placed,
        out_specs=(
            P("wide", None, None),
            P("wide", None, None),
            P(),
            P(None, None, "narrow"),
            P("narrow", None),
            P(None, "narrow"),
            P("narrow", None),
            P(None, None, "narrow"),
            P("narrow", None),
            P(None, "narrow"),
            P("narrow", None),
            P(),
            P(),
            P(),
            P(),
            P(),
            P(),
            P(None, "narrow"),
            P(None, "narrow"),
            P(None, "narrow"),
        ),
        check_vma=False,
    )
```

```python
import functools
import math

import jax
import jax.numpy as jnp
from jax import lax
from jax.experimental import pallas as pl
from jax.experimental.pallas import tpu as pltpu
from jax.sharding import PartitionSpec as P

D = 1024
HEAD = 64
FF = 4096
GRID = 32
NEWTON = 5
STEP = 10


first_decay = 0.9
second_decay = 0.999
adam_rate = 0.3
muon_rate = 0.15
muon_momentum = 0.5
weight_decay = 0.01
newton_terms = (3.4445, -4.775, 2.0315)
gelu_slope = 0.7978845608
gelu_cubic = 0.044715


MESH = pl.DeviceIdType.MESH
BLK = 256
LANES = 128
SLAB = 16
QUERIES = 1024
UNROLL = 4
MATRICES = 4
COLUMNS = (0, 2)


def partner(index, bit):
    return index + (1 - 2 * ((index // bit) % 2)) * bit


def bits_of(count):
    found = []
    bit = 1
    while bit < count:
        found.append(bit)
        bit *= 2
    return found


def place_at(axis, bit):
    place = {"wide": lax.axis_index("wide"), "narrow": lax.axis_index("narrow")}
    place[axis] = partner(place[axis], bit)
    return (place["wide"], place["narrow"])


def greet(places):
    barrier = pltpu.get_barrier_semaphore()
    for place in places:
        pl.semaphore_signal(barrier, inc=1, device_id=place, device_id_type=MESH)
    pl.semaphore_wait(barrier, len(places))


def send(src, dst, sends, arrivals, slot, place):
    copy = pltpu.make_async_remote_copy(
        src_ref=src,
        dst_ref=dst,
        send_sem=sends.at[slot],
        recv_sem=arrivals.at[slot],
        device_id=place,
        device_id_type=MESH,
    )
    copy.start()
    return copy


def core_place(half, other):
    side = lax.axis_index("narrow") % 2
    return jnp.where(
        side == 0,
        jnp.concatenate([half, other], axis=0),
        jnp.concatenate([other, half], axis=0),
    )


def permute(values, axis, bit):
    size = lax.axis_size(axis)
    return lax.ppermute(values, axis, [(index, index ^ bit) for index in range(size)])


def together(*values):
    return lax.optimization_barrier(values)


def line_gather(share):
    count = lax.axis_size("wide") // 2
    return [permute(share, "wide", 2 * offset) for offset in range(1, count)]


def line_place(share, arrived):
    count = lax.axis_size("wide") // 2
    rows = share.shape[0]
    place = lax.axis_index("wide") // 2
    whole = jnp.zeros((count * rows,) + share.shape[1:], share.dtype)
    whole = lax.dynamic_update_slice_in_dim(whole, share, place * rows, 0)
    for offset, piece in zip(range(1, count), arrived):
        whole = lax.dynamic_update_slice_in_dim(whole, piece, (place ^ offset) * rows, 0)
    return whole


def own_half(values, axis):
    extent = values.shape[axis] // 2
    side = lax.axis_index("wide") % 2
    return lax.dynamic_slice_in_dim(values, side * extent, extent, axis)


def wide_parts():
    w = lax.axis_index("wide")
    return w % 2, w // 2


def line_partner(z, offset):
    for bit in bits_of(2 * offset):
        if (offset // bit) % 2:
            z = partner(z, bit)
    return z


def block_of(ref, y, z):
    count = lax.axis_size("wide") // 2
    rows = ref.shape[0] // (2 * count)
    return ref.at[pl.ds(pl.multiple_of((y * count + z) * rows, 8), rows), :]


def line_block(ref, z):
    rows = ref.shape[0] // (lax.axis_size("wide") // 2)
    return ref.at[pl.ds(pl.multiple_of(z * rows, 8), rows), :]


def block_shape(shape):
    return (shape[0] // lax.axis_size("wide"), shape[1])


class Scatter:
    def __init__(self, src, held, beside, inbox, sends, arrivals, local, base):
        self.src, self.held, self.beside, self.inbox = src, held, beside, inbox
        self.sends, self.arrivals, self.local, self.base = sends, arrivals, local, base
        self.count = lax.axis_size("wide") // 2
        self.copies = {}
        self.loads = {}

    @staticmethod
    def slots():
        return lax.axis_size("wide") - 1

    def load(self):
        y, z = wide_parts()
        for e in reversed(range(self.count)):
            self.loads[e] = pltpu.make_async_copy(
                block_of(self.src, y, line_partner(z, e)), self.held.at[e], self.local.at[e]
            )
            self.loads[e].start()

    def give(self, e):
        y, z = wide_parts()
        self.copies[("y", e)] = send(
            block_of(self.src, 1 - y, line_partner(z, e)),
            self.beside.at[e],
            self.sends,
            self.arrivals,
            self.base + e,
            place_at("wide", 1),
        )

    def start(self):
        self.load()
        for e in reversed(range(self.count)):
            self.give(e)

    def step(self, e):
        self.loads[e].wait()
        self.copies[("y", e)].wait_recv()
        self.held[e] = self.held[e] + self.beside[e]
        bit = 1
        while bit < self.count and e % (2 * bit) == 0:
            self.copies[("z", e + bit)].wait_recv()
            self.held[e] = self.held[e] + self.inbox[e + bit - 1]
            bit *= 2
        if e:
            low = e & -e
            self.copies[("z", e)] = send(
                self.held.at[e],
                self.inbox.at[e - 1],
                self.sends,
                self.arrivals,
                self.base + self.count + e - 1,
                place_at("wide", 2 * low),
            )

    def finish(self):
        for copy in self.copies.values():
            copy.wait_send()


def scatter_scratch(shape):
    count = lax.axis_size("wide") // 2
    block = block_shape(shape)
    return [
        pltpu.VMEM((count,) + block, jnp.float32),
        pltpu.VMEM((count,) + block, jnp.float32),
        pltpu.VMEM((max(count - 1, 1),) + block, jnp.float32),
        pltpu.SemaphoreType.DMA((count,)),
    ]


class Gather:
    def __init__(self, own, spot_of, hops, sends, arrivals, base):
        self.own, self.spot_of, self.hops = own, spot_of, hops
        self.sends, self.arrivals, self.base = sends, arrivals, base
        self.copies = {}
        self.order = sorted(range(2 ** len(hops)), key=lambda item: (bin(item).count("1"), item))

    def step(self, item):
        if item:
            self.copies[item].wait_recv()
        for index in reversed(range(item.bit_length(), len(self.hops))):
            later = item + 2**index
            spot = self.spot_of(item)
            axis, bit = self.hops[index]
            self.copies[later] = send(
                spot if item else self.own,
                spot,
                self.sends,
                self.arrivals,
                self.base + later - 1,
                place_at(axis, bit),
            )

    def finish(self):
        for copy in self.copies.values():
            copy.wait_send()


def line_hops():
    return [("wide", bit) for bit in reversed(bits_of(lax.axis_size("wide"))) if bit > 1]


class NarrowSum:
    def __init__(self, far_bits, pieces, x, o, near, far, held, sends, arrivals, local, base):
        self.bits, self.pieces = far_bits, pieces
        self.x, self.o, self.near, self.far, self.held = x, o, near, far, held
        self.sends, self.arrivals, self.local, self.base = sends, arrivals, local, base
        self.rows = x.shape[0] // 2
        self.core = lax.axis_index("narrow") % 2
        self.copies = []
        self.cross = {}
        self.keeps = []

    def block(self, side, p):
        step = self.rows // self.pieces
        return pl.ds(pl.multiple_of(side * self.rows + p * step, 8), step)

    def push(self, src, dst, slot, bit):
        copy = send(
            src, dst, self.sends, self.arrivals, self.base + slot, place_at("narrow", bit)
        )
        self.copies.append(copy)
        return copy

    def start(self):
        self.first = [
            self.push(self.x.at[self.block(1 - self.core, p)], self.near.at[p], p, 1)
            for p in range(self.pieces)
        ]
        self.loads = [
            pltpu.make_async_copy(
                self.x.at[self.block(self.core, p)], self.held.at[0, p], self.local.at[p]
            )
            for p in range(self.pieces)
        ]
        for load in self.loads:
            load.start()

    def hop(self, b, p):
        slot = (b + 1) * self.pieces + p
        self.cross[(b, p)] = self.push(
            self.held.at[b, p], self.far.at[b, p], slot, self.bits[b]
        )

    def begin(self, p):
        self.loads[p].wait()
        self.first[p].wait_recv()
        self.held[0, p] = self.held[0, p] + self.near[p]
        self.hop(0, p)

    def step(self, b, p):
        self.cross[(b, p)].wait_recv()
        self.held[b + 1, p] = self.held[b, p] + self.far[b, p]
        if b + 1 < len(self.bits):
            self.hop(b + 1, p)
            return
        spot = self.o.at[self.block(self.core, p)]
        slot = (b + 2) * self.pieces + p
        self.keeps.append(self.push(self.held.at[b + 1, p], spot, slot, 1))
        keep = pltpu.make_async_copy(self.held.at[b + 1, p], spot, self.local.at[p])
        keep.start()
        self.loads[p] = keep

    def finish(self):
        for copy in self.keeps:
            copy.wait_recv()
        for keep in self.loads:
            keep.wait()
        for copy in self.copies:
            copy.wait_send()


def narrow_scratch(shape, pieces):
    count = len(bits_of(lax.axis_size("narrow"))) - 1
    step = shape[0] // (2 * pieces)
    return [
        pltpu.VMEM((pieces, step, shape[1]), jnp.float32),
        pltpu.VMEM((count, pieces, step, shape[1]), jnp.float32),
        pltpu.VMEM((count + 1, pieces, step, shape[1]), jnp.float32),
        pltpu.SemaphoreType.DMA((pieces,)),
    ]


def sum_scatter_kernel(pieces, x_ref, source_ref, o_ref, share_ref, *refs):
    near, far, held, local, block, beside, inbox, loads, sends, arrivals = refs
    far_bits = bits_of(lax.axis_size("narrow"))[1:]
    greet(
        [place_at("narrow", bit) for bit in [1] + far_bits]
        + [place_at("wide", bit) for bit in bits_of(lax.axis_size("wide"))]
    )
    narrow = NarrowSum(far_bits, pieces, x_ref, o_ref, near, far, held, sends, arrivals, local, 0)
    base = (len(far_bits) + 2) * pieces
    scatter = Scatter(source_ref, block, beside, inbox, sends, arrivals, loads, base)
    narrow.start()
    scatter.start()
    for p in range(pieces):
        narrow.begin(p)
    left = list(reversed(range(lax.axis_size("wide") // 2)))
    for b in range(len(far_bits)):
        for p in range(pieces):
            narrow.step(b, p)
            if len(left) > 1:
                scatter.step(left.pop(0))
    while left:
        scatter.step(left.pop(0))
    out = pltpu.make_async_copy(scatter.held.at[0], share_ref, scatter.local.at[0])
    out.start()
    narrow.finish()
    scatter.finish()
    out.wait()


def sum_scatter(values, gradient, number):
    pieces = 4
    narrow_bits = bits_of(lax.axis_size("narrow"))
    slots = (len(narrow_bits) + 1) * pieces + Scatter.slots()
    anywhere = pl.BlockSpec(memory_space=pl.ANY)
    scratch = narrow_scratch(values.shape, pieces) + scatter_scratch(gradient.shape)
    return pl.pallas_call(
        functools.partial(sum_scatter_kernel, pieces),
        out_shape=(
            jax.ShapeDtypeStruct(values.shape, jnp.float32),
            jax.ShapeDtypeStruct(block_shape(gradient.shape), jnp.float32),
        ),
        in_specs=[anywhere] * 2,
        out_specs=(anywhere,) * 2,
        scratch_shapes=scratch
        + [pltpu.SemaphoreType.DMA((slots,)), pltpu.SemaphoreType.DMA((slots,))],
        compiler_params=pltpu.CompilerParams(
            collective_id=number, has_side_effects=True, vmem_limit_bytes=40 * 2**20
        ),
        cost_estimate=pl.CostEstimate(
            flops=values.size, bytes_accessed=values.size * 32, transcendentals=0
        ),
    )(values, gradient)


def small_kernel(shared_rows, split_rows, x_ref, share_ref, o_ref, norm_ref, half_ref, *refs):
    slots, spare, spare_in, sends, arrivals, local = refs
    wide_bits = bits_of(lax.axis_size("wide"))
    narrow_bits = bits_of(lax.axis_size("narrow"))
    greet(
        [place_at("wide", bit) for bit in wide_bits]
        + [place_at("narrow", bit) for bit in narrow_bits]
    )
    _, z = wide_parts()
    count = len(wide_bits)
    copies = []
    slots[0] = x_ref[...]
    hops = line_hops()

    def spot_of(item):
        spot = z
        for index, (_, bit) in enumerate(hops):
            if (item >> index) % 2:
                spot = partner(spot, bit // 2)
        return line_block(half_ref, spot)

    gather = Gather(share_ref, spot_of, hops, sends, arrivals, count + len(narrow_bits))
    keep = pltpu.make_async_copy(share_ref, spot_of(0), local.at[0])
    keep.start()
    for b in range(count):
        copy = send(
            slots.at[b], slots.at[count + 1 + b], sends, arrivals, b, place_at("wide", wide_bits[b])
        )
        copies.append(copy)
        copy.wait_recv()
        slots[b + 1] = slots[b] + slots[count + 1 + b]
    gather.step(0)
    total = slots[count]
    o_ref[...] = total
    shared_part = total[:shared_rows]
    split_part = total[shared_rows : shared_rows + split_rows]
    shared = jnp.sum(shared_part * shared_part)
    split_sum = jnp.sum(split_part * split_part) + jnp.sum(
        total[shared_rows + split_rows : shared_rows + split_rows + 1]
    )
    spare[0] = jnp.full(spare.shape[1:], split_sum, jnp.float32)
    for b in range(len(narrow_bits)):
        copy = send(
            spare.at[b], spare_in.at[b], sends, arrivals, count + b, place_at("narrow", narrow_bits[b])
        )
        copies.append(copy)
        copy.wait_recv()
        spare[b + 1] = spare[b] + spare_in[b]
    norm_ref[...] = jnp.sqrt(spare[len(narrow_bits)] + shared)
    for item in gather.order[1:]:
        gather.step(item)
    keep.wait()
    gather.finish()
    for copy in copies:
        copy.wait_send()


def small_sums(stacked, share, shared_rows, split_rows, number):
    wide_bits = bits_of(lax.axis_size("wide"))
    narrow_bits = bits_of(lax.axis_size("narrow"))
    vmem = pl.BlockSpec(memory_space=pltpu.VMEM)
    anywhere = pl.BlockSpec(memory_space=pl.ANY)
    count = len(wide_bits)
    line = lax.axis_size("wide") // 2
    total = count + len(narrow_bits) + line - 1
    return pl.pallas_call(
        functools.partial(small_kernel, shared_rows, split_rows),
        out_shape=(
            jax.ShapeDtypeStruct(stacked.shape, jnp.float32),
            jax.ShapeDtypeStruct((8, LANES), jnp.float32),
            jax.ShapeDtypeStruct((line * share.shape[0], share.shape[1]), jnp.float32),
        ),
        in_specs=[vmem, vmem],
        out_specs=(vmem, vmem, anywhere),
        scratch_shapes=[
            pltpu.VMEM((2 * count + 1,) + stacked.shape, jnp.float32),
            pltpu.VMEM((len(narrow_bits) + 1, 8, LANES), jnp.float32),
            pltpu.VMEM((len(narrow_bits), 8, LANES), jnp.float32),
            pltpu.SemaphoreType.DMA((total,)),
            pltpu.SemaphoreType.DMA((total,)),
            pltpu.SemaphoreType.DMA((1,)),
        ],
        compiler_params=pltpu.CompilerParams(
            collective_id=number, has_side_effects=True, vmem_limit_bytes=16 * 2**20
        ),
    )(stacked, share)


def gram_kernel(narrow_bits, hops, x_ref, o_ref, halves, inbox, beside, sends, arrivals, local):
    parts, rows = x_ref.shape[0], x_ref.shape[1] // 2
    sub = parts // MATRICES
    w, n = lax.axis_index("wide"), lax.axis_index("narrow")
    y = w % 2
    greeted = {("narrow", bit) for bit in narrow_bits} | set(hops)
    greet([place_at(axis, bit) for axis, bit in sorted(greeted)])
    load = pltpu.make_async_copy(x_ref, halves, local.at[0])
    load.start()
    load.wait()
    base = 0 * n
    size, at, slot = parts, 0, 0
    for bit in reversed(narrow_bits):
        size //= 2
        side = (n // bit) % 2
        copy = send(
            halves.at[pl.ds(base + (1 - side) * size, size)],
            inbox.at[pl.ds(at, size)],
            sends,
            arrivals,
            slot,
            place_at("narrow", bit),
        )
        base = base + side * size
        copy.wait()
        for s in range(size):
            halves[base + s] = halves[base + s] + inbox[at + s]
        at += size
        slot += 1
    row_half = lambda side: pl.ds(pl.multiple_of(side * rows, 8), rows)
    copy = send(
        halves.at[n, row_half(1 - y)], beside.at[0], sends, arrivals, slot, place_at("wide", 1)
    )
    copy.wait()
    beside[1] = halves[n, row_half(y)] + beside[0]
    slot += 1

    def spot_of(item):
        big, small = w, n % sub
        for index, (axis, bit) in enumerate(hops):
            if (item >> index) % 2:
                if axis == "wide":
                    big = partner(big, bit)
                else:
                    small = partner(small, bit)
        start = ((big // 2) * (2 * sub) + small * 2 + big % 2) * rows
        return o_ref.at[pl.ds(pl.multiple_of(start, 8), rows), :]

    keep = pltpu.make_async_copy(beside.at[1], spot_of(0), local.at[0])
    keep.start()
    gather = Gather(beside.at[1], spot_of, hops, sends, arrivals, slot)
    for item in gather.order:
        gather.step(item)
    keep.wait()
    gather.finish()


def gram_whole(partial, number):
    narrow_bits = bits_of(lax.axis_size("narrow"))
    wide_bits = bits_of(lax.axis_size("wide"))
    parts, rows, band = partial.shape
    sub = parts // MATRICES
    hops = [("narrow", bit) for bit in bits_of(sub)]
    hops += [("wide", bit) for bit in reversed(wide_bits)]
    slots = len(narrow_bits) + 2 ** len(hops)
    return pl.pallas_call(
        functools.partial(gram_kernel, narrow_bits, hops),
        out_shape=jax.ShapeDtypeStruct((rows * sub * len_of_line(), band), jnp.float32),
        in_specs=[pl.BlockSpec(memory_space=pl.ANY)],
        out_specs=pl.BlockSpec(memory_space=pl.ANY),
        scratch_shapes=[
            pltpu.VMEM(partial.shape, jnp.float32),
            pltpu.VMEM(partial.shape, jnp.float32),
            pltpu.VMEM((2, rows // 2, band), jnp.float32),
            pltpu.SemaphoreType.DMA((slots,)),
            pltpu.SemaphoreType.DMA((slots,)),
            pltpu.SemaphoreType.DMA((1,)),
        ],
        compiler_params=pltpu.CompilerParams(
            collective_id=number, has_side_effects=True, vmem_limit_bytes=24 * 2**20
        ),
    )(partial)


def len_of_line():
    return lax.axis_size("wide") // 2


def split(values):
    high = values.astype(jnp.bfloat16)
    return high, (values - high.astype(jnp.float32)).astype(jnp.bfloat16)


def product(left_high, left_low, right_high, right_low):
    dot = functools.partial(jnp.dot, preferred_element_type=jnp.float32)
    return dot(left_high, right_high) + (dot(left_high, right_low) + dot(left_low, right_high))


def polar_kernel(g_ref, q_ref, gh, gl, ph, pw, th, tl):
    size = g_ref.shape[0]
    blocks = size // BLK
    first, second, third = newton_terms
    rows = lambda block: pl.ds(block * BLK, BLK)
    square = (BLK, BLK)
    unit = (
        lax.broadcasted_iota(jnp.int32, square, 0) == lax.broadcasted_iota(jnp.int32, square, 1)
    ).astype(jnp.float32)
    count = size // LANES
    lanes = lambda block: pl.ds((block % count) * LANES, LANES)
    trace = jnp.zeros((), jnp.float32)
    for i in range(count):
        trace = trace + jnp.sum(g_ref[lanes(i), lanes(0)] * unit[:LANES, :LANES])
    factor = 1.0 / (jnp.sqrt(trace) + 1e-07)
    for i in range(count):
        for j in range(count // 2 + 1):
            values = g_ref[lanes(i), lanes(j)] * (factor * factor)
            gh[lanes(i), lanes(i + j)], gl[lanes(i), lanes(i + j)] = split(values)
            if 0 < j < count // 2:
                values = values.T
                gh[lanes(i + j), lanes(i)], gl[lanes(i + j), lanes(i)] = split(values)

    def put(high, low, i, j, values):
        high[rows(i), rows(j)], low[rows(i), rows(j)] = split(values)
        if i != j:
            high[rows(j), rows(i)], low[rows(j), rows(i)] = split(values.T)

    def symmetric(left, right, emit):
        for i in range(blocks):
            columns = pl.ds(i * BLK, size - i * BLK)
            values = product(
                left[0][rows(i), :], left[1][rows(i), :], right[0][:, columns], right[1][:, columns]
            )
            for j in range(i, blocks):
                emit(i, j, values[:, (j - i) * BLK : (j - i + 1) * BLK])

    def emit_terms(i, j, values):
        gram = gh[rows(i), rows(j)].astype(jnp.float32) + gl[rows(i), rows(j)].astype(jnp.float32)
        terms = second * gram + third * values
        if i == j:
            terms = terms + first * unit
        put(ph, pw, i, j, terms)

    def emit_total(i, j, values):
        q_ref[rows(i), rows(j)] = values
        if i != j:
            q_ref[rows(j), rows(i)] = values.T

    symmetric((gh, gl), (gh, gl), emit_terms)
    for i in range(blocks):
        q_ref[rows(i), :] = (
            ph[rows(i), :].astype(jnp.float32) + pw[rows(i), :].astype(jnp.float32)
        ) * factor

    def one_step(step, carry):
        symmetric((ph, pw), (gh, gl), functools.partial(put, th, tl))
        symmetric((th, tl), (ph, pw), functools.partial(put, gh, gl))
        symmetric((gh, gl), (gh, gl), emit_terms)
        for i in range(blocks):
            th[rows(i), :], tl[rows(i), :] = split(q_ref[rows(i), :])
        symmetric((ph, pw), (th, tl), emit_total)
        return carry

    lax.fori_loop(0, NEWTON - 1, one_step, 0)


def polar_factor(gramian):
    size = gramian.shape[0]
    vmem = pl.BlockSpec(memory_space=pltpu.VMEM)
    return pl.pallas_call(
        polar_kernel,
        out_shape=jax.ShapeDtypeStruct((size, size), jnp.float32),
        in_specs=[vmem],
        out_specs=vmem,
        scratch_shapes=[pltpu.VMEM((size, size), jnp.bfloat16)] * 6,
        compiler_params=pltpu.CompilerParams(vmem_limit_bytes=48 * 2**20),
        cost_estimate=pl.CostEstimate(
            flops=17 * 6 * size**3, bytes_accessed=8 * size * size, transcendentals=0
        ),
    )(gramian)


def finish_kernel(sub, pieces, norm_ref, q_ref, *refs):
    lines, others, refs = refs[0:6:2], refs[1:6:2], refs[6:]
    moments, weights, refs = refs[:4], refs[4:8], refs[8:]
    carried, results, refs = refs[:4], refs[4:8], refs[8:]
    qs, refs = refs[0], refs[1:]
    staged, values, highs, lows = refs[:4], refs[4:8], refs[8:12], refs[12:16]
    sends, arrivals, near_sems, load_sems, value_sems, out_sems = refs[16:]
    size = q_ref.shape[0]
    half = size // 2
    step = half // pieces
    w, n = lax.axis_index("wide"), lax.axis_index("narrow")
    own = n // sub
    across = partner(own, 2)
    far = own // 2
    near_place, far_place = place_at("narrow", sub), place_at("narrow", 2 * sub)
    side_place = place_at("wide", 1)
    greet([near_place, far_place, side_place])
    y = w % 2
    rows = lambda side, p: pl.ds(pl.multiple_of(side * half + p * step, 8), step)
    slot = iter(range(1 + 4 * pieces))
    copies = []

    def push(src, dst, place):
        copies.append(send(src, dst, sends, arrivals, next(slot), place))
        return copies[-1]

    crossing = [
        push(q_ref.at[rows(y, p)], qs.at[own, rows(y, p)], far_place) for p in range(pieces)
    ]
    near_own = push(q_ref, qs.at[own], near_place)
    keep = pltpu.make_async_copy(q_ref, qs.at[own], near_sems.at[0])
    keep.start()
    blocks = lax.axis_size("wide")
    stages = staged
    whole = []
    for k in range(MATRICES):
        sources = (lines[max(k - 1, 0)], others[max(k - 1, 0)])
        extent = stages[k].shape[0] // 2
        for side, source in zip((y, 1 - y), sources):
            if k >= 2:
                spot = stages[k].at[pl.ds(pl.multiple_of(side * extent, 8), extent), :]
                pltpu.make_async_copy(source, spot, load_sems.at[k]).start()
                continue
            share = (stages[0].shape[0] // blocks, stages[1].shape[0] // blocks)
            for b in range(blocks // 2):
                start = b * (share[0] + share[1]) + k * share[0]
                to = pl.multiple_of(side * extent + b * share[k], 8)
                pltpu.make_async_copy(
                    source.at[pl.ds(start, share[k]), :],
                    stages[k].at[pl.ds(to, share[k]), :],
                    load_sems.at[k],
                ).start()
        whole.append(pltpu.make_async_copy(stages[k], stages[k], load_sems.at[k]))
    fills = []
    for k in range(MATRICES):
        fills.append(pltpu.make_async_copy(moments[k], values[k], value_sems.at[k]))
        fills[-1].start()
    norm = norm_ref[0:1, 0:1]
    clip = jnp.minimum(1.0, 1.0 / (norm + 1e-06))

    def blend_rows(value, stage):
        slab = 16

        def one(i, carry):
            spot = pl.ds(pl.multiple_of(i * slab, 8), slab)
            value[spot, :] = muon_momentum * value[spot, :] + clip * stage[spot, :]
            return carry

        lax.fori_loop(0, value.shape[0] // slab, one, 0, unroll=UNROLL)

    def blend_columns(value, stage):
        def one(i, carry):
            spot = pl.ds(pl.multiple_of(i * LANES, LANES), LANES)
            value[:, spot] = muon_momentum * value[:, spot] + clip * stage[spot, :].T
            return carry

        lax.fori_loop(0, value.shape[1] // LANES, one, 0)

    outs = []
    for k in range(MATRICES):
        whole[k].wait()
        fills[k].wait()
        blend = blend_columns if k in COLUMNS else blend_rows
        blend(values[k], stages[k])
    for k in range(MATRICES):
        outs.append(pltpu.make_async_copy(values[k], carried[k], out_sems.at[k]))
        outs[-1].start()
    for k in range(MATRICES):

        def cut(i, carry, k=k):
            spot = pl.ds(pl.multiple_of(i * SLAB, SLAB), SLAB)
            highs[k][spot, :], lows[k][spot, :] = split(values[k][spot, :])
            return carry

        lax.fori_loop(0, values[k].shape[0] // SLAB, cut, 0, unroll=UNROLL)
    for k in range(MATRICES):
        outs[k].wait()
        fills[k] = pltpu.make_async_copy(weights[k], values[k], value_sems.at[k])
        fills[k].start()

    dot = lambda left, right, dims: lax.dot_general(
        left, right, (dims, ((), ())), preferred_element_type=jnp.float32
    )
    lengths = (3 * D, D, FF, FF)

    def process(k, start):
        spot = pl.ds(pl.multiple_of(start, BLK), BLK)
        q_high, q_low = split(qs[k, spot, :])
        high, low = highs[k], lows[k]
        scale = muon_rate * 0.2 * math.sqrt(lengths[k])
        if k in COLUMNS:
            dims = ((1,), (0,))
            polar = dot(q_high, high[...], dims) + (
                dot(q_high, low[...], dims) + dot(q_low, high[...], dims)
            )
            where = (spot, slice(None))
        else:
            dims = ((1,), (1,))
            polar = dot(high[...], q_high, dims) + (
                dot(low[...], q_high, dims) + dot(high[...], q_low, dims)
            )
            where = (slice(None), spot)
        values[k][where] = values[k][where] * (1.0 - muon_rate * weight_decay) - scale * polar
        pltpu.make_async_copy(
            values[k].at[where], results[k].at[where], out_sems.at[k]
        ).start()

    def pair(first, starts):
        for side in range(2):
            matrices = (0, 1) if first == (side == 0) else (2, 3)

            @pl.when(far == side)
            def _(matrices=matrices):
                for k in matrices:
                    lax.fori_loop(
                        0, len(starts), lambda i, c, k=k: (process(k, starts[0] + i * BLK), c)[1], 0
                    )

    aside, near_across, near_side = [], [], []

    def forward(p):
        crossing[p].wait_recv()
        spot = qs.at[across, rows(y, p)]
        aside.append(push(spot, spot, side_place))
        near_across.append(push(spot, spot, near_place))

    def forward_side(p):
        aside[p].wait_recv()
        spot = qs.at[across, rows(1 - y, p)]
        near_side.append(push(spot, spot, near_place))

    forward(0)
    keep.wait()
    near_own.wait_recv()
    for k in range(MATRICES):
        fills[k].wait()
    pair(True, [0, BLK])
    forward(1)
    pair(True, [2 * BLK, 3 * BLK])
    forward_side(0)
    for p in range(2, pieces):
        forward(p)
        forward_side(p - 1)
    group = BLK // step
    for copy in near_across:
        copy.wait_recv()
    pair(False, [y * half + i * BLK for i in range(half // BLK)])
    for copy in near_side[:group]:
        copy.wait_recv()
    pair(False, [(1 - y) * half])
    forward_side(pieces - 1)
    for copy in near_side[group:]:
        copy.wait_recv()
    pair(False, [(1 - y) * half + BLK])
    for copy in copies:
        copy.wait_send()
    for k in range(MATRICES):
        pltpu.make_async_copy(values[k], results[k], out_sems.at[k]).wait()


def finish(norm, factor, lines, others, moments, weights, number):
    pieces = 4
    size = factor.shape[0]
    sub = lax.axis_size("narrow") // MATRICES
    anywhere = pl.BlockSpec(memory_space=pl.ANY)
    operands = [part for both in zip(lines, others) for part in both]
    shapes = [jax.ShapeDtypeStruct(moment.shape, jnp.float32) for moment in moments]
    staged = [(moment.size // size, size) for moment in moments]
    slots = 1 + 4 * pieces
    outs = pl.pallas_call(
        functools.partial(finish_kernel, sub, pieces),
        out_shape=tuple(shapes + shapes),
        in_specs=[pl.BlockSpec(memory_space=pltpu.VMEM)] + [anywhere] * (1 + len(operands) + 8),
        out_specs=(anywhere,) * 8,
        scratch_shapes=[pltpu.VMEM((MATRICES, size, size), jnp.float32)]
        + [pltpu.VMEM(shape, jnp.float32) for shape in staged]
        + [pltpu.VMEM(moment.shape, jnp.float32) for moment in moments]
        + [pltpu.VMEM(moment.shape, jnp.bfloat16) for moment in moments]
        + [pltpu.VMEM(moment.shape, jnp.bfloat16) for moment in moments]
        + [
            pltpu.SemaphoreType.DMA((slots,)),
            pltpu.SemaphoreType.DMA((slots,)),
            pltpu.SemaphoreType.DMA((1,)),
            pltpu.SemaphoreType.DMA((MATRICES,)),
            pltpu.SemaphoreType.DMA((MATRICES,)),
            pltpu.SemaphoreType.DMA((MATRICES,)),
        ],
        compiler_params=pltpu.CompilerParams(
            collective_id=number, has_side_effects=True, vmem_limit_bytes=60 * 2**20
        ),
        cost_estimate=pl.CostEstimate(
            flops=18 * size * size * size, bytes_accessed=80 * size * size, transcendentals=0
        ),
    )(norm, factor, *operands, *moments, *weights)
    return outs[:4], outs[4:]


def adam_update(weight, moment, square, gradient):
    moment_new = first_decay * moment + (1.0 - first_decay) * gradient
    square_new = second_decay * square + (1.0 - second_decay) * gradient * gradient
    moment_hat = moment_new / (1.0 - first_decay**STEP)
    square_hat = square_new / (1.0 - second_decay**STEP)
    weight_new = weight * (1.0 - adam_rate * weight_decay) - adam_rate * moment_hat / (
        jnp.sqrt(square_hat) + 1e-08
    )
    return (moment_new, square_new, weight_new)


def column_shifts(strip, column):
    rows = strip.shape[0]
    left = jnp.where(column == 0, 0.0, pltpu.roll(strip, 1, 0))
    right = jnp.where(column == rows - 1, 0.0, pltpu.roll(strip, rows - 1, 0))
    return (left, strip, right)


def tap_rows(shifts, taps):
    return [
        taps[3 * i] * shifts[0] + taps[3 * i + 1] * shifts[1] + taps[3 * i + 2] * shifts[2]
        for i in range(3)
    ]


def strip_at(index):
    return pl.ds(pl.multiple_of(index * GRID, GRID), GRID)


def convolve(load, taps, emit):
    shape = load(0).shape
    column = lax.broadcasted_iota(jnp.int32, shape, 0)

    def one(r, carry):
        above, here = carry
        upper, middle, lower = tap_rows(column_shifts(load(r), column), taps)
        emit(r - 1, here + lower)
        return (upper, above + middle)

    upper, middle, _ = tap_rows(column_shifts(load(0), column), taps)
    above, here = lax.fori_loop(1, GRID, one, (upper, middle))
    emit(GRID - 1, here)


def kernel_sums(load, weigh, width):
    column = lax.broadcasted_iota(jnp.int32, (GRID, width), 0)
    fold = lambda values: values.reshape(GRID // 8, 8, width).sum(axis=0)
    zero = jnp.zeros((8, width), jnp.float32)

    def one(r, carry):
        sums = carry
        shifts = column_shifts(load(r), column)
        later = weigh(jnp.minimum(r + 1, GRID - 1)) * jnp.where(r < GRID - 1, 1.0, 0.0)
        earlier = weigh(jnp.maximum(r - 1, 0)) * jnp.where(r > 0, 1.0, 0.0)
        terms = (later, weigh(r), earlier)
        return tuple(
            sums[3 * i + j] + fold(terms[i] * shifts[j]) for i in range(3) for j in range(3)
        )

    return lax.fori_loop(0, GRID, one, (zero,) * 9)


def middle_kernel(
    pieces,
    entry_ref,
    cotangent_ref,
    live_ref,
    gate_ref,
    expand_any,
    reduce_any,
    taps_ref,
    ffn_half_ref,
    grad_entry_any,
    reduce_share,
    expand_share,
    grad_taps_ref,
    expand_full,
    reduce_full,
    grad_ffn,
    upward,
    weight,
    active,
    grad_up,
    ffn,
    back,
    grad_reduce,
    grad_expand,
    ffn_inbox,
    near,
    far,
    held,
    local,
    reduce_held,
    reduce_beside,
    reduce_inbox,
    reduce_loads,
    expand_held,
    expand_beside,
    expand_inbox,
    expand_loads,
    weight_sems,
    sends,
    arrivals,
):
    units = expand_any.shape[1]
    block = min(BLK, units // 2)
    steps = units // block
    groups = steps // 2
    y, z = wide_parts()
    count = lax.axis_size("wide") // 2
    far_bits = bits_of(lax.axis_size("narrow"))[1:]
    greet(
        [place_at("narrow", bit) for bit in [1] + far_bits]
        + [place_at("wide", bit) for bit in bits_of(lax.axis_size("wide"))]
    )

    def block_index(step):
        side = 1 - y if step < groups else y
        return side * groups + line_partner(z // (count // groups), groups - 1 - step % groups)

    fetches = []
    for step in range(steps):
        spot = pl.ds(pl.multiple_of(block_index(step) * block, LANES), block)
        pair = (
            pltpu.make_async_copy(
                expand_any.at[:, spot], expand_full.at[:, spot], weight_sems.at[step]
            ),
            pltpu.make_async_copy(
                reduce_any.at[spot, :], reduce_full.at[spot, :], weight_sems.at[steps + step]
            ),
        )
        for copy in pair:
            copy.start()
        fetches.append(pair)
    gate, live = gate_ref[...], live_ref[...]

    def gated(i, carry):
        spot = slab_at(i)
        result = cotangent_ref[spot, :].astype(jnp.float32) * live
        grad_ffn[spot, :] = (gate * result).astype(jnp.bfloat16)
        return carry

    lax.fori_loop(0, grad_ffn.shape[0] // SLAB, gated, 0, unroll=UNROLL)

    def work(spot, fresh):
        expand_low = expand_full[:, spot].astype(jnp.bfloat16)
        reduce_low = reduce_full[spot, :].astype(jnp.bfloat16)
        taps = [taps_ref[t : t + 1, spot] for t in range(9)]
        upward[...] = dot_of(entry_ref[...], expand_low, 1, 0)
        weight[...] = dot_of(grad_ffn[...], reduce_low, 1, 1)

        def emit_middle(r, values):
            inner = gelu_slope * (values + gelu_cubic * values * values * values)
            bent = jnp.tanh(inner)
            active[strip_at(r), :] = (0.5 * values * (1.0 + bent)).astype(jnp.bfloat16)
            turn = 0.5 * (1.0 + bent) + 0.5 * values * (1.0 - bent * bent) * (
                gelu_slope * (1.0 + 3.0 * gelu_cubic * values * values)
            )
            weight[strip_at(r), :] = weight[strip_at(r), :] * turn

        convolve(lambda r: upward[strip_at(r), :], taps, emit_middle)

        def emit_grad(r, values):
            grad_up[strip_at(r), :] = values.astype(jnp.bfloat16)

        convolve(lambda r: weight[strip_at(r), :], taps[::-1], emit_grad)
        sums = kernel_sums(
            lambda r: upward[strip_at(r), :], lambda r: weight[strip_at(r), :], block
        )
        for t in range(9):
            grad_taps_ref[t : t + 1, spot] = jnp.sum(sums[t], axis=0, keepdims=True)
        grad_reduce[spot, :] = dot_of(active[...], grad_ffn[...], 0, 0)
        grad_expand[spot, :] = dot_of(grad_up[...], entry_ref[...], 0, 0)
        if fresh:
            ffn[...] = dot_of(active[...], reduce_low, 1, 0)
            back[...] = dot_of(grad_up[...], expand_low, 1, 1)
        else:
            ffn[...] += dot_of(active[...], reduce_low, 1, 0)
            back[...] += dot_of(grad_up[...], expand_low, 1, 1)

    base = (len(far_bits) + 2) * pieces + 1
    reduce_sum = Scatter(
        grad_reduce, reduce_held, reduce_beside, reduce_inbox, sends, arrivals, reduce_loads, base
    )
    expand_sum = Scatter(
        grad_expand,
        expand_held,
        expand_beside,
        expand_inbox,
        sends,
        arrivals,
        expand_loads,
        base + Scatter.slots(),
    )
    for step in range(groups):
        for copy in fetches[step]:
            copy.wait()
        work(pl.ds(pl.multiple_of(block_index(step) * block, LANES), block), step == 0)
        size = count // groups
        ready = [(groups - 1 - step) * size + e for e in reversed(range(size))]
        for scatter in (reduce_sum, expand_sum):
            for e in ready:
                scatter.give(e)
    for step in range(groups, steps):
        for copy in fetches[step]:
            copy.wait()

    def later(i, carry):
        side_block = line_partner_of(z // (count // groups), i, groups)
        work(pl.ds(pl.multiple_of((y * groups + side_block) * block, LANES), block), False)
        return carry

    lax.fori_loop(0, groups, later, 0)
    narrow = NarrowSum(
        far_bits, pieces, back, grad_entry_any, near, far, held, sends, arrivals, local, 0
    )
    narrow.start()
    core = lax.axis_index("narrow") % 2
    half = ffn.shape[0] // 2
    side_rows = lambda side: pl.ds(pl.multiple_of(side * half, 8), half)
    ffn_copy = send(
        ffn.at[side_rows(1 - core)], ffn_inbox, sends, arrivals, base - 1, place_at("narrow", 1)
    )
    for scatter in (reduce_sum, expand_sum):
        scatter.load()
    for p in range(pieces):
        narrow.begin(p)
    left = [list(reversed(range(count))), list(reversed(range(count)))]
    scatters = (reduce_sum, expand_sum)
    scatters[0].step(left[0].pop(0))
    scatters[1].step(left[1].pop(0))
    ffn_copy.wait_recv()
    ffn_half_ref[...] = ffn[side_rows(core), :] + ffn_inbox[...]
    turns = [0, 1, 0, 0, 1, 1]
    for b in range(len(far_bits)):
        for p in range(pieces):
            narrow.step(b, p)
            if turns and len(left[turns[0]]) > 1:
                which = turns.pop(0)
                scatters[which].step(left[which].pop(0))
    outs = []
    for which, share in ((0, reduce_share), (1, expand_share)):
        while left[which]:
            scatters[which].step(left[which].pop(0))
        out = pltpu.make_async_copy(scatters[which].held.at[0], share, scatters[which].local.at[0])
        out.start()
        outs.append(out)
    narrow.finish()
    ffn_copy.wait_send()
    for scatter in scatters:
        scatter.finish()
    for out in outs:
        out.wait()


def line_partner_of(place, index, count):
    flipped = 0 * place
    for bit in bits_of(count):
        one, two = (place // bit) % 2, (index // bit) % 2
        flipped = flipped + (one + two - 2 * one * two) * bit
    return flipped


def middle(entry, cotangent, live, gate, expand, reduce, taps, number):
    tokens, width = entry.shape
    units = expand.shape[1]
    block = min(BLK, units // 2)
    steps = units // block
    pieces = 4
    narrow_bits = bits_of(lax.axis_size("narrow"))
    slots = (len(narrow_bits) + 1) * pieces + 1 + 2 * Scatter.slots()
    vmem = pl.BlockSpec(memory_space=pltpu.VMEM)
    anywhere = pl.BlockSpec(memory_space=pl.ANY)
    f32 = lambda *shape: jax.ShapeDtypeStruct(shape, jnp.float32)
    wide = lambda *shape: pltpu.VMEM(shape, jnp.float32)
    low = lambda *shape: pltpu.VMEM(shape, jnp.bfloat16)
    share = block_shape((units, width))
    return pl.pallas_call(
        functools.partial(middle_kernel, pieces),
        out_shape=(
            f32(tokens // 2, width),
            f32(tokens, width),
            f32(*share),
            f32(*share),
            f32(9, units),
        ),
        in_specs=[vmem, vmem, vmem, vmem, anywhere, anywhere, vmem],
        out_specs=(vmem, anywhere, anywhere, anywhere, vmem),
        scratch_shapes=[
            wide(width, units),
            wide(units, width),
            low(tokens, width),
            wide(tokens, block),
            wide(tokens, block),
            low(tokens, block),
            low(tokens, block),
            wide(tokens, width),
            wide(tokens, width),
            wide(units, width),
            wide(units, width),
            wide(tokens // 2, width),
        ]
        + narrow_scratch((tokens, width), pieces)
        + scatter_scratch((units, width)) * 2
        + [
            pltpu.SemaphoreType.DMA((2 * steps,)),
            pltpu.SemaphoreType.DMA((slots,)),
            pltpu.SemaphoreType.DMA((slots,)),
        ],
        compiler_params=pltpu.CompilerParams(
            collective_id=number, has_side_effects=True, vmem_limit_bytes=60 * 2**20
        ),
        cost_estimate=pl.CostEstimate(
            flops=12 * tokens * width * units,
            bytes_accessed=200 * tokens * width,
            transcendentals=tokens * units,
        ),
    )(entry, cotangent, live, gate, expand, reduce, taps)


def norm_strip(values):
    average = jnp.mean(values, axis=-1, keepdims=True)
    centred = values - average
    spread_of = jnp.mean(centred * centred, axis=-1, keepdims=True)
    inverse = lax.rsqrt(spread_of + 1e-06)
    return centred * inverse, inverse


def slab_at(index):
    return pl.ds(pl.multiple_of(index * SLAB, SLAB), SLAB)


def fold_rows(values):
    return values.reshape(values.shape[0] // 8, 8, values.shape[1]).sum(axis=0)


def mixer_kernel_forward(tokens_ref, shift_ref, scale_ref, taps_ref, out_ref, entered):
    stretch = 1.0 + scale_ref[...]
    offset = shift_ref[...]

    def enter(r, carry):
        normed, _ = norm_strip(tokens_ref[slab_at(r), :].astype(jnp.float32))
        entered[slab_at(r), :] = normed * stretch + offset
        return carry

    rows, width = tokens_ref.shape
    lax.fori_loop(0, rows // SLAB, enter, 0, unroll=UNROLL)
    for start in range(0, width, BLK):
        lanes = pl.ds(start, BLK)

        def emit(r, values, lanes=lanes):
            out_ref[strip_at(r), lanes] = values.astype(jnp.bfloat16)

        taps = [taps_ref[t : t + 1, lanes] for t in range(9)]
        convolve(lambda r, lanes=lanes: entered[strip_at(r), lanes], taps, emit)


def mixer_forward(tokens, shift, scale, taps):
    rows, width = tokens.shape
    vmem = pl.BlockSpec(memory_space=pltpu.VMEM)
    return pl.pallas_call(
        mixer_kernel_forward,
        out_shape=jax.ShapeDtypeStruct((rows, width), jnp.bfloat16),
        in_specs=[vmem] * 4,
        out_specs=vmem,
        scratch_shapes=[pltpu.VMEM((rows, width), jnp.float32)],
        compiler_params=pltpu.CompilerParams(vmem_limit_bytes=40 * 2**20),
        cost_estimate=pl.CostEstimate(
            flops=40 * rows * width, bytes_accessed=4 * rows * width, transcendentals=0
        ),
    )(tokens, shift, scale, taps)


def mixer_kernel_backward(
    tokens_ref,
    shift_ref,
    scale_ref,
    taps_ref,
    grad_mixed_ref,
    grad_hidden_ref,
    out_ref,
    grad_taps_ref,
    grad_shift_ref,
    grad_scale_ref,
    normed_ref,
    back_ref,
    inverse_ref,
):
    width = tokens_ref.shape[1]
    stretch = 1.0 + scale_ref[...]

    def enter(r, carry):
        normed, inverse = norm_strip(tokens_ref[slab_at(r), :].astype(jnp.float32))
        normed_ref[slab_at(r), :] = normed
        inverse_ref[slab_at(r), :] = jnp.broadcast_to(inverse, (SLAB, LANES))
        return carry

    rows = tokens_ref.shape[0]
    lax.fori_loop(0, rows // SLAB, enter, 0, unroll=UNROLL)
    for start in range(0, width, BLK):
        lanes = pl.ds(start, BLK)
        taps = [taps_ref[t : t + 1, lanes] for t in range(9)]
        stretch_part = 1.0 + scale_ref[:, lanes]
        offset_part = shift_ref[:, lanes]

        def emit(r, values, lanes=lanes):
            back_ref[strip_at(r), lanes] = values

        def entered(r, lanes=lanes, stretch_part=stretch_part, offset_part=offset_part):
            return normed_ref[strip_at(r), lanes] * stretch_part + offset_part

        weigh = lambda r, lanes=lanes: grad_mixed_ref[strip_at(r), lanes]
        convolve(weigh, taps[::-1], emit)
        sums = kernel_sums(entered, weigh, BLK)
        for t in range(9):
            grad_taps_ref[t : t + 1, lanes] = jnp.sum(sums[t], axis=0, keepdims=True)

    def leave(r, carry):
        shifts, scales = carry
        normed = normed_ref[slab_at(r), :]
        back = back_ref[slab_at(r), :]
        stretched = back * stretch
        first = jnp.mean(stretched, axis=-1, keepdims=True)
        second = jnp.mean(stretched * normed, axis=-1, keepdims=True)
        inverse = inverse_ref[slab_at(r), :][:, :1]
        out = grad_hidden_ref[slab_at(r), :] + (stretched - first - normed * second) * inverse
        out_ref[slab_at(r), :] = out.astype(jnp.bfloat16)
        return shifts + fold_rows(back), scales + fold_rows(back * normed)

    zero = jnp.zeros((8, width), jnp.float32)
    shifts, scales = lax.fori_loop(0, rows // SLAB, leave, (zero, zero), unroll=UNROLL)
    grad_shift_ref[...] = jnp.sum(shifts, axis=0, keepdims=True)
    grad_scale_ref[...] = jnp.sum(scales, axis=0, keepdims=True)


def mixer_backward(tokens, shift, scale, taps, grad_mixed, grad_hidden):
    rows, width = tokens.shape
    vmem = pl.BlockSpec(memory_space=pltpu.VMEM)
    f32 = lambda *shape: jax.ShapeDtypeStruct(shape, jnp.float32)
    return pl.pallas_call(
        mixer_kernel_backward,
        out_shape=(
            jax.ShapeDtypeStruct((rows, width), jnp.bfloat16),
            f32(9, width),
            f32(1, width),
            f32(1, width),
        ),
        in_specs=[vmem] * 6,
        out_specs=(vmem,) * 4,
        scratch_shapes=[
            pltpu.VMEM((rows, width), jnp.float32),
            pltpu.VMEM((rows, width), jnp.float32),
            pltpu.VMEM((rows, LANES), jnp.float32),
        ],
        compiler_params=pltpu.CompilerParams(vmem_limit_bytes=48 * 2**20),
        cost_estimate=pl.CostEstimate(
            flops=100 * rows * width, bytes_accessed=12 * rows * width, transcendentals=0
        ),
    )(tokens, shift, scale, taps, grad_mixed, grad_hidden)


def hidden_kernel_backward(
    hidden_ref,
    branch_ref,
    grad_entry_ref,
    cotangent_ref,
    live_ref,
    scale_ref,
    gate_ref,
    grad_hidden_ref,
    grad_branch_ref,
    grad_shift_ref,
    grad_scale_ref,
    grad_gate_ref,
):
    width = hidden_ref.shape[1]
    stretch = 1.0 + scale_ref[...]
    gate = gate_ref[...]
    live = live_ref[...]

    def one(r, carry):
        shifts, scales, gates = carry
        normed, inverse = norm_strip(hidden_ref[slab_at(r), :])
        back = grad_entry_ref[slab_at(r), :]
        stretched = back * stretch
        first = jnp.mean(stretched, axis=-1, keepdims=True)
        second = jnp.mean(stretched * normed, axis=-1, keepdims=True)
        grad = cotangent_ref[slab_at(r), :].astype(jnp.float32) * live + (
            stretched - first - normed * second
        ) * inverse
        grad_hidden_ref[slab_at(r), :] = grad
        grad_branch_ref[slab_at(r), :] = (gate * grad).astype(jnp.bfloat16)
        return (
            shifts + fold_rows(back),
            scales + fold_rows(back * normed),
            gates + fold_rows(branch_ref[slab_at(r), :] * grad),
        )

    zero = jnp.zeros((8, width), jnp.float32)
    shifts, scales, gates = lax.fori_loop(
        0, hidden_ref.shape[0] // SLAB, one, (zero, zero, zero), unroll=UNROLL
    )
    grad_shift_ref[...] = jnp.sum(shifts, axis=0, keepdims=True)
    grad_scale_ref[...] = jnp.sum(scales, axis=0, keepdims=True)
    grad_gate_ref[...] = jnp.sum(gates, axis=0, keepdims=True)


def hidden_backward(hidden, branch, grad_entry, cotangent, live, scale, gate):
    rows, width = hidden.shape
    vmem = pl.BlockSpec(memory_space=pltpu.VMEM)
    f32 = lambda *shape: jax.ShapeDtypeStruct(shape, jnp.float32)
    return pl.pallas_call(
        hidden_kernel_backward,
        out_shape=(
            f32(rows, width),
            jax.ShapeDtypeStruct((rows, width), jnp.bfloat16),
            f32(1, width),
            f32(1, width),
            f32(1, width),
        ),
        in_specs=[vmem] * 7,
        out_specs=(vmem,) * 5,
        compiler_params=pltpu.CompilerParams(vmem_limit_bytes=48 * 2**20),
        cost_estimate=pl.CostEstimate(
            flops=30 * rows * width, bytes_accessed=22 * rows * width, transcendentals=0
        ),
    )(hidden, branch, grad_entry, cotangent, live, scale, gate)


def dot_of(left, right, left_axis, right_axis):
    return lax.dot_general(
        left,
        right,
        (((left_axis,), (right_axis,)), ((), ())),
        preferred_element_type=jnp.float32,
    )


def head_only(values, head):
    lane = lax.broadcasted_iota(jnp.int32, values.shape, 1)
    return jnp.where(lane // HEAD == head, values, jnp.zeros_like(values))


def attend_kernel(
    mixed_ref, attend_ref, triple_ref, context_ref, logsum_ref, low_ref, turned, values_t
):
    tokens = mixed_ref.shape[0]
    width = context_ref.shape[1]
    step = min(BLK, width)
    for start in range(0, 3 * width, step):
        columns = pl.ds(start, step)
        low_ref[:, columns] = attend_ref[:, columns].astype(jnp.bfloat16)
        triple_ref[:, columns] = dot_of(mixed_ref[...], low_ref[:, columns], 1, 0).astype(
            jnp.bfloat16
        )
    values_t[...] = triple_ref[:, pl.ds(2 * width, width)].T
    scale = jnp.bfloat16(HEAD ** (-0.5))
    for head in range(width // HEAD):
        pair = head * HEAD // LANES * LANES
        inside = head % (LANES // HEAD)

        def one(block, carry, head=head, pair=pair, inside=inside):
            spot = pl.ds(pl.multiple_of(block * QUERIES, QUERIES), QUERIES)
            queries = head_only(triple_ref[spot, pl.ds(pair, LANES)], inside) * scale
            scores = dot_of(triple_ref[:, pl.ds(width + pair, LANES)], queries, 1, 1)
            peak = jnp.max(scores, axis=0, keepdims=True)
            weights = jnp.exp(scores - peak)
            total = jnp.sum(weights, axis=0, keepdims=True)
            soft_low = (weights * (1.0 / total)).astype(jnp.bfloat16)
            turned[pl.ds(head * HEAD, HEAD), spot] = dot_of(
                values_t[pl.ds(head * HEAD, HEAD), :], soft_low, 1, 0
            )
            logsum_ref[pl.ds(head, 1), spot] = peak + jnp.log(total)
            return carry

        lax.fori_loop(0, tokens // QUERIES, one, 0)
    context_ref[...] = turned[...].T.astype(jnp.bfloat16)


def attend(mixed, attend_weight):
    tokens, width = mixed.shape
    own = attend_weight.shape[1] // 3
    vmem = pl.BlockSpec(memory_space=pltpu.VMEM)
    return pl.pallas_call(
        attend_kernel,
        out_shape=(
            jax.ShapeDtypeStruct((tokens, 3 * own), jnp.bfloat16),
            jax.ShapeDtypeStruct((tokens, own), jnp.bfloat16),
            jax.ShapeDtypeStruct((8, tokens), jnp.float32),
            jax.ShapeDtypeStruct(attend_weight.shape, jnp.bfloat16),
        ),
        in_specs=[vmem] * 2,
        out_specs=(vmem,) * 4,
        scratch_shapes=[
            pltpu.VMEM((own, tokens), jnp.float32),
            pltpu.VMEM((own, tokens), jnp.bfloat16),
        ],
        compiler_params=pltpu.CompilerParams(vmem_limit_bytes=40 * 2**20),
        cost_estimate=pl.CostEstimate(
            flops=16 * tokens * tokens * own,
            bytes_accessed=12 * tokens * width,
            transcendentals=tokens * tokens * own // HEAD,
        ),
    )(mixed, attend_weight)


def attend_back_kernel(
    mixed_ref,
    attend_ref,
    output_ref,
    triple_ref,
    context_ref,
    logsum_ref,
    grad_branch_ref,
    attend_out_ref,
    grad_mixed_ref,
    grad_context,
    keys_t,
    grad_queries_t,
    grad_keys,
    grad_values,
    grad_triple,
):
    tokens = mixed_ref.shape[0]
    width = output_ref.shape[0]
    grad_context[...] = dot_of(grad_branch_ref[...], output_ref[...], 1, 1).astype(jnp.bfloat16)
    keys_t[...] = triple_ref[:, pl.ds(width, width)].T
    grad_keys[...] = jnp.zeros_like(grad_keys)
    grad_values[...] = jnp.zeros_like(grad_values)
    scale = HEAD ** (-0.5)
    low_scale = jnp.bfloat16(scale)
    for head in range(width // HEAD):
        pair = head * HEAD // LANES * LANES
        inside = head % (LANES // HEAD)
        lanes = pl.ds(pair, LANES)

        def one(block, carry, head=head, pair=pair, inside=inside, lanes=lanes):
            spot = pl.ds(pl.multiple_of(block * QUERIES, QUERIES), QUERIES)
            queries = head_only(triple_ref[spot, lanes], inside)
            back = head_only(grad_context[spot, lanes], inside)
            scores = dot_of(triple_ref[:, pl.ds(width + pair, LANES)], queries * low_scale, 1, 1)
            weights = jnp.exp(scores - logsum_ref[pl.ds(head, 1), spot])
            grad_weights = dot_of(triple_ref[:, pl.ds(2 * width + pair, LANES)], back, 1, 1)
            grad_values[:, lanes] += dot_of(weights.astype(jnp.bfloat16), back, 1, 0)
            inner = jnp.sum(weights * grad_weights, axis=0, keepdims=True)
            grad_low = (weights * (grad_weights - inner)).astype(jnp.bfloat16)
            grad_keys[:, lanes] += dot_of(grad_low, queries, 1, 0)
            grad_queries_t[pl.ds(head * HEAD, HEAD), spot] = dot_of(
                keys_t[pl.ds(head * HEAD, HEAD), :], grad_low, 1, 0
            )
            return carry

        lax.fori_loop(0, tokens // QUERIES, one, 0)
    grad_triple[:, pl.ds(0, width)] = (grad_queries_t[...].T * scale).astype(jnp.bfloat16)
    grad_triple[:, pl.ds(width, width)] = (grad_keys[...] * scale).astype(jnp.bfloat16)
    grad_triple[:, pl.ds(2 * width, width)] = grad_values[...].astype(jnp.bfloat16)
    grad_output = dot_of(context_ref[...], grad_branch_ref[...], 0, 0)
    grad_attend = dot_of(grad_triple[...], mixed_ref[...], 0, 0)
    blocks = lax.axis_size("wide")
    first, second = 3 * width // blocks, width // blocks
    for b in range(blocks):
        start = b * (first + second)
        attend_out_ref[pl.ds(start, first), :] = grad_attend[b * first : (b + 1) * first]
        attend_out_ref[pl.ds(start + first, second), :] = grad_output[b * second : (b + 1) * second]
    grad_mixed_ref[...] = dot_of(grad_triple[...], attend_ref[...], 1, 1)


def attend_back(mixed, attend_low, output_low, triple, context, logsum, grad_branch):
    tokens, width = mixed.shape
    own = output_low.shape[0]
    vmem = pl.BlockSpec(memory_space=pltpu.VMEM)
    f32 = lambda *shape: jax.ShapeDtypeStruct(shape, jnp.float32)
    return pl.pallas_call(
        attend_back_kernel,
        out_shape=(f32(4 * own, width), f32(tokens, width)),
        in_specs=[vmem] * 7,
        out_specs=(vmem,) * 2,
        scratch_shapes=[
            pltpu.VMEM((tokens, own), jnp.bfloat16),
            pltpu.VMEM((own, tokens), jnp.bfloat16),
            pltpu.VMEM((own, tokens), jnp.float32),
            pltpu.VMEM((tokens, own), jnp.float32),
            pltpu.VMEM((tokens, own), jnp.float32),
            pltpu.VMEM((tokens, 3 * own), jnp.bfloat16),
        ],
        compiler_params=pltpu.CompilerParams(vmem_limit_bytes=52 * 2**20),
        cost_estimate=pl.CostEstimate(
            flops=40 * tokens * tokens * own,
            bytes_accessed=20 * tokens * width,
            transcendentals=tokens * tokens * own // HEAD,
        ),
    )(mixed, attend_low, output_low, triple, context, logsum, grad_branch)


def narrow_hops():
    return [("narrow", bit) for bit in reversed(bits_of(lax.axis_size("narrow")))]


def narrow_position(item):
    n = lax.axis_index("narrow")
    position = 0
    for index, (_, bit) in enumerate(narrow_hops()):
        value = (n // bit) % 2
        if (item >> index) % 2:
            value = 1 - value
        position = position + value * 2**index
    return position


def entry_kernel(
    pieces,
    context_ref,
    tokens_ref,
    output_ref,
    gate_ref,
    shift_ref,
    scale_ref,
    branch_ref,
    hidden_ref,
    entry_ref,
    slots,
    output_low,
    output_inbox,
    sends,
    arrivals,
):
    rows, own = context_ref.shape
    step = rows // pieces
    hops = narrow_hops()
    count = 2 ** len(hops)
    greet([place_at(axis, bit) for axis, bit in hops])
    chunk = lambda p: pl.ds(p * step, step)
    slots[narrow_position(0)] = context_ref[...].astype(jnp.float32)
    output_copy = send(
        output_ref, output_inbox, sends, arrivals, pieces * (count - 1), place_at("narrow", 1)
    )
    gathers = []
    for p in range(pieces):
        spot_of = lambda item, p=p: slots.at[narrow_position(item), chunk(p)]
        gathers.append(Gather(spot_of(0), spot_of, hops, sends, arrivals, p * (count - 1)))
        gathers[p].step(0)
    core = lax.axis_index("narrow") % 2
    half = output_ref.shape[0]
    output_low[pl.ds(pl.multiple_of(core * half, SLAB), half), :] = output_ref[...].astype(
        jnp.bfloat16
    )
    output_copy.wait_recv()
    output_low[pl.ds(pl.multiple_of((1 - core) * half, SLAB), half), :] = output_inbox[...].astype(
        jnp.bfloat16
    )
    gate, offset, stretch = gate_ref[...], shift_ref[...], 1.0 + scale_ref[...]
    for p in range(pieces):
        for item in gathers[p].order[1:]:
            gathers[p].step(item)
        branch = jnp.zeros((step, output_ref.shape[1]), jnp.float32)
        for position in range(count):
            branch = branch + dot_of(
                slots[position, chunk(p)].astype(jnp.bfloat16),
                output_low[pl.ds(position * own, own), :],
                1,
                0,
            )
        branch_ref[chunk(p), :] = branch

        def one(i, carry, p=p):
            spot = pl.ds(pl.multiple_of(p * step + i * SLAB, SLAB), SLAB)
            hidden = tokens_ref[spot, :].astype(jnp.float32) + gate * branch_ref[spot, :]
            hidden_ref[spot, :] = hidden
            normed, _ = norm_strip(hidden)
            entry_ref[spot, :] = (normed * stretch + offset).astype(jnp.bfloat16)
            return carry

        lax.fori_loop(0, step // SLAB, one, 0, unroll=UNROLL)
    for gather in gathers:
        gather.finish()
    output_copy.wait_send()


def enter(context, tokens, output_rows, gate, shift, scale, number):
    pieces = 4
    rows, own = context.shape
    width = tokens.shape[1]
    count = lax.axis_size("narrow")
    vmem = pl.BlockSpec(memory_space=pltpu.VMEM)
    slots = pieces * (count - 1) + 1
    return pl.pallas_call(
        functools.partial(entry_kernel, pieces),
        out_shape=(
            jax.ShapeDtypeStruct((rows, width), jnp.float32),
            jax.ShapeDtypeStruct((rows, width), jnp.float32),
            jax.ShapeDtypeStruct((rows, width), jnp.bfloat16),
        ),
        in_specs=[vmem] * 6,
        out_specs=(vmem,) * 3,
        scratch_shapes=[
            pltpu.VMEM((count, rows, own), jnp.float32),
            pltpu.VMEM((width, width), jnp.bfloat16),
            pltpu.VMEM(output_rows.shape, jnp.float32),
            pltpu.SemaphoreType.DMA((slots,)),
            pltpu.SemaphoreType.DMA((slots,)),
        ],
        compiler_params=pltpu.CompilerParams(
            collective_id=number, has_side_effects=True, vmem_limit_bytes=40 * 2**20
        ),
        cost_estimate=pl.CostEstimate(
            flops=2 * rows * width * width, bytes_accessed=100 * rows * width, transcendentals=0
        ),
    )(context, tokens, output_rows, gate, shift, scale)


def all_rows(values):
    for _, bit in narrow_hops()[:-1]:
        side = (lax.axis_index("narrow") // bit) % 2
        other = permute(values, "narrow", bit)
        values = jnp.where(
            side == 0,
            jnp.concatenate([values, other], axis=0),
            jnp.concatenate([other, values], axis=0),
        )
    return values


def part(rows, second_rows):
    width = rows.shape[1]
    size = second_rows // lax.axis_size("wide")
    total = 4 * size
    blocks = rows.reshape(-1, total, width)
    return blocks[:, : total - size].reshape(-1, width), blocks[:, total - size :].reshape(-1, width)


def gram_band(matrix):
    width = matrix.shape[1]
    count = 2 * width // lax.axis_size("wide")
    start = (lax.axis_index("wide") // 2) * count
    rows = lax.dynamic_slice_in_dim(matrix, start, count, 1)
    product_rows = lax.dot_general(
        rows,
        matrix,
        (((0,), (0,)), ((), ())),
        precision=lax.Precision.HIGH,
        preferred_element_type=jnp.float32,
    )
    band = width // 2 + LANES
    twice = jnp.concatenate([product_rows, product_rows[:, :band]], axis=1)
    return jnp.concatenate(
        [
            lax.dynamic_slice_in_dim(twice[at : at + LANES], start + at, band, 1)
            for at in range(0, count, LANES)
        ],
        axis=0,
    )


def local(
    tokens,
    conditions,
    item_live,
    cotangent,
    modulation_table,
    mixer_kernel,
    hidden_kernel,
    attend_weight,
    output_weight,
    expand_weight,
    reduce_weight,
    attend_moment,
    output_moment,
    expand_moment,
    reduce_moment,
    table_first,
    table_second,
    mixer_first,
    mixer_second,
    hidden_first,
    hidden_second,
):
    live_mask = item_live.astype(jnp.float32)[:, None, None]
    modulation = modulation_table[None] + conditions
    shift_one = modulation[:, 0:1]
    scale_one = modulation[:, 1:2]
    gate_one = modulation[:, 2:3]
    shift_two = modulation[:, 3:4]
    scale_two = modulation[:, 4:5]
    gate_two = modulation[:, 5:6]
    width = tokens.shape[2]
    flat_tokens = tokens.reshape(-1, width)
    mixed_low = mixer_forward(flat_tokens, shift_one[0], scale_one[0], mixer_kernel)
    attend_flat = attend_weight.reshape(width, -1)
    triple, context, logsum, attend_low = attend(mixed_low, attend_flat)
    output_low = output_weight.astype(jnp.bfloat16)
    output_rows, context = together(all_rows(output_weight), context)
    branch, hidden, entry_low = enter(
        context, flat_tokens, output_rows, gate_one[0], shift_two[0], scale_two[0], 1
    )
    flat_cotangent = cotangent.reshape(-1, width)
    live_row = jnp.broadcast_to(live_mask[0], (1, width))
    ffn_half, grad_entry, reduce_share, expand_share, grad_hidden_kernel = middle(
        entry_low,
        flat_cotangent,
        live_row,
        gate_two[0],
        expand_weight,
        reduce_weight,
        hidden_kernel,
        2,
    )
    grad_entry, reduce_share, expand_share, ffn_half = together(
        grad_entry, reduce_share, expand_share, ffn_half
    )
    reduce_pieces = line_gather(reduce_share)
    ffn_across = permute(ffn_half, "narrow", 2)
    grad_hidden, grad_branch_low, grad_shift_two, grad_scale_two, grad_gate_one = hidden_backward(
        hidden,
        branch,
        grad_entry,
        flat_cotangent,
        live_row,
        scale_two[0],
        gate_one[0],
    )
    attend_out, mixed_partial = attend_back(
        mixed_low, attend_low, output_low, triple, context, logsum, grad_branch_low
    )
    *reduce_pieces, ffn_across, mixed_partial = together(
        *reduce_pieces, ffn_across, mixed_partial
    )
    ffn_half = ffn_half + ffn_across
    for bit in bits_of(lax.axis_size("narrow"))[2:]:
        ffn_half = ffn_half + permute(ffn_half, "narrow", bit)
    reduce_line = line_place(reduce_share, reduce_pieces)
    ffn_other = permute(ffn_half, "narrow", 1)
    grad_mixed, attend_out_share = sum_scatter(mixed_partial, attend_out, 3)
    ffn_other, grad_mixed, attend_out_share, reduce_line, expand_share = together(
        ffn_other, grad_mixed, attend_out_share, reduce_line, expand_share
    )
    expand_pieces = line_gather(expand_share)
    reduce_other = permute(reduce_line, "wide", 1)
    ffn_branch = core_place(ffn_half, ffn_other).reshape(tokens.shape)
    block_out = (live_mask * (hidden[None] + gate_two * ffn_branch)).astype(jnp.bfloat16)
    grad_result = cotangent.astype(jnp.float32) * live_mask
    grad_gate_two = jnp.sum(ffn_branch * grad_result, axis=1)
    tokens_gradient, grad_mixer_kernel, grad_shift_one, grad_scale_one = mixer_backward(
        flat_tokens,
        shift_one[0],
        scale_one[0],
        mixer_kernel,
        grad_mixed,
        grad_hidden,
    )
    tokens_gradient = tokens_gradient.reshape(tokens.shape)
    grad_table = jnp.concatenate(
        [
            grad_shift_one,
            grad_scale_one,
            grad_gate_one,
            grad_shift_two,
            grad_scale_two,
            grad_gate_two,
        ],
        axis=0,
    )
    shares = [attend_out_share, expand_share, reduce_share]
    squares = sum(
        jnp.sum((share * share).reshape(-1, width), axis=0) for share in shares
    )
    shared_rows = grad_table.shape[0] + grad_mixer_kernel.shape[0]
    hidden_rows = -(-grad_hidden_kernel.size // width)
    padding = hidden_rows * width - grad_hidden_kernel.size
    hidden_flat = jnp.pad(grad_hidden_kernel.reshape(-1), (0, padding))
    stacked = jnp.concatenate(
        [grad_table, grad_mixer_kernel, hidden_flat.reshape(hidden_rows, width), squares[None]],
        axis=0,
    )
    stacked = jnp.pad(stacked, ((0, -stacked.shape[0] % 8), (0, 0)))
    small, norm, attend_out_line = small_sums(
        stacked, attend_out_share, shared_rows, hidden_rows, 4
    )
    summed_table = small[: grad_table.shape[0]]
    summed_mixer = small[grad_table.shape[0] : shared_rows]
    summed_hidden = small[shared_rows : shared_rows + hidden_rows].reshape(-1)
    summed_hidden = summed_hidden[: hidden_kernel.size].reshape(hidden_kernel.shape)
    *expand_pieces, norm = together(*expand_pieces, norm)
    gradient_norm = norm[0, 0]
    clip_factor = jnp.minimum(1.0, 1.0 / (gradient_norm + 1e-06))
    expand_line = line_place(expand_share, expand_pieces)
    attend_line, output_line = part(attend_out_line, output_weight.shape[0])
    attend_moment_flat = attend_moment.reshape(width, -1)
    blend = lambda moment, gradient: muon_momentum * moment + clip_factor * gradient
    halves = [
        blend(own_half(attend_moment_flat, 1).T, attend_line),
        blend(own_half(output_moment, 0), output_line),
        blend(own_half(expand_moment, 1).T, expand_line),
        blend(own_half(reduce_moment, 0), reduce_line),
    ]
    bands = jnp.stack([gram_band(matrix) for matrix in halves])
    sub = lax.axis_size("narrow") // MATRICES
    gramian = gram_whole(bands.reshape(MATRICES * sub, -1, bands.shape[2]), 5)
    gramian, expand_line, attend_out_line = together(gramian, expand_line, attend_out_line)
    expand_other = permute(expand_line, "wide", 1)
    attend_out_other = permute(attend_out_line, "wide", 1)
    factor = polar_factor(gramian)
    factor, expand_other, attend_out_other, reduce_other = together(
        factor, expand_other, attend_out_other, reduce_other
    )
    carried, results = finish(
        norm,
        factor,
        [attend_out_line, expand_line, reduce_line],
        [attend_out_other, expand_other, reduce_other],
        [attend_moment_flat, output_moment, expand_moment, reduce_moment],
        [attend_flat, output_weight, expand_weight, reduce_weight],
        6,
    )
    attend_carried = carried[0].reshape(attend_weight.shape)
    attend_result = results[0].reshape(attend_weight.shape)
    table_moment, table_square, table_result = adam_update(
        modulation_table, table_first, table_second, clip_factor * summed_table
    )
    mixer_moment, mixer_square, mixer_result = adam_update(
        mixer_kernel, mixer_first, mixer_second, clip_factor * summed_mixer
    )
    hidden_moment, hidden_square, hidden_result = adam_update(
        hidden_kernel, hidden_first, hidden_second, clip_factor * summed_hidden
    )
    return (
        block_out,
        tokens_gradient,
        gradient_norm,
        attend_carried,
        carried[1],
        carried[2],
        carried[3],
        attend_result,
        results[1],
        results[2],
        results[3],
        table_moment,
        table_square,
        table_result,
        mixer_moment,
        mixer_square,
        mixer_result,
        hidden_moment,
        hidden_square,
        hidden_result,
    )


def solution(mesh):
    placed = (
        P("wide", None, None),
        P("wide", None, None),
        P("wide"),
        P("wide", None, None),
        P(),
        P(),
        P(None, "narrow"),
        P(None, None, "narrow"),
        P("narrow", None),
        P(None, "narrow"),
        P("narrow", None),
        P(None, None, "narrow"),
        P("narrow", None),
        P(None, "narrow"),
        P("narrow", None),
        P(),
        P(),
        P(),
        P(),
        P(None, "narrow"),
        P(None, "narrow"),
    )
    return jax.shard_map(
        local,
        mesh=mesh,
        in_specs=placed,
        out_specs=(
            P("wide", None, None),
            P("wide", None, None),
            P(),
            P(None, None, "narrow"),
            P("narrow", None),
            P(None, "narrow"),
            P("narrow", None),
            P(None, None, "narrow"),
            P("narrow", None),
            P(None, "narrow"),
            P("narrow", None),
            P(),
            P(),
            P(),
            P(),
            P(),
            P(),
            P(None, "narrow"),
            P(None, "narrow"),
            P(None, "narrow"),
        ),
        check_vma=False,
    )
```

```python
import functools
import math

import jax
import jax.numpy as jnp
from jax import lax
from jax.experimental import pallas as pl
from jax.experimental.pallas import tpu as pltpu
from jax.sharding import PartitionSpec as P

D = 1024
HEAD = 64
FF = 4096
GRID = 32
NEWTON = 5
STEP = 10


first_decay = 0.9
second_decay = 0.999
adam_rate = 0.3
muon_rate = 0.15
muon_momentum = 0.5
weight_decay = 0.01
newton_terms = (3.4445, -4.775, 2.0315)
gelu_slope = 0.7978845608
gelu_cubic = 0.044715


MESH = pl.DeviceIdType.MESH
BLK = 256
LANES = 128
SLAB = 16
QUERIES = 512
UNROLL = 4
MATRICES = 4
COLUMNS = (0, 2)


def partner(index, bit):
    return index + (1 - 2 * ((index // bit) % 2)) * bit


def bits_of(count):
    found = []
    bit = 1
    while bit < count:
        found.append(bit)
        bit *= 2
    return found


def place_at(axis, bit):
    place = {"wide": lax.axis_index("wide"), "narrow": lax.axis_index("narrow")}
    place[axis] = partner(place[axis], bit)
    return (place["wide"], place["narrow"])


def greet(places):
    barrier = pltpu.get_barrier_semaphore()
    for place in places:
        pl.semaphore_signal(barrier, inc=1, device_id=place, device_id_type=MESH)
    pl.semaphore_wait(barrier, len(places))


def send(src, dst, sends, arrivals, slot, place):
    copy = pltpu.make_async_remote_copy(
        src_ref=src,
        dst_ref=dst,
        send_sem=sends.at[slot],
        recv_sem=arrivals.at[slot],
        device_id=place,
        device_id_type=MESH,
    )
    copy.start()
    return copy


def permute(values, axis, bit):
    size = lax.axis_size(axis)
    return lax.ppermute(values, axis, [(index, index ^ bit) for index in range(size)])


def together(*values):
    return lax.optimization_barrier(values)


def own_half(values, axis):
    extent = values.shape[axis] // 2
    side = lax.axis_index("wide") % 2
    return lax.dynamic_slice_in_dim(values, side * extent, extent, axis)


def wide_parts():
    w = lax.axis_index("wide")
    return w % 2, w // 2


def line_partner(z, offset):
    for bit in bits_of(2 * offset):
        if (offset // bit) % 2:
            z = partner(z, bit)
    return z


def block_of(ref, y, z):
    count = lax.axis_size("wide") // 2
    rows = ref.shape[0] // (2 * count)
    return ref.at[pl.ds(pl.multiple_of((y * count + z) * rows, 8), rows), :]


def line_block(ref, z):
    rows = ref.shape[0] // (lax.axis_size("wide") // 2)
    return ref.at[pl.ds(pl.multiple_of(z * rows, 8), rows), :]


def block_shape(shape):
    return (shape[0] // lax.axis_size("wide"), shape[1])


class Scatter:
    def __init__(self, src, held, beside, inbox, sends, arrivals, local, base):
        self.src, self.held, self.beside, self.inbox = src, held, beside, inbox
        self.sends, self.arrivals, self.local, self.base = sends, arrivals, local, base
        self.count = lax.axis_size("wide") // 2
        self.copies = {}
        self.loads = {}

    @staticmethod
    def slots():
        return lax.axis_size("wide") - 1

    def load(self):
        y, z = wide_parts()
        for e in reversed(range(self.count)):
            self.loads[e] = pltpu.make_async_copy(
                block_of(self.src, y, line_partner(z, e)), self.held.at[e], self.local.at[e]
            )
            self.loads[e].start()

    def give(self, e):
        y, z = wide_parts()
        self.copies[("y", e)] = send(
            block_of(self.src, 1 - y, line_partner(z, e)),
            self.beside.at[e],
            self.sends,
            self.arrivals,
            self.base + e,
            place_at("wide", 1),
        )

    def start(self):
        self.load()
        for e in reversed(range(self.count)):
            self.give(e)

    def step(self, e):
        self.loads[e].wait()
        self.copies[("y", e)].wait_recv()
        self.held[e] = self.held[e] + self.beside[e]
        bit = 1
        while bit < self.count and e % (2 * bit) == 0:
            self.copies[("z", e + bit)].wait_recv()
            self.held[e] = self.held[e] + self.inbox[e + bit - 1]
            bit *= 2
        if e:
            low = e & -e
            self.copies[("z", e)] = send(
                self.held.at[e],
                self.inbox.at[e - 1],
                self.sends,
                self.arrivals,
                self.base + self.count + e - 1,
                place_at("wide", 2 * low),
            )

    def finish(self):
        for copy in self.copies.values():
            copy.wait_send()


def scatter_scratch(shape):
    count = lax.axis_size("wide") // 2
    block = block_shape(shape)
    return [
        pltpu.VMEM((count,) + block, jnp.float32),
        pltpu.VMEM((count,) + block, jnp.float32),
        pltpu.VMEM((max(count - 1, 1),) + block, jnp.float32),
        pltpu.SemaphoreType.DMA((count,)),
    ]


class Gather:
    def __init__(self, own, spot_of, hops, sends, arrivals, base):
        self.own, self.spot_of, self.hops = own, spot_of, hops
        self.sends, self.arrivals, self.base = sends, arrivals, base
        self.copies = {}
        self.order = sorted(range(2 ** len(hops)), key=lambda item: (bin(item).count("1"), item))

    def step(self, item):
        if item:
            self.copies[item].wait_recv()
        for index in range(item.bit_length(), len(self.hops)):
            later = item + 2**index
            spot = self.spot_of(item)
            axis, bit = self.hops[index]
            self.copies[later] = send(
                spot if item else self.own,
                spot,
                self.sends,
                self.arrivals,
                self.base + later - 1,
                place_at(axis, bit),
            )

    def finish(self):
        for copy in self.copies.values():
            copy.wait_send()


def line_hops():
    return [("wide", bit) for bit in reversed(bits_of(lax.axis_size("wide"))) if bit > 1]


class NarrowSum:
    def __init__(self, far_bits, pieces, x, o, near, far, held, sends, arrivals, local, base):
        self.bits, self.pieces = far_bits, pieces
        self.x, self.o, self.near, self.far, self.held = x, o, near, far, held
        self.sends, self.arrivals, self.local, self.base = sends, arrivals, local, base
        self.rows = x.shape[0] // 2
        self.core = lax.axis_index("narrow") % 2
        self.copies = []
        self.cross = {}
        self.keeps = []

    def block(self, side, p):
        step = self.rows // self.pieces
        return pl.ds(pl.multiple_of(side * self.rows + p * step, 8), step)

    def push(self, src, dst, slot, bit):
        copy = send(
            src, dst, self.sends, self.arrivals, self.base + slot, place_at("narrow", bit)
        )
        self.copies.append(copy)
        return copy

    def start(self):
        self.first = [
            self.push(self.x.at[self.block(1 - self.core, p)], self.near.at[p], p, 1)
            for p in range(self.pieces)
        ]
        self.loads = [
            pltpu.make_async_copy(
                self.x.at[self.block(self.core, p)], self.held.at[0, p], self.local.at[p]
            )
            for p in range(self.pieces)
        ]
        for load in self.loads:
            load.start()

    def hop(self, b, p):
        slot = (b + 1) * self.pieces + p
        self.cross[(b, p)] = self.push(
            self.held.at[b, p], self.far.at[b, p], slot, self.bits[b]
        )

    def begin(self, p):
        self.loads[p].wait()
        self.first[p].wait_recv()
        self.held[0, p] = self.held[0, p] + self.near[p]
        self.hop(0, p)

    def step(self, b, p):
        self.cross[(b, p)].wait_recv()
        self.held[b + 1, p] = self.held[b, p] + self.far[b, p]
        if b + 1 < len(self.bits):
            self.hop(b + 1, p)
            return
        spot = self.o.at[self.block(self.core, p)]
        slot = (b + 2) * self.pieces + p
        self.keeps.append(self.push(self.held.at[b + 1, p], spot, slot, 1))
        keep = pltpu.make_async_copy(self.held.at[b + 1, p], spot, self.local.at[p])
        keep.start()
        self.loads[p] = keep

    def finish(self):
        for copy in self.keeps:
            copy.wait_recv()
        for keep in self.loads:
            keep.wait()
        for copy in self.copies:
            copy.wait_send()


def narrow_scratch(shape, pieces):
    count = len(bits_of(lax.axis_size("narrow"))) - 1
    step = shape[0] // (2 * pieces)
    return [
        pltpu.VMEM((pieces, step, shape[1]), jnp.float32),
        pltpu.VMEM((count, pieces, step, shape[1]), jnp.float32),
        pltpu.VMEM((count + 1, pieces, step, shape[1]), jnp.float32),
        pltpu.SemaphoreType.DMA((pieces,)),
    ]


def gram_kernel(
    norm_ref,
    attend_out_any,
    expand_any,
    reduce_any,
    attend_moment_any,
    output_moment_any,
    expand_moment_any,
    reduce_moment_any,
    band_ref,
    attend_out,
    expand,
    reduce,
    attend_moment,
    output_moment,
    expand_moment,
    reduce_moment,
    *refs,
):
    highs, lows, refs = refs[:MATRICES], refs[MATRICES : 2 * MATRICES], refs[2 * MATRICES :]
    twice, halves, inbox, block, load_sems, sends, arrivals, local = refs
    narrow_bits = bits_of(lax.axis_size("narrow"))
    wide_bits = bits_of(lax.axis_size("wide"))
    parts, rows = halves.shape[0], halves.shape[1]
    sub = parts // MATRICES
    size = attend_out.shape[1]
    hops = [("narrow", bit) for bit in bits_of(sub)]
    hops += [("wide", bit) for bit in reversed(wide_bits)]
    w, n = lax.axis_index("wide"), lax.axis_index("narrow")
    y, z = wide_parts()
    greet(
        [place_at("narrow", bit) for bit in narrow_bits]
        + [place_at("wide", bit) for bit in wide_bits]
    )
    own_rows = lambda ref: ref.at[
        pl.ds(pl.multiple_of(y * (ref.shape[0] // 2), 8), ref.shape[0] // 2), :
    ]
    own_columns = lambda ref: ref.at[
        :, pl.ds(pl.multiple_of(y * (ref.shape[1] // 2), LANES), ref.shape[1] // 2)
    ]
    loads = []
    for src, dst in (
        (attend_out_any, attend_out),
        (attend_moment_any, attend_moment),
        (own_rows(output_moment_any), output_moment),
        (expand_any, expand),
        (own_columns(expand_moment_any), expand_moment),
        (reduce_any, reduce),
        (own_rows(reduce_moment_any), reduce_moment),
    ):
        loads.append(pltpu.make_async_copy(src, dst, load_sems.at[len(loads)]))
        loads[-1].start()
    clip = jnp.minimum(1.0, 1.0 / (norm_ref[0:1, 0:1] + 1e-06))
    count = halves.shape[1] * sub
    start = z * count
    lines = lax.axis_size("wide") // 2
    band = halves.shape[2]

    def blend(k, moment, gradient):
        total = highs[k].shape[0]

        def one(i, carry):
            spot = slab_at(i)
            highs[k][spot, :], lows[k][spot, :] = split(
                muon_momentum * moment[spot, :] + clip * gradient[spot, :]
            )
            return carry

        lax.fori_loop(0, total // SLAB, one, 0, unroll=UNROLL)

    def multiply(k):
        columns = pl.ds(pl.multiple_of(start, LANES), count)
        high, low = highs[k][:, columns], lows[k][:, columns]
        values = dot_of(high, highs[k][...], 0, 0) + (
            dot_of(high, lows[k][...], 0, 0) + dot_of(low, highs[k][...], 0, 0)
        )
        twice[:, :size] = values
        twice[:, size:] = values[:, :band]
        for s in range(sub):
            for at in range(0, rows, LANES):
                extent = min(LANES, rows)
                first = s * rows + at
                lanes = pl.ds(pl.multiple_of(start + first // LANES * LANES, LANES), band)
                halves[k * sub + s, at : at + extent, :] = twice[first : first + extent, lanes]

    share = attend_out.shape[0] // lines
    first_rows, second_rows = 3 * share // 4, share // 4
    loads[0].wait()
    loads[1].wait()
    loads[2].wait()
    for b in range(lines):
        for moment, gradient_at, extent in (
            (attend_moment, b * share, first_rows),
            (output_moment, b * share + first_rows, second_rows),
        ):
            spot = pl.ds(b * extent, extent)
            moment[spot, :] = (
                muon_momentum * moment[spot, :]
                + clip * attend_out[gradient_at : gradient_at + extent, :]
            )

    def cut(k, values):
        def one(i, carry):
            spot = slab_at(i)
            highs[k][spot, :], lows[k][spot, :] = split(values[spot, :])
            return carry

        lax.fori_loop(0, highs[k].shape[0] // SLAB, one, 0, unroll=UNROLL)

    cut(0, attend_moment)
    multiply(0)
    cut(1, output_moment)
    multiply(1)
    loads[3].wait()
    loads[4].wait()
    for at in range(0, expand.shape[0], LANES):
        spot = pl.ds(at, LANES)
        highs[2][spot, :], lows[2][spot, :] = split(
            muon_momentum * expand_moment[:, spot].T + clip * expand[spot, :]
        )
    multiply(2)
    loads[5].wait()
    loads[6].wait()
    blend(3, reduce_moment, reduce)
    multiply(3)
    half = rows // 2
    row_half = lambda side: pl.ds(pl.multiple_of(side * half, 8), half)
    slot = iter(range(sends.shape[0]))
    copies = []

    def push(src, dst, place):
        copies.append(send(src, dst, sends, arrivals, next(slot), place))
        return copies[-1]

    at = 0
    for bit in narrow_bits:
        value = (n // bit) % 2
        last = 2 * bit == parts
        waits = []
        for j in range(parts // (2 * bit)):
            mine = n % bit + value * bit + j * 2 * bit
            theirs = n % bit + (1 - value) * bit + j * 2 * bit
            for side in (1 - y, y) if last else (None,):
                spot = slice(None) if side is None else row_half(side)
                copy = push(
                    halves.at[theirs] if side is None else halves.at[theirs, spot],
                    inbox.at[at + j] if side is None else inbox.at[at + j, spot],
                    place_at("narrow", bit),
                )
                waits.append((copy, mine, at + j, spot))
        at += parts // (2 * bit)
        for copy, mine, where, spot in waits:
            copy.wait_recv()
            halves[mine, spot] = halves[mine, spot] + inbox[where, spot]
            if last and copy is waits[0][0]:
                side_copy = push(halves.at[n, row_half(1 - y)], block.at[0], place_at("wide", 1))
    side_copy.wait_recv()
    block[1] = halves[n, row_half(y)] + block[0]

    def spot_of(item):
        big, small = w, n % sub
        for index, (axis, bit) in enumerate(hops):
            if (item >> index) % 2:
                if axis == "wide":
                    big = partner(big, bit)
                else:
                    small = partner(small, bit)
        first = ((big // 2) * (2 * sub) + small * 2 + big % 2) * half
        return band_ref.at[pl.ds(pl.multiple_of(first, 8), half), :]

    keep = pltpu.make_async_copy(block.at[1], spot_of(0), local.at[0])
    keep.start()
    gather = Gather(block.at[1], spot_of, hops, sends, arrivals, next(slot))
    for item in gather.order:
        gather.step(item)
    keep.wait()
    gather.finish()
    for copy in copies:
        copy.wait_send()


def gram_whole(norm, lines, moments, number):
    narrow_bits = bits_of(lax.axis_size("narrow"))
    wide_bits = bits_of(lax.axis_size("wide"))
    size = lines[0].shape[1]
    sub = lax.axis_size("narrow") // MATRICES
    parts = lax.axis_size("narrow")
    count = 2 * size // lax.axis_size("wide")
    band = size // 2 + LANES
    halves = (parts, count // sub, band)
    line_rows = [lines[0].shape[0] * 3 // 4, lines[0].shape[0] // 4]
    line_rows += [lines[1].shape[0], lines[2].shape[0]]
    gathers = len(bits_of(sub)) + len(wide_bits)
    slots = parts + 2 + 2**gathers
    vmem = pl.BlockSpec(memory_space=pltpu.VMEM)
    anywhere = pl.BlockSpec(memory_space=pl.ANY)
    wide = lambda *shape: pltpu.VMEM(shape, jnp.float32)
    return pl.pallas_call(
        gram_kernel,
        out_shape=jax.ShapeDtypeStruct((size, band), jnp.float32),
        in_specs=[vmem] + [anywhere] * 7,
        out_specs=anywhere,
        scratch_shapes=[
            wide(*lines[0].shape),
            wide(*lines[1].shape),
            wide(*lines[2].shape),
            wide(line_rows[0], size),
            wide(line_rows[1], size),
            wide(size, line_rows[2]),
            wide(line_rows[3], size),
        ]
        + [pltpu.VMEM((rows, size), jnp.bfloat16) for rows in line_rows] * 2
        + [
            wide(count, size + band),
            wide(*halves),
            wide(*halves),
            wide(2, halves[1] // 2, band),
            pltpu.SemaphoreType.DMA((7,)),
            pltpu.SemaphoreType.DMA((slots,)),
            pltpu.SemaphoreType.DMA((slots,)),
            pltpu.SemaphoreType.DMA((1,)),
        ],
        compiler_params=pltpu.CompilerParams(
            collective_id=number, has_side_effects=True, vmem_limit_bytes=48 * 2**20
        ),
        cost_estimate=pl.CostEstimate(
            flops=3 * size * size * size, bytes_accessed=80 * size * size, transcendentals=0
        ),
    )(norm, *lines, *moments)


def split(values):
    high = values.astype(jnp.bfloat16)
    return high, (values - high.astype(jnp.float32)).astype(jnp.bfloat16)


def product(left_high, left_low, right_high, right_low):
    dot = functools.partial(jnp.dot, preferred_element_type=jnp.float32)
    return dot(left_high, right_high) + (dot(left_high, right_low) + dot(left_low, right_high))


def polar_kernel(g_ref, band_ref, q_ref, gh, gl, ph, pw, th, tl):
    size = g_ref.shape[0]
    blocks = size // BLK
    first, second, third = newton_terms
    rows = lambda block: pl.ds(block * BLK, BLK)
    square = (BLK, BLK)
    unit = (
        lax.broadcasted_iota(jnp.int32, square, 0) == lax.broadcasted_iota(jnp.int32, square, 1)
    ).astype(jnp.float32)
    count = size // LANES
    lanes = lambda block: pl.ds((block % count) * LANES, LANES)
    trace = jnp.zeros((), jnp.float32)
    for i in range(count):
        trace = trace + jnp.sum(g_ref[lanes(i), lanes(0)] * unit[:LANES, :LANES])
    factor = 1.0 / (jnp.sqrt(trace) + 1e-07)
    for i in range(count):
        for j in range(count // 2 + 1):
            values = g_ref[lanes(i), lanes(j)] * (factor * factor)
            gh[lanes(i), lanes(i + j)], gl[lanes(i), lanes(i + j)] = split(values)
            if 0 < j < count // 2:
                values = values.T
                gh[lanes(i + j), lanes(i)], gl[lanes(i + j), lanes(i)] = split(values)

    def put(high, low, i, j, values):
        high[rows(i), rows(j)], low[rows(i), rows(j)] = split(values)
        if i != j:
            high[rows(j), rows(i)], low[rows(j), rows(i)] = split(values.T)

    def symmetric(left, right, emit):
        for i in range(blocks):
            columns = pl.ds(i * BLK, size - i * BLK)
            values = product(
                left[0][rows(i), :], left[1][rows(i), :], right[0][:, columns], right[1][:, columns]
            )
            for j in range(i, blocks):
                emit(i, j, values[:, (j - i) * BLK : (j - i + 1) * BLK])

    def emit_terms(i, j, values):
        gram = gh[rows(i), rows(j)].astype(jnp.float32) + gl[rows(i), rows(j)].astype(jnp.float32)
        terms = second * gram + third * values
        if i == j:
            terms = terms + first * unit
        put(ph, pw, i, j, terms)

    def emit_total(i, j, values):
        q_ref[rows(i), rows(j)] = values
        if i != j:
            q_ref[rows(j), rows(i)] = values.T

    symmetric((gh, gl), (gh, gl), emit_terms)
    for i in range(blocks):
        q_ref[rows(i), :] = (
            ph[rows(i), :].astype(jnp.float32) + pw[rows(i), :].astype(jnp.float32)
        ) * factor

    def one_step(step, carry):
        symmetric((ph, pw), (gh, gl), functools.partial(put, th, tl))
        symmetric((th, tl), (ph, pw), functools.partial(put, gh, gl))
        symmetric((gh, gl), (gh, gl), emit_terms)
        for i in range(blocks):
            th[rows(i), :], tl[rows(i), :] = split(q_ref[rows(i), :])
        symmetric((ph, pw), (th, tl), emit_total)
        return carry

    lax.fori_loop(0, NEWTON - 1, one_step, 0)
    for i in range(count):
        for j in range(count // 2 + 1):
            band_ref[lanes(i), lanes(j)] = q_ref[lanes(i), lanes(i + j)]


def polar_factor(gramian):
    size = gramian.shape[0]
    vmem = pl.BlockSpec(memory_space=pltpu.VMEM)
    return pl.pallas_call(
        polar_kernel,
        out_shape=jax.ShapeDtypeStruct(gramian.shape, jnp.float32),
        in_specs=[vmem],
        out_specs=vmem,
        scratch_shapes=[pltpu.VMEM((size, size), jnp.float32)]
        + [pltpu.VMEM((size, size), jnp.bfloat16)] * 6,
        compiler_params=pltpu.CompilerParams(vmem_limit_bytes=48 * 2**20),
        cost_estimate=pl.CostEstimate(
            flops=17 * 6 * size**3, bytes_accessed=8 * size * size, transcendentals=0
        ),
    )(gramian)


def spread_kernel(sub, pieces, q_ref, o_ref, sends, arrivals, local):
    half = q_ref.shape[0] // 2
    step = half // pieces
    w, n = lax.axis_index("wide"), lax.axis_index("narrow")
    own = n // sub
    across = partner(own, 2)
    near_place, far_place = place_at("narrow", sub), place_at("narrow", 2 * sub)
    side_place = place_at("wide", 1)
    greet([near_place, far_place, side_place])
    y = w % 2
    rows = lambda side, p: pl.ds(pl.multiple_of(side * half + p * step, 8), step)
    copies = []

    def push(src, dst, place):
        copies.append(send(src, dst, sends, arrivals, len(copies), place))
        return copies[-1]

    crossing = [
        push(q_ref.at[rows(y, p)], o_ref.at[own, rows(y, p)], far_place) for p in range(pieces)
    ]
    landing = [push(q_ref, o_ref.at[own], near_place)]
    keep = pltpu.make_async_copy(q_ref, o_ref.at[own], local.at[0])
    keep.start()
    aside = []

    def forward(p):
        crossing[p].wait_recv()
        spot = o_ref.at[across, rows(y, p)]
        aside.append(push(spot, spot, side_place))
        landing.append(push(spot, spot, near_place))

    def forward_side(p):
        aside[p].wait_recv()
        spot = o_ref.at[across, rows(1 - y, p)]
        landing.append(push(spot, spot, near_place))

    forward(0)
    for p in range(1, pieces):
        forward(p)
        forward_side(p - 1)
    forward_side(pieces - 1)
    keep.wait()
    for copy in landing:
        copy.wait_recv()
    for copy in copies:
        copy.wait_send()


def spread(band, number):
    pieces = 4
    slots = 1 + 4 * pieces
    sub = lax.axis_size("narrow") // MATRICES
    return pl.pallas_call(
        functools.partial(spread_kernel, sub, pieces),
        out_shape=jax.ShapeDtypeStruct((MATRICES,) + band.shape, jnp.float32),
        in_specs=[pl.BlockSpec(memory_space=pltpu.VMEM)],
        out_specs=pl.BlockSpec(memory_space=pl.ANY),
        scratch_shapes=[
            pltpu.SemaphoreType.DMA((slots,)),
            pltpu.SemaphoreType.DMA((slots,)),
            pltpu.SemaphoreType.DMA((1,)),
        ],
        compiler_params=pltpu.CompilerParams(collective_id=number, has_side_effects=True),
    )(band)


def finish_kernel(norm_ref, bands_any, *refs):
    lines, others, refs = refs[0:6:2], refs[1:6:2], refs[6:]
    moments, weights, refs = refs[:4], refs[4:8], refs[8:]
    carried, results, refs = refs[:4], refs[4:8], refs[8:]
    bands, factor_high, factor_low = refs[:3]
    staged, values, highs, lows = refs[3:7], refs[7:11], refs[11:15], refs[15:19]
    load_sems, value_sems, out_sems, band_sems = refs[19:]
    size = factor_high.shape[0]
    y, _ = wide_parts()
    blocks = lax.axis_size("wide")
    whole = []
    fills = []
    for k in range(MATRICES):
        sources = (lines[max(k - 1, 0)], others[max(k - 1, 0)])
        extent = staged[k].shape[0] // 2
        for side, source in zip((y, 1 - y), sources):
            if k >= 2:
                spot = staged[k].at[pl.ds(pl.multiple_of(side * extent, 8), extent), :]
                pltpu.make_async_copy(source, spot, load_sems.at[k]).start()
                continue
            share = (staged[0].shape[0] // blocks, staged[1].shape[0] // blocks)
            for b in range(blocks // 2):
                start = b * (share[0] + share[1]) + k * share[0]
                to = pl.multiple_of(side * extent + b * share[k], 8)
                pltpu.make_async_copy(
                    source.at[pl.ds(start, share[k]), :],
                    staged[k].at[pl.ds(to, share[k]), :],
                    load_sems.at[k],
                ).start()
        whole.append(pltpu.make_async_copy(staged[k], staged[k], load_sems.at[k]))
        fills.append(pltpu.make_async_copy(moments[k], values[k], value_sems.at[k]))
        fills[-1].start()
    arrivals = []
    for k in range(MATRICES):
        arrivals.append(pltpu.make_async_copy(bands_any.at[k], bands.at[k], band_sems.at[k]))
        arrivals[-1].start()
    clip = jnp.minimum(1.0, 1.0 / (norm_ref[0:1, 0:1] + 1e-06))

    def blend_rows(value, stage):
        def one(i, carry):
            spot = slab_at(i)
            value[spot, :] = muon_momentum * value[spot, :] + clip * stage[spot, :]
            return carry

        lax.fori_loop(0, value.shape[0] // SLAB, one, 0, unroll=UNROLL)

    def blend_columns(value, stage):
        def one(i, carry):
            spot = pl.ds(pl.multiple_of(i * LANES, LANES), LANES)
            value[:, spot] = muon_momentum * value[:, spot] + clip * stage[spot, :].T
            return carry

        lax.fori_loop(0, value.shape[1] // LANES, one, 0)

    outs = []
    for k in range(MATRICES):
        whole[k].wait()
        fills[k].wait()
        blend = blend_columns if k in COLUMNS else blend_rows
        blend(values[k], staged[k])
        outs.append(pltpu.make_async_copy(values[k], carried[k], out_sems.at[k]))
        outs[-1].start()

        def cut(i, carry, k=k):
            highs[k][slab_at(i), :], lows[k][slab_at(i), :] = split(values[k][slab_at(i), :])
            return carry

        lax.fori_loop(0, values[k].shape[0] // SLAB, cut, 0, unroll=UNROLL)
    for k in range(MATRICES):
        outs[k].wait()
        fills[k] = pltpu.make_async_copy(weights[k], values[k], value_sems.at[k])
        fills[k].start()
    lengths = (3 * D, D, FF, FF)
    count = size // LANES
    lanes = lambda block: pl.ds((block % count) * LANES, LANES)
    for k in range(MATRICES):
        arrivals[k].wait()
        for i in range(count):
            for j in range(count // 2 + 1):
                part = bands[k, lanes(i), lanes(j)]
                spot = (lanes(i), lanes(i + j))
                factor_high[spot], factor_low[spot] = split(part)
                if 0 < j < count // 2:
                    spot = (lanes(i + j), lanes(i))
                    factor_high[spot], factor_low[spot] = split(part.T)
        fills[k].wait()

        def process(i, carry, k=k):
            spot = pl.ds(pl.multiple_of(i * BLK, BLK), BLK)
            q_high, q_low = factor_high[spot, :], factor_low[spot, :]
            high, low = highs[k], lows[k]
            if k in COLUMNS:
                polar = dot_of(q_high, high[...], 1, 0) + (
                    dot_of(q_high, low[...], 1, 0) + dot_of(q_low, high[...], 1, 0)
                )
                where = (spot, slice(None))
            else:
                polar = dot_of(high[...], q_high, 1, 1) + (
                    dot_of(low[...], q_high, 1, 1) + dot_of(high[...], q_low, 1, 1)
                )
                where = (slice(None), spot)
            scale = muon_rate * 0.2 * math.sqrt(lengths[k])
            values[k][where] = values[k][where] * (1.0 - muon_rate * weight_decay) - scale * polar
            pltpu.make_async_copy(
                values[k].at[where], results[k].at[where], out_sems.at[k]
            ).start()
            return carry

        lax.fori_loop(0, size // BLK, process, 0)
    for k in range(MATRICES):
        pltpu.make_async_copy(values[k], results[k], out_sems.at[k]).wait()


def finish(norm, bands, lines, others, moments, weights):
    size = bands.shape[1]
    anywhere = pl.BlockSpec(memory_space=pl.ANY)
    operands = [part for both in zip(lines, others) for part in both]
    shapes = [jax.ShapeDtypeStruct(moment.shape, jnp.float32) for moment in moments]
    staged = [(moment.size // size, size) for moment in moments]
    outs = pl.pallas_call(
        finish_kernel,
        out_shape=tuple(shapes + shapes),
        in_specs=[pl.BlockSpec(memory_space=pltpu.VMEM)] + [anywhere] * (1 + len(operands) + 8),
        out_specs=(anywhere,) * 8,
        scratch_shapes=[
            pltpu.VMEM(bands.shape, jnp.float32),
            pltpu.VMEM((size, size), jnp.bfloat16),
            pltpu.VMEM((size, size), jnp.bfloat16),
        ]
        + [pltpu.VMEM(shape, jnp.float32) for shape in staged]
        + [pltpu.VMEM(moment.shape, jnp.float32) for moment in moments]
        + [pltpu.VMEM(moment.shape, jnp.bfloat16) for moment in moments]
        + [pltpu.VMEM(moment.shape, jnp.bfloat16) for moment in moments]
        + [pltpu.SemaphoreType.DMA((MATRICES,))] * 4,
        compiler_params=pltpu.CompilerParams(vmem_limit_bytes=60 * 2**20),
        cost_estimate=pl.CostEstimate(
            flops=18 * size * size * size, bytes_accessed=80 * size * size, transcendentals=0
        ),
    )(norm, bands, *operands, *moments, *weights)
    return outs[:4], outs[4:]


def adam_update(weight, moment, square, gradient):
    moment_new = first_decay * moment + (1.0 - first_decay) * gradient
    square_new = second_decay * square + (1.0 - second_decay) * gradient * gradient
    moment_hat = moment_new / (1.0 - first_decay**STEP)
    square_hat = square_new / (1.0 - second_decay**STEP)
    weight_new = weight * (1.0 - adam_rate * weight_decay) - adam_rate * moment_hat / (
        jnp.sqrt(square_hat) + 1e-08
    )
    return (moment_new, square_new, weight_new)


def column_shifts(strip, column):
    rows = strip.shape[0]
    left = jnp.where(column == 0, 0.0, pltpu.roll(strip, 1, 0))
    right = jnp.where(column == rows - 1, 0.0, pltpu.roll(strip, rows - 1, 0))
    return (left, strip, right)


def tap_rows(shifts, taps):
    return [
        taps[3 * i] * shifts[0] + taps[3 * i + 1] * shifts[1] + taps[3 * i + 2] * shifts[2]
        for i in range(3)
    ]


def strip_at(index):
    return pl.ds(pl.multiple_of(index * GRID, GRID), GRID)


def convolve(load, taps, emit):
    shape = load(0).shape
    column = lax.broadcasted_iota(jnp.int32, shape, 0)

    def one(r, carry):
        above, here = carry
        upper, middle, lower = tap_rows(column_shifts(load(r), column), taps)
        emit(r - 1, here + lower)
        return (upper, above + middle)

    upper, middle, _ = tap_rows(column_shifts(load(0), column), taps)
    above, here = lax.fori_loop(1, GRID, one, (upper, middle))
    emit(GRID - 1, here)


def kernel_sums(load, weigh, width):
    column = lax.broadcasted_iota(jnp.int32, (GRID, width), 0)
    fold = lambda values: values.reshape(GRID // 8, 8, width).sum(axis=0)
    zero = jnp.zeros((8, width), jnp.float32)

    def one(r, carry):
        sums = carry
        shifts = column_shifts(load(r), column)
        later = weigh(jnp.minimum(r + 1, GRID - 1)) * jnp.where(r < GRID - 1, 1.0, 0.0)
        earlier = weigh(jnp.maximum(r - 1, 0)) * jnp.where(r > 0, 1.0, 0.0)
        terms = (later, weigh(r), earlier)
        return tuple(
            sums[3 * i + j] + fold(terms[i] * shifts[j]) for i in range(3) for j in range(3)
        )

    return lax.fori_loop(0, GRID, one, (zero,) * 9)


def middle_kernel(
    pieces,
    entry_ref,
    cotangent_ref,
    live_ref,
    gate_ref,
    expand_any,
    reduce_any,
    taps_ref,
    ffn_half_ref,
    grad_entry_any,
    reduce_share,
    expand_share,
    grad_taps_ref,
    expand_full,
    reduce_full,
    grad_ffn,
    upward,
    weight,
    active,
    grad_up,
    ffn,
    back,
    grad_reduce,
    grad_expand,
    ffn_inbox,
    near,
    far,
    held,
    local,
    reduce_held,
    reduce_beside,
    reduce_inbox,
    reduce_loads,
    expand_held,
    expand_beside,
    expand_inbox,
    expand_loads,
    weight_sems,
    sends,
    arrivals,
):
    units = expand_any.shape[1]
    block = min(BLK, units // 2)
    steps = units // block
    groups = steps // 2
    y, z = wide_parts()
    count = lax.axis_size("wide") // 2
    far_bits = bits_of(lax.axis_size("narrow"))[1:]
    greet(
        [place_at("narrow", bit) for bit in [1] + far_bits]
        + [place_at("wide", bit) for bit in bits_of(lax.axis_size("wide"))]
    )

    def block_index(step):
        side = 1 - y if step < groups else y
        return side * groups + line_partner(z // (count // groups), groups - 1 - step % groups)

    fetches = []
    for step in range(steps):
        spot = pl.ds(pl.multiple_of(block_index(step) * block, LANES), block)
        pair = (
            pltpu.make_async_copy(
                expand_any.at[:, spot], expand_full.at[:, spot], weight_sems.at[step]
            ),
            pltpu.make_async_copy(
                reduce_any.at[spot, :], reduce_full.at[spot, :], weight_sems.at[steps + step]
            ),
        )
        for copy in pair:
            copy.start()
        fetches.append(pair)
    gate, live = gate_ref[...], live_ref[...]

    def gated(i, carry):
        spot = slab_at(i)
        result = cotangent_ref[spot, :].astype(jnp.float32) * live
        grad_ffn[spot, :] = (gate * result).astype(jnp.bfloat16)
        return carry

    lax.fori_loop(0, grad_ffn.shape[0] // SLAB, gated, 0, unroll=UNROLL)

    def work(spot, fresh):
        expand_low = expand_full[:, spot].astype(jnp.bfloat16)
        reduce_low = reduce_full[spot, :].astype(jnp.bfloat16)
        taps = [taps_ref[t : t + 1, spot] for t in range(9)]
        upward[...] = dot_of(entry_ref[...], expand_low, 1, 0)
        weight[...] = dot_of(grad_ffn[...], reduce_low, 1, 1)

        def emit_middle(r, values):
            inner = gelu_slope * (values + gelu_cubic * values * values * values)
            bent = jnp.tanh(inner)
            active[strip_at(r), :] = (0.5 * values * (1.0 + bent)).astype(jnp.bfloat16)
            turn = 0.5 * (1.0 + bent) + 0.5 * values * (1.0 - bent * bent) * (
                gelu_slope * (1.0 + 3.0 * gelu_cubic * values * values)
            )
            weight[strip_at(r), :] = weight[strip_at(r), :] * turn

        convolve(lambda r: upward[strip_at(r), :], taps, emit_middle)

        def emit_grad(r, values):
            grad_up[strip_at(r), :] = values.astype(jnp.bfloat16)

        convolve(lambda r: weight[strip_at(r), :], taps[::-1], emit_grad)
        sums = kernel_sums(
            lambda r: upward[strip_at(r), :], lambda r: weight[strip_at(r), :], block
        )
        for t in range(9):
            grad_taps_ref[t : t + 1, spot] = jnp.sum(sums[t], axis=0, keepdims=True)
        grad_reduce[spot, :] = dot_of(active[...], grad_ffn[...], 0, 0)
        grad_expand[spot, :] = dot_of(grad_up[...], entry_ref[...], 0, 0)
        if fresh:
            ffn[...] = dot_of(active[...], reduce_low, 1, 0)
            back[...] = dot_of(grad_up[...], expand_low, 1, 1)
        else:
            ffn[...] += dot_of(active[...], reduce_low, 1, 0)
            back[...] += dot_of(grad_up[...], expand_low, 1, 1)

    base = (len(far_bits) + 2) * pieces + 1
    reduce_sum = Scatter(
        grad_reduce, reduce_held, reduce_beside, reduce_inbox, sends, arrivals, reduce_loads, base
    )
    expand_sum = Scatter(
        grad_expand,
        expand_held,
        expand_beside,
        expand_inbox,
        sends,
        arrivals,
        expand_loads,
        base + Scatter.slots(),
    )
    for step in range(groups):
        for copy in fetches[step]:
            copy.wait()
        work(pl.ds(pl.multiple_of(block_index(step) * block, LANES), block), step == 0)
        size = count // groups
        ready = [(groups - 1 - step) * size + e for e in reversed(range(size))]
        for scatter in (reduce_sum, expand_sum):
            for e in ready:
                scatter.give(e)
    for step in range(groups, steps):
        for copy in fetches[step]:
            copy.wait()

    def later(i, carry):
        side_block = line_partner_of(z // (count // groups), i, groups)
        work(pl.ds(pl.multiple_of((y * groups + side_block) * block, LANES), block), False)
        return carry

    lax.fori_loop(0, groups, later, 0)
    narrow = NarrowSum(
        far_bits, pieces, back, grad_entry_any, near, far, held, sends, arrivals, local, 0
    )
    narrow.start()
    core = lax.axis_index("narrow") % 2
    half = ffn.shape[0] // 2
    side_rows = lambda side: pl.ds(pl.multiple_of(side * half, 8), half)
    ffn_copy = send(
        ffn.at[side_rows(1 - core)], ffn_inbox, sends, arrivals, base - 1, place_at("narrow", 1)
    )
    for scatter in (reduce_sum, expand_sum):
        scatter.load()
    for p in range(pieces):
        narrow.begin(p)
    left = [list(reversed(range(count))), list(reversed(range(count)))]
    scatters = (reduce_sum, expand_sum)
    scatters[0].step(left[0].pop(0))
    scatters[1].step(left[1].pop(0))
    ffn_copy.wait_recv()
    ffn_half_ref[...] = ffn[side_rows(core), :] + ffn_inbox[...]
    turns = [0, 1, 0, 0, 1, 1]
    for b in range(len(far_bits)):
        for p in range(pieces):
            narrow.step(b, p)
            if turns and len(left[turns[0]]) > 1:
                which = turns.pop(0)
                scatters[which].step(left[which].pop(0))
    outs = []
    for which, share in ((0, reduce_share), (1, expand_share)):
        while left[which]:
            scatters[which].step(left[which].pop(0))
        out = pltpu.make_async_copy(scatters[which].held.at[0], share, scatters[which].local.at[0])
        out.start()
        outs.append(out)
    narrow.finish()
    ffn_copy.wait_send()
    for scatter in scatters:
        scatter.finish()
    for out in outs:
        out.wait()


def line_partner_of(place, index, count):
    flipped = 0 * place
    for bit in bits_of(count):
        one, two = (place // bit) % 2, (index // bit) % 2
        flipped = flipped + (one + two - 2 * one * two) * bit
    return flipped


def middle(entry, cotangent, live, gate, expand, reduce, taps, number):
    tokens, width = entry.shape
    units = expand.shape[1]
    block = min(BLK, units // 2)
    steps = units // block
    pieces = 4
    narrow_bits = bits_of(lax.axis_size("narrow"))
    slots = (len(narrow_bits) + 1) * pieces + 1 + 2 * Scatter.slots()
    vmem = pl.BlockSpec(memory_space=pltpu.VMEM)
    anywhere = pl.BlockSpec(memory_space=pl.ANY)
    f32 = lambda *shape: jax.ShapeDtypeStruct(shape, jnp.float32)
    wide = lambda *shape: pltpu.VMEM(shape, jnp.float32)
    low = lambda *shape: pltpu.VMEM(shape, jnp.bfloat16)
    share = block_shape((units, width))
    return pl.pallas_call(
        functools.partial(middle_kernel, pieces),
        out_shape=(
            f32(tokens // 2, width),
            f32(tokens, width),
            f32(*share),
            f32(*share),
            f32(9, units),
        ),
        in_specs=[vmem, vmem, vmem, vmem, anywhere, anywhere, vmem],
        out_specs=(vmem, anywhere, anywhere, anywhere, vmem),
        scratch_shapes=[
            wide(width, units),
            wide(units, width),
            low(tokens, width),
            wide(tokens, block),
            wide(tokens, block),
            low(tokens, block),
            low(tokens, block),
            wide(tokens, width),
            wide(tokens, width),
            wide(units, width),
            wide(units, width),
            wide(tokens // 2, width),
        ]
        + narrow_scratch((tokens, width), pieces)
        + scatter_scratch((units, width)) * 2
        + [
            pltpu.SemaphoreType.DMA((2 * steps,)),
            pltpu.SemaphoreType.DMA((slots,)),
            pltpu.SemaphoreType.DMA((slots,)),
        ],
        compiler_params=pltpu.CompilerParams(
            collective_id=number, has_side_effects=True, vmem_limit_bytes=60 * 2**20
        ),
        cost_estimate=pl.CostEstimate(
            flops=12 * tokens * width * units,
            bytes_accessed=200 * tokens * width,
            transcendentals=tokens * units,
        ),
    )(entry, cotangent, live, gate, expand, reduce, taps)


def norm_strip(values):
    average = jnp.mean(values, axis=-1, keepdims=True)
    centred = values - average
    spread_of = jnp.mean(centred * centred, axis=-1, keepdims=True)
    inverse = lax.rsqrt(spread_of + 1e-06)
    return centred * inverse, inverse


def slab_at(index):
    return pl.ds(pl.multiple_of(index * SLAB, SLAB), SLAB)


def fold_rows(values):
    return values.reshape(values.shape[0] // 8, 8, values.shape[1]).sum(axis=0)


def mixer_kernel_forward(tokens_ref, shift_ref, scale_ref, taps_ref, out_ref, entered):
    stretch = 1.0 + scale_ref[...]
    offset = shift_ref[...]

    def enter(r, carry):
        normed, _ = norm_strip(tokens_ref[slab_at(r), :].astype(jnp.float32))
        entered[slab_at(r), :] = normed * stretch + offset
        return carry

    rows, width = tokens_ref.shape
    lax.fori_loop(0, rows // SLAB, enter, 0, unroll=UNROLL)
    for start in range(0, width, BLK):
        lanes = pl.ds(start, BLK)

        def emit(r, values, lanes=lanes):
            out_ref[strip_at(r), lanes] = values.astype(jnp.bfloat16)

        taps = [taps_ref[t : t + 1, lanes] for t in range(9)]
        convolve(lambda r, lanes=lanes: entered[strip_at(r), lanes], taps, emit)


def mixer_forward(tokens, shift, scale, taps):
    rows, width = tokens.shape
    vmem = pl.BlockSpec(memory_space=pltpu.VMEM)
    return pl.pallas_call(
        mixer_kernel_forward,
        out_shape=jax.ShapeDtypeStruct((rows, width), jnp.bfloat16),
        in_specs=[vmem] * 4,
        out_specs=vmem,
        scratch_shapes=[pltpu.VMEM((rows, width), jnp.float32)],
        compiler_params=pltpu.CompilerParams(vmem_limit_bytes=40 * 2**20),
        cost_estimate=pl.CostEstimate(
            flops=40 * rows * width, bytes_accessed=4 * rows * width, transcendentals=0
        ),
    )(tokens, shift, scale, taps)


def mixer_kernel_backward(
    tokens_ref,
    shift_ref,
    scale_ref,
    taps_ref,
    grad_mixed_ref,
    grad_hidden_ref,
    out_ref,
    grad_taps_ref,
    grad_shift_ref,
    grad_scale_ref,
    normed_ref,
    back_ref,
    inverse_ref,
):
    width = tokens_ref.shape[1]
    stretch = 1.0 + scale_ref[...]

    def enter(r, carry):
        normed, inverse = norm_strip(tokens_ref[slab_at(r), :].astype(jnp.float32))
        normed_ref[slab_at(r), :] = normed
        inverse_ref[slab_at(r), :] = jnp.broadcast_to(inverse, (SLAB, LANES))
        return carry

    rows = tokens_ref.shape[0]
    lax.fori_loop(0, rows // SLAB, enter, 0, unroll=UNROLL)
    for start in range(0, width, BLK):
        lanes = pl.ds(start, BLK)
        taps = [taps_ref[t : t + 1, lanes] for t in range(9)]
        stretch_part = 1.0 + scale_ref[:, lanes]
        offset_part = shift_ref[:, lanes]

        def emit(r, values, lanes=lanes):
            back_ref[strip_at(r), lanes] = values

        def entered(r, lanes=lanes, stretch_part=stretch_part, offset_part=offset_part):
            return normed_ref[strip_at(r), lanes] * stretch_part + offset_part

        weigh = lambda r, lanes=lanes: grad_mixed_ref[strip_at(r), lanes]
        convolve(weigh, taps[::-1], emit)
        sums = kernel_sums(entered, weigh, BLK)
        for t in range(9):
            grad_taps_ref[t : t + 1, lanes] = jnp.sum(sums[t], axis=0, keepdims=True)

    def leave(r, carry):
        shifts, scales = carry
        normed = normed_ref[slab_at(r), :]
        back = back_ref[slab_at(r), :]
        stretched = back * stretch
        first = jnp.mean(stretched, axis=-1, keepdims=True)
        second = jnp.mean(stretched * normed, axis=-1, keepdims=True)
        inverse = inverse_ref[slab_at(r), :][:, :1]
        out = grad_hidden_ref[slab_at(r), :] + (stretched - first - normed * second) * inverse
        out_ref[slab_at(r), :] = out.astype(jnp.bfloat16)
        return shifts + fold_rows(back), scales + fold_rows(back * normed)

    zero = jnp.zeros((8, width), jnp.float32)
    shifts, scales = lax.fori_loop(0, rows // SLAB, leave, (zero, zero), unroll=UNROLL)
    grad_shift_ref[...] = jnp.sum(shifts, axis=0, keepdims=True)
    grad_scale_ref[...] = jnp.sum(scales, axis=0, keepdims=True)


def dot_of(left, right, left_axis, right_axis):
    return lax.dot_general(
        left,
        right,
        (((left_axis,), (right_axis,)), ((), ())),
        preferred_element_type=jnp.float32,
    )


def head_only(values, head):
    lane = lax.broadcasted_iota(jnp.int32, values.shape, 1)
    return jnp.where(lane // HEAD == head, values, jnp.zeros_like(values))


def attend_kernel(
    mixed_ref, attend_ref, triple_ref, context_ref, logsum_ref, low_ref, turned, values_t
):
    tokens = mixed_ref.shape[0]
    width = context_ref.shape[1]
    step = min(BLK, width)
    for start in range(0, 3 * width, step):
        columns = pl.ds(start, step)
        low_ref[:, columns] = attend_ref[:, columns].astype(jnp.bfloat16)
        triple_ref[:, columns] = dot_of(mixed_ref[...], low_ref[:, columns], 1, 0).astype(
            jnp.bfloat16
        )
    values_t[...] = triple_ref[:, pl.ds(2 * width, width)].T
    scale = jnp.bfloat16(HEAD ** (-0.5))
    for head in range(width // HEAD):
        pair = head * HEAD // LANES * LANES
        inside = head % (LANES // HEAD)

        def one(block, carry, head=head, pair=pair, inside=inside):
            spot = pl.ds(pl.multiple_of(block * QUERIES, QUERIES), QUERIES)
            queries = head_only(triple_ref[spot, pl.ds(pair, LANES)], inside) * scale
            scores = dot_of(triple_ref[:, pl.ds(width + pair, LANES)], queries, 1, 1)
            peak = jnp.max(scores, axis=0, keepdims=True)
            weights = jnp.exp(scores - peak)
            total = jnp.sum(weights, axis=0, keepdims=True)
            soft_low = (weights * (1.0 / total)).astype(jnp.bfloat16)
            turned[pl.ds(head * HEAD, HEAD), spot] = dot_of(
                values_t[pl.ds(head * HEAD, HEAD), :], soft_low, 1, 0
            )
            logsum_ref[pl.ds(head, 1), spot] = peak + jnp.log(total)
            return carry

        lax.fori_loop(0, tokens // QUERIES, one, 0)
    context_ref[...] = turned[...].T.astype(jnp.bfloat16)


def attend(mixed, attend_weight):
    tokens, width = mixed.shape
    own = attend_weight.shape[1] // 3
    vmem = pl.BlockSpec(memory_space=pltpu.VMEM)
    return pl.pallas_call(
        attend_kernel,
        out_shape=(
            jax.ShapeDtypeStruct((tokens, 3 * own), jnp.bfloat16),
            jax.ShapeDtypeStruct((tokens, own), jnp.bfloat16),
            jax.ShapeDtypeStruct((8, tokens), jnp.float32),
            jax.ShapeDtypeStruct(attend_weight.shape, jnp.bfloat16),
        ),
        in_specs=[vmem] * 2,
        out_specs=(vmem,) * 4,
        scratch_shapes=[
            pltpu.VMEM((own, tokens), jnp.float32),
            pltpu.VMEM((own, tokens), jnp.bfloat16),
        ],
        compiler_params=pltpu.CompilerParams(vmem_limit_bytes=40 * 2**20),
        cost_estimate=pl.CostEstimate(
            flops=16 * tokens * tokens * own,
            bytes_accessed=12 * tokens * width,
            transcendentals=tokens * tokens * own // HEAD,
        ),
    )(mixed, attend_weight)


def narrow_hops():
    return [("narrow", bit) for bit in reversed(bits_of(lax.axis_size("narrow")))]


def narrow_position(item):
    n = lax.axis_index("narrow")
    position = 0
    for index, (_, bit) in enumerate(narrow_hops()):
        value = (n // bit) % 2
        if (item >> index) % 2:
            value = 1 - value
        position = position + value * 2**index
    return position


def entry_kernel(
    pieces,
    context_ref,
    tokens_ref,
    output_ref,
    gate_ref,
    shift_ref,
    scale_ref,
    branch_ref,
    hidden_ref,
    entry_ref,
    slots,
    output_low,
    output_inbox,
    sends,
    arrivals,
):
    rows, own = context_ref.shape
    step = rows // pieces
    hops = narrow_hops()
    count = 2 ** len(hops)
    greet([place_at(axis, bit) for axis, bit in hops])
    chunk = lambda p: pl.ds(p * step, step)
    slots[narrow_position(0)] = context_ref[...].astype(jnp.float32)
    output_copy = send(
        output_ref, output_inbox, sends, arrivals, pieces * (count - 1), place_at("narrow", 1)
    )
    gathers = []
    for p in range(pieces):
        spot_of = lambda item, p=p: slots.at[narrow_position(item), chunk(p)]
        gathers.append(Gather(spot_of(0), spot_of, hops, sends, arrivals, p * (count - 1)))
        gathers[p].step(0)
    core = lax.axis_index("narrow") % 2
    half = output_ref.shape[0]
    output_low[pl.ds(pl.multiple_of(core * half, SLAB), half), :] = output_ref[...].astype(
        jnp.bfloat16
    )
    output_copy.wait_recv()
    output_low[pl.ds(pl.multiple_of((1 - core) * half, SLAB), half), :] = output_inbox[...].astype(
        jnp.bfloat16
    )
    gate, offset, stretch = gate_ref[...], shift_ref[...], 1.0 + scale_ref[...]
    for p in range(pieces):
        for item in gathers[p].order[1:]:
            gathers[p].step(item)
        branch = jnp.zeros((step, output_ref.shape[1]), jnp.float32)
        for position in range(count):
            branch = branch + dot_of(
                slots[position, chunk(p)].astype(jnp.bfloat16),
                output_low[pl.ds(position * own, own), :],
                1,
                0,
            )
        branch_ref[chunk(p), :] = branch

        def one(i, carry, p=p):
            spot = pl.ds(pl.multiple_of(p * step + i * SLAB, SLAB), SLAB)
            hidden = tokens_ref[spot, :].astype(jnp.float32) + gate * branch_ref[spot, :]
            hidden_ref[spot, :] = hidden
            normed, _ = norm_strip(hidden)
            entry_ref[spot, :] = (normed * stretch + offset).astype(jnp.bfloat16)
            return carry

        lax.fori_loop(0, step // SLAB, one, 0, unroll=UNROLL)
    for gather in gathers:
        gather.finish()
    output_copy.wait_send()


def enter(context, tokens, output_rows, gate, shift, scale, number):
    pieces = 4
    rows, own = context.shape
    width = tokens.shape[1]
    count = lax.axis_size("narrow")
    vmem = pl.BlockSpec(memory_space=pltpu.VMEM)
    slots = pieces * (count - 1) + 1
    return pl.pallas_call(
        functools.partial(entry_kernel, pieces),
        out_shape=(
            jax.ShapeDtypeStruct((rows, width), jnp.float32),
            jax.ShapeDtypeStruct((rows, width), jnp.float32),
            jax.ShapeDtypeStruct((rows, width), jnp.bfloat16),
        ),
        in_specs=[vmem] * 6,
        out_specs=(vmem,) * 3,
        scratch_shapes=[
            pltpu.VMEM((count, rows, own), jnp.float32),
            pltpu.VMEM((width, width), jnp.bfloat16),
            pltpu.VMEM(output_rows.shape, jnp.float32),
            pltpu.SemaphoreType.DMA((slots,)),
            pltpu.SemaphoreType.DMA((slots,)),
        ],
        compiler_params=pltpu.CompilerParams(
            collective_id=number, has_side_effects=True, vmem_limit_bytes=40 * 2**20
        ),
        cost_estimate=pl.CostEstimate(
            flops=2 * rows * width * width, bytes_accessed=100 * rows * width, transcendentals=0
        ),
    )(context, tokens, output_rows, gate, shift, scale)


def all_rows(values):
    for _, bit in narrow_hops()[:-1]:
        side = (lax.axis_index("narrow") // bit) % 2
        other = permute(values, "narrow", bit)
        values = jnp.where(
            side == 0,
            jnp.concatenate([values, other], axis=0),
            jnp.concatenate([other, values], axis=0),
        )
    return values


def back_kernel(
    pieces,
    hidden_any,
    branch_any,
    grad_entry_any,
    cotangent_any,
    live_ref,
    scale_ref,
    gate_ref,
    mixed_ref,
    attend_ref,
    output_ref,
    triple_ref,
    context_ref,
    logsum_ref,
    reduce_share_ref,
    expand_share_ref,
    grad_hidden_ref,
    grad_shift_ref,
    grad_scale_ref,
    grad_gate_ref,
    grad_mixed_any,
    attend_out_share,
    reduce_line,
    expand_line,
    hidden,
    branch,
    grad_entry,
    cotangent,
    grad_branch,
    output_low,
    grad_context,
    keys_t,
    grad_queries_t,
    grad_keys,
    grad_values,
    grad_triple,
    near,
    far,
    held,
    local,
    scatter_held,
    scatter_beside,
    scatter_inbox,
    scatter_loads,
    load_sems,
    keep_sems,
    sends,
    arrivals,
):
    tokens, width = hidden.shape
    own = output_ref.shape[0]
    _, z = wide_parts()
    far_bits = bits_of(lax.axis_size("narrow"))[1:]
    greet(
        [place_at("narrow", bit) for bit in [1] + far_bits]
        + [place_at("wide", bit) for bit in bits_of(lax.axis_size("wide"))]
    )
    hops = line_hops()
    base = (len(far_bits) + 2) * pieces + Scatter.slots()

    def spot_in(line):
        def spot_of(item):
            spot = z
            for index, (_, bit) in enumerate(hops):
                if (item >> index) % 2:
                    spot = partner(spot, bit // 2)
            return line_block(line, spot)

        return spot_of

    gathers, keeps = [], []
    for index, (share, line) in enumerate(
        ((reduce_share_ref, reduce_line), (expand_share_ref, expand_line))
    ):
        start = base + index * (2 ** len(hops) - 1)
        gathers.append(Gather(share, spot_in(line), hops, sends, arrivals, start))
        gathers[index].step(0)
        keeps.append(pltpu.make_async_copy(share, spot_in(line)(0), keep_sems.at[index]))
        keeps[index].start()
    step = tokens // pieces
    loads = []
    for p in range(pieces):
        spot = pl.ds(p * step, step)
        pairs = (
            (hidden_any, hidden),
            (branch_any, branch),
            (grad_entry_any, grad_entry),
            (cotangent_any, cotangent),
        )
        loads.append(
            [
                pltpu.make_async_copy(src.at[spot, :], dst.at[spot, :], load_sems.at[4 * p + i])
                for i, (src, dst) in enumerate(pairs)
            ]
        )
        for load in loads[p]:
            load.start()
    output_low[...] = output_ref[...].astype(jnp.bfloat16)
    stretch, gate, live = 1.0 + scale_ref[...], gate_ref[...], live_ref[...]

    def one_slab(r, carry):
        shifts, scales, gates = carry
        spot = slab_at(r)
        normed, inverse = norm_strip(hidden[spot, :])
        back = grad_entry[spot, :]
        stretched = back * stretch
        first = jnp.mean(stretched, axis=-1, keepdims=True)
        second = jnp.mean(stretched * normed, axis=-1, keepdims=True)
        grad = cotangent[spot, :].astype(jnp.float32) * live + (
            stretched - first - normed * second
        ) * inverse
        grad_hidden_ref[spot, :] = grad
        grad_branch[spot, :] = (gate * grad).astype(jnp.bfloat16)
        return (
            shifts + fold_rows(back),
            scales + fold_rows(back * normed),
            gates + fold_rows(branch[spot, :] * grad),
        )

    sums = (jnp.zeros((8, width), jnp.float32),) * 3
    for p in range(pieces):
        for load in loads[p]:
            load.wait()
        first_slab = p * step // SLAB
        sums = lax.fori_loop(
            first_slab, first_slab + step // SLAB, one_slab, sums, unroll=UNROLL
        )
    for ref, total in zip((grad_shift_ref, grad_scale_ref, grad_gate_ref), sums):
        ref[...] = jnp.sum(total, axis=0, keepdims=True)
    grad_context[...] = dot_of(grad_branch[...], output_low[...], 1, 1).astype(jnp.bfloat16)
    keys_t[...] = triple_ref[:, pl.ds(own, own)].T
    grad_keys[...] = jnp.zeros_like(grad_keys)
    grad_values[...] = jnp.zeros_like(grad_values)
    scale = HEAD ** (-0.5)
    low_scale = jnp.bfloat16(scale)
    heads = own // HEAD
    for head in range(heads):
        pair = head * HEAD // LANES * LANES
        inside = head % (LANES // HEAD)
        lanes = pl.ds(pair, LANES)

        def one(block, carry, head=head, pair=pair, inside=inside, lanes=lanes):
            spot = pl.ds(pl.multiple_of(block * QUERIES, QUERIES), QUERIES)
            queries = head_only(triple_ref[spot, lanes], inside)
            back = head_only(grad_context[spot, lanes], inside)
            scores = dot_of(triple_ref[:, pl.ds(own + pair, LANES)], queries * low_scale, 1, 1)
            weights = jnp.exp(scores - logsum_ref[pl.ds(head, 1), spot])
            grad_weights = dot_of(triple_ref[:, pl.ds(2 * own + pair, LANES)], back, 1, 1)
            grad_values[:, lanes] += dot_of(weights.astype(jnp.bfloat16), back, 1, 0)
            inner = jnp.sum(weights * grad_weights, axis=0, keepdims=True)
            grad_low = (weights * (grad_weights - inner)).astype(jnp.bfloat16)
            grad_keys[:, lanes] += dot_of(grad_low, queries, 1, 0)
            grad_queries_t[pl.ds(head * HEAD, HEAD), spot] = dot_of(
                keys_t[pl.ds(head * HEAD, HEAD), :], grad_low, 1, 0
            )
            return carry

        lax.fori_loop(0, tokens // QUERIES, one, 0)
        if head == max(heads - 2, 0):
            gathers[0].step(1)
    grad_triple[:, pl.ds(0, own)] = (grad_queries_t[...].T * scale).astype(jnp.bfloat16)
    grad_triple[:, pl.ds(own, own)] = (grad_keys[...] * scale).astype(jnp.bfloat16)
    grad_triple[:, pl.ds(2 * own, own)] = grad_values[...].astype(jnp.bfloat16)
    mixed_partial, attend_out = grad_entry, branch.at[pl.ds(0, 4 * own), :]
    mixed_partial[...] = dot_of(grad_triple[...], attend_ref[...], 1, 1)
    narrow = NarrowSum(
        far_bits, pieces, mixed_partial, grad_mixed_any, near, far, held, sends, arrivals, local, 0
    )
    narrow.start()
    grad_attend = dot_of(grad_triple[...], mixed_ref[...], 0, 0)
    grad_output = dot_of(context_ref[...], grad_branch[...], 0, 0)
    blocks = lax.axis_size("wide")
    first, second = 3 * own // blocks, own // blocks
    for b in range(blocks):
        start = b * (first + second)
        attend_out[pl.ds(start, first), :] = grad_attend[b * first : (b + 1) * first]
        attend_out[pl.ds(start + first, second), :] = grad_output[b * second : (b + 1) * second]
    scatter = Scatter(
        attend_out,
        scatter_held,
        scatter_beside,
        scatter_inbox,
        sends,
        arrivals,
        scatter_loads,
        (len(far_bits) + 2) * pieces,
    )
    for p in range(pieces):
        narrow.begin(p)
    scatter.start()
    left = list(reversed(range(blocks // 2)))
    forwards = [(0, item) for item in gathers[0].order[2:]] + [
        (1, item) for item in gathers[1].order[1:]
    ]
    urgent = [(1, 1)]
    for b in range(len(far_bits)):
        for p in range(pieces):
            narrow.step(b, p)
            if urgent:
                index, item = urgent.pop(0)
                gathers[index].step(item)
            if len(left) > 1:
                scatter.step(left.pop(0))
    for index, item in forwards:
        if (index, item) != (1, 1):
            gathers[index].step(item)
    while left:
        scatter.step(left.pop(0))
    out = pltpu.make_async_copy(scatter.held.at[0], attend_out_share, scatter.local.at[0])
    out.start()
    narrow.finish()
    scatter.finish()
    for gather in gathers:
        gather.finish()
    for keep in keeps:
        keep.wait()
    out.wait()


def back(
    hidden,
    branch,
    grad_entry,
    cotangent,
    live,
    scale,
    gate,
    mixed,
    attend_low,
    output_weight,
    triple,
    context,
    logsum,
    reduce_share,
    expand_share,
    number,
):
    tokens, width = hidden.shape
    own = output_weight.shape[0]
    pieces = 4
    line = lax.axis_size("wide") // 2
    narrow_bits = bits_of(lax.axis_size("narrow"))
    slots = (len(narrow_bits) + 1) * pieces + Scatter.slots() + 2 * (line - 1)
    vmem = pl.BlockSpec(memory_space=pltpu.VMEM)
    anywhere = pl.BlockSpec(memory_space=pl.ANY)
    f32 = lambda *shape: jax.ShapeDtypeStruct(shape, jnp.float32)
    wide = lambda *shape: pltpu.VMEM(shape, jnp.float32)
    low = lambda *shape: pltpu.VMEM(shape, jnp.bfloat16)
    return pl.pallas_call(
        functools.partial(back_kernel, pieces),
        out_shape=(
            f32(tokens, width),
            f32(1, width),
            f32(1, width),
            f32(1, width),
            f32(tokens, width),
            f32(4 * own // (2 * line), width),
            f32(line * reduce_share.shape[0], width),
            f32(line * expand_share.shape[0], width),
        ),
        in_specs=[anywhere] * 4 + [vmem] * 11,
        out_specs=(vmem,) * 4 + (anywhere,) * 4,
        scratch_shapes=[
            wide(tokens, width),
            wide(max(tokens, 4 * own), width),
            wide(tokens, width),
            low(tokens, width),
            low(tokens, width),
            low(own, width),
            low(tokens, own),
            low(own, tokens),
            wide(own, tokens),
            wide(tokens, own),
            wide(tokens, own),
            low(tokens, 3 * own),
        ]
        + narrow_scratch((tokens, width), pieces)
        + scatter_scratch((4 * own, width))
        + [
            pltpu.SemaphoreType.DMA((4 * pieces,)),
            pltpu.SemaphoreType.DMA((2,)),
            pltpu.SemaphoreType.DMA((slots,)),
            pltpu.SemaphoreType.DMA((slots,)),
        ],
        compiler_params=pltpu.CompilerParams(
            collective_id=number, has_side_effects=True, vmem_limit_bytes=60 * 2**20
        ),
        cost_estimate=pl.CostEstimate(
            flops=40 * tokens * tokens * own,
            bytes_accessed=150 * tokens * width,
            transcendentals=tokens * tokens * own // HEAD,
        ),
    )(
        hidden,
        branch,
        grad_entry,
        cotangent,
        live,
        scale,
        gate,
        mixed,
        attend_low,
        output_weight,
        triple,
        context,
        logsum,
        reduce_share,
        expand_share,
    )


def tail_kernel(
    tokens_ref,
    shift_ref,
    scale_ref,
    taps_ref,
    grad_mixed_ref,
    grad_hidden_ref,
    hidden_ref,
    ffn_half_ref,
    ffn_across_ref,
    cotangent_ref,
    live_ref,
    gate_ref,
    rows_ref,
    split_ref,
    attend_out_ref,
    reduce_ref,
    expand_ref,
    tokens_grad_ref,
    block_out_ref,
    small_ref,
    norm_ref,
    line_ref,
    ffn,
    normed_ref,
    back_ref,
    inverse_ref,
    grad_taps,
    grad_shift,
    grad_scale,
    slots,
    spare,
    spare_in,
    keep_sems,
    sends,
    arrivals,
):
    width = tokens_ref.shape[1]
    wide_bits = bits_of(lax.axis_size("wide"))
    narrow_bits = bits_of(lax.axis_size("narrow"))
    greet(
        [place_at("wide", bit) for bit in wide_bits]
        + [place_at("narrow", bit) for bit in narrow_bits]
    )
    _, z = wide_parts()
    count = len(wide_bits)
    hops = line_hops()

    def spot_of(item):
        spot = z
        for index, (_, bit) in enumerate(hops):
            if (item >> index) % 2:
                spot = partner(spot, bit // 2)
        return line_block(line_ref, spot)

    gather = Gather(attend_out_ref, spot_of, hops, sends, arrivals, count + len(narrow_bits))
    gather.step(0)
    keep = pltpu.make_async_copy(attend_out_ref, spot_of(0), keep_sems.at[0])
    keep.start()
    core = lax.axis_index("narrow") % 2
    half = ffn.shape[0] // 2
    mine = pl.ds(pl.multiple_of(core * half, SLAB), half)
    ffn[mine, :] = ffn_half_ref[...] + ffn_across_ref[...]
    last = count + len(narrow_bits) + 2 ** len(hops) - 1
    ffn_copy = send(ffn.at[mine, :], ffn.at[mine, :], sends, arrivals, last, place_at("narrow", 1))
    mixer_kernel_backward(
        tokens_ref,
        shift_ref,
        scale_ref,
        taps_ref,
        grad_mixed_ref,
        grad_hidden_ref,
        tokens_grad_ref,
        grad_taps,
        grad_shift,
        grad_scale,
        normed_ref,
        back_ref,
        inverse_ref,
    )
    ffn_copy.wait_recv()
    gate, live = gate_ref[...], live_ref[...]

    def leave(r, gates):
        spot = slab_at(r)
        branch = ffn[spot, :]
        block_out_ref[spot, :] = (live * (hidden_ref[spot, :] + gate * branch)).astype(jnp.bfloat16)
        return gates + fold_rows(branch * (cotangent_ref[spot, :].astype(jnp.float32) * live))

    gates = lax.fori_loop(
        0, ffn.shape[0] // SLAB, leave, jnp.zeros((8, width), jnp.float32), unroll=UNROLL
    )
    slots[0] = jnp.zeros(slots.shape[1:], jnp.float32)
    slots[0, 0:1, :] = grad_shift[...]
    slots[0, 1:2, :] = grad_scale[...]
    slots[0, 2:5, :] = rows_ref[...]
    slots[0, 5:6, :] = jnp.sum(gates, axis=0, keepdims=True)
    shared_rows = 6 + taps_ref.shape[0]
    slots[0, 6:shared_rows, :] = grad_taps[...]
    split_rows = split_ref.shape[0]
    slots[0, shared_rows : shared_rows + split_rows, :] = split_ref[...]
    squares = jnp.zeros((8, width), jnp.float32)
    for share in (attend_out_ref, reduce_ref, expand_ref):
        squares = squares + fold_rows(share[...] * share[...])
    end = shared_rows + split_rows
    slots[0, end : end + 1, :] = jnp.sum(squares, axis=0, keepdims=True)
    copies = []
    for b in range(count):
        copy = send(
            slots.at[b], slots.at[count + 1 + b], sends, arrivals, b, place_at("wide", wide_bits[b])
        )
        copies.append(copy)
        if b == 0:
            gather.step(1)
        copy.wait_recv()
        slots[b + 1] = slots[b] + slots[count + 1 + b]
    total = slots[count]
    small_ref[...] = total
    shared_part = total[:shared_rows]
    split_part = total[shared_rows:end]
    shared = jnp.sum(shared_part * shared_part)
    split_sum = jnp.sum(split_part * split_part) + jnp.sum(total[end : end + 1])
    spare[0] = jnp.full(spare.shape[1:], split_sum, jnp.float32)
    for b in range(len(narrow_bits)):
        copy = send(
            spare.at[b], spare_in.at[b], sends, arrivals, count + b, place_at("narrow", narrow_bits[b])
        )
        copies.append(copy)
        copy.wait_recv()
        spare[b + 1] = spare[b] + spare_in[b]
    norm_ref[...] = jnp.sqrt(spare[len(narrow_bits)] + shared)
    for item in gather.order[2:]:
        gather.step(item)
    keep.wait()
    gather.finish()
    ffn_copy.wait_send()
    for copy in copies:
        copy.wait_send()


def tail(
    tokens,
    shift,
    scale,
    taps,
    grad_mixed,
    grad_hidden,
    hidden,
    ffn_half,
    ffn_across,
    cotangent,
    live,
    gate,
    table_rows,
    split_rows,
    shares,
    number,
):
    rows, width = tokens.shape
    wide_bits = bits_of(lax.axis_size("wide"))
    narrow_bits = bits_of(lax.axis_size("narrow"))
    count = len(wide_bits)
    line = lax.axis_size("wide") // 2
    total = count + len(narrow_bits) + line
    small = -(-(6 + taps.shape[0] + split_rows.shape[0] + 1) // 8) * 8
    vmem = pl.BlockSpec(memory_space=pltpu.VMEM)
    anywhere = pl.BlockSpec(memory_space=pl.ANY)
    f32 = lambda *shape: jax.ShapeDtypeStruct(shape, jnp.float32)
    low = lambda *shape: jax.ShapeDtypeStruct(shape, jnp.bfloat16)
    wide = lambda *shape: pltpu.VMEM(shape, jnp.float32)
    return pl.pallas_call(
        tail_kernel,
        out_shape=(
            low(rows, width),
            low(rows, width),
            f32(small, width),
            f32(8, LANES),
            f32(line * shares[0].shape[0], width),
        ),
        in_specs=[vmem] * 17,
        out_specs=(vmem,) * 4 + (anywhere,),
        scratch_shapes=[
            wide(rows, width),
            wide(rows, width),
            wide(rows, width),
            wide(rows, LANES),
            wide(9, width),
            wide(1, width),
            wide(1, width),
            wide(2 * count + 1, small, width),
            wide(len(narrow_bits) + 1, 8, LANES),
            wide(len(narrow_bits), 8, LANES),
            pltpu.SemaphoreType.DMA((1,)),
            pltpu.SemaphoreType.DMA((total,)),
            pltpu.SemaphoreType.DMA((total,)),
        ],
        compiler_params=pltpu.CompilerParams(
            collective_id=number, has_side_effects=True, vmem_limit_bytes=56 * 2**20
        ),
        cost_estimate=pl.CostEstimate(
            flops=100 * rows * width, bytes_accessed=60 * rows * width, transcendentals=0
        ),
    )(
        tokens,
        shift,
        scale,
        taps,
        grad_mixed,
        grad_hidden,
        hidden,
        ffn_half,
        ffn_across,
        cotangent,
        live,
        gate,
        table_rows,
        split_rows,
        *shares,
    )


def local(
    tokens,
    conditions,
    item_live,
    cotangent,
    modulation_table,
    mixer_kernel,
    hidden_kernel,
    attend_weight,
    output_weight,
    expand_weight,
    reduce_weight,
    attend_moment,
    output_moment,
    expand_moment,
    reduce_moment,
    table_first,
    table_second,
    mixer_first,
    mixer_second,
    hidden_first,
    hidden_second,
):
    live_mask = item_live.astype(jnp.float32)[:, None, None]
    modulation = modulation_table[None] + conditions
    shift_one = modulation[:, 0:1]
    scale_one = modulation[:, 1:2]
    gate_one = modulation[:, 2:3]
    shift_two = modulation[:, 3:4]
    scale_two = modulation[:, 4:5]
    gate_two = modulation[:, 5:6]
    width = tokens.shape[2]
    flat_tokens = tokens.reshape(-1, width)
    mixed_low = mixer_forward(flat_tokens, shift_one[0], scale_one[0], mixer_kernel)
    attend_flat = attend_weight.reshape(width, -1)
    triple, context, logsum, attend_low = attend(mixed_low, attend_flat)
    output_rows, context = together(all_rows(output_weight), context)
    branch, hidden, entry_low = enter(
        context, flat_tokens, output_rows, gate_one[0], shift_two[0], scale_two[0], 1
    )
    flat_cotangent = cotangent.reshape(-1, width)
    live_row = jnp.broadcast_to(live_mask[0], (1, width))
    ffn_half, grad_entry, reduce_share, expand_share, grad_hidden_kernel = middle(
        entry_low,
        flat_cotangent,
        live_row,
        gate_two[0],
        expand_weight,
        reduce_weight,
        hidden_kernel,
        2,
    )
    grad_entry, reduce_share, expand_share, ffn_half = together(
        grad_entry, reduce_share, expand_share, ffn_half
    )
    for bit in bits_of(lax.axis_size("narrow"))[1:-1]:
        ffn_half = ffn_half + permute(ffn_half, "narrow", bit)
    ffn_across = permute(ffn_half, "narrow", lax.axis_size("narrow") // 2)
    (
        grad_hidden,
        grad_shift_two,
        grad_scale_two,
        grad_gate_one,
        grad_mixed,
        attend_out_share,
        reduce_line,
        expand_line,
    ) = back(
        hidden,
        branch,
        grad_entry,
        flat_cotangent,
        live_row,
        scale_two[0],
        gate_one[0],
        mixed_low,
        attend_low,
        output_weight,
        triple,
        context,
        logsum,
        reduce_share,
        expand_share,
        3,
    )
    ffn_across, grad_mixed, reduce_line, attend_out_share = together(
        ffn_across, grad_mixed, reduce_line, attend_out_share
    )
    reduce_other = permute(reduce_line, "wide", 1)
    shared_rows = modulation_table.shape[0] + mixer_kernel.shape[0]
    hidden_rows = -(-grad_hidden_kernel.size // width)
    padding = hidden_rows * width - grad_hidden_kernel.size
    hidden_flat = jnp.pad(grad_hidden_kernel.reshape(-1), (0, padding))
    tokens_gradient, block_out, small, norm, attend_out_line = tail(
        flat_tokens,
        shift_one[0],
        scale_one[0],
        mixer_kernel,
        grad_mixed,
        grad_hidden,
        hidden,
        ffn_half,
        ffn_across,
        flat_cotangent,
        live_row,
        gate_two[0],
        jnp.concatenate([grad_gate_one, grad_shift_two, grad_scale_two], axis=0),
        hidden_flat.reshape(hidden_rows, width),
        [attend_out_share, reduce_share, expand_share],
        4,
    )
    tokens_gradient = tokens_gradient.reshape(tokens.shape)
    block_out = block_out.reshape(tokens.shape)
    summed_table = small[: modulation_table.shape[0]]
    summed_mixer = small[modulation_table.shape[0] : shared_rows]
    summed_hidden = small[shared_rows : shared_rows + hidden_rows].reshape(-1)
    summed_hidden = summed_hidden[: hidden_kernel.size].reshape(hidden_kernel.shape)
    gradient_norm = norm[0, 0]
    clip_factor = jnp.minimum(1.0, 1.0 / (gradient_norm + 1e-06))
    attend_moment_flat = attend_moment.reshape(width, -1)
    attend_half = own_half(attend_moment_flat, 1).T
    gramian = gram_whole(
        norm,
        [attend_out_line, expand_line, reduce_line],
        [attend_half, output_moment, expand_moment, reduce_moment],
        5,
    )
    gramian, expand_line, attend_out_line = together(gramian, expand_line, attend_out_line)
    expand_other = permute(expand_line, "wide", 1)
    attend_out_other = permute(attend_out_line, "wide", 1)
    factor = spread(polar_factor(gramian), 6)
    factor, expand_other, attend_out_other, reduce_other = together(
        factor, expand_other, attend_out_other, reduce_other
    )
    carried, results = finish(
        norm,
        factor,
        [attend_out_line, expand_line, reduce_line],
        [attend_out_other, expand_other, reduce_other],
        [attend_moment_flat, output_moment, expand_moment, reduce_moment],
        [attend_flat, output_weight, expand_weight, reduce_weight],
    )
    attend_carried = carried[0].reshape(attend_weight.shape)
    attend_result = results[0].reshape(attend_weight.shape)
    table_moment, table_square, table_result = adam_update(
        modulation_table, table_first, table_second, clip_factor * summed_table
    )
    mixer_moment, mixer_square, mixer_result = adam_update(
        mixer_kernel, mixer_first, mixer_second, clip_factor * summed_mixer
    )
    hidden_moment, hidden_square, hidden_result = adam_update(
        hidden_kernel, hidden_first, hidden_second, clip_factor * summed_hidden
    )
    return (
        block_out,
        tokens_gradient,
        gradient_norm,
        attend_carried,
        carried[1],
        carried[2],
        carried[3],
        attend_result,
        results[1],
        results[2],
        results[3],
        table_moment,
        table_square,
        table_result,
        mixer_moment,
        mixer_square,
        mixer_result,
        hidden_moment,
        hidden_square,
        hidden_result,
    )


def solution(mesh):
    placed = (
        P("wide", None, None),
        P("wide", None, None),
        P("wide"),
        P("wide", None, None),
        P(),
        P(),
        P(None, "narrow"),
        P(None, None, "narrow"),
        P("narrow", None),
        P(None, "narrow"),
        P("narrow", None),
        P(None, None, "narrow"),
        P("narrow", None),
        P(None, "narrow"),
        P("narrow", None),
        P(),
        P(),
        P(),
        P(),
        P(None, "narrow"),
        P(None, "narrow"),
    )
    return jax.shard_map(
        local,
        mesh=mesh,
        in_specs=placed,
        out_specs=(
            P("wide", None, None),
            P("wide", None, None),
            P(),
            P(None, None, "narrow"),
            P("narrow", None),
            P(None, "narrow"),
            P("narrow", None),
            P(None, None, "narrow"),
            P("narrow", None),
            P(None, "narrow"),
            P("narrow", None),
            P(),
            P(),
            P(),
            P(),
            P(),
            P(),
            P(None, "narrow"),
            P(None, "narrow"),
            P(None, "narrow"),
        ),
        check_vma=False,
    )
```

```python
import functools
import math

import jax
import jax.numpy as jnp
from jax import lax
from jax.experimental import pallas as pl
from jax.experimental.pallas import tpu as pltpu
from jax.sharding import PartitionSpec as P

D = 1024
HEAD = 64
FF = 4096
GRID = 32
NEWTON = 5
STEP = 10


first_decay = 0.9
second_decay = 0.999
adam_rate = 0.3
muon_rate = 0.15
muon_momentum = 0.5
weight_decay = 0.01
newton_terms = (3.4445, -4.775, 2.0315)
gelu_slope = 0.7978845608
gelu_cubic = 0.044715


MESH = pl.DeviceIdType.MESH
BLK = 256
LANES = 128
SLAB = 16
QUERIES = 512
UNROLL = 4
MATRICES = 4
COLUMNS = (0, 2)


def partner(index, bit):
    return index + (1 - 2 * ((index // bit) % 2)) * bit


def bits_of(count):
    found = []
    bit = 1
    while bit < count:
        found.append(bit)
        bit *= 2
    return found


def place_at(axis, bit):
    place = {"wide": lax.axis_index("wide"), "narrow": lax.axis_index("narrow")}
    place[axis] = partner(place[axis], bit)
    return (place["wide"], place["narrow"])


def greet(places):
    barrier = pltpu.get_barrier_semaphore()
    for place in places:
        pl.semaphore_signal(barrier, inc=1, device_id=place, device_id_type=MESH)
    pl.semaphore_wait(barrier, len(places))


def send(src, dst, sends, arrivals, slot, place):
    copy = pltpu.make_async_remote_copy(
        src_ref=src,
        dst_ref=dst,
        send_sem=sends.at[slot],
        recv_sem=arrivals.at[slot],
        device_id=place,
        device_id_type=MESH,
    )
    copy.start()
    return copy


def permute(values, axis, bit):
    size = lax.axis_size(axis)
    return lax.ppermute(values, axis, [(index, index ^ bit) for index in range(size)])


def together(*values):
    return lax.optimization_barrier(values)


def wide_parts():
    w = lax.axis_index("wide")
    return w % 2, w // 2


def line_partner(z, offset):
    for bit in bits_of(2 * offset):
        if (offset // bit) % 2:
            z = partner(z, bit)
    return z


def block_of(ref, y, z):
    count = lax.axis_size("wide") // 2
    rows = ref.shape[0] // (2 * count)
    return ref.at[pl.ds(pl.multiple_of((y * count + z) * rows, 8), rows), :]


def line_block(ref, z):
    rows = ref.shape[0] // (lax.axis_size("wide") // 2)
    return ref.at[pl.ds(pl.multiple_of(z * rows, 8), rows), :]


def block_shape(shape):
    return (shape[0] // lax.axis_size("wide"), shape[1])


class Scatter:
    def __init__(self, src, held, beside, inbox, sends, arrivals, local, base, blocks=None):
        self.src, self.held, self.beside, self.inbox = src, held, beside, inbox
        self.blocks = blocks
        self.sends, self.arrivals, self.local, self.base = sends, arrivals, local, base
        self.count = lax.axis_size("wide") // 2 if blocks is None else blocks[0].shape[0]
        self.copies = {}
        self.loads = {}

    @staticmethod
    def slots():
        return lax.axis_size("wide") - 1

    def load(self):
        y, z = wide_parts()
        for e in reversed(range(self.count)):
            own = self.blocks[0].at[e] if self.blocks else block_of(self.src, y, line_partner(z, e))
            self.loads[e] = pltpu.make_async_copy(own, self.held.at[e], self.local.at[e])
            self.loads[e].start()

    def give(self, e):
        y, z = wide_parts()
        self.copies[("y", e)] = send(
            self.blocks[1].at[e] if self.blocks else block_of(self.src, 1 - y, line_partner(z, e)),
            self.beside.at[e],
            self.sends,
            self.arrivals,
            self.base + e,
            place_at("wide", 1),
        )

    def start(self):
        self.load()
        for e in reversed(range(self.count)):
            self.give(e)

    def step(self, e):
        self.loads[e].wait()
        self.copies[("y", e)].wait_recv()
        self.held[e] = self.held[e] + self.beside[e]
        bit = 1
        while bit < self.count and e % (2 * bit) == 0:
            self.copies[("z", e + bit)].wait_recv()
            self.held[e] = self.held[e] + self.inbox[e + bit - 1]
            bit *= 2
        if e:
            low = e & -e
            self.copies[("z", e)] = send(
                self.held.at[e],
                self.inbox.at[e - 1],
                self.sends,
                self.arrivals,
                self.base + self.count + e - 1,
                place_at("wide", 2 * low),
            )

    def finish(self):
        for copy in self.copies.values():
            copy.wait_send()


def scatter_scratch(shape):
    count = lax.axis_size("wide") // 2
    block = block_shape(shape)
    return [
        pltpu.VMEM((count,) + block, jnp.float32),
        pltpu.VMEM((count,) + block, jnp.float32),
        pltpu.VMEM((max(count - 1, 1),) + block, jnp.float32),
        pltpu.SemaphoreType.DMA((count,)),
    ]


class Gather:
    def __init__(self, own, spot_of, hops, sends, arrivals, base):
        self.own, self.spot_of, self.hops = own, spot_of, hops
        self.sends, self.arrivals, self.base = sends, arrivals, base
        self.copies = {}
        self.order = sorted(range(2 ** len(hops)), key=lambda item: (bin(item).count("1"), item))

    def step(self, item):
        if item:
            self.copies[item].wait_recv()
        for index in range(item.bit_length(), len(self.hops)):
            later = item + 2**index
            spot = self.spot_of(item)
            axis, bit = self.hops[index]
            self.copies[later] = send(
                spot if item else self.own,
                spot,
                self.sends,
                self.arrivals,
                self.base + later - 1,
                place_at(axis, bit),
            )

    def finish(self):
        for copy in self.copies.values():
            copy.wait_send()


def line_hops():
    return [("wide", bit) for bit in reversed(bits_of(lax.axis_size("wide"))) if bit > 1]


class NarrowSum:
    def __init__(self, far_bits, pieces, x, o, near, far, held, sends, arrivals, local, base):
        self.bits, self.pieces = far_bits, pieces
        self.x, self.o, self.near, self.far, self.held = x, o, near, far, held
        self.sends, self.arrivals, self.local, self.base = sends, arrivals, local, base
        self.rows = x.shape[0] // 2
        self.core = lax.axis_index("narrow") % 2
        self.copies = []
        self.cross = {}
        self.keeps = []

    def block(self, side, p):
        step = self.rows // self.pieces
        return pl.ds(pl.multiple_of(side * self.rows + p * step, 8), step)

    def push(self, src, dst, slot, bit):
        copy = send(
            src, dst, self.sends, self.arrivals, self.base + slot, place_at("narrow", bit)
        )
        self.copies.append(copy)
        return copy

    def start(self):
        self.first = [
            self.push(self.x.at[self.block(1 - self.core, p)], self.near.at[p], p, 1)
            for p in range(self.pieces)
        ]
        self.loads = [
            pltpu.make_async_copy(
                self.x.at[self.block(self.core, p)], self.held.at[0, p], self.local.at[p]
            )
            for p in range(self.pieces)
        ]
        for load in self.loads:
            load.start()

    def hop(self, b, p):
        slot = (b + 1) * self.pieces + p
        self.cross[(b, p)] = self.push(
            self.held.at[b, p], self.far.at[b, p], slot, self.bits[b]
        )

    def begin(self, p):
        self.loads[p].wait()
        self.first[p].wait_recv()
        self.held[0, p] = self.held[0, p] + self.near[p]
        self.hop(0, p)

    def step(self, b, p):
        self.cross[(b, p)].wait_recv()
        self.held[b + 1, p] = self.held[b, p] + self.far[b, p]
        if b + 1 < len(self.bits):
            self.hop(b + 1, p)
            return
        spot = self.o.at[self.block(self.core, p)]
        slot = (b + 2) * self.pieces + p
        self.keeps.append(self.push(self.held.at[b + 1, p], spot, slot, 1))
        keep = pltpu.make_async_copy(self.held.at[b + 1, p], spot, self.local.at[p])
        keep.start()
        self.loads[p] = keep

    def finish(self):
        for copy in self.keeps:
            copy.wait_recv()
        for keep in self.loads:
            keep.wait()
        for copy in self.copies:
            copy.wait_send()


def narrow_scratch(shape, pieces):
    count = len(bits_of(lax.axis_size("narrow"))) - 1
    step = shape[0] // (2 * pieces)
    return [
        pltpu.VMEM((pieces, step, shape[1]), jnp.float32),
        pltpu.VMEM((count, pieces, step, shape[1]), jnp.float32),
        pltpu.VMEM((count + 1, pieces, step, shape[1]), jnp.float32),
        pltpu.SemaphoreType.DMA((pieces,)),
    ]


def gram_kernel(
    norm_ref,
    attend_out_any,
    expand_any,
    reduce_any,
    attend_moment_any,
    output_moment_any,
    expand_moment_any,
    reduce_moment_any,
    band_ref,
    expand_beside,
    attend_out,
    expand,
    reduce,
    attend_moment,
    output_moment,
    expand_moment,
    reduce_moment,
    *refs,
):
    highs, lows, refs = refs[:MATRICES], refs[MATRICES : 2 * MATRICES], refs[2 * MATRICES :]
    attend_turned, attend_blend, refs = refs[0], refs[1], refs[2:]
    twice, halves, inbox, block, load_sems, sends, arrivals, local = refs
    narrow_bits = bits_of(lax.axis_size("narrow"))
    wide_bits = bits_of(lax.axis_size("wide"))
    parts, rows = halves.shape[0], halves.shape[1]
    sub = parts // MATRICES
    size = attend_out.shape[1]
    hops = [("narrow", bit) for bit in bits_of(sub)]
    hops += [("wide", bit) for bit in reversed(wide_bits)]
    w, n = lax.axis_index("wide"), lax.axis_index("narrow")
    y, z = wide_parts()
    greet(
        [place_at("narrow", bit) for bit in narrow_bits]
        + [place_at("wide", bit) for bit in wide_bits]
    )
    early = expand_beside.shape[0]
    expand_copy = send(
        expand_any.at[pl.ds(0, early), :],
        expand_beside,
        sends,
        arrivals,
        sends.shape[0] - 1,
        place_at("wide", 1),
    )
    own_rows = lambda ref: ref.at[
        pl.ds(pl.multiple_of(y * (ref.shape[0] // 2), 8), ref.shape[0] // 2), :
    ]
    own_columns = lambda ref: ref.at[
        :, pl.ds(pl.multiple_of(y * (ref.shape[1] // 2), LANES), ref.shape[1] // 2)
    ]
    loads = []
    own = attend_moment_any.shape[2]
    for j in range(3):
        pltpu.make_async_copy(
            attend_moment_any.at[j], attend_moment.at[:, pl.ds(j * own, own)], load_sems.at[1]
        ).start()
    for src, dst in (
        (attend_out_any, attend_out),
        (None, None),
        (own_rows(output_moment_any), output_moment),
        (expand_any, expand),
        (own_columns(expand_moment_any), expand_moment),
        (reduce_any, reduce),
        (own_rows(reduce_moment_any), reduce_moment),
    ):
        if src is None:
            loads.append(pltpu.make_async_copy(attend_moment, attend_moment, load_sems.at[1]))
            continue
        loads.append(pltpu.make_async_copy(src, dst, load_sems.at[len(loads)]))
        loads[-1].start()
    clip = jnp.minimum(1.0, 1.0 / (norm_ref[0:1, 0:1] + 1e-06))
    count = halves.shape[1] * sub
    start = z * count
    lines = lax.axis_size("wide") // 2
    band = halves.shape[2]

    def blend(k, moment, gradient):
        total = highs[k].shape[0]

        def one(i, carry):
            spot = slab_at(i)
            highs[k][spot, :], lows[k][spot, :] = split(
                muon_momentum * moment[spot, :] + clip * gradient[spot, :]
            )
            return carry

        lax.fori_loop(0, total // SLAB, one, 0, unroll=UNROLL)

    def multiply(k):
        columns = pl.ds(pl.multiple_of(start, LANES), count)
        high, low = highs[k][:, columns], lows[k][:, columns]
        values = dot_of(high, highs[k][...], 0, 0) + (
            dot_of(high, lows[k][...], 0, 0) + dot_of(low, highs[k][...], 0, 0)
        )
        twice[:, :size] = values
        twice[:, size:] = values[:, :band]
        for s in range(sub):
            for at in range(0, rows, LANES):
                extent = min(LANES, rows)
                first = s * rows + at
                lanes = pl.ds(pl.multiple_of(start + first // LANES * LANES, LANES), band)
                halves[k * sub + s, at : at + extent, :] = twice[first : first + extent, lanes]

    share = attend_out.shape[0] // lines
    first_rows, second_rows = 3 * share // 4, share // 4
    loads[0].wait()
    loads[1].wait()
    loads[2].wait()
    for at in range(0, 3 * own, LANES):
        attend_turned[pl.ds(at, LANES), :] = attend_moment[:, pl.ds(at, LANES)].T
    offset = y * (3 * own // 2)
    for b in range(lines):
        gradient = attend_out[b * share : (b + 1) * share, :]
        spot = pl.ds(pl.multiple_of(offset + b * first_rows, 8), first_rows)
        attend_blend[pl.ds(b * first_rows, first_rows), :] = (
            muon_momentum * attend_turned[spot, :] + clip * gradient[:first_rows]
        )
        spot = pl.ds(b * second_rows, second_rows)
        output_moment[spot, :] = (
            muon_momentum * output_moment[spot, :] + clip * gradient[first_rows:]
        )

    def cut(k, values):
        def one(i, carry):
            spot = slab_at(i)
            highs[k][spot, :], lows[k][spot, :] = split(values[spot, :])
            return carry

        lax.fori_loop(0, highs[k].shape[0] // SLAB, one, 0, unroll=UNROLL)

    cut(0, attend_blend)
    multiply(0)
    cut(1, output_moment)
    multiply(1)
    loads[3].wait()
    loads[4].wait()
    for at in range(0, expand.shape[0], LANES):
        spot = pl.ds(at, LANES)
        highs[2][spot, :], lows[2][spot, :] = split(
            muon_momentum * expand_moment[:, spot].T + clip * expand[spot, :]
        )
    multiply(2)
    loads[5].wait()
    loads[6].wait()
    blend(3, reduce_moment, reduce)
    multiply(3)
    half = rows // 2
    row_half = lambda side: pl.ds(pl.multiple_of(side * half, 8), half)
    slot = iter(range(sends.shape[0]))
    copies = []

    def push(src, dst, place):
        copies.append(send(src, dst, sends, arrivals, next(slot), place))
        return copies[-1]

    at = 0
    for bit in narrow_bits:
        value = (n // bit) % 2
        last = 2 * bit == parts
        waits = []
        for j in range(parts // (2 * bit)):
            mine = n % bit + value * bit + j * 2 * bit
            theirs = n % bit + (1 - value) * bit + j * 2 * bit
            for side in (1 - y, y) if last else (None,):
                spot = slice(None) if side is None else row_half(side)
                copy = push(
                    halves.at[theirs] if side is None else halves.at[theirs, spot],
                    inbox.at[at + j] if side is None else inbox.at[at + j, spot],
                    place_at("narrow", bit),
                )
                waits.append((copy, mine, at + j, spot))
        at += parts // (2 * bit)
        for copy, mine, where, spot in waits:
            copy.wait_recv()
            halves[mine, spot] = halves[mine, spot] + inbox[where, spot]
            if last and copy is waits[0][0]:
                side_copy = push(halves.at[n, row_half(1 - y)], block.at[0], place_at("wide", 1))
    side_copy.wait_recv()
    block[1] = halves[n, row_half(y)] + block[0]

    def spot_of(item):
        big, small = w, n % sub
        for index, (axis, bit) in enumerate(hops):
            if (item >> index) % 2:
                if axis == "wide":
                    big = partner(big, bit)
                else:
                    small = partner(small, bit)
        first = ((big // 2) * (2 * sub) + small * 2 + big % 2) * half
        return band_ref.at[pl.ds(pl.multiple_of(first, 8), half), :]

    keep = pltpu.make_async_copy(block.at[1], spot_of(0), local.at[0])
    keep.start()
    gather = Gather(block.at[1], spot_of, hops, sends, arrivals, next(slot))
    for item in gather.order:
        gather.step(item)
    keep.wait()
    gather.finish()
    expand_copy.wait()
    for copy in copies:
        copy.wait_send()


def gram_whole(norm, lines, moments, number):
    narrow_bits = bits_of(lax.axis_size("narrow"))
    wide_bits = bits_of(lax.axis_size("wide"))
    size = lines[0].shape[1]
    sub = lax.axis_size("narrow") // MATRICES
    parts = lax.axis_size("narrow")
    count = 2 * size // lax.axis_size("wide")
    band = size // 2 + LANES
    halves = (parts, count // sub, band)
    line_rows = [lines[0].shape[0] * 3 // 4, lines[0].shape[0] // 4]
    line_rows += [lines[1].shape[0], lines[2].shape[0]]
    gathers = len(bits_of(sub)) + len(wide_bits)
    slots = parts + 3 + 2**gathers
    vmem = pl.BlockSpec(memory_space=pltpu.VMEM)
    anywhere = pl.BlockSpec(memory_space=pl.ANY)
    wide = lambda *shape: pltpu.VMEM(shape, jnp.float32)
    return pl.pallas_call(
        gram_kernel,
        out_shape=(
            jax.ShapeDtypeStruct((size, band), jnp.float32),
            jax.ShapeDtypeStruct((lines[1].shape[0] // 2, size), jnp.float32),
        ),
        in_specs=[vmem] + [anywhere] * 7,
        out_specs=(anywhere, anywhere),
        scratch_shapes=[
            wide(*lines[0].shape),
            wide(*lines[1].shape),
            wide(*lines[2].shape),
            wide(size, 2 * line_rows[0]),
            wide(line_rows[1], size),
            wide(size, line_rows[2]),
            wide(line_rows[3], size),
        ]
        + [pltpu.VMEM((rows, size), jnp.bfloat16) for rows in line_rows] * 2
        + [
            wide(2 * line_rows[0], size),
            wide(line_rows[0], size),
            wide(count, size + band),
            wide(*halves),
            wide(*halves),
            wide(2, halves[1] // 2, band),
            pltpu.SemaphoreType.DMA((7,)),
            pltpu.SemaphoreType.DMA((slots,)),
            pltpu.SemaphoreType.DMA((slots,)),
            pltpu.SemaphoreType.DMA((1,)),
        ],
        compiler_params=pltpu.CompilerParams(
            collective_id=number, has_side_effects=True, vmem_limit_bytes=48 * 2**20
        ),
        cost_estimate=pl.CostEstimate(
            flops=3 * size * size * size, bytes_accessed=80 * size * size, transcendentals=0
        ),
    )(norm, *lines, *moments)


def split(values):
    high = values.astype(jnp.bfloat16)
    return high, (values - high.astype(jnp.float32)).astype(jnp.bfloat16)


def product(left_high, left_low, right_high, right_low):
    dot = functools.partial(jnp.dot, preferred_element_type=jnp.float32)
    return dot(left_high, right_high) + (dot(left_high, right_low) + dot(left_low, right_high))


def polar_kernel(g_ref, band_ref, q_ref, gh, gl, ph, pw, th, tl):
    size = g_ref.shape[0]
    blocks = size // BLK
    first, second, third = newton_terms
    rows = lambda block: pl.ds(block * BLK, BLK)
    square = (BLK, BLK)
    unit = (
        lax.broadcasted_iota(jnp.int32, square, 0) == lax.broadcasted_iota(jnp.int32, square, 1)
    ).astype(jnp.float32)
    count = size // LANES
    lanes = lambda block: pl.ds((block % count) * LANES, LANES)
    trace = jnp.zeros((), jnp.float32)
    for i in range(count):
        trace = trace + jnp.sum(g_ref[lanes(i), lanes(0)] * unit[:LANES, :LANES])
    factor = 1.0 / (jnp.sqrt(trace) + 1e-07)
    for i in range(count):
        for j in range(count // 2 + 1):
            values = g_ref[lanes(i), lanes(j)] * (factor * factor)
            gh[lanes(i), lanes(i + j)], gl[lanes(i), lanes(i + j)] = split(values)
            if 0 < j < count // 2:
                values = values.T
                gh[lanes(i + j), lanes(i)], gl[lanes(i + j), lanes(i)] = split(values)

    def put(high, low, i, j, values):
        high[rows(i), rows(j)], low[rows(i), rows(j)] = split(values)
        if i != j:
            high[rows(j), rows(i)], low[rows(j), rows(i)] = split(values.T)

    def symmetric(left, right, emit):
        for i in range(blocks):
            columns = pl.ds(i * BLK, size - i * BLK)
            values = product(
                left[0][rows(i), :], left[1][rows(i), :], right[0][:, columns], right[1][:, columns]
            )
            for j in range(i, blocks):
                emit(i, j, values[:, (j - i) * BLK : (j - i + 1) * BLK])

    def emit_terms(i, j, values):
        gram = gh[rows(i), rows(j)].astype(jnp.float32) + gl[rows(i), rows(j)].astype(jnp.float32)
        terms = second * gram + third * values
        if i == j:
            terms = terms + first * unit
        put(ph, pw, i, j, terms)

    def emit_total(i, j, values):
        q_ref[rows(i), rows(j)] = values
        if i != j:
            q_ref[rows(j), rows(i)] = values.T

    symmetric((gh, gl), (gh, gl), emit_terms)
    for i in range(blocks):
        q_ref[rows(i), :] = (
            ph[rows(i), :].astype(jnp.float32) + pw[rows(i), :].astype(jnp.float32)
        ) * factor

    def one_step(step, carry):
        symmetric((ph, pw), (gh, gl), functools.partial(put, th, tl))
        symmetric((th, tl), (ph, pw), functools.partial(put, gh, gl))
        symmetric((gh, gl), (gh, gl), emit_terms)
        for i in range(blocks):
            th[rows(i), :], tl[rows(i), :] = split(q_ref[rows(i), :])
        symmetric((ph, pw), (th, tl), emit_total)
        return carry

    lax.fori_loop(0, NEWTON - 1, one_step, 0)
    for i in range(count):
        for j in range(count // 2 + 1):
            band_ref[lanes(i), lanes(j)] = q_ref[lanes(i), lanes(i + j)]


def polar_factor(gramian):
    size = gramian.shape[0]
    vmem = pl.BlockSpec(memory_space=pltpu.VMEM)
    return pl.pallas_call(
        polar_kernel,
        out_shape=jax.ShapeDtypeStruct(gramian.shape, jnp.float32),
        in_specs=[vmem],
        out_specs=vmem,
        scratch_shapes=[pltpu.VMEM((size, size), jnp.float32)]
        + [pltpu.VMEM((size, size), jnp.bfloat16)] * 6,
        compiler_params=pltpu.CompilerParams(vmem_limit_bytes=48 * 2**20),
        cost_estimate=pl.CostEstimate(
            flops=17 * 6 * size**3, bytes_accessed=8 * size * size, transcendentals=0
        ),
    )(gramian)


class Matrices:
    def __init__(self, own):
        self.own = own

    def move(self, outer, inner, sem, k, inward, rows=slice(None), columns=slice(None)):
        if k:
            pairs = [(outer.at[rows, columns], inner.at[rows, columns])]
        else:
            pairs = [
                (outer.at[j, rows], inner.at[rows, pl.ds(j * self.own, self.own)]) for j in range(3)
            ]
        for there, here in pairs:
            src, dst = (there, here) if inward else (here, there)
            pltpu.make_async_copy(src, dst, sem).start()


def whole_of(ref, sem):
    return pltpu.make_async_copy(ref, ref, sem)


def assemble(band, factor_high, factor_low):
    count = factor_high.shape[0] // LANES
    lanes = lambda block: pl.ds((block % count) * LANES, LANES)
    for i in range(count):
        for j in range(count // 2 + 1):
            part = band[lanes(i), lanes(j)]
            spot = (lanes(i), lanes(i + j))
            factor_high[spot], factor_low[spot] = split(part)
            if 0 < j < count // 2:
                spot = (lanes(i + j), lanes(i))
                factor_high[spot], factor_low[spot] = split(part.T)


def update(k, start, factor_high, factor_low, high, low, value):
    spot = pl.ds(pl.multiple_of(start, BLK), BLK)
    q_high, q_low = factor_high[spot, :], factor_low[spot, :]
    if k in COLUMNS:
        polar = dot_of(q_high, high[...], 1, 0) + (
            dot_of(q_high, low[...], 1, 0) + dot_of(q_low, high[...], 1, 0)
        )
        where = (spot, slice(None))
    else:
        polar = dot_of(high[...], q_high, 1, 1) + (
            dot_of(low[...], q_high, 1, 1) + dot_of(high[...], q_low, 1, 1)
        )
        where = (slice(None), spot)
    scale = muon_rate * 0.2 * math.sqrt((3 * D, D, FF, FF)[k])
    value[where] = value[where] * (1.0 - muon_rate * weight_decay) - scale * polar
    return where


def spread_kernel(sub, pieces, norm_ref, q_ref, *refs):
    lines, others, refs = refs[:3], refs[3:7], refs[7:]
    moments, weights, refs = refs[:4], refs[4:8], refs[8:]
    o_ref, carried, fresh, high_outs, low_outs = refs[0], refs[1:5], refs[5:9], refs[9:13], refs[13:17]
    refs = refs[17:]
    pair_bands, factor_high, factor_low = refs[:3]
    staged, values, highs, lows = refs[3:7], refs[7:11], refs[11:15], refs[15:19]
    load_sems, value_sems, out_sems, split_sems, band_sems, sends, arrivals = refs[19:]
    size = q_ref.shape[0]
    half = size // 2
    step = half // pieces
    w, n = lax.axis_index("wide"), lax.axis_index("narrow")
    own = n // sub
    across, near = partner(own, 2), partner(own, 1)
    far = own // 2
    near_place, far_place = place_at("narrow", sub), place_at("narrow", 2 * sub)
    side_place = place_at("wide", 1)
    greet([near_place, far_place, side_place])
    y = w % 2
    rows = lambda side, p: pl.ds(pl.multiple_of(side * half + p * step, 8), step)
    copies = []

    def push(src, dst, place):
        copies.append(send(src, dst, sends, arrivals, len(copies), place))
        return copies[-1]

    crossing = [
        push(q_ref.at[rows(y, p)], o_ref.at[own, rows(y, p)], far_place) for p in range(pieces)
    ]
    landing = [push(q_ref, o_ref.at[own], near_place)]
    keep = pltpu.make_async_copy(q_ref, o_ref.at[own], band_sems.at[0])
    keep.start()
    own_band = pltpu.make_async_copy(q_ref, pair_bands.at[own % 2], band_sems.at[1])
    own_band.start()
    matrices = Matrices(moments[0].shape[2])
    blocks = lax.axis_size("wide")
    for k in range(MATRICES):
        extent = staged[k].shape[0] // 2
        if k >= 2:
            pieces_of = [(y, 0, lines[k - 1])]
            if k == 2:
                pieces_of += [(1 - y, 0, others[1]), (1 - y, extent // 2, others[2])]
            else:
                pieces_of += [(1 - y, 0, others[3])]
            for side, at, source in pieces_of:
                to = pl.multiple_of(side * extent + at, 8)
                spot = staged[k].at[pl.ds(to, source.shape[0]), :]
                pltpu.make_async_copy(source, spot, load_sems.at[k]).start()
        for side, source in ((y, lines[0]), (1 - y, others[0])):
            if k >= 2:
                continue
            share = (staged[0].shape[0] // blocks, staged[1].shape[0] // blocks)
            for b in range(blocks // 2):
                start = b * (share[0] + share[1]) + k * share[0]
                to = pl.multiple_of(side * extent + b * share[k], 8)
                pltpu.make_async_copy(
                    source.at[pl.ds(start, share[k]), :],
                    staged[k].at[pl.ds(to, share[k]), :],
                    load_sems.at[k],
                ).start()
        matrices.move(moments[k], values[k], value_sems.at[k], k, True)
    clip = jnp.minimum(1.0, 1.0 / (norm_ref[0:1, 0:1] + 1e-06))

    def blend_rows(value, stage):
        def one(i, carry):
            spot = slab_at(i)
            value[spot, :] = muon_momentum * value[spot, :] + clip * stage[spot, :]
            return carry

        lax.fori_loop(0, value.shape[0] // SLAB, one, 0, unroll=UNROLL)

    def blend_columns(value, stage):
        def one(i, carry):
            spot = pl.ds(pl.multiple_of(i * LANES, LANES), LANES)
            value[:, spot] = muon_momentum * value[:, spot] + clip * stage[spot, :].T
            return carry

        lax.fori_loop(0, value.shape[1] // LANES, one, 0)

    aside = []

    def forward(p):
        crossing[p].wait_recv()
        spot = o_ref.at[across, rows(y, p)]
        aside.append(push(spot, spot, side_place))
        landing.append(push(spot, spot, near_place))

    def forward_side(p):
        aside[p].wait_recv()
        spot = o_ref.at[across, rows(1 - y, p)]
        landing.append(push(spot, spot, near_place))

    for k in range(MATRICES):
        whole_of(staged[k], load_sems.at[k]).wait()
        whole_of(values[k], value_sems.at[k]).wait()
        blend = blend_columns if k in COLUMNS else blend_rows
        blend(values[k], staged[k])
        matrices.move(carried[k], values[k], out_sems.at[k], k, False)

        def cut(i, carry, k=k):
            highs[k][slab_at(i), :], lows[k][slab_at(i), :] = split(values[k][slab_at(i), :])
            return carry

        lax.fori_loop(0, values[k].shape[0] // SLAB, cut, 0, unroll=UNROLL)

        @pl.when(far != k // 2)
        def _(k=k):
            pltpu.make_async_copy(highs[k], high_outs[k], split_sems.at[2 * k]).start()
            pltpu.make_async_copy(lows[k], low_outs[k], split_sems.at[2 * k + 1]).start()

        if k == 1:
            forward(0)
    for k in range(MATRICES):
        whole_of(values[k], out_sems.at[k]).wait()

        @pl.when(far == k // 2)
        def _(k=k):
            matrices.move(weights[k], values[k], value_sems.at[k], k, True)

    forward(1)
    landing[0].wait_recv()
    near_band = pltpu.make_async_copy(o_ref.at[near], pair_bands.at[1 - own % 2], band_sems.at[2])
    near_band.start()
    own_band.wait()
    near_band.wait()

    def pair(index):
        for side in range(2):

            @pl.when(far == side)
            def _(k=2 * side + index):
                assemble(pair_bands.at[index], factor_high, factor_low)
                whole_of(values[k], value_sems.at[k]).wait()

                def one(i, carry):
                    where = update(
                        k, i * BLK, factor_high, factor_low, highs[k], lows[k], values[k]
                    )
                    matrices.move(fresh[k], values[k], out_sems.at[k], k, False, *where)
                    return carry

                lax.fori_loop(0, size // BLK, one, 0)

    pair(0)
    forward(2)
    forward_side(0)
    pair(1)
    forward_side(1)
    for p in range(3, pieces):
        forward(p)
        forward_side(p - 1)
    forward_side(pieces - 1)
    keep.wait()
    for k in range(MATRICES):

        @pl.when(far == k // 2)
        def _(k=k):
            whole_of(values[k], out_sems.at[k]).wait()

        @pl.when(far != k // 2)
        def _(k=k):
            pltpu.make_async_copy(highs[k], high_outs[k], split_sems.at[2 * k]).wait()
            pltpu.make_async_copy(lows[k], low_outs[k], split_sems.at[2 * k + 1]).wait()

    for copy in landing[1:]:
        copy.wait_recv()
    for copy in copies:
        copy.wait_send()


def spread(norm, band, lines, others, moments, weights, number):
    pieces = 4
    size = band.shape[0]
    slots = 1 + 4 * pieces
    sub = lax.axis_size("narrow") // MATRICES
    vmem = pl.BlockSpec(memory_space=pltpu.VMEM)
    anywhere = pl.BlockSpec(memory_space=pl.ANY)
    operands = [*lines, *others]
    f32 = [jax.ShapeDtypeStruct(moment.shape, jnp.float32) for moment in moments]
    staged = [(moment.size // size, size) for moment in moments]
    flat = [(size, 3 * moments[0].shape[2])] + [moment.shape for moment in moments[1:]]
    low = [jax.ShapeDtypeStruct(shape, jnp.bfloat16) for shape in flat]
    outs = pl.pallas_call(
        functools.partial(spread_kernel, sub, pieces),
        out_shape=tuple(
            [jax.ShapeDtypeStruct((MATRICES,) + band.shape, jnp.float32)] + f32 + f32 + low + low
        ),
        in_specs=[vmem] * 2 + [anywhere] * (len(operands) + 8),
        out_specs=(anywhere,) * 17,
        scratch_shapes=[
            pltpu.VMEM((2,) + band.shape, jnp.float32),
            pltpu.VMEM((size, size), jnp.bfloat16),
            pltpu.VMEM((size, size), jnp.bfloat16),
        ]
        + [pltpu.VMEM(shape, jnp.float32) for shape in staged]
        + [pltpu.VMEM(shape, jnp.float32) for shape in flat]
        + [pltpu.VMEM(shape, jnp.bfloat16) for shape in flat] * 2
        + [pltpu.SemaphoreType.DMA((MATRICES,))] * 3
        + [
            pltpu.SemaphoreType.DMA((2 * MATRICES,)),
            pltpu.SemaphoreType.DMA((3,)),
            pltpu.SemaphoreType.DMA((slots,)),
            pltpu.SemaphoreType.DMA((slots,)),
        ],
        compiler_params=pltpu.CompilerParams(
            collective_id=number, has_side_effects=True, vmem_limit_bytes=58 * 2**20
        ),
        cost_estimate=pl.CostEstimate(
            flops=9 * size * size * size, bytes_accessed=80 * size * size, transcendentals=0
        ),
    )(norm, band, *operands, *moments, *weights)
    return outs[0], outs[1:5], outs[5:9], outs[9:13], outs[13:17]


def finish_kernel(sub, bands_any, *refs):
    ready, fresh, high_ins, low_ins, weights = (refs[4 * i : 4 * i + 4] for i in range(5))
    carried, results, refs = refs[20:24], refs[24:28], refs[28:]
    bands, factor_high, factor_low = refs[:3]
    news, values, highs, lows = refs[3:7], refs[7:11], refs[11:15], refs[15:19]
    news_sems, value_sems, split_sems, band_sems, carried_sems, out_sems = refs[19:]
    size = factor_high.shape[0]
    far = lax.axis_index("narrow") // sub // 2
    matrices = Matrices(weights[0].shape[2])
    for side in range(2):

        @pl.when(far == side)
        def _(side=side):
            for index in range(2):
                k = 2 * (1 - side) + index
                pltpu.make_async_copy(bands_any.at[k], bands.at[index], band_sems.at[index]).start()
                pltpu.make_async_copy(high_ins[k], highs[k], split_sems.at[2 * index]).start()
                pltpu.make_async_copy(low_ins[k], lows[k], split_sems.at[2 * index + 1]).start()
                matrices.move(weights[k], values[k], value_sems.at[k], k, True)
            for k in (2 * side, 2 * side + 1):
                matrices.move(fresh[k], values[k], value_sems.at[k], k, True)

    for k in range(MATRICES):
        matrices.move(ready[k], news[k], news_sems.at[k], k, True)
    for index in range(2):
        whole_of(bands.at[index], band_sems.at[index]).wait()
        for k in range(MATRICES):
            if index == 0:
                whole_of(news[k], news_sems.at[k]).wait()
                matrices.move(carried[k], news[k], carried_sems.at[k], k, False)
        for side in range(2):

            @pl.when(far == side)
            def _(k=2 * (1 - side) + index, done=2 * side + index):
                whole_of(values[done], value_sems.at[done]).wait()
                matrices.move(results[done], values[done], out_sems.at[done], done, False)
                assemble(bands.at[index], factor_high, factor_low)
                whole_of(highs[k], split_sems.at[2 * index]).wait()
                whole_of(lows[k], split_sems.at[2 * index + 1]).wait()
                whole_of(values[k], value_sems.at[k]).wait()

                def one(i, carry):
                    where = update(
                        k, i * BLK, factor_high, factor_low, highs[k], lows[k], values[k]
                    )
                    matrices.move(results[k], values[k], out_sems.at[k], k, False, *where)
                    return carry

                lax.fori_loop(0, size // BLK, one, 0)

    for k in range(MATRICES):
        whole_of(news[k], carried_sems.at[k]).wait()
        whole_of(values[k], out_sems.at[k]).wait()


def finish(bands, ready, fresh, highs, lows, weights):
    size = bands.shape[1]
    sub = lax.axis_size("narrow") // MATRICES
    anywhere = pl.BlockSpec(memory_space=pl.ANY)
    shapes = [jax.ShapeDtypeStruct(weight.shape, jnp.float32) for weight in weights]
    flat = [(size, 3 * weights[0].shape[2])] + [weight.shape for weight in weights[1:]]
    outs = pl.pallas_call(
        functools.partial(finish_kernel, sub),
        out_shape=tuple(shapes + shapes),
        in_specs=[anywhere] * 21,
        out_specs=(anywhere,) * 8,
        scratch_shapes=[
            pltpu.VMEM((2,) + bands.shape[1:], jnp.float32),
            pltpu.VMEM((size, size), jnp.bfloat16),
            pltpu.VMEM((size, size), jnp.bfloat16),
        ]
        + [pltpu.VMEM(shape, jnp.float32) for shape in flat] * 2
        + [pltpu.VMEM(shape, jnp.bfloat16) for shape in flat] * 2
        + [pltpu.SemaphoreType.DMA((MATRICES,))] * 6,
        compiler_params=pltpu.CompilerParams(vmem_limit_bytes=58 * 2**20),
        cost_estimate=pl.CostEstimate(
            flops=9 * size * size * size, bytes_accessed=60 * size * size, transcendentals=0
        ),
    )(bands, *ready, *fresh, *highs, *lows, *weights)
    return outs[:4], outs[4:]


def adam_update(weight, moment, square, gradient):
    moment_new = first_decay * moment + (1.0 - first_decay) * gradient
    square_new = second_decay * square + (1.0 - second_decay) * gradient * gradient
    moment_hat = moment_new / (1.0 - first_decay**STEP)
    square_hat = square_new / (1.0 - second_decay**STEP)
    weight_new = weight * (1.0 - adam_rate * weight_decay) - adam_rate * moment_hat / (
        jnp.sqrt(square_hat) + 1e-08
    )
    return (moment_new, square_new, weight_new)


def column_shifts(strip, column):
    rows = strip.shape[0]
    left = jnp.where(column == 0, 0.0, pltpu.roll(strip, 1, 0))
    right = jnp.where(column == rows - 1, 0.0, pltpu.roll(strip, rows - 1, 0))
    return (left, strip, right)


def tap_rows(shifts, taps):
    return [
        taps[3 * i] * shifts[0] + taps[3 * i + 1] * shifts[1] + taps[3 * i + 2] * shifts[2]
        for i in range(3)
    ]


def strip_at(index):
    return pl.ds(pl.multiple_of(index * GRID, GRID), GRID)


def convolve(load, taps, emit):
    shape = load(0).shape
    column = lax.broadcasted_iota(jnp.int32, shape, 0)

    def one(r, carry):
        above, here = carry
        upper, middle, lower = tap_rows(column_shifts(load(r), column), taps)
        emit(r - 1, here + lower)
        return (upper, above + middle)

    upper, middle, _ = tap_rows(column_shifts(load(0), column), taps)
    above, here = lax.fori_loop(1, GRID, one, (upper, middle))
    emit(GRID - 1, here)


def kernel_sums(load, weigh, width):
    column = lax.broadcasted_iota(jnp.int32, (GRID, width), 0)
    fold = lambda values: values.reshape(GRID // 8, 8, width).sum(axis=0)
    zero = jnp.zeros((8, width), jnp.float32)

    def one(r, carry):
        sums = carry
        shifts = column_shifts(load(r), column)
        later = weigh(jnp.minimum(r + 1, GRID - 1)) * jnp.where(r < GRID - 1, 1.0, 0.0)
        earlier = weigh(jnp.maximum(r - 1, 0)) * jnp.where(r > 0, 1.0, 0.0)
        terms = (later, weigh(r), earlier)
        return tuple(
            sums[3 * i + j] + fold(terms[i] * shifts[j]) for i in range(3) for j in range(3)
        )

    return lax.fori_loop(0, GRID, one, (zero,) * 9)


def middle_kernel(
    pieces,
    entry_ref,
    cotangent_ref,
    live_ref,
    gate_ref,
    expand_any,
    reduce_any,
    taps_ref,
    ffn_half_ref,
    grad_entry_any,
    reduce_share,
    expand_hold,
    expand_give,
    grad_taps_ref,
    expand_full,
    reduce_full,
    grad_ffn,
    upward,
    weight,
    active,
    grad_up,
    ffn,
    back,
    grad_reduce,
    grad_expand,
    ffn_inbox,
    near,
    far,
    held,
    local,
    reduce_held,
    reduce_beside,
    reduce_inbox,
    reduce_loads,
    expand_held,
    expand_beside,
    expand_inbox,
    expand_loads,
    give_sems,
    weight_sems,
    sends,
    arrivals,
):
    units = expand_any.shape[1]
    block = min(BLK, units // 2)
    steps = units // block
    groups = steps // 2
    y, z = wide_parts()
    count = lax.axis_size("wide") // 2
    far_bits = bits_of(lax.axis_size("narrow"))[1:]
    greet(
        [place_at("narrow", bit) for bit in [1] + far_bits]
        + [place_at("wide", bit) for bit in bits_of(lax.axis_size("wide"))]
    )

    def block_index(step):
        side = 1 - y if step < groups else y
        return side * groups + line_partner(z // (count // groups), groups - 1 - step % groups)

    fetches = []
    for step in range(steps):
        spot = pl.ds(pl.multiple_of(block_index(step) * block, LANES), block)
        pair = (
            pltpu.make_async_copy(
                expand_any.at[:, spot], expand_full.at[:, spot], weight_sems.at[step]
            ),
            pltpu.make_async_copy(
                reduce_any.at[spot, :], reduce_full.at[spot, :], weight_sems.at[steps + step]
            ),
        )
        for copy in pair:
            copy.start()
        fetches.append(pair)
    gate, live = gate_ref[...], live_ref[...]

    def gated(i, carry):
        spot = slab_at(i)
        result = cotangent_ref[spot, :].astype(jnp.float32) * live
        grad_ffn[spot, :] = (gate * result).astype(jnp.bfloat16)
        return carry

    lax.fori_loop(0, grad_ffn.shape[0] // SLAB, gated, 0, unroll=UNROLL)

    def work(spot, fresh):
        expand_low = expand_full[:, spot].astype(jnp.bfloat16)
        reduce_low = reduce_full[spot, :].astype(jnp.bfloat16)
        taps = [taps_ref[t : t + 1, spot] for t in range(9)]
        upward[...] = dot_of(entry_ref[...], expand_low, 1, 0)
        weight[...] = dot_of(grad_ffn[...], reduce_low, 1, 1)

        def emit_middle(r, values):
            inner = gelu_slope * (values + gelu_cubic * values * values * values)
            bent = jnp.tanh(inner)
            active[strip_at(r), :] = (0.5 * values * (1.0 + bent)).astype(jnp.bfloat16)
            turn = 0.5 * (1.0 + bent) + 0.5 * values * (1.0 - bent * bent) * (
                gelu_slope * (1.0 + 3.0 * gelu_cubic * values * values)
            )
            weight[strip_at(r), :] = weight[strip_at(r), :] * turn

        convolve(lambda r: upward[strip_at(r), :], taps, emit_middle)

        def emit_grad(r, values):
            grad_up[strip_at(r), :] = values.astype(jnp.bfloat16)

        convolve(lambda r: weight[strip_at(r), :], taps[::-1], emit_grad)
        sums = kernel_sums(
            lambda r: upward[strip_at(r), :], lambda r: weight[strip_at(r), :], block
        )
        for t in range(9):
            grad_taps_ref[t : t + 1, spot] = jnp.sum(sums[t], axis=0, keepdims=True)
        grad_reduce[spot, :] = dot_of(active[...], grad_ffn[...], 0, 0)
        grad_expand[spot, :] = dot_of(grad_up[...], entry_ref[...], 0, 0)
        if fresh:
            ffn[...] = dot_of(active[...], reduce_low, 1, 0)
            back[...] = dot_of(grad_up[...], expand_low, 1, 1)
        else:
            ffn[...] += dot_of(active[...], reduce_low, 1, 0)
            back[...] += dot_of(grad_up[...], expand_low, 1, 1)

    base = (len(far_bits) + 2) * pieces + 1
    reduce_sum = Scatter(
        grad_reduce, reduce_held, reduce_beside, reduce_inbox, sends, arrivals, reduce_loads, base
    )
    expand_sum = Scatter(
        grad_expand,
        expand_held,
        expand_beside,
        expand_inbox,
        sends,
        arrivals,
        expand_loads,
        base + Scatter.slots(),
    )
    for step in range(groups):
        for copy in fetches[step]:
            copy.wait()
        work(pl.ds(pl.multiple_of(block_index(step) * block, LANES), block), step == 0)
        size = count // groups
        ready = [(groups - 1 - step) * size + e for e in reversed(range(size))]
        for scatter in (reduce_sum, expand_sum):
            for e in ready:
                if scatter is reduce_sum or e >= count // 2:
                    scatter.give(e)
    for step in range(groups, steps):
        for copy in fetches[step]:
            copy.wait()

    def later(i, carry):
        side_block = line_partner_of(z // (count // groups), i, groups)
        work(pl.ds(pl.multiple_of((y * groups + side_block) * block, LANES), block), False)
        return carry

    lax.fori_loop(0, groups, later, 0)
    narrow = NarrowSum(
        far_bits, pieces, back, grad_entry_any, near, far, held, sends, arrivals, local, 0
    )
    narrow.start()
    core = lax.axis_index("narrow") % 2
    half = ffn.shape[0] // 2
    side_rows = lambda side: pl.ds(pl.multiple_of(side * half, 8), half)
    ffn_copy = send(
        ffn.at[side_rows(1 - core)], ffn_inbox, sends, arrivals, base - 1, place_at("narrow", 1)
    )
    for scatter in (reduce_sum, expand_sum):
        scatter.load()
    for p in range(pieces):
        narrow.begin(p)
    left = [list(reversed(range(count))), list(reversed(range(count // 2, count)))]
    gives = []
    for e in range(count // 2):
        gives.append(
            pltpu.make_async_copy(
                block_of(grad_expand, 1 - y, line_partner(z, e)), expand_give.at[e], give_sems.at[e]
            )
        )
        gives[e].start()
    scatters = (reduce_sum, expand_sum)
    scatters[0].step(left[0].pop(0))
    scatters[1].step(left[1].pop(0))
    ffn_copy.wait_recv()
    ffn_half_ref[...] = ffn[side_rows(core), :] + ffn_inbox[...]
    turns = [0, 1, 0]
    for b in range(len(far_bits)):
        for p in range(pieces):
            narrow.step(b, p)
            if turns and len(left[turns[0]]) > (turns[0] == 0):
                which = turns.pop(0)
                scatters[which].step(left[which].pop(0))
    for which in range(2):
        while left[which]:
            scatters[which].step(left[which].pop(0))
    for e in range(count // 2):
        expand_sum.loads[e].wait()
    expand_sum.copies[("z", count // 2)].wait_recv()
    expand_held[0] = expand_held[0] + expand_inbox[count // 2 - 1]
    outs = [
        pltpu.make_async_copy(reduce_held.at[0], reduce_share, reduce_loads.at[0]),
        pltpu.make_async_copy(
            expand_held.at[pl.ds(0, count // 2)], expand_hold, expand_loads.at[0]
        ),
    ]
    for out in outs:
        out.start()
    outs += gives
    narrow.finish()
    ffn_copy.wait_send()
    for scatter in scatters:
        scatter.finish()
    for out in outs:
        out.wait()


def line_partner_of(place, index, count):
    flipped = 0 * place
    for bit in bits_of(count):
        one, two = (place // bit) % 2, (index // bit) % 2
        flipped = flipped + (one + two - 2 * one * two) * bit
    return flipped


def middle(entry, cotangent, live, gate, expand, reduce, taps, number):
    tokens, width = entry.shape
    units = expand.shape[1]
    block = min(BLK, units // 2)
    steps = units // block
    pieces = 4
    narrow_bits = bits_of(lax.axis_size("narrow"))
    slots = (len(narrow_bits) + 1) * pieces + 1 + 2 * Scatter.slots()
    vmem = pl.BlockSpec(memory_space=pltpu.VMEM)
    anywhere = pl.BlockSpec(memory_space=pl.ANY)
    f32 = lambda *shape: jax.ShapeDtypeStruct(shape, jnp.float32)
    wide = lambda *shape: pltpu.VMEM(shape, jnp.float32)
    low = lambda *shape: pltpu.VMEM(shape, jnp.bfloat16)
    share = block_shape((units, width))
    line = lax.axis_size("wide") // 2
    return pl.pallas_call(
        functools.partial(middle_kernel, pieces),
        out_shape=(
            f32(tokens // 2, width),
            f32(tokens, width),
            f32(*share),
            f32(line // 2, *share),
            f32(line // 2, *share),
            f32(9, units),
        ),
        in_specs=[vmem, vmem, vmem, vmem, anywhere, anywhere, vmem],
        out_specs=(vmem,) + (anywhere,) * 4 + (vmem,),
        scratch_shapes=[
            wide(width, units),
            wide(units, width),
            low(tokens, width),
            wide(tokens, block),
            wide(tokens, block),
            low(tokens, block),
            low(tokens, block),
            wide(tokens, width),
            wide(tokens, width),
            wide(units, width),
            wide(units, width),
            wide(tokens // 2, width),
        ]
        + narrow_scratch((tokens, width), pieces)
        + scatter_scratch((units, width)) * 2
        + [
            pltpu.SemaphoreType.DMA((line // 2,)),
            pltpu.SemaphoreType.DMA((2 * steps,)),
            pltpu.SemaphoreType.DMA((slots,)),
            pltpu.SemaphoreType.DMA((slots,)),
        ],
        compiler_params=pltpu.CompilerParams(
            collective_id=number, has_side_effects=True, vmem_limit_bytes=60 * 2**20
        ),
        cost_estimate=pl.CostEstimate(
            flops=12 * tokens * width * units,
            bytes_accessed=200 * tokens * width,
            transcendentals=tokens * units,
        ),
    )(entry, cotangent, live, gate, expand, reduce, taps)


def norm_strip(values):
    average = jnp.mean(values, axis=-1, keepdims=True)
    centred = values - average
    spread_of = jnp.mean(centred * centred, axis=-1, keepdims=True)
    inverse = lax.rsqrt(spread_of + 1e-06)
    return centred * inverse, inverse


def slab_at(index):
    return pl.ds(pl.multiple_of(index * SLAB, SLAB), SLAB)


def fold_rows(values):
    return values.reshape(values.shape[0] // 8, 8, values.shape[1]).sum(axis=0)


def mixer_kernel_forward(tokens_ref, shift_ref, scale_ref, taps_ref, out_ref, entered):
    stretch = 1.0 + scale_ref[...]
    offset = shift_ref[...]

    def enter(r, carry):
        normed, _ = norm_strip(tokens_ref[slab_at(r), :].astype(jnp.float32))
        entered[slab_at(r), :] = normed * stretch + offset
        return carry

    rows, width = tokens_ref.shape
    lax.fori_loop(0, rows // SLAB, enter, 0, unroll=UNROLL)
    for start in range(0, width, BLK):
        lanes = pl.ds(start, BLK)

        def emit(r, values, lanes=lanes):
            out_ref[strip_at(r), lanes] = values.astype(jnp.bfloat16)

        taps = [taps_ref[t : t + 1, lanes] for t in range(9)]
        convolve(lambda r, lanes=lanes: entered[strip_at(r), lanes], taps, emit)


def mixer_forward(tokens, shift, scale, taps):
    rows, width = tokens.shape
    vmem = pl.BlockSpec(memory_space=pltpu.VMEM)
    return pl.pallas_call(
        mixer_kernel_forward,
        out_shape=jax.ShapeDtypeStruct((rows, width), jnp.bfloat16),
        in_specs=[vmem] * 4,
        out_specs=vmem,
        scratch_shapes=[pltpu.VMEM((rows, width), jnp.float32)],
        compiler_params=pltpu.CompilerParams(vmem_limit_bytes=40 * 2**20),
        cost_estimate=pl.CostEstimate(
            flops=40 * rows * width, bytes_accessed=4 * rows * width, transcendentals=0
        ),
    )(tokens, shift, scale, taps)


def mixer_kernel_backward(
    tokens_ref,
    shift_ref,
    scale_ref,
    taps_ref,
    grad_mixed_ref,
    grad_hidden_ref,
    out_ref,
    grad_taps_ref,
    grad_shift_ref,
    grad_scale_ref,
    normed_ref,
    back_ref,
    inverse_ref,
    wait_tokens,
    wait_mixed,
    wait_hidden,
):
    width = tokens_ref.shape[1]
    stretch = 1.0 + scale_ref[...]
    wait_tokens()

    def enter(r, carry):
        normed, inverse = norm_strip(tokens_ref[slab_at(r), :].astype(jnp.float32))
        normed_ref[slab_at(r), :] = normed
        inverse_ref[slab_at(r), :] = jnp.broadcast_to(inverse, (SLAB, LANES))
        return carry

    rows = tokens_ref.shape[0]
    lax.fori_loop(0, rows // SLAB, enter, 0, unroll=UNROLL)
    wait_mixed()
    for start in range(0, width, BLK):
        lanes = pl.ds(start, BLK)
        taps = [taps_ref[t : t + 1, lanes] for t in range(9)]
        stretch_part = 1.0 + scale_ref[:, lanes]
        offset_part = shift_ref[:, lanes]

        def emit(r, values, lanes=lanes):
            back_ref[strip_at(r), lanes] = values

        def entered(r, lanes=lanes, stretch_part=stretch_part, offset_part=offset_part):
            return normed_ref[strip_at(r), lanes] * stretch_part + offset_part

        weigh = lambda r, lanes=lanes: grad_mixed_ref[strip_at(r), lanes]
        convolve(weigh, taps[::-1], emit)
        sums = kernel_sums(entered, weigh, BLK)
        for t in range(9):
            grad_taps_ref[t : t + 1, lanes] = jnp.sum(sums[t], axis=0, keepdims=True)

    def leave(r, carry):
        shifts, scales = carry
        normed = normed_ref[slab_at(r), :]
        back = back_ref[slab_at(r), :]
        stretched = back * stretch
        first = jnp.mean(stretched, axis=-1, keepdims=True)
        second = jnp.mean(stretched * normed, axis=-1, keepdims=True)
        inverse = inverse_ref[slab_at(r), :][:, :1]
        out = grad_hidden_ref[slab_at(r), :] + (stretched - first - normed * second) * inverse
        out_ref[slab_at(r), :] = out.astype(jnp.bfloat16)
        return shifts + fold_rows(back), scales + fold_rows(back * normed)

    wait_hidden()
    zero = jnp.zeros((8, width), jnp.float32)
    shifts, scales = lax.fori_loop(0, rows // SLAB, leave, (zero, zero), unroll=UNROLL)
    grad_shift_ref[...] = jnp.sum(shifts, axis=0, keepdims=True)
    grad_scale_ref[...] = jnp.sum(scales, axis=0, keepdims=True)


def dot_of(left, right, left_axis, right_axis):
    return lax.dot_general(
        left,
        right,
        (((left_axis,), (right_axis,)), ((), ())),
        preferred_element_type=jnp.float32,
    )


def head_only(values, head):
    lane = lax.broadcasted_iota(jnp.int32, values.shape, 1)
    return jnp.where(lane // HEAD == head, values, jnp.zeros_like(values))


def attend_kernel(
    mixed_ref, attend_ref, triple_ref, context_ref, logsum_ref, low_ref, turned, values_t
):
    tokens = mixed_ref.shape[0]
    width = context_ref.shape[1]
    for j in range(3):
        columns = pl.ds(j * width, width)
        low_ref[:, columns] = attend_ref[j].astype(jnp.bfloat16)
        triple_ref[:, columns] = dot_of(mixed_ref[...], low_ref[:, columns], 1, 0).astype(
            jnp.bfloat16
        )
    values_t[...] = triple_ref[:, pl.ds(2 * width, width)].T
    scale = jnp.bfloat16(HEAD ** (-0.5))
    for head in range(width // HEAD):
        pair = head * HEAD // LANES * LANES
        inside = head % (LANES // HEAD)

        def one(block, carry, head=head, pair=pair, inside=inside):
            spot = pl.ds(pl.multiple_of(block * QUERIES, QUERIES), QUERIES)
            queries = head_only(triple_ref[spot, pl.ds(pair, LANES)], inside) * scale
            scores = dot_of(triple_ref[:, pl.ds(width + pair, LANES)], queries, 1, 1)
            peak = jnp.max(scores, axis=0, keepdims=True)
            weights = jnp.exp(scores - peak)
            total = jnp.sum(weights, axis=0, keepdims=True)
            soft_low = (weights * (1.0 / total)).astype(jnp.bfloat16)
            turned[pl.ds(head * HEAD, HEAD), spot] = dot_of(
                values_t[pl.ds(head * HEAD, HEAD), :], soft_low, 1, 0
            )
            logsum_ref[pl.ds(head, 1), spot] = peak + jnp.log(total)
            return carry

        lax.fori_loop(0, tokens // QUERIES, one, 0)
    context_ref[...] = turned[...].T.astype(jnp.bfloat16)


def attend(mixed, attend_weight):
    tokens, width = mixed.shape
    own = attend_weight.shape[2]
    vmem = pl.BlockSpec(memory_space=pltpu.VMEM)
    return pl.pallas_call(
        attend_kernel,
        out_shape=(
            jax.ShapeDtypeStruct((tokens, 3 * own), jnp.bfloat16),
            jax.ShapeDtypeStruct((tokens, own), jnp.bfloat16),
            jax.ShapeDtypeStruct((8, tokens), jnp.float32),
            jax.ShapeDtypeStruct((width, 3 * own), jnp.bfloat16),
        ),
        in_specs=[vmem] * 2,
        out_specs=(vmem,) * 4,
        scratch_shapes=[
            pltpu.VMEM((own, tokens), jnp.float32),
            pltpu.VMEM((own, tokens), jnp.bfloat16),
        ],
        compiler_params=pltpu.CompilerParams(vmem_limit_bytes=40 * 2**20),
        cost_estimate=pl.CostEstimate(
            flops=16 * tokens * tokens * own,
            bytes_accessed=12 * tokens * width,
            transcendentals=tokens * tokens * own // HEAD,
        ),
    )(mixed, attend_weight)


def narrow_hops():
    return [("narrow", bit) for bit in reversed(bits_of(lax.axis_size("narrow")))]


def narrow_position(item):
    n = lax.axis_index("narrow")
    position = 0
    for index, (_, bit) in enumerate(narrow_hops()):
        value = (n // bit) % 2
        if (item >> index) % 2:
            value = 1 - value
        position = position + value * 2**index
    return position


def entry_kernel(
    pieces,
    context_ref,
    tokens_ref,
    output_ref,
    gate_ref,
    shift_ref,
    scale_ref,
    branch_ref,
    hidden_ref,
    entry_ref,
    slots,
    output_low,
    output_inbox,
    sends,
    arrivals,
):
    rows, own = context_ref.shape
    step = rows // pieces
    hops = narrow_hops()
    count = 2 ** len(hops)
    greet([place_at(axis, bit) for axis, bit in hops])
    chunk = lambda p: pl.ds(p * step, step)
    slots[narrow_position(0)] = context_ref[...].astype(jnp.float32)
    output_copy = send(
        output_ref, output_inbox, sends, arrivals, pieces * (count - 1), place_at("narrow", 1)
    )
    gathers = []
    for p in range(pieces):
        spot_of = lambda item, p=p: slots.at[narrow_position(item), chunk(p)]
        gathers.append(Gather(spot_of(0), spot_of, hops, sends, arrivals, p * (count - 1)))
        gathers[p].step(0)
    core = lax.axis_index("narrow") % 2
    half = output_ref.shape[0]
    output_low[pl.ds(pl.multiple_of(core * half, SLAB), half), :] = output_ref[...].astype(
        jnp.bfloat16
    )
    output_copy.wait_recv()
    output_low[pl.ds(pl.multiple_of((1 - core) * half, SLAB), half), :] = output_inbox[...].astype(
        jnp.bfloat16
    )
    gate, offset, stretch = gate_ref[...], shift_ref[...], 1.0 + scale_ref[...]
    for p in range(pieces):
        for item in gathers[p].order[1:]:
            gathers[p].step(item)
        branch = jnp.zeros((step, output_ref.shape[1]), jnp.float32)
        for position in range(count):
            branch = branch + dot_of(
                slots[position, chunk(p)].astype(jnp.bfloat16),
                output_low[pl.ds(position * own, own), :],
                1,
                0,
            )
        branch_ref[chunk(p), :] = branch

        def one(i, carry, p=p):
            spot = pl.ds(pl.multiple_of(p * step + i * SLAB, SLAB), SLAB)
            hidden = tokens_ref[spot, :].astype(jnp.float32) + gate * branch_ref[spot, :]
            hidden_ref[spot, :] = hidden
            normed, _ = norm_strip(hidden)
            entry_ref[spot, :] = (normed * stretch + offset).astype(jnp.bfloat16)
            return carry

        lax.fori_loop(0, step // SLAB, one, 0, unroll=UNROLL)
    for gather in gathers:
        gather.finish()
    output_copy.wait_send()


def enter(context, tokens, output_rows, gate, shift, scale, number):
    pieces = 4
    rows, own = context.shape
    width = tokens.shape[1]
    count = lax.axis_size("narrow")
    vmem = pl.BlockSpec(memory_space=pltpu.VMEM)
    slots = pieces * (count - 1) + 1
    return pl.pallas_call(
        functools.partial(entry_kernel, pieces),
        out_shape=(
            jax.ShapeDtypeStruct((rows, width), jnp.float32),
            jax.ShapeDtypeStruct((rows, width), jnp.float32),
            jax.ShapeDtypeStruct((rows, width), jnp.bfloat16),
        ),
        in_specs=[vmem] * 6,
        out_specs=(vmem,) * 3,
        scratch_shapes=[
            pltpu.VMEM((count, rows, own), jnp.float32),
            pltpu.VMEM((width, width), jnp.bfloat16),
            pltpu.VMEM(output_rows.shape, jnp.float32),
            pltpu.SemaphoreType.DMA((slots,)),
            pltpu.SemaphoreType.DMA((slots,)),
        ],
        compiler_params=pltpu.CompilerParams(
            collective_id=number, has_side_effects=True, vmem_limit_bytes=40 * 2**20
        ),
        cost_estimate=pl.CostEstimate(
            flops=2 * rows * width * width, bytes_accessed=100 * rows * width, transcendentals=0
        ),
    )(context, tokens, output_rows, gate, shift, scale)


def all_rows(values):
    for _, bit in narrow_hops()[:-1]:
        side = (lax.axis_index("narrow") // bit) % 2
        other = permute(values, "narrow", bit)
        values = jnp.where(
            side == 0,
            jnp.concatenate([values, other], axis=0),
            jnp.concatenate([other, values], axis=0),
        )
    return values


def back_kernel(
    pieces,
    hidden_any,
    branch_any,
    grad_entry_any,
    cotangent_any,
    live_ref,
    scale_ref,
    gate_ref,
    mixed_ref,
    attend_ref,
    output_ref,
    triple_ref,
    context_ref,
    logsum_ref,
    reduce_share_ref,
    expand_hold,
    expand_give,
    grad_hidden_ref,
    grad_shift_ref,
    grad_scale_ref,
    grad_gate_ref,
    grad_mixed_any,
    attend_out_share,
    reduce_line,
    expand_line,
    expand_share,
    hidden,
    branch,
    grad_entry,
    cotangent,
    grad_branch,
    output_low,
    grad_context,
    keys_t,
    grad_queries_t,
    grad_keys,
    grad_values,
    grad_triple,
    near,
    far,
    held,
    local,
    scatter_held,
    scatter_beside,
    scatter_inbox,
    scatter_loads,
    rest_held,
    rest_beside,
    rest_inbox,
    rest_loads,
    load_sems,
    keep_sems,
    sends,
    arrivals,
):
    tokens, width = hidden.shape
    own = output_ref.shape[0]
    _, z = wide_parts()
    far_bits = bits_of(lax.axis_size("narrow"))[1:]
    greet(
        [place_at("narrow", bit) for bit in [1] + far_bits]
        + [place_at("wide", bit) for bit in bits_of(lax.axis_size("wide"))]
    )
    hops = line_hops()
    base = (len(far_bits) + 2) * pieces + Scatter.slots()

    def spot_in(line):
        def spot_of(item):
            spot = z
            for index, (_, bit) in enumerate(hops):
                if (item >> index) % 2:
                    spot = partner(spot, bit // 2)
            return line_block(line, spot)

        return spot_of

    gathers, keeps = [], []
    rest_base = base + 2 * (2 ** len(hops) - 1)
    rest = Scatter(
        None, rest_held, rest_beside, rest_inbox, sends, arrivals, rest_loads, rest_base,
        (expand_hold, expand_give),
    )
    rest.start()
    for index, (share, line) in enumerate(
        ((reduce_share_ref, reduce_line), (rest_held.at[0], expand_line))
    ):
        start = base + index * (2 ** len(hops) - 1)
        gathers.append(Gather(share, spot_in(line), hops, sends, arrivals, start))
        keeps.append(pltpu.make_async_copy(share, spot_in(line)(0), keep_sems.at[index]))
    gathers[0].step(0)
    keeps[0].start()
    step = tokens // pieces
    loads = []
    for p in range(pieces):
        spot = pl.ds(p * step, step)
        pairs = (
            (hidden_any, hidden),
            (branch_any, branch),
            (grad_entry_any, grad_entry),
            (cotangent_any, cotangent),
        )
        loads.append(
            [
                pltpu.make_async_copy(src.at[spot, :], dst.at[spot, :], load_sems.at[4 * p + i])
                for i, (src, dst) in enumerate(pairs)
            ]
        )
        for load in loads[p]:
            load.start()
    output_low[...] = output_ref[...].astype(jnp.bfloat16)
    stretch, gate, live = 1.0 + scale_ref[...], gate_ref[...], live_ref[...]

    def one_slab(r, carry):
        shifts, scales, gates = carry
        spot = slab_at(r)
        normed, inverse = norm_strip(hidden[spot, :])
        back = grad_entry[spot, :]
        stretched = back * stretch
        first = jnp.mean(stretched, axis=-1, keepdims=True)
        second = jnp.mean(stretched * normed, axis=-1, keepdims=True)
        grad = cotangent[spot, :].astype(jnp.float32) * live + (
            stretched - first - normed * second
        ) * inverse
        grad_hidden_ref[spot, :] = grad
        grad_branch[spot, :] = (gate * grad).astype(jnp.bfloat16)
        return (
            shifts + fold_rows(back),
            scales + fold_rows(back * normed),
            gates + fold_rows(branch[spot, :] * grad),
        )

    sums = (jnp.zeros((8, width), jnp.float32),) * 3
    for p in range(pieces):
        for load in loads[p]:
            load.wait()
        first_slab = p * step // SLAB
        sums = lax.fori_loop(
            first_slab, first_slab + step // SLAB, one_slab, sums, unroll=UNROLL
        )
    for ref, total in zip((grad_shift_ref, grad_scale_ref, grad_gate_ref), sums):
        ref[...] = jnp.sum(total, axis=0, keepdims=True)
    for e in reversed(range(1, rest.count)):
        rest.step(e)
    grad_context[...] = dot_of(grad_branch[...], output_low[...], 1, 1).astype(jnp.bfloat16)
    keys_t[...] = triple_ref[:, pl.ds(own, own)].T
    grad_keys[...] = jnp.zeros_like(grad_keys)
    grad_values[...] = jnp.zeros_like(grad_values)
    scale = HEAD ** (-0.5)
    low_scale = jnp.bfloat16(scale)
    heads = own // HEAD
    for head in range(heads):
        pair = head * HEAD // LANES * LANES
        inside = head % (LANES // HEAD)
        lanes = pl.ds(pair, LANES)

        def one(block, carry, head=head, pair=pair, inside=inside, lanes=lanes):
            spot = pl.ds(pl.multiple_of(block * QUERIES, QUERIES), QUERIES)
            queries = head_only(triple_ref[spot, lanes], inside)
            back = head_only(grad_context[spot, lanes], inside)
            scores = dot_of(triple_ref[:, pl.ds(own + pair, LANES)], queries * low_scale, 1, 1)
            weights = jnp.exp(scores - logsum_ref[pl.ds(head, 1), spot])
            grad_weights = dot_of(triple_ref[:, pl.ds(2 * own + pair, LANES)], back, 1, 1)
            grad_values[:, lanes] += dot_of(weights.astype(jnp.bfloat16), back, 1, 0)
            inner = jnp.sum(weights * grad_weights, axis=0, keepdims=True)
            grad_low = (weights * (grad_weights - inner)).astype(jnp.bfloat16)
            grad_keys[:, lanes] += dot_of(grad_low, queries, 1, 0)
            grad_queries_t[pl.ds(head * HEAD, HEAD), spot] = dot_of(
                keys_t[pl.ds(head * HEAD, HEAD), :], grad_low, 1, 0
            )
            return carry

        lax.fori_loop(0, tokens // QUERIES, one, 0)
        if head == max(heads - 2, 0):
            gathers[0].step(1)
            rest.step(0)
            gathers[1].step(0)
            keeps[1].start()
            keeps.append(pltpu.make_async_copy(rest_held.at[0], expand_share, keep_sems.at[2]))
            keeps[2].start()
    grad_triple[:, pl.ds(0, own)] = (grad_queries_t[...].T * scale).astype(jnp.bfloat16)
    grad_triple[:, pl.ds(own, own)] = (grad_keys[...] * scale).astype(jnp.bfloat16)
    grad_triple[:, pl.ds(2 * own, own)] = grad_values[...].astype(jnp.bfloat16)
    mixed_partial, attend_out = grad_entry, branch.at[pl.ds(0, 4 * own), :]
    mixed_partial[...] = dot_of(grad_triple[...], attend_ref[...], 1, 1)
    narrow = NarrowSum(
        far_bits, pieces, mixed_partial, grad_mixed_any, near, far, held, sends, arrivals, local, 0
    )
    narrow.start()
    grad_attend = dot_of(grad_triple[...], mixed_ref[...], 0, 0)
    grad_output = dot_of(context_ref[...], grad_branch[...], 0, 0)
    blocks = lax.axis_size("wide")
    first, second = 3 * own // blocks, own // blocks
    for b in range(blocks):
        start = b * (first + second)
        attend_out[pl.ds(start, first), :] = grad_attend[b * first : (b + 1) * first]
        attend_out[pl.ds(start + first, second), :] = grad_output[b * second : (b + 1) * second]
    scatter = Scatter(
        attend_out,
        scatter_held,
        scatter_beside,
        scatter_inbox,
        sends,
        arrivals,
        scatter_loads,
        (len(far_bits) + 2) * pieces,
    )
    for p in range(pieces):
        narrow.begin(p)
    scatter.start()
    left = list(reversed(range(blocks // 2)))
    forwards = [(0, item) for item in gathers[0].order[2:]] + [
        (1, item) for item in gathers[1].order[1:]
    ]
    urgent = [(1, 1)]
    for b in range(len(far_bits)):
        for p in range(pieces):
            narrow.step(b, p)
            if urgent:
                index, item = urgent.pop(0)
                gathers[index].step(item)
            if len(left) > 1:
                scatter.step(left.pop(0))
    for index, item in forwards:
        if (index, item) != (1, 1):
            gathers[index].step(item)
    while left:
        scatter.step(left.pop(0))
    out = pltpu.make_async_copy(scatter.held.at[0], attend_out_share, scatter.local.at[0])
    out.start()
    narrow.finish()
    scatter.finish()
    rest.finish()
    for gather in gathers:
        gather.finish()
    for keep in keeps:
        keep.wait()
    out.wait()


def back(
    hidden,
    branch,
    grad_entry,
    cotangent,
    live,
    scale,
    gate,
    mixed,
    attend_low,
    output_weight,
    triple,
    context,
    logsum,
    reduce_share,
    expand_hold,
    expand_give,
    number,
):
    tokens, width = hidden.shape
    own = output_weight.shape[0]
    pieces = 4
    line = lax.axis_size("wide") // 2
    narrow_bits = bits_of(lax.axis_size("narrow"))
    slots = (len(narrow_bits) + 1) * pieces + Scatter.slots() + 2 * (line - 1) + line - 1
    block = reduce_share.shape
    vmem = pl.BlockSpec(memory_space=pltpu.VMEM)
    anywhere = pl.BlockSpec(memory_space=pl.ANY)
    f32 = lambda *shape: jax.ShapeDtypeStruct(shape, jnp.float32)
    wide = lambda *shape: pltpu.VMEM(shape, jnp.float32)
    low = lambda *shape: pltpu.VMEM(shape, jnp.bfloat16)
    return pl.pallas_call(
        functools.partial(back_kernel, pieces),
        out_shape=(
            f32(tokens, width),
            f32(1, width),
            f32(1, width),
            f32(1, width),
            f32(tokens, width),
            f32(4 * own // (2 * line), width),
            f32(line * reduce_share.shape[0], width),
            f32(line * reduce_share.shape[0], width),
            f32(*block),
        ),
        in_specs=[anywhere] * 4 + [vmem] * 10 + [anywhere] * 2,
        out_specs=(vmem,) * 4 + (anywhere,) * 5,
        scratch_shapes=[
            wide(tokens, width),
            wide(max(tokens, 4 * own), width),
            wide(tokens, width),
            low(tokens, width),
            low(tokens, width),
            low(own, width),
            low(tokens, own),
            low(own, tokens),
            wide(own, tokens),
            wide(tokens, own),
            wide(tokens, own),
            low(tokens, 3 * own),
        ]
        + narrow_scratch((tokens, width), pieces)
        + scatter_scratch((4 * own, width))
        + [
            wide(line // 2, *block),
            wide(line // 2, *block),
            wide(max(line // 2 - 1, 1), *block),
            pltpu.SemaphoreType.DMA((line // 2,)),
            pltpu.SemaphoreType.DMA((4 * pieces,)),
            pltpu.SemaphoreType.DMA((3,)),
            pltpu.SemaphoreType.DMA((slots,)),
            pltpu.SemaphoreType.DMA((slots,)),
        ],
        compiler_params=pltpu.CompilerParams(
            collective_id=number, has_side_effects=True, vmem_limit_bytes=60 * 2**20
        ),
        cost_estimate=pl.CostEstimate(
            flops=40 * tokens * tokens * own,
            bytes_accessed=150 * tokens * width,
            transcendentals=tokens * tokens * own // HEAD,
        ),
    )(
        hidden,
        branch,
        grad_entry,
        cotangent,
        live,
        scale,
        gate,
        mixed,
        attend_low,
        output_weight,
        triple,
        context,
        logsum,
        reduce_share,
        expand_hold,
        expand_give,
    )


def tail_kernel(
    tokens_any,
    shift_ref,
    scale_ref,
    taps_ref,
    grad_mixed_any,
    grad_hidden_any,
    hidden_any,
    ffn_half_any,
    ffn_across_any,
    cotangent_any,
    live_ref,
    gate_ref,
    rows_ref,
    split_ref,
    attend_out_ref,
    reduce_ref,
    expand_ref,
    tokens_grad_ref,
    block_out_ref,
    small_ref,
    norm_ref,
    line_ref,
    tokens_ref,
    grad_mixed_ref,
    grad_hidden_ref,
    hidden_ref,
    cotangent_ref,
    ffn_across_ref,
    ffn,
    normed_ref,
    back_ref,
    inverse_ref,
    grad_taps,
    grad_shift,
    grad_scale,
    slots,
    spare,
    spare_in,
    keep_sems,
    load_sems,
    sends,
    arrivals,
):
    width = tokens_ref.shape[1]
    core = lax.axis_index("narrow") % 2
    half = ffn.shape[0] // 2
    mine = pl.ds(pl.multiple_of(core * half, SLAB), half)
    loads = []
    for src, dst in (
        (ffn_half_any, ffn.at[mine, :]),
        (ffn_across_any, ffn_across_ref),
        (tokens_any, tokens_ref),
        (grad_mixed_any, grad_mixed_ref),
        (cotangent_any, cotangent_ref),
        (grad_hidden_any, grad_hidden_ref),
        (hidden_any, hidden_ref),
    ):
        loads.append(pltpu.make_async_copy(src, dst, load_sems.at[len(loads)]))
        loads[-1].start()
    wide_bits = bits_of(lax.axis_size("wide"))
    narrow_bits = bits_of(lax.axis_size("narrow"))
    greet(
        [place_at("wide", bit) for bit in wide_bits]
        + [place_at("narrow", bit) for bit in narrow_bits]
    )
    _, z = wide_parts()
    count = len(wide_bits)
    hops = line_hops()

    def spot_of(item):
        spot = z
        for index, (_, bit) in enumerate(hops):
            if (item >> index) % 2:
                spot = partner(spot, bit // 2)
        return line_block(line_ref, spot)

    gather = Gather(attend_out_ref, spot_of, hops, sends, arrivals, count + len(narrow_bits))
    gather.step(0)
    keep = pltpu.make_async_copy(attend_out_ref, spot_of(0), keep_sems.at[0])
    keep.start()
    loads[0].wait()
    loads[1].wait()
    ffn[mine, :] = ffn[mine, :] + ffn_across_ref[...]
    last = count + len(narrow_bits) + 2 ** len(hops) - 1
    ffn_copy = send(ffn.at[mine, :], ffn.at[mine, :], sends, arrivals, last, place_at("narrow", 1))
    mixer_kernel_backward(
        tokens_ref,
        shift_ref,
        scale_ref,
        taps_ref,
        grad_mixed_ref,
        grad_hidden_ref,
        tokens_grad_ref,
        grad_taps,
        grad_shift,
        grad_scale,
        normed_ref,
        back_ref,
        inverse_ref,
        loads[2].wait,
        loads[3].wait,
        loads[5].wait,
    )
    ffn_copy.wait_recv()
    loads[4].wait()
    gate, live = gate_ref[...], live_ref[...]

    def weigh(r, gates):
        spot = slab_at(r)
        return gates + fold_rows(ffn[spot, :] * (cotangent_ref[spot, :].astype(jnp.float32) * live))

    def leave(r, carry):
        spot = slab_at(r)
        block_out_ref[spot, :] = (live * (hidden_ref[spot, :] + gate * ffn[spot, :])).astype(
            jnp.bfloat16
        )
        return carry

    gates = lax.fori_loop(
        0, ffn.shape[0] // SLAB, weigh, jnp.zeros((8, width), jnp.float32), unroll=UNROLL
    )
    slots[0] = jnp.zeros(slots.shape[1:], jnp.float32)
    slots[0, 0:1, :] = grad_shift[...]
    slots[0, 1:2, :] = grad_scale[...]
    slots[0, 2:5, :] = rows_ref[...]
    slots[0, 5:6, :] = jnp.sum(gates, axis=0, keepdims=True)
    shared_rows = 6 + taps_ref.shape[0]
    slots[0, 6:shared_rows, :] = grad_taps[...]
    split_rows = split_ref.shape[0]
    slots[0, shared_rows : shared_rows + split_rows, :] = split_ref[...]
    squares = jnp.zeros((8, width), jnp.float32)
    for share in (attend_out_ref, reduce_ref, expand_ref):
        squares = squares + fold_rows(share[...] * share[...])
    end = shared_rows + split_rows
    slots[0, end : end + 1, :] = jnp.sum(squares, axis=0, keepdims=True)
    copies = []
    for b in range(count):
        copy = send(
            slots.at[b], slots.at[count + 1 + b], sends, arrivals, b, place_at("wide", wide_bits[b])
        )
        copies.append(copy)
        if b == 0:
            gather.step(1)
            loads[6].wait()
            lax.fori_loop(0, ffn.shape[0] // SLAB, leave, 0, unroll=UNROLL)
        copy.wait_recv()
        slots[b + 1] = slots[b] + slots[count + 1 + b]
    total = slots[count]
    small_ref[...] = total
    shared_part = total[:shared_rows]
    split_part = total[shared_rows:end]
    shared = jnp.sum(shared_part * shared_part)
    split_sum = jnp.sum(split_part * split_part) + jnp.sum(total[end : end + 1])
    spare[0] = jnp.full(spare.shape[1:], split_sum, jnp.float32)
    for b in range(len(narrow_bits)):
        copy = send(
            spare.at[b], spare_in.at[b], sends, arrivals, count + b, place_at("narrow", narrow_bits[b])
        )
        copies.append(copy)
        copy.wait_recv()
        spare[b + 1] = spare[b] + spare_in[b]
    norm_ref[...] = jnp.sqrt(spare[len(narrow_bits)] + shared)
    for item in gather.order[2:]:
        gather.step(item)
    keep.wait()
    gather.finish()
    ffn_copy.wait_send()
    for copy in copies:
        copy.wait_send()


def tail(
    tokens,
    shift,
    scale,
    taps,
    grad_mixed,
    grad_hidden,
    hidden,
    ffn_half,
    ffn_across,
    cotangent,
    live,
    gate,
    table_rows,
    split_rows,
    shares,
    number,
):
    rows, width = tokens.shape
    wide_bits = bits_of(lax.axis_size("wide"))
    narrow_bits = bits_of(lax.axis_size("narrow"))
    count = len(wide_bits)
    line = lax.axis_size("wide") // 2
    total = count + len(narrow_bits) + line
    small = -(-(6 + taps.shape[0] + split_rows.shape[0] + 1) // 8) * 8
    vmem = pl.BlockSpec(memory_space=pltpu.VMEM)
    anywhere = pl.BlockSpec(memory_space=pl.ANY)
    f32 = lambda *shape: jax.ShapeDtypeStruct(shape, jnp.float32)
    low = lambda *shape: jax.ShapeDtypeStruct(shape, jnp.bfloat16)
    wide = lambda *shape: pltpu.VMEM(shape, jnp.float32)
    return pl.pallas_call(
        tail_kernel,
        out_shape=(
            low(rows, width),
            low(rows, width),
            f32(small, width),
            f32(8, LANES),
            f32(line * shares[0].shape[0], width),
        ),
        in_specs=[anywhere] + [vmem] * 3 + [anywhere] * 6 + [vmem] * 7,
        out_specs=(vmem,) * 4 + (anywhere,),
        scratch_shapes=[
            pltpu.VMEM((rows, width), jnp.bfloat16),
            wide(rows, width),
            wide(rows, width),
            wide(rows, width),
            pltpu.VMEM((rows, width), jnp.bfloat16),
            wide(rows // 2, width),
            wide(rows, width),
            wide(rows, width),
            wide(rows, width),
            wide(rows, LANES),
            wide(9, width),
            wide(1, width),
            wide(1, width),
            wide(2 * count + 1, small, width),
            wide(len(narrow_bits) + 1, 8, LANES),
            wide(len(narrow_bits), 8, LANES),
            pltpu.SemaphoreType.DMA((1,)),
            pltpu.SemaphoreType.DMA((7,)),
            pltpu.SemaphoreType.DMA((total,)),
            pltpu.SemaphoreType.DMA((total,)),
        ],
        compiler_params=pltpu.CompilerParams(
            collective_id=number, has_side_effects=True, vmem_limit_bytes=56 * 2**20
        ),
        cost_estimate=pl.CostEstimate(
            flops=100 * rows * width, bytes_accessed=60 * rows * width, transcendentals=0
        ),
    )(
        tokens,
        shift,
        scale,
        taps,
        grad_mixed,
        grad_hidden,
        hidden,
        ffn_half,
        ffn_across,
        cotangent,
        live,
        gate,
        table_rows,
        split_rows,
        *shares,
    )


def local(
    tokens,
    conditions,
    item_live,
    cotangent,
    modulation_table,
    mixer_kernel,
    hidden_kernel,
    attend_weight,
    output_weight,
    expand_weight,
    reduce_weight,
    attend_moment,
    output_moment,
    expand_moment,
    reduce_moment,
    table_first,
    table_second,
    mixer_first,
    mixer_second,
    hidden_first,
    hidden_second,
):
    live_mask = item_live.astype(jnp.float32)[:, None, None]
    modulation = modulation_table[None] + conditions
    shift_one = modulation[:, 0:1]
    scale_one = modulation[:, 1:2]
    gate_one = modulation[:, 2:3]
    shift_two = modulation[:, 3:4]
    scale_two = modulation[:, 4:5]
    gate_two = modulation[:, 5:6]
    width = tokens.shape[2]
    flat_tokens = tokens.reshape(-1, width)
    mixed_low = mixer_forward(flat_tokens, shift_one[0], scale_one[0], mixer_kernel)
    three = lambda matrix: jnp.transpose(matrix, (1, 0, 2))
    triple, context, logsum, attend_low = attend(mixed_low, three(attend_weight))
    output_rows, context = together(all_rows(output_weight), context)
    branch, hidden, entry_low = enter(
        context, flat_tokens, output_rows, gate_one[0], shift_two[0], scale_two[0], 1
    )
    flat_cotangent = cotangent.reshape(-1, width)
    live_row = jnp.broadcast_to(live_mask[0], (1, width))
    ffn_half, grad_entry, reduce_share, expand_hold, expand_give, grad_hidden_kernel = middle(
        entry_low,
        flat_cotangent,
        live_row,
        gate_two[0],
        expand_weight,
        reduce_weight,
        hidden_kernel,
        2,
    )
    grad_entry, reduce_share, expand_hold, ffn_half = together(
        grad_entry, reduce_share, expand_hold, ffn_half
    )
    for bit in bits_of(lax.axis_size("narrow"))[1:-1]:
        ffn_half = ffn_half + permute(ffn_half, "narrow", bit)
    ffn_across = permute(ffn_half, "narrow", lax.axis_size("narrow") // 2)
    (
        grad_hidden,
        grad_shift_two,
        grad_scale_two,
        grad_gate_one,
        grad_mixed,
        attend_out_share,
        reduce_line,
        expand_line,
        expand_share,
    ) = back(
        hidden,
        branch,
        grad_entry,
        flat_cotangent,
        live_row,
        scale_two[0],
        gate_one[0],
        mixed_low,
        attend_low,
        output_weight,
        triple,
        context,
        logsum,
        reduce_share,
        expand_hold,
        expand_give,
        3,
    )
    ffn_across, grad_mixed, reduce_line, attend_out_share = together(
        ffn_across, grad_mixed, reduce_line, attend_out_share
    )
    reduce_other = permute(reduce_line, "wide", 1)
    shared_rows = modulation_table.shape[0] + mixer_kernel.shape[0]
    hidden_rows = -(-grad_hidden_kernel.size // width)
    padding = hidden_rows * width - grad_hidden_kernel.size
    hidden_flat = jnp.pad(grad_hidden_kernel.reshape(-1), (0, padding))
    tokens_gradient, block_out, small, norm, attend_out_line = tail(
        flat_tokens,
        shift_one[0],
        scale_one[0],
        mixer_kernel,
        grad_mixed,
        grad_hidden,
        hidden,
        ffn_half,
        ffn_across,
        flat_cotangent,
        live_row,
        gate_two[0],
        jnp.concatenate([grad_gate_one, grad_shift_two, grad_scale_two], axis=0),
        hidden_flat.reshape(hidden_rows, width),
        [attend_out_share, reduce_share, expand_share],
        4,
    )
    tokens_gradient = tokens_gradient.reshape(tokens.shape)
    block_out = block_out.reshape(tokens.shape)
    summed_table = small[: modulation_table.shape[0]]
    summed_mixer = small[modulation_table.shape[0] : shared_rows]
    summed_hidden = small[shared_rows : shared_rows + hidden_rows].reshape(-1)
    summed_hidden = summed_hidden[: hidden_kernel.size].reshape(hidden_kernel.shape)
    gradient_norm = norm[0, 0]
    clip_factor = jnp.minimum(1.0, 1.0 / (gradient_norm + 1e-06))
    gramian, expand_first = gram_whole(
        norm,
        [attend_out_line, expand_line, reduce_line],
        [three(attend_moment), output_moment, expand_moment, reduce_moment],
        5,
    )
    gramian, expand_line, attend_out_line = together(gramian, expand_line, attend_out_line)
    expand_other = permute(expand_line[expand_line.shape[0] // 2 :], "wide", 1)
    attend_out_other = permute(attend_out_line, "wide", 1)
    factor = polar_factor(gramian)
    factor, expand_other, attend_out_other, reduce_other = together(
        factor, expand_other, attend_out_other, reduce_other
    )
    weights = [three(attend_weight), output_weight, expand_weight, reduce_weight]
    bands, ready, fresh, highs, lows = spread(
        norm,
        factor,
        [attend_out_line, expand_line, reduce_line],
        [attend_out_other, expand_first, expand_other, reduce_other],
        [three(attend_moment), output_moment, expand_moment, reduce_moment],
        weights,
        6,
    )
    carried, results = finish(bands, ready, fresh, highs, lows, weights)
    attend_carried = jnp.transpose(carried[0], (1, 0, 2))
    attend_result = jnp.transpose(results[0], (1, 0, 2))
    table_moment, table_square, table_result = adam_update(
        modulation_table, table_first, table_second, clip_factor * summed_table
    )
    mixer_moment, mixer_square, mixer_result = adam_update(
        mixer_kernel, mixer_first, mixer_second, clip_factor * summed_mixer
    )
    hidden_moment, hidden_square, hidden_result = adam_update(
        hidden_kernel, hidden_first, hidden_second, clip_factor * summed_hidden
    )
    return (
        block_out,
        tokens_gradient,
        gradient_norm,
        attend_carried,
        carried[1],
        carried[2],
        carried[3],
        attend_result,
        results[1],
        results[2],
        results[3],
        table_moment,
        table_square,
        table_result,
        mixer_moment,
        mixer_square,
        mixer_result,
        hidden_moment,
        hidden_square,
        hidden_result,
    )


def solution(mesh):
    placed = (
        P("wide", None, None),
        P("wide", None, None),
        P("wide"),
        P("wide", None, None),
        P(),
        P(),
        P(None, "narrow"),
        P(None, None, "narrow"),
        P("narrow", None),
        P(None, "narrow"),
        P("narrow", None),
        P(None, None, "narrow"),
        P("narrow", None),
        P(None, "narrow"),
        P("narrow", None),
        P(),
        P(),
        P(),
        P(),
        P(None, "narrow"),
        P(None, "narrow"),
    )
    return jax.shard_map(
        local,
        mesh=mesh,
        in_specs=placed,
        out_specs=(
            P("wide", None, None),
            P("wide", None, None),
            P(),
            P(None, None, "narrow"),
            P("narrow", None),
            P(None, "narrow"),
            P("narrow", None),
            P(None, None, "narrow"),
            P("narrow", None),
            P(None, "narrow"),
            P("narrow", None),
            P(),
            P(),
            P(),
            P(),
            P(),
            P(),
            P(None, "narrow"),
            P(None, "narrow"),
            P(None, "narrow"),
        ),
        check_vma=False,
    )
```

```python
import functools
import math

import jax
import jax.numpy as jnp
from jax import lax
from jax.experimental import pallas as pl
from jax.experimental.pallas import tpu as pltpu
from jax.sharding import PartitionSpec as P

D = 1024
HEAD = 64
FF = 4096
GRID = 32
NEWTON = 5
STEP = 10


first_decay = 0.9
second_decay = 0.999
adam_rate = 0.3
muon_rate = 0.15
muon_momentum = 0.5
weight_decay = 0.01
newton_terms = (3.4445, -4.775, 2.0315)
gelu_slope = 0.7978845608
gelu_cubic = 0.044715


MESH = pl.DeviceIdType.MESH
BLK = 256
LANES = 128
SLAB = 16
QUERIES = 512
UNROLL = 4
MATRICES = 4
COLUMNS = (0, 2)


def partner(index, bit):
    return index + (1 - 2 * ((index // bit) % 2)) * bit


def bits_of(count):
    found = []
    bit = 1
    while bit < count:
        found.append(bit)
        bit *= 2
    return found


def place_at(axis, bit):
    place = {"wide": lax.axis_index("wide"), "narrow": lax.axis_index("narrow")}
    place[axis] = partner(place[axis], bit)
    return (place["wide"], place["narrow"])


def greet(places):
    barrier = pltpu.get_barrier_semaphore()
    for place in places:
        pl.semaphore_signal(barrier, inc=1, device_id=place, device_id_type=MESH)
    pl.semaphore_wait(barrier, len(places))


def send(src, dst, sends, arrivals, slot, place):
    copy = pltpu.make_async_remote_copy(
        src_ref=src,
        dst_ref=dst,
        send_sem=sends.at[slot],
        recv_sem=arrivals.at[slot],
        device_id=place,
        device_id_type=MESH,
    )
    copy.start()
    return copy


def permute(values, axis, bit):
    size = lax.axis_size(axis)
    return lax.ppermute(values, axis, [(index, index ^ bit) for index in range(size)])


def together(*values):
    return lax.optimization_barrier(values)


def wide_parts():
    w = lax.axis_index("wide")
    return w % 2, w // 2


def line_partner(z, offset):
    for bit in bits_of(2 * offset):
        if (offset // bit) % 2:
            z = partner(z, bit)
    return z


def block_of(ref, y, z):
    count = lax.axis_size("wide") // 2
    rows = ref.shape[0] // (2 * count)
    return ref.at[pl.ds(pl.multiple_of((y * count + z) * rows, 8), rows), :]


def line_block(ref, z):
    rows = ref.shape[0] // (lax.axis_size("wide") // 2)
    return ref.at[pl.ds(pl.multiple_of(z * rows, 8), rows), :]


def block_shape(shape):
    return (shape[0] // lax.axis_size("wide"), shape[1])


class Scatter:
    def __init__(self, src, held, beside, inbox, sends, arrivals, local, base, blocks=None):
        self.src, self.held, self.beside, self.inbox = src, held, beside, inbox
        self.blocks = blocks
        self.sends, self.arrivals, self.local, self.base = sends, arrivals, local, base
        self.count = lax.axis_size("wide") // 2 if blocks is None else blocks[0].shape[0]
        self.copies = {}
        self.loads = {}

    @staticmethod
    def slots():
        return lax.axis_size("wide") - 1

    def load(self):
        y, z = wide_parts()
        for e in reversed(range(self.count)):
            own = self.blocks[0].at[e] if self.blocks else block_of(self.src, y, line_partner(z, e))
            self.loads[e] = pltpu.make_async_copy(own, self.held.at[e], self.local.at[e])
            self.loads[e].start()

    def give(self, e):
        y, z = wide_parts()
        self.copies[("y", e)] = send(
            self.blocks[1].at[e] if self.blocks else block_of(self.src, 1 - y, line_partner(z, e)),
            self.beside.at[e],
            self.sends,
            self.arrivals,
            self.base + e,
            place_at("wide", 1),
        )

    def start(self):
        self.load()
        for e in reversed(range(self.count)):
            self.give(e)

    def step(self, e):
        self.loads[e].wait()
        self.copies[("y", e)].wait_recv()
        self.held[e] = self.held[e] + self.beside[e]
        bit = 1
        while bit < self.count and e % (2 * bit) == 0:
            self.copies[("z", e + bit)].wait_recv()
            self.held[e] = self.held[e] + self.inbox[e + bit - 1]
            bit *= 2
        if e:
            low = e & -e
            self.copies[("z", e)] = send(
                self.held.at[e],
                self.inbox.at[e - 1],
                self.sends,
                self.arrivals,
                self.base + self.count + e - 1,
                place_at("wide", 2 * low),
            )

    def finish(self):
        for copy in self.copies.values():
            copy.wait_send()


def scatter_scratch(shape):
    count = lax.axis_size("wide") // 2
    block = block_shape(shape)
    return [
        pltpu.VMEM((count,) + block, jnp.float32),
        pltpu.VMEM((count,) + block, jnp.float32),
        pltpu.VMEM((max(count - 1, 1),) + block, jnp.float32),
        pltpu.SemaphoreType.DMA((count,)),
    ]


class Gather:
    def __init__(self, own, spot_of, hops, sends, arrivals, base):
        self.own, self.spot_of, self.hops = own, spot_of, hops
        self.sends, self.arrivals, self.base = sends, arrivals, base
        self.copies = {}
        last = 2 ** (len(hops) - 1)
        self.order = sorted(
            range(2 * last), key=lambda item: (item >= last, bin(item).count("1"), -item)
        )

    def step(self, item):
        if item:
            self.copies[item].wait_recv()
        for index in range(item.bit_length(), len(self.hops)):
            later = item + 2**index
            spot = self.spot_of(item)
            axis, bit = self.hops[index]
            self.copies[later] = send(
                spot if item else self.own,
                spot,
                self.sends,
                self.arrivals,
                self.base + later - 1,
                place_at(axis, bit),
            )

    def finish(self):
        for copy in self.copies.values():
            copy.wait_send()


def line_hops():
    return [("wide", bit) for bit in reversed(bits_of(lax.axis_size("wide"))) if bit > 1]


class NarrowSum:
    def __init__(self, far_bits, pieces, x, o, near, far, held, sends, arrivals, local, base):
        self.bits, self.pieces = far_bits, pieces
        self.x, self.o, self.near, self.far, self.held = x, o, near, far, held
        self.sends, self.arrivals, self.local, self.base = sends, arrivals, local, base
        self.rows = x.shape[0] // 2
        self.core = lax.axis_index("narrow") % 2
        self.copies = []
        self.cross = {}
        self.keeps = []

    def block(self, side, p):
        step = self.rows // self.pieces
        return pl.ds(pl.multiple_of(side * self.rows + p * step, 8), step)

    def push(self, src, dst, slot, bit):
        copy = send(
            src, dst, self.sends, self.arrivals, self.base + slot, place_at("narrow", bit)
        )
        self.copies.append(copy)
        return copy

    def start(self):
        self.first = [
            self.push(self.x.at[self.block(1 - self.core, p)], self.near.at[p], p, 1)
            for p in range(self.pieces)
        ]
        self.loads = [
            pltpu.make_async_copy(
                self.x.at[self.block(self.core, p)], self.held.at[0, p], self.local.at[p]
            )
            for p in range(self.pieces)
        ]
        for load in self.loads:
            load.start()

    def hop(self, b, p):
        slot = (b + 1) * self.pieces + p
        self.cross[(b, p)] = self.push(
            self.held.at[b, p], self.far.at[b, p], slot, self.bits[b]
        )

    def begin(self, p):
        self.loads[p].wait()
        self.first[p].wait_recv()
        self.held[0, p] = self.held[0, p] + self.near[p]
        self.hop(0, p)

    def step(self, b, p):
        self.cross[(b, p)].wait_recv()
        self.held[b + 1, p] = self.held[b, p] + self.far[b, p]
        if b + 1 < len(self.bits):
            self.hop(b + 1, p)
            return
        spot = self.o.at[self.block(self.core, p)]
        slot = (b + 2) * self.pieces + p
        self.keeps.append(self.push(self.held.at[b + 1, p], spot, slot, 1))
        keep = pltpu.make_async_copy(self.held.at[b + 1, p], spot, self.local.at[p])
        keep.start()
        self.loads[p] = keep

    def finish(self):
        for copy in self.keeps:
            copy.wait_recv()
        for keep in self.loads:
            keep.wait()
        for copy in self.copies:
            copy.wait_send()


def narrow_scratch(shape, pieces):
    count = len(bits_of(lax.axis_size("narrow"))) - 1
    step = shape[0] // (2 * pieces)
    return [
        pltpu.VMEM((pieces, step, shape[1]), jnp.float32),
        pltpu.VMEM((count, pieces, step, shape[1]), jnp.float32),
        pltpu.VMEM((count + 1, pieces, step, shape[1]), jnp.float32),
        pltpu.SemaphoreType.DMA((pieces,)),
    ]


def gram_kernel(
    norm_ref,
    attend_out_any,
    expand_any,
    reduce_any,
    attend_moment_any,
    output_moment_any,
    expand_moment_any,
    reduce_moment_any,
    band_ref,
    expand_beside,
    attend_out,
    expand,
    reduce,
    attend_moment,
    output_moment,
    expand_moment,
    reduce_moment,
    *refs,
):
    highs, lows, refs = refs[:MATRICES], refs[MATRICES : 2 * MATRICES], refs[2 * MATRICES :]
    attend_turned, attend_blend, refs = refs[0], refs[1], refs[2:]
    twice, halves, inbox, block, load_sems, sends, arrivals, local = refs
    narrow_bits = bits_of(lax.axis_size("narrow"))
    wide_bits = bits_of(lax.axis_size("wide"))
    parts, rows = halves.shape[0], halves.shape[1]
    sub = parts // MATRICES
    size = attend_out.shape[1]
    hops = [("narrow", bit) for bit in bits_of(sub)]
    hops += [("wide", bit) for bit in reversed(wide_bits)]
    w, n = lax.axis_index("wide"), lax.axis_index("narrow")
    y, z = wide_parts()
    greet(
        [place_at("narrow", bit) for bit in narrow_bits]
        + [place_at("wide", bit) for bit in wide_bits]
    )
    early = expand_beside.shape[0]
    expand_copy = send(
        expand_any.at[pl.ds(0, early), :],
        expand_beside,
        sends,
        arrivals,
        sends.shape[0] - 1,
        place_at("wide", 1),
    )
    own_rows = lambda ref: ref.at[
        pl.ds(pl.multiple_of(y * (ref.shape[0] // 2), 8), ref.shape[0] // 2), :
    ]
    own_columns = lambda ref: ref.at[
        :, pl.ds(pl.multiple_of(y * (ref.shape[1] // 2), LANES), ref.shape[1] // 2)
    ]
    loads = []
    own = attend_moment_any.shape[2]
    for j in range(3):
        pltpu.make_async_copy(
            attend_moment_any.at[j], attend_moment.at[:, pl.ds(j * own, own)], load_sems.at[1]
        ).start()
    for src, dst in (
        (attend_out_any, attend_out),
        (None, None),
        (own_rows(output_moment_any), output_moment),
        (expand_any, expand),
        (own_columns(expand_moment_any), expand_moment),
        (reduce_any, reduce),
        (own_rows(reduce_moment_any), reduce_moment),
    ):
        if src is None:
            loads.append(pltpu.make_async_copy(attend_moment, attend_moment, load_sems.at[1]))
            continue
        loads.append(pltpu.make_async_copy(src, dst, load_sems.at[len(loads)]))
        loads[-1].start()
    clip = jnp.minimum(1.0, 1.0 / (norm_ref[0:1, 0:1] + 1e-06))
    count = halves.shape[1] * sub
    start = z * count
    lines = lax.axis_size("wide") // 2
    band = halves.shape[2]

    def blend(k, moment, gradient):
        total = highs[k].shape[0]

        def one(i, carry):
            spot = slab_at(i)
            highs[k][spot, :], lows[k][spot, :] = split(
                muon_momentum * moment[spot, :] + clip * gradient[spot, :]
            )
            return carry

        lax.fori_loop(0, total // SLAB, one, 0, unroll=UNROLL)

    def multiply(k):
        columns = pl.ds(pl.multiple_of(start, LANES), count)
        high, low = highs[k][:, columns], lows[k][:, columns]
        values = dot_of(high, highs[k][...], 0, 0) + (
            dot_of(high, lows[k][...], 0, 0) + dot_of(low, highs[k][...], 0, 0)
        )
        twice[:, :size] = values
        twice[:, size:] = values[:, :band]
        for s in range(sub):
            for at in range(0, rows, LANES):
                extent = min(LANES, rows)
                first = s * rows + at
                lanes = pl.ds(pl.multiple_of(start + first // LANES * LANES, LANES), band)
                halves[k * sub + s, at : at + extent, :] = twice[first : first + extent, lanes]

    share = attend_out.shape[0] // lines
    first_rows, second_rows = 3 * share // 4, share // 4
    loads[0].wait()
    loads[1].wait()
    loads[2].wait()
    for at in range(0, 3 * own, LANES):
        attend_turned[pl.ds(at, LANES), :] = attend_moment[:, pl.ds(at, LANES)].T
    offset = y * (3 * own // 2)
    for b in range(lines):
        gradient = attend_out[b * share : (b + 1) * share, :]
        spot = pl.ds(pl.multiple_of(offset + b * first_rows, 8), first_rows)
        attend_blend[pl.ds(b * first_rows, first_rows), :] = (
            muon_momentum * attend_turned[spot, :] + clip * gradient[:first_rows]
        )
        spot = pl.ds(b * second_rows, second_rows)
        output_moment[spot, :] = (
            muon_momentum * output_moment[spot, :] + clip * gradient[first_rows:]
        )

    def cut(k, values):
        def one(i, carry):
            spot = slab_at(i)
            highs[k][spot, :], lows[k][spot, :] = split(values[spot, :])
            return carry

        lax.fori_loop(0, highs[k].shape[0] // SLAB, one, 0, unroll=UNROLL)

    cut(0, attend_blend)
    multiply(0)
    cut(1, output_moment)
    multiply(1)
    loads[3].wait()
    loads[4].wait()
    for at in range(0, expand.shape[0], LANES):
        spot = pl.ds(at, LANES)
        highs[2][spot, :], lows[2][spot, :] = split(
            muon_momentum * expand_moment[:, spot].T + clip * expand[spot, :]
        )
    multiply(2)
    loads[5].wait()
    loads[6].wait()
    blend(3, reduce_moment, reduce)
    multiply(3)
    half = rows // 2
    row_half = lambda side: pl.ds(pl.multiple_of(side * half, 8), half)
    slot = iter(range(sends.shape[0]))
    copies = []

    def push(src, dst, place):
        copies.append(send(src, dst, sends, arrivals, next(slot), place))
        return copies[-1]

    at = 0
    for bit in narrow_bits:
        value = (n // bit) % 2
        last = 2 * bit == parts
        waits = []
        for j in range(parts // (2 * bit)):
            mine = n % bit + value * bit + j * 2 * bit
            theirs = n % bit + (1 - value) * bit + j * 2 * bit
            for side in (1 - y, y) if last else (None,):
                spot = slice(None) if side is None else row_half(side)
                copy = push(
                    halves.at[theirs] if side is None else halves.at[theirs, spot],
                    inbox.at[at + j] if side is None else inbox.at[at + j, spot],
                    place_at("narrow", bit),
                )
                waits.append((copy, mine, at + j, spot))
        at += parts // (2 * bit)
        for copy, mine, where, spot in waits:
            copy.wait_recv()
            halves[mine, spot] = halves[mine, spot] + inbox[where, spot]
            if last and copy is waits[0][0]:
                side_copy = push(halves.at[n, row_half(1 - y)], block.at[0], place_at("wide", 1))
    side_copy.wait_recv()
    block[1] = halves[n, row_half(y)] + block[0]

    def spot_of(item):
        big, small = w, n % sub
        for index, (axis, bit) in enumerate(hops):
            if (item >> index) % 2:
                if axis == "wide":
                    big = partner(big, bit)
                else:
                    small = partner(small, bit)
        first = ((big // 2) * (2 * sub) + small * 2 + big % 2) * half
        return band_ref.at[pl.ds(pl.multiple_of(first, 8), half), :]

    keep = pltpu.make_async_copy(block.at[1], spot_of(0), local.at[0])
    keep.start()
    gather = Gather(block.at[1], spot_of, hops, sends, arrivals, next(slot))
    for item in gather.order:
        gather.step(item)
    keep.wait()
    gather.finish()
    expand_copy.wait()
    for copy in copies:
        copy.wait_send()


def gram_whole(norm, lines, moments, number):
    narrow_bits = bits_of(lax.axis_size("narrow"))
    wide_bits = bits_of(lax.axis_size("wide"))
    size = lines[0].shape[1]
    sub = lax.axis_size("narrow") // MATRICES
    parts = lax.axis_size("narrow")
    count = 2 * size // lax.axis_size("wide")
    band = size // 2 + LANES
    halves = (parts, count // sub, band)
    line_rows = [lines[0].shape[0] * 3 // 4, lines[0].shape[0] // 4]
    line_rows += [lines[1].shape[0], lines[2].shape[0]]
    gathers = len(bits_of(sub)) + len(wide_bits)
    slots = parts + 3 + 2**gathers
    vmem = pl.BlockSpec(memory_space=pltpu.VMEM)
    anywhere = pl.BlockSpec(memory_space=pl.ANY)
    wide = lambda *shape: pltpu.VMEM(shape, jnp.float32)
    return pl.pallas_call(
        gram_kernel,
        out_shape=(
            jax.ShapeDtypeStruct((size, band), jnp.float32),
            jax.ShapeDtypeStruct((lines[1].shape[0] // 2, size), jnp.float32),
        ),
        in_specs=[vmem] + [anywhere] * 7,
        out_specs=(anywhere, anywhere),
        scratch_shapes=[
            wide(*lines[0].shape),
            wide(*lines[1].shape),
            wide(*lines[2].shape),
            wide(size, 2 * line_rows[0]),
            wide(line_rows[1], size),
            wide(size, line_rows[2]),
            wide(line_rows[3], size),
        ]
        + [pltpu.VMEM((rows, size), jnp.bfloat16) for rows in line_rows] * 2
        + [
            wide(2 * line_rows[0], size),
            wide(line_rows[0], size),
            wide(count, size + band),
            wide(*halves),
            wide(*halves),
            wide(2, halves[1] // 2, band),
            pltpu.SemaphoreType.DMA((7,)),
            pltpu.SemaphoreType.DMA((slots,)),
            pltpu.SemaphoreType.DMA((slots,)),
            pltpu.SemaphoreType.DMA((1,)),
        ],
        compiler_params=pltpu.CompilerParams(
            collective_id=number, has_side_effects=True, vmem_limit_bytes=48 * 2**20
        ),
        cost_estimate=pl.CostEstimate(
            flops=3 * size * size * size, bytes_accessed=80 * size * size, transcendentals=0
        ),
    )(norm, *lines, *moments)


def split(values):
    high = values.astype(jnp.bfloat16)
    return high, (values - high.astype(jnp.float32)).astype(jnp.bfloat16)


def product(left_high, left_low, right_high, right_low):
    dot = functools.partial(jnp.dot, preferred_element_type=jnp.float32)
    return dot(left_high, right_high) + (dot(left_high, right_low) + dot(left_low, right_high))


def polar_kernel(g_ref, band_ref, q_ref, gh, gl, ph, pw, th, tl):
    size = g_ref.shape[0]
    blocks = size // BLK
    first, second, third = newton_terms
    rows = lambda block: pl.ds(block * BLK, BLK)
    square = (BLK, BLK)
    unit = (
        lax.broadcasted_iota(jnp.int32, square, 0) == lax.broadcasted_iota(jnp.int32, square, 1)
    ).astype(jnp.float32)
    count = size // LANES
    lanes = lambda block: pl.ds((block % count) * LANES, LANES)
    trace = jnp.zeros((), jnp.float32)
    for i in range(count):
        trace = trace + jnp.sum(g_ref[lanes(i), lanes(0)] * unit[:LANES, :LANES])
    factor = 1.0 / (jnp.sqrt(trace) + 1e-07)
    for i in range(count):
        for j in range(count // 2 + 1):
            values = g_ref[lanes(i), lanes(j)] * (factor * factor)
            gh[lanes(i), lanes(i + j)], gl[lanes(i), lanes(i + j)] = split(values)
            if 0 < j < count // 2:
                values = values.T
                gh[lanes(i + j), lanes(i)], gl[lanes(i + j), lanes(i)] = split(values)

    def put(high, low, i, j, values):
        high[rows(i), rows(j)], low[rows(i), rows(j)] = split(values)
        if i != j:
            high[rows(j), rows(i)], low[rows(j), rows(i)] = split(values.T)

    def symmetric(left, right, emit):
        for i in range(blocks):
            columns = pl.ds(i * BLK, size - i * BLK)
            values = product(
                left[0][rows(i), :], left[1][rows(i), :], right[0][:, columns], right[1][:, columns]
            )
            for j in range(i, blocks):
                emit(i, j, values[:, (j - i) * BLK : (j - i + 1) * BLK])

    def emit_terms(i, j, values):
        gram = gh[rows(i), rows(j)].astype(jnp.float32) + gl[rows(i), rows(j)].astype(jnp.float32)
        terms = second * gram + third * values
        if i == j:
            terms = terms + first * unit
        put(ph, pw, i, j, terms)

    def emit_total(i, j, values):
        q_ref[rows(i), rows(j)] = values
        if i != j:
            q_ref[rows(j), rows(i)] = values.T

    symmetric((gh, gl), (gh, gl), emit_terms)
    for i in range(blocks):
        q_ref[rows(i), :] = (
            ph[rows(i), :].astype(jnp.float32) + pw[rows(i), :].astype(jnp.float32)
        ) * factor

    def one_step(step, carry):
        symmetric((ph, pw), (gh, gl), functools.partial(put, th, tl))
        symmetric((th, tl), (ph, pw), functools.partial(put, gh, gl))
        symmetric((gh, gl), (gh, gl), emit_terms)
        for i in range(blocks):
            th[rows(i), :], tl[rows(i), :] = split(q_ref[rows(i), :])
        symmetric((ph, pw), (th, tl), emit_total)
        return carry

    lax.fori_loop(0, NEWTON - 1, one_step, 0)
    for i in range(count):
        for j in range(count // 2 + 1):
            band_ref[lanes(i), lanes(j)] = q_ref[lanes(i), lanes(i + j)]


def polar_factor(gramian):
    size = gramian.shape[0]
    vmem = pl.BlockSpec(memory_space=pltpu.VMEM)
    return pl.pallas_call(
        polar_kernel,
        out_shape=jax.ShapeDtypeStruct(gramian.shape, jnp.float32),
        in_specs=[vmem],
        out_specs=vmem,
        scratch_shapes=[pltpu.VMEM((size, size), jnp.float32)]
        + [pltpu.VMEM((size, size), jnp.bfloat16)] * 6,
        compiler_params=pltpu.CompilerParams(vmem_limit_bytes=48 * 2**20),
        cost_estimate=pl.CostEstimate(
            flops=17 * 6 * size**3, bytes_accessed=8 * size * size, transcendentals=0
        ),
    )(gramian)


class Matrices:
    def __init__(self, own):
        self.own = own

    def move(self, outer, inner, sem, k, inward, rows=slice(None), columns=slice(None)):
        if k:
            pairs = [(outer.at[rows, columns], inner.at[rows, columns])]
        else:
            pairs = [
                (outer.at[j, rows], inner.at[rows, pl.ds(j * self.own, self.own)]) for j in range(3)
            ]
        for there, here in pairs:
            src, dst = (there, here) if inward else (here, there)
            pltpu.make_async_copy(src, dst, sem).start()


def whole_of(ref, sem):
    return pltpu.make_async_copy(ref, ref, sem)


def assemble(band, factor_high, factor_low):
    count = factor_high.shape[0] // LANES
    lanes = lambda block: pl.ds((block % count) * LANES, LANES)
    for i in range(count):
        for j in range(count // 2 + 1):
            part = band[lanes(i), lanes(j)]
            spot = (lanes(i), lanes(i + j))
            factor_high[spot], factor_low[spot] = split(part)
            if 0 < j < count // 2:
                spot = (lanes(i + j), lanes(i))
                factor_high[spot], factor_low[spot] = split(part.T)


def update(k, start, factor_high, factor_low, high, low, value):
    spot = pl.ds(pl.multiple_of(start, BLK), BLK)
    q_high, q_low = factor_high[spot, :], factor_low[spot, :]
    if k in COLUMNS:
        polar = dot_of(q_high, high[...], 1, 0) + (
            dot_of(q_high, low[...], 1, 0) + dot_of(q_low, high[...], 1, 0)
        )
        where = (spot, slice(None))
    else:
        polar = dot_of(high[...], q_high, 1, 1) + (
            dot_of(low[...], q_high, 1, 1) + dot_of(high[...], q_low, 1, 1)
        )
        where = (slice(None), spot)
    scale = muon_rate * 0.2 * math.sqrt((3 * D, D, FF, FF)[k])
    value[where] = value[where] * (1.0 - muon_rate * weight_decay) - scale * polar
    return where


def spread_kernel(sub, pieces, norm_ref, q_ref, *refs):
    lines, others, refs = refs[:3], refs[3:7], refs[7:]
    moments, weights, refs = refs[:4], refs[4:8], refs[8:]
    o_ref, carried, fresh, high_outs, low_outs = refs[0], refs[1:5], refs[5:9], refs[9:13], refs[13:17]
    refs = refs[17:]
    pair_bands, factor_high, factor_low = refs[:3]
    staged, values, highs, lows = refs[3:7], refs[7:11], refs[11:15], refs[15:19]
    load_sems, value_sems, out_sems, split_sems, band_sems, sends, arrivals = refs[19:]
    size = q_ref.shape[0]
    half = size // 2
    step = half // pieces
    w, n = lax.axis_index("wide"), lax.axis_index("narrow")
    own = n // sub
    across, near = partner(own, 2), partner(own, 1)
    far = own // 2
    near_place, far_place = place_at("narrow", sub), place_at("narrow", 2 * sub)
    side_place = place_at("wide", 1)
    greet([near_place, far_place, side_place])
    y = w % 2
    rows = lambda side, p: pl.ds(pl.multiple_of(side * half + p * step, 8), step)
    copies = []

    def push(src, dst, place):
        copies.append(send(src, dst, sends, arrivals, len(copies), place))
        return copies[-1]

    crossing = [
        push(q_ref.at[rows(y, p)], o_ref.at[own, rows(y, p)], far_place) for p in range(pieces)
    ]
    landing = [push(q_ref, o_ref.at[own], near_place)]
    keep = pltpu.make_async_copy(q_ref, o_ref.at[own], band_sems.at[0])
    keep.start()
    own_band = pltpu.make_async_copy(q_ref, pair_bands.at[own % 2], band_sems.at[1])
    own_band.start()
    matrices = Matrices(moments[0].shape[2])
    blocks = lax.axis_size("wide")
    for k in range(MATRICES):
        extent = staged[k].shape[0] // 2
        if k >= 2:
            pieces_of = [(y, 0, lines[k - 1])]
            if k == 2:
                pieces_of += [(1 - y, 0, others[1]), (1 - y, extent // 2, others[2])]
            else:
                pieces_of += [(1 - y, 0, others[3])]
            for side, at, source in pieces_of:
                to = pl.multiple_of(side * extent + at, 8)
                spot = staged[k].at[pl.ds(to, source.shape[0]), :]
                pltpu.make_async_copy(source, spot, load_sems.at[k]).start()
        for side, source in ((y, lines[0]), (1 - y, others[0])):
            if k >= 2:
                continue
            share = (staged[0].shape[0] // blocks, staged[1].shape[0] // blocks)
            for b in range(blocks // 2):
                start = b * (share[0] + share[1]) + k * share[0]
                to = pl.multiple_of(side * extent + b * share[k], 8)
                pltpu.make_async_copy(
                    source.at[pl.ds(start, share[k]), :],
                    staged[k].at[pl.ds(to, share[k]), :],
                    load_sems.at[k],
                ).start()
        matrices.move(moments[k], values[k], value_sems.at[k], k, True)
    clip = jnp.minimum(1.0, 1.0 / (norm_ref[0:1, 0:1] + 1e-06))

    def blend_rows(value, stage):
        def one(i, carry):
            spot = slab_at(i)
            value[spot, :] = muon_momentum * value[spot, :] + clip * stage[spot, :]
            return carry

        lax.fori_loop(0, value.shape[0] // SLAB, one, 0, unroll=UNROLL)

    def blend_columns(value, stage):
        def one(i, carry):
            spot = pl.ds(pl.multiple_of(i * LANES, LANES), LANES)
            value[:, spot] = muon_momentum * value[:, spot] + clip * stage[spot, :].T
            return carry

        lax.fori_loop(0, value.shape[1] // LANES, one, 0)

    aside = []

    def forward(p):
        crossing[p].wait_recv()
        spot = o_ref.at[across, rows(y, p)]
        aside.append(push(spot, spot, side_place))
        landing.append(push(spot, spot, near_place))

    def forward_side(p):
        aside[p].wait_recv()
        spot = o_ref.at[across, rows(1 - y, p)]
        landing.append(push(spot, spot, near_place))

    for k in range(MATRICES):
        whole_of(staged[k], load_sems.at[k]).wait()
        whole_of(values[k], value_sems.at[k]).wait()
        blend = blend_columns if k in COLUMNS else blend_rows
        blend(values[k], staged[k])
        matrices.move(carried[k], values[k], out_sems.at[k], k, False)

        def cut(i, carry, k=k):
            highs[k][slab_at(i), :], lows[k][slab_at(i), :] = split(values[k][slab_at(i), :])
            return carry

        lax.fori_loop(0, values[k].shape[0] // SLAB, cut, 0, unroll=UNROLL)

        @pl.when(far != k // 2)
        def _(k=k):
            pltpu.make_async_copy(highs[k], high_outs[k], split_sems.at[2 * k]).start()
            pltpu.make_async_copy(lows[k], low_outs[k], split_sems.at[2 * k + 1]).start()

        if k == 1:
            forward(0)
    for k in range(MATRICES):
        whole_of(values[k], out_sems.at[k]).wait()

        @pl.when(far == k // 2)
        def _(k=k):
            matrices.move(weights[k], values[k], value_sems.at[k], k, True)

    forward(1)
    landing[0].wait_recv()
    near_band = pltpu.make_async_copy(o_ref.at[near], pair_bands.at[1 - own % 2], band_sems.at[2])
    near_band.start()
    own_band.wait()
    near_band.wait()

    def pair(index):
        for side in range(2):

            @pl.when(far == side)
            def _(k=2 * side + index):
                assemble(pair_bands.at[index], factor_high, factor_low)
                whole_of(values[k], value_sems.at[k]).wait()

                def one(i, carry):
                    where = update(
                        k, i * BLK, factor_high, factor_low, highs[k], lows[k], values[k]
                    )
                    matrices.move(fresh[k], values[k], out_sems.at[k], k, False, *where)
                    return carry

                lax.fori_loop(0, size // BLK, one, 0)

    pair(0)
    forward(2)
    forward_side(0)
    pair(1)
    forward_side(1)
    for p in range(3, pieces):
        forward(p)
        forward_side(p - 1)
    forward_side(pieces - 1)
    keep.wait()
    for k in range(MATRICES):

        @pl.when(far == k // 2)
        def _(k=k):
            whole_of(values[k], out_sems.at[k]).wait()

        @pl.when(far != k // 2)
        def _(k=k):
            pltpu.make_async_copy(highs[k], high_outs[k], split_sems.at[2 * k]).wait()
            pltpu.make_async_copy(lows[k], low_outs[k], split_sems.at[2 * k + 1]).wait()

    for copy in landing[1:]:
        copy.wait_recv()
    for copy in copies:
        copy.wait_send()


def spread(norm, band, lines, others, moments, weights, number):
    pieces = 4
    size = band.shape[0]
    slots = 1 + 4 * pieces
    sub = lax.axis_size("narrow") // MATRICES
    vmem = pl.BlockSpec(memory_space=pltpu.VMEM)
    anywhere = pl.BlockSpec(memory_space=pl.ANY)
    operands = [*lines, *others]
    f32 = [jax.ShapeDtypeStruct(moment.shape, jnp.float32) for moment in moments]
    staged = [(moment.size // size, size) for moment in moments]
    flat = [(size, 3 * moments[0].shape[2])] + [moment.shape for moment in moments[1:]]
    low = [jax.ShapeDtypeStruct(shape, jnp.bfloat16) for shape in flat]
    outs = pl.pallas_call(
        functools.partial(spread_kernel, sub, pieces),
        out_shape=tuple(
            [jax.ShapeDtypeStruct((MATRICES,) + band.shape, jnp.float32)] + f32 + f32 + low + low
        ),
        in_specs=[vmem] * 2 + [anywhere] * (len(operands) + 8),
        out_specs=(anywhere,) * 17,
        scratch_shapes=[
            pltpu.VMEM((2,) + band.shape, jnp.float32),
            pltpu.VMEM((size, size), jnp.bfloat16),
            pltpu.VMEM((size, size), jnp.bfloat16),
        ]
        + [pltpu.VMEM(shape, jnp.float32) for shape in staged]
        + [pltpu.VMEM(shape, jnp.float32) for shape in flat]
        + [pltpu.VMEM(shape, jnp.bfloat16) for shape in flat] * 2
        + [pltpu.SemaphoreType.DMA((MATRICES,))] * 3
        + [
            pltpu.SemaphoreType.DMA((2 * MATRICES,)),
            pltpu.SemaphoreType.DMA((3,)),
            pltpu.SemaphoreType.DMA((slots,)),
            pltpu.SemaphoreType.DMA((slots,)),
        ],
        compiler_params=pltpu.CompilerParams(
            collective_id=number, has_side_effects=True, vmem_limit_bytes=58 * 2**20
        ),
        cost_estimate=pl.CostEstimate(
            flops=9 * size * size * size, bytes_accessed=80 * size * size, transcendentals=0
        ),
    )(norm, band, *operands, *moments, *weights)
    return outs[0], outs[1:5], outs[5:9], outs[9:13], outs[13:17]


def finish_kernel(sub, bands_any, *refs):
    ready, fresh, high_ins, low_ins, weights = (refs[4 * i : 4 * i + 4] for i in range(5))
    carried, results, refs = refs[20:24], refs[24:28], refs[28:]
    bands, factor_high, factor_low = refs[:3]
    news, values, highs, lows = refs[3:7], refs[7:11], refs[11:15], refs[15:19]
    news_sems, value_sems, split_sems, band_sems, carried_sems, out_sems = refs[19:]
    size = factor_high.shape[0]
    far = lax.axis_index("narrow") // sub // 2
    matrices = Matrices(weights[0].shape[2])
    for side in range(2):

        @pl.when(far == side)
        def _(side=side):
            for index in range(2):
                k = 2 * (1 - side) + index
                pltpu.make_async_copy(bands_any.at[k], bands.at[index], band_sems.at[index]).start()
                pltpu.make_async_copy(high_ins[k], highs[k], split_sems.at[2 * index]).start()
                pltpu.make_async_copy(low_ins[k], lows[k], split_sems.at[2 * index + 1]).start()
                matrices.move(weights[k], values[k], value_sems.at[k], k, True)
            for k in (2 * side, 2 * side + 1):
                matrices.move(fresh[k], values[k], value_sems.at[k], k, True)

    for k in range(MATRICES):
        matrices.move(ready[k], news[k], news_sems.at[k], k, True)
    for index in range(2):
        whole_of(bands.at[index], band_sems.at[index]).wait()
        if index:
            for k in range(MATRICES):
                whole_of(news[k], news_sems.at[k]).wait()
                matrices.move(carried[k], news[k], carried_sems.at[k], k, False)
        for side in range(2):

            @pl.when(far == side)
            def _(k=2 * (1 - side) + index, done=2 * side + index):
                if index:
                    for late in (done - 1, done):
                        whole_of(values[late], value_sems.at[late]).wait()
                        matrices.move(results[late], values[late], out_sems.at[late], late, False)
                assemble(bands.at[index], factor_high, factor_low)
                whole_of(highs[k], split_sems.at[2 * index]).wait()
                whole_of(lows[k], split_sems.at[2 * index + 1]).wait()
                whole_of(values[k], value_sems.at[k]).wait()

                def one(i, carry):
                    where = update(
                        k, i * BLK, factor_high, factor_low, highs[k], lows[k], values[k]
                    )
                    matrices.move(results[k], values[k], out_sems.at[k], k, False, *where)
                    return carry

                lax.fori_loop(0, size // BLK, one, 0)

    for k in range(MATRICES):
        whole_of(news[k], carried_sems.at[k]).wait()
        whole_of(values[k], out_sems.at[k]).wait()


def finish(bands, ready, fresh, highs, lows, weights):
    size = bands.shape[1]
    sub = lax.axis_size("narrow") // MATRICES
    anywhere = pl.BlockSpec(memory_space=pl.ANY)
    shapes = [jax.ShapeDtypeStruct(weight.shape, jnp.float32) for weight in weights]
    flat = [(size, 3 * weights[0].shape[2])] + [weight.shape for weight in weights[1:]]
    outs = pl.pallas_call(
        functools.partial(finish_kernel, sub),
        out_shape=tuple(shapes + shapes),
        in_specs=[anywhere] * 21,
        out_specs=(anywhere,) * 8,
        scratch_shapes=[
            pltpu.VMEM((2,) + bands.shape[1:], jnp.float32),
            pltpu.VMEM((size, size), jnp.bfloat16),
            pltpu.VMEM((size, size), jnp.bfloat16),
        ]
        + [pltpu.VMEM(shape, jnp.float32) for shape in flat] * 2
        + [pltpu.VMEM(shape, jnp.bfloat16) for shape in flat] * 2
        + [pltpu.SemaphoreType.DMA((MATRICES,))] * 6,
        compiler_params=pltpu.CompilerParams(vmem_limit_bytes=58 * 2**20),
        cost_estimate=pl.CostEstimate(
            flops=9 * size * size * size, bytes_accessed=60 * size * size, transcendentals=0
        ),
    )(bands, *ready, *fresh, *highs, *lows, *weights)
    return outs[:4], outs[4:]


def adam_update(weight, moment, square, gradient):
    moment_new = first_decay * moment + (1.0 - first_decay) * gradient
    square_new = second_decay * square + (1.0 - second_decay) * gradient * gradient
    moment_hat = moment_new / (1.0 - first_decay**STEP)
    square_hat = square_new / (1.0 - second_decay**STEP)
    weight_new = weight * (1.0 - adam_rate * weight_decay) - adam_rate * moment_hat / (
        jnp.sqrt(square_hat) + 1e-08
    )
    return (moment_new, square_new, weight_new)


def column_shifts(strip, column):
    rows = strip.shape[0]
    left = jnp.where(column == 0, 0.0, pltpu.roll(strip, 1, 0))
    right = jnp.where(column == rows - 1, 0.0, pltpu.roll(strip, rows - 1, 0))
    return (left, strip, right)


def tap_rows(shifts, taps):
    return [
        taps[3 * i] * shifts[0] + taps[3 * i + 1] * shifts[1] + taps[3 * i + 2] * shifts[2]
        for i in range(3)
    ]


def strip_at(index):
    return pl.ds(pl.multiple_of(index * GRID, GRID), GRID)


def convolve(load, taps, emit):
    shape = load(0).shape
    column = lax.broadcasted_iota(jnp.int32, shape, 0)

    def one(r, carry):
        above, here = carry
        upper, middle, lower = tap_rows(column_shifts(load(r), column), taps)
        emit(r - 1, here + lower)
        return (upper, above + middle)

    upper, middle, _ = tap_rows(column_shifts(load(0), column), taps)
    above, here = lax.fori_loop(1, GRID, one, (upper, middle))
    emit(GRID - 1, here)


def kernel_sums(load, weigh, width):
    column = lax.broadcasted_iota(jnp.int32, (GRID, width), 0)
    fold = lambda values: values.reshape(GRID // 8, 8, width).sum(axis=0)
    zero = jnp.zeros((8, width), jnp.float32)

    def one(r, carry):
        sums = carry
        shifts = column_shifts(load(r), column)
        later = weigh(jnp.minimum(r + 1, GRID - 1)) * jnp.where(r < GRID - 1, 1.0, 0.0)
        earlier = weigh(jnp.maximum(r - 1, 0)) * jnp.where(r > 0, 1.0, 0.0)
        terms = (later, weigh(r), earlier)
        return tuple(
            sums[3 * i + j] + fold(terms[i] * shifts[j]) for i in range(3) for j in range(3)
        )

    return lax.fori_loop(0, GRID, one, (zero,) * 9)


def middle_kernel(
    pieces,
    entry_ref,
    cotangent_ref,
    live_ref,
    gate_ref,
    expand_any,
    reduce_any,
    taps_ref,
    ffn_half_ref,
    grad_entry_any,
    reduce_share,
    expand_hold,
    expand_give,
    grad_taps_ref,
    expand_full,
    reduce_full,
    grad_ffn,
    upward,
    weight,
    active,
    grad_up,
    ffn,
    back,
    grad_reduce,
    grad_expand,
    ffn_inbox,
    near,
    far,
    held,
    local,
    reduce_held,
    reduce_beside,
    reduce_inbox,
    reduce_loads,
    expand_held,
    expand_beside,
    expand_inbox,
    expand_loads,
    give_sems,
    weight_sems,
    sends,
    arrivals,
):
    units = expand_any.shape[1]
    block = min(BLK, units // 2)
    steps = units // block
    groups = steps // 2
    y, z = wide_parts()
    count = lax.axis_size("wide") // 2
    far_bits = bits_of(lax.axis_size("narrow"))[1:]
    greet(
        [place_at("narrow", bit) for bit in [1] + far_bits]
        + [place_at("wide", bit) for bit in bits_of(lax.axis_size("wide"))]
    )

    def block_index(step):
        side = 1 - y if step < groups else y
        return side * groups + line_partner(z // (count // groups), groups - 1 - step % groups)

    fetches = []
    for step in range(steps):
        spot = pl.ds(pl.multiple_of(block_index(step) * block, LANES), block)
        pair = (
            pltpu.make_async_copy(
                expand_any.at[:, spot], expand_full.at[:, spot], weight_sems.at[step]
            ),
            pltpu.make_async_copy(
                reduce_any.at[spot, :], reduce_full.at[spot, :], weight_sems.at[steps + step]
            ),
        )
        for copy in pair:
            copy.start()
        fetches.append(pair)
    gate, live = gate_ref[...], live_ref[...]

    def gated(i, carry):
        spot = slab_at(i)
        result = cotangent_ref[spot, :].astype(jnp.float32) * live
        grad_ffn[spot, :] = (gate * result).astype(jnp.bfloat16)
        return carry

    lax.fori_loop(0, grad_ffn.shape[0] // SLAB, gated, 0, unroll=UNROLL)

    def work(spot, fresh):
        expand_low = expand_full[:, spot].astype(jnp.bfloat16)
        reduce_low = reduce_full[spot, :].astype(jnp.bfloat16)
        taps = [taps_ref[t : t + 1, spot] for t in range(9)]
        upward[...] = dot_of(entry_ref[...], expand_low, 1, 0)
        weight[...] = dot_of(grad_ffn[...], reduce_low, 1, 1)

        def emit_middle(r, values):
            inner = gelu_slope * (values + gelu_cubic * values * values * values)
            bent = jnp.tanh(inner)
            active[strip_at(r), :] = (0.5 * values * (1.0 + bent)).astype(jnp.bfloat16)
            turn = 0.5 * (1.0 + bent) + 0.5 * values * (1.0 - bent * bent) * (
                gelu_slope * (1.0 + 3.0 * gelu_cubic * values * values)
            )
            weight[strip_at(r), :] = weight[strip_at(r), :] * turn

        convolve(lambda r: upward[strip_at(r), :], taps, emit_middle)

        def emit_grad(r, values):
            grad_up[strip_at(r), :] = values.astype(jnp.bfloat16)

        convolve(lambda r: weight[strip_at(r), :], taps[::-1], emit_grad)
        sums = kernel_sums(
            lambda r: upward[strip_at(r), :], lambda r: weight[strip_at(r), :], block
        )
        for t in range(9):
            grad_taps_ref[t : t + 1, spot] = jnp.sum(sums[t], axis=0, keepdims=True)
        grad_reduce[spot, :] = dot_of(active[...], grad_ffn[...], 0, 0)
        grad_expand[spot, :] = dot_of(grad_up[...], entry_ref[...], 0, 0)
        if fresh:
            ffn[...] = dot_of(active[...], reduce_low, 1, 0)
            back[...] = dot_of(grad_up[...], expand_low, 1, 1)
        else:
            ffn[...] += dot_of(active[...], reduce_low, 1, 0)
            back[...] += dot_of(grad_up[...], expand_low, 1, 1)

    base = (len(far_bits) + 2) * pieces + 1
    reduce_sum = Scatter(
        grad_reduce, reduce_held, reduce_beside, reduce_inbox, sends, arrivals, reduce_loads, base
    )
    expand_sum = Scatter(
        grad_expand,
        expand_held,
        expand_beside,
        expand_inbox,
        sends,
        arrivals,
        expand_loads,
        base + Scatter.slots(),
    )
    for step in range(groups):
        for copy in fetches[step]:
            copy.wait()
        work(pl.ds(pl.multiple_of(block_index(step) * block, LANES), block), step == 0)
        size = count // groups
        ready = [(groups - 1 - step) * size + e for e in reversed(range(size))]
        for scatter in (reduce_sum, expand_sum):
            for e in ready:
                if scatter is reduce_sum or e >= count // 2:
                    scatter.give(e)
    for step in range(groups, steps):
        for copy in fetches[step]:
            copy.wait()

    def later(i, carry):
        side_block = line_partner_of(z // (count // groups), i, groups)
        work(pl.ds(pl.multiple_of((y * groups + side_block) * block, LANES), block), False)
        return carry

    lax.fori_loop(0, groups, later, 0)
    narrow = NarrowSum(
        far_bits, pieces, back, grad_entry_any, near, far, held, sends, arrivals, local, 0
    )
    narrow.start()
    core = lax.axis_index("narrow") % 2
    half = ffn.shape[0] // 2
    side_rows = lambda side: pl.ds(pl.multiple_of(side * half, 8), half)
    ffn_copy = send(
        ffn.at[side_rows(1 - core)], ffn_inbox, sends, arrivals, base - 1, place_at("narrow", 1)
    )
    for scatter in (reduce_sum, expand_sum):
        scatter.load()
    for p in range(pieces):
        narrow.begin(p)
    left = [list(reversed(range(count))), list(reversed(range(count // 2, count)))]
    gives = []
    for e in range(count // 2):
        gives.append(
            pltpu.make_async_copy(
                block_of(grad_expand, 1 - y, line_partner(z, e)), expand_give.at[e], give_sems.at[e]
            )
        )
        gives[e].start()
    scatters = (reduce_sum, expand_sum)
    scatters[0].step(left[0].pop(0))
    scatters[1].step(left[1].pop(0))
    ffn_copy.wait_recv()
    ffn_half_ref[...] = ffn[side_rows(core), :] + ffn_inbox[...]
    turns = [0, 1, 0]
    for b in range(len(far_bits)):
        for p in range(pieces):
            narrow.step(b, p)
            if turns and len(left[turns[0]]) > (turns[0] == 0):
                which = turns.pop(0)
                scatters[which].step(left[which].pop(0))
    for which in range(2):
        while left[which]:
            scatters[which].step(left[which].pop(0))
    for e in range(count // 2):
        expand_sum.loads[e].wait()
    expand_sum.copies[("z", count // 2)].wait_recv()
    expand_held[0] = expand_held[0] + expand_inbox[count // 2 - 1]
    outs = [
        pltpu.make_async_copy(reduce_held.at[0], reduce_share, reduce_loads.at[0]),
        pltpu.make_async_copy(
            expand_held.at[pl.ds(0, count // 2)], expand_hold, expand_loads.at[0]
        ),
    ]
    for out in outs:
        out.start()
    outs += gives
    narrow.finish()
    ffn_copy.wait_send()
    for scatter in scatters:
        scatter.finish()
    for out in outs:
        out.wait()


def line_partner_of(place, index, count):
    flipped = 0 * place
    for bit in bits_of(count):
        one, two = (place // bit) % 2, (index // bit) % 2
        flipped = flipped + (one + two - 2 * one * two) * bit
    return flipped


def middle(entry, cotangent, live, gate, expand, reduce, taps, number):
    tokens, width = entry.shape
    units = expand.shape[1]
    block = min(BLK, units // 2)
    steps = units // block
    pieces = 4
    narrow_bits = bits_of(lax.axis_size("narrow"))
    slots = (len(narrow_bits) + 1) * pieces + 1 + 2 * Scatter.slots()
    vmem = pl.BlockSpec(memory_space=pltpu.VMEM)
    anywhere = pl.BlockSpec(memory_space=pl.ANY)
    f32 = lambda *shape: jax.ShapeDtypeStruct(shape, jnp.float32)
    wide = lambda *shape: pltpu.VMEM(shape, jnp.float32)
    low = lambda *shape: pltpu.VMEM(shape, jnp.bfloat16)
    share = block_shape((units, width))
    line = lax.axis_size("wide") // 2
    return pl.pallas_call(
        functools.partial(middle_kernel, pieces),
        out_shape=(
            f32(tokens // 2, width),
            f32(tokens, width),
            f32(*share),
            f32(line // 2, *share),
            f32(line // 2, *share),
            f32(9, units),
        ),
        in_specs=[vmem, vmem, vmem, vmem, anywhere, anywhere, vmem],
        out_specs=(vmem,) + (anywhere,) * 4 + (vmem,),
        scratch_shapes=[
            wide(width, units),
            wide(units, width),
            low(tokens, width),
            wide(tokens, block),
            wide(tokens, block),
            low(tokens, block),
            low(tokens, block),
            wide(tokens, width),
            wide(tokens, width),
            wide(units, width),
            wide(units, width),
            wide(tokens // 2, width),
        ]
        + narrow_scratch((tokens, width), pieces)
        + scatter_scratch((units, width)) * 2
        + [
            pltpu.SemaphoreType.DMA((line // 2,)),
            pltpu.SemaphoreType.DMA((2 * steps,)),
            pltpu.SemaphoreType.DMA((slots,)),
            pltpu.SemaphoreType.DMA((slots,)),
        ],
        compiler_params=pltpu.CompilerParams(
            collective_id=number, has_side_effects=True, vmem_limit_bytes=60 * 2**20
        ),
        cost_estimate=pl.CostEstimate(
            flops=12 * tokens * width * units,
            bytes_accessed=200 * tokens * width,
            transcendentals=tokens * units,
        ),
    )(entry, cotangent, live, gate, expand, reduce, taps)


def norm_strip(values):
    average = jnp.mean(values, axis=-1, keepdims=True)
    centred = values - average
    spread_of = jnp.mean(centred * centred, axis=-1, keepdims=True)
    inverse = lax.rsqrt(spread_of + 1e-06)
    return centred * inverse, inverse


def slab_at(index):
    return pl.ds(pl.multiple_of(index * SLAB, SLAB), SLAB)


def fold_rows(values):
    return values.reshape(values.shape[0] // 8, 8, values.shape[1]).sum(axis=0)


def mixer_kernel_forward(tokens_ref, shift_ref, scale_ref, taps_ref, out_ref, entered):
    stretch = 1.0 + scale_ref[...]
    offset = shift_ref[...]

    def enter(r, carry):
        normed, _ = norm_strip(tokens_ref[slab_at(r), :].astype(jnp.float32))
        entered[slab_at(r), :] = normed * stretch + offset
        return carry

    rows, width = tokens_ref.shape
    lax.fori_loop(0, rows // SLAB, enter, 0, unroll=UNROLL)
    for start in range(0, width, BLK):
        lanes = pl.ds(start, BLK)

        def emit(r, values, lanes=lanes):
            out_ref[strip_at(r), lanes] = values.astype(jnp.bfloat16)

        taps = [taps_ref[t : t + 1, lanes] for t in range(9)]
        convolve(lambda r, lanes=lanes: entered[strip_at(r), lanes], taps, emit)


def mixer_forward(tokens, shift, scale, taps):
    rows, width = tokens.shape
    vmem = pl.BlockSpec(memory_space=pltpu.VMEM)
    return pl.pallas_call(
        mixer_kernel_forward,
        out_shape=jax.ShapeDtypeStruct((rows, width), jnp.bfloat16),
        in_specs=[vmem] * 4,
        out_specs=vmem,
        scratch_shapes=[pltpu.VMEM((rows, width), jnp.float32)],
        compiler_params=pltpu.CompilerParams(vmem_limit_bytes=40 * 2**20),
        cost_estimate=pl.CostEstimate(
            flops=40 * rows * width, bytes_accessed=4 * rows * width, transcendentals=0
        ),
    )(tokens, shift, scale, taps)


def mixer_kernel_backward(
    tokens_ref,
    shift_ref,
    scale_ref,
    taps_ref,
    grad_mixed_ref,
    grad_hidden_ref,
    out_ref,
    grad_taps_ref,
    grad_shift_ref,
    grad_scale_ref,
    normed_ref,
    back_ref,
    inverse_ref,
    wait_tokens,
    wait_mixed,
    wait_hidden,
):
    width = tokens_ref.shape[1]
    stretch = 1.0 + scale_ref[...]
    wait_tokens()

    def enter(r, carry):
        normed, inverse = norm_strip(tokens_ref[slab_at(r), :].astype(jnp.float32))
        normed_ref[slab_at(r), :] = normed
        inverse_ref[slab_at(r), :] = jnp.broadcast_to(inverse, (SLAB, LANES))
        return carry

    rows = tokens_ref.shape[0]
    lax.fori_loop(0, rows // SLAB, enter, 0, unroll=UNROLL)
    wait_mixed()
    for start in range(0, width, BLK):
        lanes = pl.ds(start, BLK)
        taps = [taps_ref[t : t + 1, lanes] for t in range(9)]
        stretch_part = 1.0 + scale_ref[:, lanes]
        offset_part = shift_ref[:, lanes]

        def emit(r, values, lanes=lanes):
            back_ref[strip_at(r), lanes] = values

        def entered(r, lanes=lanes, stretch_part=stretch_part, offset_part=offset_part):
            return normed_ref[strip_at(r), lanes] * stretch_part + offset_part

        weigh = lambda r, lanes=lanes: grad_mixed_ref[strip_at(r), lanes]
        convolve(weigh, taps[::-1], emit)
        sums = kernel_sums(entered, weigh, BLK)
        for t in range(9):
            grad_taps_ref[t : t + 1, lanes] = jnp.sum(sums[t], axis=0, keepdims=True)

    def leave(r, carry):
        shifts, scales = carry
        normed = normed_ref[slab_at(r), :]
        back = back_ref[slab_at(r), :]
        stretched = back * stretch
        first = jnp.mean(stretched, axis=-1, keepdims=True)
        second = jnp.mean(stretched * normed, axis=-1, keepdims=True)
        inverse = inverse_ref[slab_at(r), :][:, :1]
        out = grad_hidden_ref[slab_at(r), :] + (stretched - first - normed * second) * inverse
        out_ref[slab_at(r), :] = out.astype(jnp.bfloat16)
        return shifts + fold_rows(back), scales + fold_rows(back * normed)

    wait_hidden()
    zero = jnp.zeros((8, width), jnp.float32)
    shifts, scales = lax.fori_loop(0, rows // SLAB, leave, (zero, zero), unroll=UNROLL)
    grad_shift_ref[...] = jnp.sum(shifts, axis=0, keepdims=True)
    grad_scale_ref[...] = jnp.sum(scales, axis=0, keepdims=True)


def dot_of(left, right, left_axis, right_axis):
    return lax.dot_general(
        left,
        right,
        (((left_axis,), (right_axis,)), ((), ())),
        preferred_element_type=jnp.float32,
    )


def head_only(values, head):
    lane = lax.broadcasted_iota(jnp.int32, values.shape, 1)
    return jnp.where(lane // HEAD == head, values, jnp.zeros_like(values))


def attend_kernel(
    mixed_ref, attend_ref, triple_ref, context_ref, logsum_ref, low_ref, turned, values_t
):
    tokens = mixed_ref.shape[0]
    width = context_ref.shape[1]
    for j in range(3):
        columns = pl.ds(j * width, width)
        low_ref[:, columns] = attend_ref[j].astype(jnp.bfloat16)
        triple_ref[:, columns] = dot_of(mixed_ref[...], low_ref[:, columns], 1, 0).astype(
            jnp.bfloat16
        )
    values_t[...] = triple_ref[:, pl.ds(2 * width, width)].T
    scale = jnp.bfloat16(HEAD ** (-0.5))
    for head in range(width // HEAD):
        pair = head * HEAD // LANES * LANES
        inside = head % (LANES // HEAD)

        def one(block, carry, head=head, pair=pair, inside=inside):
            spot = pl.ds(pl.multiple_of(block * QUERIES, QUERIES), QUERIES)
            queries = head_only(triple_ref[spot, pl.ds(pair, LANES)], inside) * scale
            scores = dot_of(triple_ref[:, pl.ds(width + pair, LANES)], queries, 1, 1)
            peak = jnp.max(scores, axis=0, keepdims=True)
            weights = jnp.exp(scores - peak)
            total = jnp.sum(weights, axis=0, keepdims=True)
            soft_low = (weights * (1.0 / total)).astype(jnp.bfloat16)
            turned[pl.ds(head * HEAD, HEAD), spot] = dot_of(
                values_t[pl.ds(head * HEAD, HEAD), :], soft_low, 1, 0
            )
            logsum_ref[pl.ds(head, 1), spot] = peak + jnp.log(total)
            return carry

        lax.fori_loop(0, tokens // QUERIES, one, 0)
    context_ref[...] = turned[...].T.astype(jnp.bfloat16)


def attend(mixed, attend_weight):
    tokens, width = mixed.shape
    own = attend_weight.shape[2]
    vmem = pl.BlockSpec(memory_space=pltpu.VMEM)
    return pl.pallas_call(
        attend_kernel,
        out_shape=(
            jax.ShapeDtypeStruct((tokens, 3 * own), jnp.bfloat16),
            jax.ShapeDtypeStruct((tokens, own), jnp.bfloat16),
            jax.ShapeDtypeStruct((8, tokens), jnp.float32),
            jax.ShapeDtypeStruct((width, 3 * own), jnp.bfloat16),
        ),
        in_specs=[vmem] * 2,
        out_specs=(vmem,) * 4,
        scratch_shapes=[
            pltpu.VMEM((own, tokens), jnp.float32),
            pltpu.VMEM((own, tokens), jnp.bfloat16),
        ],
        compiler_params=pltpu.CompilerParams(vmem_limit_bytes=40 * 2**20),
        cost_estimate=pl.CostEstimate(
            flops=16 * tokens * tokens * own,
            bytes_accessed=12 * tokens * width,
            transcendentals=tokens * tokens * own // HEAD,
        ),
    )(mixed, attend_weight)


def narrow_hops():
    return [("narrow", bit) for bit in reversed(bits_of(lax.axis_size("narrow")))]


def narrow_position(item):
    n = lax.axis_index("narrow")
    position = 0
    for index, (_, bit) in enumerate(narrow_hops()):
        value = (n // bit) % 2
        if (item >> index) % 2:
            value = 1 - value
        position = position + value * 2**index
    return position


def entry_kernel(
    pieces,
    context_ref,
    tokens_ref,
    output_ref,
    gate_ref,
    shift_ref,
    scale_ref,
    branch_any,
    hidden_any,
    entry_ref,
    branch_ref,
    hidden_ref,
    out_sems,
    slots,
    output_low,
    output_inbox,
    sends,
    arrivals,
):
    rows, own = context_ref.shape
    step = rows // pieces
    hops = narrow_hops()
    count = 2 ** len(hops)
    greet([place_at(axis, bit) for axis, bit in hops])
    chunk = lambda p: pl.ds(p * step, step)
    slots[narrow_position(0)] = context_ref[...].astype(jnp.float32)
    output_copy = send(
        output_ref, output_inbox, sends, arrivals, pieces * (count - 1), place_at("narrow", 1)
    )
    gathers = []
    for p in range(pieces):
        spot_of = lambda item, p=p: slots.at[narrow_position(item), chunk(p)]
        gathers.append(Gather(spot_of(0), spot_of, hops, sends, arrivals, p * (count - 1)))
        gathers[p].step(0)
    core = lax.axis_index("narrow") % 2
    half = output_ref.shape[0]
    output_low[pl.ds(pl.multiple_of(core * half, SLAB), half), :] = output_ref[...].astype(
        jnp.bfloat16
    )
    output_copy.wait_recv()
    output_low[pl.ds(pl.multiple_of((1 - core) * half, SLAB), half), :] = output_inbox[...].astype(
        jnp.bfloat16
    )
    gate, offset, stretch = gate_ref[...], shift_ref[...], 1.0 + scale_ref[...]
    outs = []
    for p in range(pieces):
        for item in gathers[p].order[1:]:
            gathers[p].step(item)
        branch = jnp.zeros((step, output_ref.shape[1]), jnp.float32)
        for position in range(count):
            branch = branch + dot_of(
                slots[position, chunk(p)].astype(jnp.bfloat16),
                output_low[pl.ds(position * own, own), :],
                1,
                0,
            )
        branch_ref[chunk(p), :] = branch

        def one(i, carry, p=p):
            spot = pl.ds(pl.multiple_of(p * step + i * SLAB, SLAB), SLAB)
            hidden = tokens_ref[spot, :].astype(jnp.float32) + gate * branch_ref[spot, :]
            hidden_ref[spot, :] = hidden
            normed, _ = norm_strip(hidden)
            entry_ref[spot, :] = (normed * stretch + offset).astype(jnp.bfloat16)
            return carry

        lax.fori_loop(0, step // SLAB, one, 0, unroll=UNROLL)
        for index, (src, dst) in enumerate(((branch_ref, branch_any), (hidden_ref, hidden_any))):
            outs.append(
                pltpu.make_async_copy(
                    src.at[chunk(p), :], dst.at[chunk(p), :], out_sems.at[2 * p + index]
                )
            )
            outs[-1].start()
    for gather in gathers:
        gather.finish()
    output_copy.wait_send()
    for out in outs:
        out.wait()


def enter(context, tokens, output_rows, gate, shift, scale, number):
    pieces = 4
    rows, own = context.shape
    width = tokens.shape[1]
    count = lax.axis_size("narrow")
    vmem = pl.BlockSpec(memory_space=pltpu.VMEM)
    slots = pieces * (count - 1) + 1
    return pl.pallas_call(
        functools.partial(entry_kernel, pieces),
        out_shape=(
            jax.ShapeDtypeStruct((rows, width), jnp.float32),
            jax.ShapeDtypeStruct((rows, width), jnp.float32),
            jax.ShapeDtypeStruct((rows, width), jnp.bfloat16),
        ),
        in_specs=[vmem] * 6,
        out_specs=(pl.BlockSpec(memory_space=pl.ANY),) * 2 + (vmem,),
        scratch_shapes=[
            pltpu.VMEM((rows, width), jnp.float32),
            pltpu.VMEM((rows, width), jnp.float32),
            pltpu.SemaphoreType.DMA((2 * pieces,)),
            pltpu.VMEM((count, rows, own), jnp.float32),
            pltpu.VMEM((width, width), jnp.bfloat16),
            pltpu.VMEM(output_rows.shape, jnp.float32),
            pltpu.SemaphoreType.DMA((slots,)),
            pltpu.SemaphoreType.DMA((slots,)),
        ],
        compiler_params=pltpu.CompilerParams(
            collective_id=number, has_side_effects=True, vmem_limit_bytes=40 * 2**20
        ),
        cost_estimate=pl.CostEstimate(
            flops=2 * rows * width * width, bytes_accessed=100 * rows * width, transcendentals=0
        ),
    )(context, tokens, output_rows, gate, shift, scale)


def all_rows(values):
    for _, bit in narrow_hops()[:-1]:
        side = (lax.axis_index("narrow") // bit) % 2
        other = permute(values, "narrow", bit)
        values = jnp.where(
            side == 0,
            jnp.concatenate([values, other], axis=0),
            jnp.concatenate([other, values], axis=0),
        )
    return values


def back_kernel(
    pieces,
    hidden_any,
    branch_any,
    grad_entry_any,
    cotangent_any,
    live_ref,
    scale_ref,
    gate_ref,
    mixed_ref,
    attend_ref,
    output_ref,
    triple_ref,
    context_ref,
    logsum_ref,
    reduce_share_ref,
    expand_hold,
    expand_give,
    grad_hidden_ref,
    grad_shift_ref,
    grad_scale_ref,
    grad_gate_ref,
    grad_mixed_any,
    attend_out_share,
    reduce_line,
    expand_line,
    expand_share,
    hidden,
    branch,
    grad_entry,
    cotangent,
    grad_branch,
    output_low,
    grad_context,
    keys_t,
    grad_queries_t,
    grad_keys,
    grad_values,
    grad_triple,
    near,
    far,
    held,
    local,
    scatter_held,
    scatter_beside,
    scatter_inbox,
    scatter_loads,
    output_held,
    output_beside,
    output_inbox,
    output_loads,
    rest_held,
    rest_beside,
    rest_inbox,
    rest_loads,
    load_sems,
    keep_sems,
    sends,
    arrivals,
):
    tokens, width = hidden.shape
    own = output_ref.shape[0]
    _, z = wide_parts()
    far_bits = bits_of(lax.axis_size("narrow"))[1:]
    greet(
        [place_at("narrow", bit) for bit in [1] + far_bits]
        + [place_at("wide", bit) for bit in bits_of(lax.axis_size("wide"))]
    )
    hops = line_hops()
    base = (len(far_bits) + 2) * pieces + Scatter.slots()

    def spot_in(line):
        def spot_of(item):
            spot = z
            for index, (_, bit) in enumerate(hops):
                if (item >> index) % 2:
                    spot = partner(spot, bit // 2)
            return line_block(line, spot)

        return spot_of

    gathers, keeps = [], []
    rest_base = base + 2 * (2 ** len(hops) - 1)
    rest = Scatter(
        None, rest_held, rest_beside, rest_inbox, sends, arrivals, rest_loads, rest_base,
        (expand_hold, expand_give),
    )
    rest.start()
    for index, (share, line) in enumerate(
        ((reduce_share_ref, reduce_line), (rest_held.at[0], expand_line))
    ):
        start = base + index * (2 ** len(hops) - 1)
        gathers.append(Gather(share, spot_in(line), hops, sends, arrivals, start))
        keeps.append(pltpu.make_async_copy(share, spot_in(line)(0), keep_sems.at[index]))
    gathers[0].step(0)
    keeps[0].start()
    step = tokens // pieces
    loads = []
    for p in range(pieces):
        spot = pl.ds(p * step, step)
        pairs = (
            (hidden_any, hidden),
            (branch_any, branch),
            (grad_entry_any, grad_entry),
            (cotangent_any, cotangent),
        )
        loads.append(
            [
                pltpu.make_async_copy(src.at[spot, :], dst.at[spot, :], load_sems.at[4 * p + i])
                for i, (src, dst) in enumerate(pairs)
            ]
        )
        for load in loads[p]:
            load.start()
    output_low[...] = output_ref[...].astype(jnp.bfloat16)
    stretch, gate, live = 1.0 + scale_ref[...], gate_ref[...], live_ref[...]

    def one_slab(r, carry):
        shifts, scales, gates = carry
        spot = slab_at(r)
        normed, inverse = norm_strip(hidden[spot, :])
        back = grad_entry[spot, :]
        stretched = back * stretch
        first = jnp.mean(stretched, axis=-1, keepdims=True)
        second = jnp.mean(stretched * normed, axis=-1, keepdims=True)
        grad = cotangent[spot, :].astype(jnp.float32) * live + (
            stretched - first - normed * second
        ) * inverse
        grad_hidden_ref[spot, :] = grad
        grad_branch[spot, :] = (gate * grad).astype(jnp.bfloat16)
        return (
            shifts + fold_rows(back),
            scales + fold_rows(back * normed),
            gates + fold_rows(branch[spot, :] * grad),
        )

    sums = (jnp.zeros((8, width), jnp.float32),) * 3
    for p in range(pieces):
        for load in loads[p]:
            load.wait()
        first_slab = p * step // SLAB
        sums = lax.fori_loop(
            first_slab, first_slab + step // SLAB, one_slab, sums, unroll=UNROLL
        )
    for ref, total in zip((grad_shift_ref, grad_scale_ref, grad_gate_ref), sums):
        ref[...] = jnp.sum(total, axis=0, keepdims=True)
    output_grad = branch.at[pl.ds(3 * own, own), :]
    output_grad[...] = dot_of(context_ref[...], grad_branch[...], 0, 0)
    output_sum = Scatter(
        output_grad,
        output_held,
        output_beside,
        output_inbox,
        sends,
        arrivals,
        output_loads,
        rest_base + rest.count * 2 - 1,
    )
    output_sum.start()
    for e in reversed(range(1, rest.count)):
        rest.step(e)
    grad_context[...] = dot_of(grad_branch[...], output_low[...], 1, 1).astype(jnp.bfloat16)
    keys_t[...] = triple_ref[:, pl.ds(own, own)].T
    grad_keys[...] = jnp.zeros_like(grad_keys)
    grad_values[...] = jnp.zeros_like(grad_values)
    scale = HEAD ** (-0.5)
    low_scale = jnp.bfloat16(scale)
    heads = own // HEAD
    for head in range(heads):
        pair = head * HEAD // LANES * LANES
        inside = head % (LANES // HEAD)
        lanes = pl.ds(pair, LANES)

        def one(block, carry, head=head, pair=pair, inside=inside, lanes=lanes):
            spot = pl.ds(pl.multiple_of(block * QUERIES, QUERIES), QUERIES)
            queries = head_only(triple_ref[spot, lanes], inside)
            back = head_only(grad_context[spot, lanes], inside)
            scores = dot_of(triple_ref[:, pl.ds(own + pair, LANES)], queries * low_scale, 1, 1)
            weights = jnp.exp(scores - logsum_ref[pl.ds(head, 1), spot])
            grad_weights = dot_of(triple_ref[:, pl.ds(2 * own + pair, LANES)], back, 1, 1)
            grad_values[:, lanes] += dot_of(weights.astype(jnp.bfloat16), back, 1, 0)
            inner = jnp.sum(weights * grad_weights, axis=0, keepdims=True)
            grad_low = (weights * (grad_weights - inner)).astype(jnp.bfloat16)
            grad_keys[:, lanes] += dot_of(grad_low, queries, 1, 0)
            grad_queries_t[pl.ds(head * HEAD, HEAD), spot] = dot_of(
                keys_t[pl.ds(head * HEAD, HEAD), :], grad_low, 1, 0
            )
            return carry

        lax.fori_loop(0, tokens // QUERIES, one, 0)
        if head == max(heads - 2, 0):
            gathers[0].step(gathers[0].order[1])
            rest.step(0)
            gathers[1].step(0)
            keeps[1].start()
            keeps.append(pltpu.make_async_copy(rest_held.at[0], expand_share, keep_sems.at[2]))
            keeps[2].start()
    grad_triple[:, pl.ds(0, own)] = (grad_queries_t[...].T * scale).astype(jnp.bfloat16)
    grad_triple[:, pl.ds(own, own)] = (grad_keys[...] * scale).astype(jnp.bfloat16)
    grad_triple[:, pl.ds(2 * own, own)] = grad_values[...].astype(jnp.bfloat16)
    mixed_partial, attend_grad = grad_entry, branch.at[pl.ds(0, 3 * own), :]
    mixed_partial[...] = dot_of(grad_triple[...], attend_ref[...], 1, 1)
    narrow = NarrowSum(
        far_bits, pieces, mixed_partial, grad_mixed_any, near, far, held, sends, arrivals, local, 0
    )
    narrow.start()
    attend_grad[...] = dot_of(grad_triple[...], mixed_ref[...], 0, 0)
    blocks = lax.axis_size("wide")
    scatter = Scatter(
        attend_grad,
        scatter_held,
        scatter_beside,
        scatter_inbox,
        sends,
        arrivals,
        scatter_loads,
        (len(far_bits) + 2) * pieces,
    )
    for p in range(pieces):
        narrow.begin(p)
    scatter.start()
    for e in reversed(range(1, blocks // 2)):
        output_sum.step(e)
    left = list(reversed(range(blocks // 2)))
    forwards = [(0, item) for item in gathers[0].order[2:]] + [
        (1, item) for item in gathers[1].order[1:]
    ]
    urgent = [(1, gathers[1].order[1])]
    for b in range(len(far_bits)):
        for p in range(pieces):
            narrow.step(b, p)
            if urgent:
                index, item = urgent.pop(0)
                gathers[index].step(item)
            if len(left) > 1:
                scatter.step(left.pop(0))
    for index, item in forwards:
        if (index, item) != (1, gathers[1].order[1]):
            gathers[index].step(item)
    while left:
        scatter.step(left.pop(0))
    output_sum.step(0)
    first = 3 * own // blocks
    outs = [
        pltpu.make_async_copy(
            scatter.held.at[0], attend_out_share.at[pl.ds(0, first), :], scatter.local.at[0]
        ),
        pltpu.make_async_copy(
            output_sum.held.at[0],
            attend_out_share.at[pl.ds(first, own // blocks), :],
            output_sum.local.at[0],
        ),
    ]
    for out in outs:
        out.start()
    narrow.finish()
    scatter.finish()
    output_sum.finish()
    rest.finish()
    for gather in gathers:
        gather.finish()
    for keep in keeps:
        keep.wait()
    for out in outs:
        out.wait()


def back(
    hidden,
    branch,
    grad_entry,
    cotangent,
    live,
    scale,
    gate,
    mixed,
    attend_low,
    output_weight,
    triple,
    context,
    logsum,
    reduce_share,
    expand_hold,
    expand_give,
    number,
):
    tokens, width = hidden.shape
    own = output_weight.shape[0]
    pieces = 4
    line = lax.axis_size("wide") // 2
    narrow_bits = bits_of(lax.axis_size("narrow"))
    slots = (len(narrow_bits) + 1) * pieces + 2 * Scatter.slots() + 2 * (line - 1) + line - 1
    block = reduce_share.shape
    vmem = pl.BlockSpec(memory_space=pltpu.VMEM)
    anywhere = pl.BlockSpec(memory_space=pl.ANY)
    f32 = lambda *shape: jax.ShapeDtypeStruct(shape, jnp.float32)
    wide = lambda *shape: pltpu.VMEM(shape, jnp.float32)
    low = lambda *shape: pltpu.VMEM(shape, jnp.bfloat16)
    return pl.pallas_call(
        functools.partial(back_kernel, pieces),
        out_shape=(
            f32(tokens, width),
            f32(1, width),
            f32(1, width),
            f32(1, width),
            f32(tokens, width),
            f32(4 * own // (2 * line), width),
            f32(line * reduce_share.shape[0], width),
            f32(line * reduce_share.shape[0], width),
            f32(*block),
        ),
        in_specs=[anywhere] * 4 + [vmem] * 10 + [anywhere] * 2,
        out_specs=(vmem,) * 4 + (anywhere,) * 5,
        scratch_shapes=[
            wide(tokens, width),
            wide(max(tokens, 4 * own), width),
            wide(tokens, width),
            low(tokens, width),
            low(tokens, width),
            low(own, width),
            low(tokens, own),
            low(own, tokens),
            wide(own, tokens),
            wide(tokens, own),
            wide(tokens, own),
            low(tokens, 3 * own),
        ]
        + narrow_scratch((tokens, width), pieces)
        + scatter_scratch((3 * own, width))
        + scatter_scratch((own, width))
        + [
            wide(line // 2, *block),
            wide(line // 2, *block),
            wide(max(line // 2 - 1, 1), *block),
            pltpu.SemaphoreType.DMA((line // 2,)),
            pltpu.SemaphoreType.DMA((4 * pieces,)),
            pltpu.SemaphoreType.DMA((3,)),
            pltpu.SemaphoreType.DMA((slots,)),
            pltpu.SemaphoreType.DMA((slots,)),
        ],
        compiler_params=pltpu.CompilerParams(
            collective_id=number, has_side_effects=True, vmem_limit_bytes=60 * 2**20
        ),
        cost_estimate=pl.CostEstimate(
            flops=40 * tokens * tokens * own,
            bytes_accessed=150 * tokens * width,
            transcendentals=tokens * tokens * own // HEAD,
        ),
    )(
        hidden,
        branch,
        grad_entry,
        cotangent,
        live,
        scale,
        gate,
        mixed,
        attend_low,
        output_weight,
        triple,
        context,
        logsum,
        reduce_share,
        expand_hold,
        expand_give,
    )


def tail_kernel(
    tokens_any,
    shift_ref,
    scale_ref,
    taps_ref,
    grad_mixed_any,
    grad_hidden_any,
    hidden_any,
    ffn_half_any,
    ffn_across_any,
    cotangent_any,
    live_ref,
    gate_ref,
    rows_ref,
    split_ref,
    attend_out_ref,
    reduce_ref,
    expand_ref,
    reduce_line,
    tokens_grad_ref,
    block_out_ref,
    small_ref,
    norm_ref,
    line_ref,
    reduce_other,
    tokens_ref,
    grad_mixed_ref,
    grad_hidden_ref,
    hidden_ref,
    cotangent_ref,
    ffn_across_ref,
    ffn,
    normed_ref,
    back_ref,
    inverse_ref,
    grad_taps,
    grad_shift,
    grad_scale,
    slots,
    spare,
    spare_in,
    keep_sems,
    load_sems,
    sends,
    arrivals,
):
    width = tokens_ref.shape[1]
    core = lax.axis_index("narrow") % 2
    half = ffn.shape[0] // 2
    mine = pl.ds(pl.multiple_of(core * half, SLAB), half)
    loads = []
    for src, dst in (
        (ffn_half_any, ffn.at[mine, :]),
        (ffn_across_any, ffn_across_ref),
        (tokens_any, tokens_ref),
        (grad_mixed_any, grad_mixed_ref),
        (cotangent_any, cotangent_ref),
        (grad_hidden_any, grad_hidden_ref),
        (hidden_any, hidden_ref),
    ):
        loads.append(pltpu.make_async_copy(src, dst, load_sems.at[len(loads)]))
        loads[-1].start()
    wide_bits = bits_of(lax.axis_size("wide"))
    narrow_bits = bits_of(lax.axis_size("narrow"))
    greet(
        [place_at("wide", bit) for bit in wide_bits]
        + [place_at("narrow", bit) for bit in narrow_bits]
    )
    _, z = wide_parts()
    count = len(wide_bits)
    hops = line_hops()

    def spot_of(item):
        spot = z
        for index, (_, bit) in enumerate(hops):
            if (item >> index) % 2:
                spot = partner(spot, bit // 2)
        return line_block(line_ref, spot)

    gather = Gather(attend_out_ref, spot_of, hops, sends, arrivals, count + len(narrow_bits))
    gather.step(0)
    across = []

    def cross(part):
        extent = reduce_line.shape[0] // 2
        spot = pl.ds(part * extent, extent)
        slot = sends.shape[0] - 2 + part
        across.append(
            send(
                reduce_line.at[spot, :],
                reduce_other.at[spot, :],
                sends,
                arrivals,
                slot,
                place_at("wide", 1),
            )
        )

    cross(0)
    keep = pltpu.make_async_copy(attend_out_ref, spot_of(0), keep_sems.at[0])
    keep.start()
    loads[0].wait()
    loads[1].wait()
    ffn[mine, :] = ffn[mine, :] + ffn_across_ref[...]
    last = count + len(narrow_bits) + 2 ** len(hops) - 1
    ffn_copy = send(ffn.at[mine, :], ffn.at[mine, :], sends, arrivals, last, place_at("narrow", 1))
    mixer_kernel_backward(
        tokens_ref,
        shift_ref,
        scale_ref,
        taps_ref,
        grad_mixed_ref,
        grad_hidden_ref,
        tokens_grad_ref,
        grad_taps,
        grad_shift,
        grad_scale,
        normed_ref,
        back_ref,
        inverse_ref,
        loads[2].wait,
        loads[3].wait,
        loads[5].wait,
    )
    gather.step(gather.order[1])
    ffn_copy.wait_recv()
    loads[4].wait()
    gate, live = gate_ref[...], live_ref[...]

    def weigh(r, gates):
        spot = slab_at(r)
        return gates + fold_rows(ffn[spot, :] * (cotangent_ref[spot, :].astype(jnp.float32) * live))

    def leave(r, carry):
        spot = slab_at(r)
        block_out_ref[spot, :] = (live * (hidden_ref[spot, :] + gate * ffn[spot, :])).astype(
            jnp.bfloat16
        )
        return carry

    gates = lax.fori_loop(
        0, ffn.shape[0] // SLAB, weigh, jnp.zeros((8, width), jnp.float32), unroll=UNROLL
    )
    slots[0] = jnp.zeros(slots.shape[1:], jnp.float32)
    slots[0, 0:1, :] = grad_shift[...]
    slots[0, 1:2, :] = grad_scale[...]
    slots[0, 2:5, :] = rows_ref[...]
    slots[0, 5:6, :] = jnp.sum(gates, axis=0, keepdims=True)
    shared_rows = 6 + taps_ref.shape[0]
    slots[0, 6:shared_rows, :] = grad_taps[...]
    split_rows = split_ref.shape[0]
    slots[0, shared_rows : shared_rows + split_rows, :] = split_ref[...]
    squares = jnp.zeros((8, width), jnp.float32)
    for share in (attend_out_ref, reduce_ref, expand_ref):
        squares = squares + fold_rows(share[...] * share[...])
    end = shared_rows + split_rows
    slots[0, end : end + 1, :] = jnp.sum(squares, axis=0, keepdims=True)
    copies = []
    for b in range(count):
        copy = send(
            slots.at[b], slots.at[count + 1 + b], sends, arrivals, b, place_at("wide", wide_bits[b])
        )
        copies.append(copy)
        if b == 0:
            cross(1)
            loads[6].wait()
            lax.fori_loop(0, ffn.shape[0] // SLAB, leave, 0, unroll=UNROLL)
        copy.wait_recv()
        slots[b + 1] = slots[b] + slots[count + 1 + b]
    total = slots[count]
    small_ref[...] = total
    shared_part = total[:shared_rows]
    split_part = total[shared_rows:end]
    shared = jnp.sum(shared_part * shared_part)
    split_sum = jnp.sum(split_part * split_part) + jnp.sum(total[end : end + 1])
    spare[0] = jnp.full(spare.shape[1:], split_sum, jnp.float32)
    for b in range(len(narrow_bits)):
        copy = send(
            spare.at[b], spare_in.at[b], sends, arrivals, count + b, place_at("narrow", narrow_bits[b])
        )
        copies.append(copy)
        copy.wait_recv()
        spare[b + 1] = spare[b] + spare_in[b]
    norm_ref[...] = jnp.sqrt(spare[len(narrow_bits)] + shared)
    for item in gather.order[2:]:
        gather.step(item)
    keep.wait()
    gather.finish()
    ffn_copy.wait_send()
    for copy in across:
        copy.wait()
    for copy in copies:
        copy.wait_send()


def tail(
    tokens,
    shift,
    scale,
    taps,
    grad_mixed,
    grad_hidden,
    hidden,
    ffn_half,
    ffn_across,
    cotangent,
    live,
    gate,
    table_rows,
    split_rows,
    shares,
    reduce_line,
    number,
):
    rows, width = tokens.shape
    wide_bits = bits_of(lax.axis_size("wide"))
    narrow_bits = bits_of(lax.axis_size("narrow"))
    count = len(wide_bits)
    line = lax.axis_size("wide") // 2
    total = count + len(narrow_bits) + line + 2
    small = -(-(6 + taps.shape[0] + split_rows.shape[0] + 1) // 8) * 8
    vmem = pl.BlockSpec(memory_space=pltpu.VMEM)
    anywhere = pl.BlockSpec(memory_space=pl.ANY)
    f32 = lambda *shape: jax.ShapeDtypeStruct(shape, jnp.float32)
    low = lambda *shape: jax.ShapeDtypeStruct(shape, jnp.bfloat16)
    wide = lambda *shape: pltpu.VMEM(shape, jnp.float32)
    return pl.pallas_call(
        tail_kernel,
        out_shape=(
            low(rows, width),
            low(rows, width),
            f32(small, width),
            f32(8, LANES),
            f32(line * shares[0].shape[0], width),
            f32(*reduce_line.shape),
        ),
        in_specs=[anywhere] + [vmem] * 3 + [anywhere] * 6 + [vmem] * 7 + [anywhere],
        out_specs=(vmem,) * 4 + (anywhere,) * 2,
        scratch_shapes=[
            pltpu.VMEM((rows, width), jnp.bfloat16),
            wide(rows, width),
            wide(rows, width),
            wide(rows, width),
            pltpu.VMEM((rows, width), jnp.bfloat16),
            wide(rows // 2, width),
            wide(rows, width),
            wide(rows, width),
            wide(rows, width),
            wide(rows, LANES),
            wide(9, width),
            wide(1, width),
            wide(1, width),
            wide(2 * count + 1, small, width),
            wide(len(narrow_bits) + 1, 8, LANES),
            wide(len(narrow_bits), 8, LANES),
            pltpu.SemaphoreType.DMA((1,)),
            pltpu.SemaphoreType.DMA((7,)),
            pltpu.SemaphoreType.DMA((total,)),
            pltpu.SemaphoreType.DMA((total,)),
        ],
        compiler_params=pltpu.CompilerParams(
            collective_id=number, has_side_effects=True, vmem_limit_bytes=56 * 2**20
        ),
        cost_estimate=pl.CostEstimate(
            flops=100 * rows * width, bytes_accessed=60 * rows * width, transcendentals=0
        ),
    )(
        tokens,
        shift,
        scale,
        taps,
        grad_mixed,
        grad_hidden,
        hidden,
        ffn_half,
        ffn_across,
        cotangent,
        live,
        gate,
        table_rows,
        split_rows,
        *shares,
        reduce_line,
    )


def local(
    tokens,
    conditions,
    item_live,
    cotangent,
    modulation_table,
    mixer_kernel,
    hidden_kernel,
    attend_weight,
    output_weight,
    expand_weight,
    reduce_weight,
    attend_moment,
    output_moment,
    expand_moment,
    reduce_moment,
    table_first,
    table_second,
    mixer_first,
    mixer_second,
    hidden_first,
    hidden_second,
):
    live_mask = item_live.astype(jnp.float32)[:, None, None]
    modulation = modulation_table[None] + conditions
    shift_one = modulation[:, 0:1]
    scale_one = modulation[:, 1:2]
    gate_one = modulation[:, 2:3]
    shift_two = modulation[:, 3:4]
    scale_two = modulation[:, 4:5]
    gate_two = modulation[:, 5:6]
    width = tokens.shape[2]
    flat_tokens = tokens.reshape(-1, width)
    mixed_low = mixer_forward(flat_tokens, shift_one[0], scale_one[0], mixer_kernel)
    three = lambda matrix: jnp.transpose(matrix, (1, 0, 2))
    triple, context, logsum, attend_low = attend(mixed_low, three(attend_weight))
    output_rows, context = together(all_rows(output_weight), context)
    branch, hidden, entry_low = enter(
        context, flat_tokens, output_rows, gate_one[0], shift_two[0], scale_two[0], 1
    )
    flat_cotangent = cotangent.reshape(-1, width)
    live_row = jnp.broadcast_to(live_mask[0], (1, width))
    ffn_half, grad_entry, reduce_share, expand_hold, expand_give, grad_hidden_kernel = middle(
        entry_low,
        flat_cotangent,
        live_row,
        gate_two[0],
        expand_weight,
        reduce_weight,
        hidden_kernel,
        2,
    )
    grad_entry, reduce_share, expand_hold, ffn_half = together(
        grad_entry, reduce_share, expand_hold, ffn_half
    )
    for bit in bits_of(lax.axis_size("narrow"))[1:-1]:
        ffn_half = ffn_half + permute(ffn_half, "narrow", bit)
    ffn_across = permute(ffn_half, "narrow", lax.axis_size("narrow") // 2)
    (
        grad_hidden,
        grad_shift_two,
        grad_scale_two,
        grad_gate_one,
        grad_mixed,
        attend_out_share,
        reduce_line,
        expand_line,
        expand_share,
    ) = back(
        hidden,
        branch,
        grad_entry,
        flat_cotangent,
        live_row,
        scale_two[0],
        gate_one[0],
        mixed_low,
        attend_low,
        output_weight,
        triple,
        context,
        logsum,
        reduce_share,
        expand_hold,
        expand_give,
        3,
    )
    ffn_across, grad_mixed = together(ffn_across, grad_mixed)
    shared_rows = modulation_table.shape[0] + mixer_kernel.shape[0]
    hidden_rows = -(-grad_hidden_kernel.size // width)
    padding = hidden_rows * width - grad_hidden_kernel.size
    hidden_flat = jnp.pad(grad_hidden_kernel.reshape(-1), (0, padding))
    tokens_gradient, block_out, small, norm, attend_out_line, reduce_other = tail(
        flat_tokens,
        shift_one[0],
        scale_one[0],
        mixer_kernel,
        grad_mixed,
        grad_hidden,
        hidden,
        ffn_half,
        ffn_across,
        flat_cotangent,
        live_row,
        gate_two[0],
        jnp.concatenate([grad_gate_one, grad_shift_two, grad_scale_two], axis=0),
        hidden_flat.reshape(hidden_rows, width),
        [attend_out_share, reduce_share, expand_share],
        reduce_line,
        4,
    )
    tokens_gradient = tokens_gradient.reshape(tokens.shape)
    block_out = block_out.reshape(tokens.shape)
    summed_table = small[: modulation_table.shape[0]]
    summed_mixer = small[modulation_table.shape[0] : shared_rows]
    summed_hidden = small[shared_rows : shared_rows + hidden_rows].reshape(-1)
    summed_hidden = summed_hidden[: hidden_kernel.size].reshape(hidden_kernel.shape)
    gradient_norm = norm[0, 0]
    clip_factor = jnp.minimum(1.0, 1.0 / (gradient_norm + 1e-06))
    gramian, expand_first = gram_whole(
        norm,
        [attend_out_line, expand_line, reduce_line],
        [three(attend_moment), output_moment, expand_moment, reduce_moment],
        5,
    )
    gramian, expand_line, attend_out_line = together(gramian, expand_line, attend_out_line)
    expand_other = permute(expand_line[expand_line.shape[0] // 2 :], "wide", 1)
    attend_out_other = permute(attend_out_line, "wide", 1)
    factor = polar_factor(gramian)
    factor, expand_other, attend_out_other = together(factor, expand_other, attend_out_other)
    weights = [three(attend_weight), output_weight, expand_weight, reduce_weight]
    bands, ready, fresh, highs, lows = spread(
        norm,
        factor,
        [attend_out_line, expand_line, reduce_line],
        [attend_out_other, expand_first, expand_other, reduce_other],
        [three(attend_moment), output_moment, expand_moment, reduce_moment],
        weights,
        6,
    )
    carried, results = finish(bands, ready, fresh, highs, lows, weights)
    attend_carried = jnp.transpose(carried[0], (1, 0, 2))
    attend_result = jnp.transpose(results[0], (1, 0, 2))
    table_moment, table_square, table_result = adam_update(
        modulation_table, table_first, table_second, clip_factor * summed_table
    )
    mixer_moment, mixer_square, mixer_result = adam_update(
        mixer_kernel, mixer_first, mixer_second, clip_factor * summed_mixer
    )
    hidden_moment, hidden_square, hidden_result = adam_update(
        hidden_kernel, hidden_first, hidden_second, clip_factor * summed_hidden
    )
    return (
        block_out,
        tokens_gradient,
        gradient_norm,
        attend_carried,
        carried[1],
        carried[2],
        carried[3],
        attend_result,
        results[1],
        results[2],
        results[3],
        table_moment,
        table_square,
        table_result,
        mixer_moment,
        mixer_square,
        mixer_result,
        hidden_moment,
        hidden_square,
        hidden_result,
    )


def solution(mesh):
    placed = (
        P("wide", None, None),
        P("wide", None, None),
        P("wide"),
        P("wide", None, None),
        P(),
        P(),
        P(None, "narrow"),
        P(None, None, "narrow"),
        P("narrow", None),
        P(None, "narrow"),
        P("narrow", None),
        P(None, None, "narrow"),
        P("narrow", None),
        P(None, "narrow"),
        P("narrow", None),
        P(),
        P(),
        P(),
        P(),
        P(None, "narrow"),
        P(None, "narrow"),
    )
    return jax.shard_map(
        local,
        mesh=mesh,
        in_specs=placed,
        out_specs=(
            P("wide", None, None),
            P("wide", None, None),
            P(),
            P(None, None, "narrow"),
            P("narrow", None),
            P(None, "narrow"),
            P("narrow", None),
            P(None, None, "narrow"),
            P("narrow", None),
            P(None, "narrow"),
            P("narrow", None),
            P(),
            P(),
            P(),
            P(),
            P(),
            P(),
            P(None, "narrow"),
            P(None, "narrow"),
            P(None, "narrow"),
        ),
        check_vma=False,
    )
```

```python
import functools
import math

import jax
import jax.numpy as jnp
from jax import lax
from jax.experimental import pallas as pl
from jax.experimental.pallas import tpu as pltpu
from jax.sharding import PartitionSpec as P

D = 1024
HEAD = 64
FF = 4096
GRID = 32
NEWTON = 5
STEP = 10


first_decay = 0.9
second_decay = 0.999
adam_rate = 0.3
muon_rate = 0.15
muon_momentum = 0.5
weight_decay = 0.01
newton_terms = (3.4445, -4.775, 2.0315)
gelu_slope = 0.7978845608
gelu_cubic = 0.044715


MESH = pl.DeviceIdType.MESH
BLK = 256
LANES = 128
SLAB = 16
QUERIES = 512
UNROLL = 4
MATRICES = 4
COLUMNS = (0, 2)


def partner(index, bit):
    return index + (1 - 2 * ((index // bit) % 2)) * bit


def bits_of(count):
    found = []
    bit = 1
    while bit < count:
        found.append(bit)
        bit *= 2
    return found


def place_at(axis, bit):
    place = {"wide": lax.axis_index("wide"), "narrow": lax.axis_index("narrow")}
    place[axis] = partner(place[axis], bit)
    return (place["wide"], place["narrow"])


def greet(places):
    barrier = pltpu.get_barrier_semaphore()
    for place in places:
        pl.semaphore_signal(barrier, inc=1, device_id=place, device_id_type=MESH)
    pl.semaphore_wait(barrier, len(places))


def send(src, dst, sends, arrivals, slot, place):
    copy = pltpu.make_async_remote_copy(
        src_ref=src,
        dst_ref=dst,
        send_sem=sends.at[slot],
        recv_sem=arrivals.at[slot],
        device_id=place,
        device_id_type=MESH,
    )
    copy.start()
    return copy


def permute(values, axis, bit):
    size = lax.axis_size(axis)
    return lax.ppermute(values, axis, [(index, index ^ bit) for index in range(size)])


def together(*values):
    return lax.optimization_barrier(values)


def wide_parts():
    w = lax.axis_index("wide")
    return w % 2, w // 2


def line_partner(z, offset):
    for bit in bits_of(2 * offset):
        if (offset // bit) % 2:
            z = partner(z, bit)
    return z


def block_of(ref, y, z):
    count = lax.axis_size("wide") // 2
    rows = ref.shape[0] // (2 * count)
    return ref.at[pl.ds(pl.multiple_of((y * count + z) * rows, 8), rows), :]


def line_block(ref, z):
    rows = ref.shape[0] // (lax.axis_size("wide") // 2)
    return ref.at[pl.ds(pl.multiple_of(z * rows, 8), rows), :]


def block_shape(shape):
    return (shape[0] // lax.axis_size("wide"), shape[1])


class Scatter:
    def __init__(self, src, held, beside, inbox, sends, arrivals, local, base, blocks=None):
        self.src, self.held, self.beside, self.inbox = src, held, beside, inbox
        self.blocks = blocks
        self.sends, self.arrivals, self.local, self.base = sends, arrivals, local, base
        self.count = lax.axis_size("wide") // 2 if blocks is None else blocks[0].shape[0]
        self.copies = {}
        self.loads = {}

    @staticmethod
    def slots():
        return lax.axis_size("wide") - 1

    def load(self):
        y, z = wide_parts()
        for e in reversed(range(self.count)):
            own = self.blocks[0].at[e] if self.blocks else block_of(self.src, y, line_partner(z, e))
            self.loads[e] = pltpu.make_async_copy(own, self.held.at[e], self.local.at[e])
            self.loads[e].start()

    def give(self, e):
        y, z = wide_parts()
        self.copies[("y", e)] = send(
            self.blocks[1].at[e] if self.blocks else block_of(self.src, 1 - y, line_partner(z, e)),
            self.beside.at[e],
            self.sends,
            self.arrivals,
            self.base + e,
            place_at("wide", 1),
        )

    def start(self):
        self.load()
        for e in reversed(range(self.count)):
            self.give(e)

    def step(self, e):
        self.loads[e].wait()
        self.copies[("y", e)].wait_recv()
        self.held[e] = self.held[e] + self.beside[e]
        bit = 1
        while bit < self.count and e % (2 * bit) == 0:
            self.copies[("z", e + bit)].wait_recv()
            self.held[e] = self.held[e] + self.inbox[e + bit - 1]
            bit *= 2
        if e:
            low = e & -e
            self.copies[("z", e)] = send(
                self.held.at[e],
                self.inbox.at[e - 1],
                self.sends,
                self.arrivals,
                self.base + self.count + e - 1,
                place_at("wide", 2 * low),
            )

    def finish(self):
        for copy in self.copies.values():
            copy.wait_send()


def scatter_scratch(shape):
    count = lax.axis_size("wide") // 2
    block = block_shape(shape)
    return [
        pltpu.VMEM((count,) + block, jnp.float32),
        pltpu.VMEM((count,) + block, jnp.float32),
        pltpu.VMEM((max(count - 1, 1),) + block, jnp.float32),
        pltpu.SemaphoreType.DMA((count,)),
    ]


class Gather:
    def __init__(self, own, spot_of, hops, sends, arrivals, base):
        self.own, self.spot_of, self.hops = own, spot_of, hops
        self.sends, self.arrivals, self.base = sends, arrivals, base
        self.copies = {}
        last = 2 ** (len(hops) - 1)
        self.order = sorted(
            range(2 * last), key=lambda item: (item >= last, bin(item).count("1"), -item)
        )

    def step(self, item):
        if item:
            self.copies[item].wait_recv()
        for index in range(item.bit_length(), len(self.hops)):
            later = item + 2**index
            spot = self.spot_of(item)
            axis, bit = self.hops[index]
            self.copies[later] = send(
                spot if item else self.own,
                spot,
                self.sends,
                self.arrivals,
                self.base + later - 1,
                place_at(axis, bit),
            )

    def finish(self):
        for copy in self.copies.values():
            copy.wait_send()


def line_hops():
    return [("wide", bit) for bit in reversed(bits_of(lax.axis_size("wide"))) if bit > 1]


class NarrowSum:
    def __init__(self, far_bits, pieces, x, o, near, far, held, sends, arrivals, local, base):
        self.bits, self.pieces = far_bits, pieces
        self.x, self.o, self.near, self.far, self.held = x, o, near, far, held
        self.sends, self.arrivals, self.local, self.base = sends, arrivals, local, base
        self.rows = x.shape[0] // 2
        self.core = lax.axis_index("narrow") % 2
        self.copies = []
        self.cross = {}
        self.keeps = []

    def block(self, side, p):
        step = self.rows // self.pieces
        return pl.ds(pl.multiple_of(side * self.rows + p * step, 8), step)

    def push(self, src, dst, slot, bit):
        copy = send(
            src, dst, self.sends, self.arrivals, self.base + slot, place_at("narrow", bit)
        )
        self.copies.append(copy)
        return copy

    def start(self):
        self.first = [
            self.push(self.x.at[self.block(1 - self.core, p)], self.near.at[p], p, 1)
            for p in range(self.pieces)
        ]
        self.loads = [
            pltpu.make_async_copy(
                self.x.at[self.block(self.core, p)], self.held.at[0, p], self.local.at[p]
            )
            for p in range(self.pieces)
        ]
        for load in self.loads:
            load.start()

    def hop(self, b, p):
        slot = (b + 1) * self.pieces + p
        self.cross[(b, p)] = self.push(
            self.held.at[b, p], self.far.at[b, p], slot, self.bits[b]
        )

    def begin(self, p):
        self.loads[p].wait()
        self.first[p].wait_recv()
        self.held[0, p] = self.held[0, p] + self.near[p]
        self.hop(0, p)

    def step(self, b, p):
        self.cross[(b, p)].wait_recv()
        self.held[b + 1, p] = self.held[b, p] + self.far[b, p]
        if b + 1 < len(self.bits):
            self.hop(b + 1, p)
            return
        spot = self.o.at[self.block(self.core, p)]
        slot = (b + 2) * self.pieces + p
        self.keeps.append(self.push(self.held.at[b + 1, p], spot, slot, 1))
        keep = pltpu.make_async_copy(self.held.at[b + 1, p], spot, self.local.at[p])
        keep.start()
        self.loads[p] = keep

    def finish(self):
        for copy in self.keeps:
            copy.wait_recv()
        for keep in self.loads:
            keep.wait()
        for copy in self.copies:
            copy.wait_send()


def narrow_scratch(shape, pieces):
    count = len(bits_of(lax.axis_size("narrow"))) - 1
    step = shape[0] // (2 * pieces)
    return [
        pltpu.VMEM((pieces, step, shape[1]), jnp.float32),
        pltpu.VMEM((count, pieces, step, shape[1]), jnp.float32),
        pltpu.VMEM((count + 1, pieces, step, shape[1]), jnp.float32),
        pltpu.SemaphoreType.DMA((pieces,)),
    ]


def gram_kernel(
    norm_ref,
    attend_out_any,
    expand_any,
    reduce_any,
    attend_moment_any,
    output_moment_any,
    expand_moment_any,
    reduce_moment_any,
    band_ref,
    expand_beside,
    expand_later,
    attend_out,
    expand,
    reduce,
    attend_moment,
    output_moment,
    expand_moment,
    reduce_moment,
    *refs,
):
    highs, lows, refs = refs[:MATRICES], refs[MATRICES : 2 * MATRICES], refs[2 * MATRICES :]
    attend_turned, attend_blend, refs = refs[0], refs[1], refs[2:]
    twice, halves, inbox, block, load_sems, sends, arrivals, local = refs
    narrow_bits = bits_of(lax.axis_size("narrow"))
    wide_bits = bits_of(lax.axis_size("wide"))
    parts, rows = halves.shape[0], halves.shape[1]
    sub = parts // MATRICES
    size = attend_out.shape[1]
    hops = [("narrow", bit) for bit in bits_of(sub)]
    hops += [("wide", bit) for bit in reversed(wide_bits)]
    w, n = lax.axis_index("wide"), lax.axis_index("narrow")
    y, z = wide_parts()
    greet(
        [place_at("narrow", bit) for bit in narrow_bits]
        + [place_at("wide", bit) for bit in wide_bits]
    )
    early = expand_beside.shape[0]
    expand_copy = send(
        expand_any.at[pl.ds(0, early), :],
        expand_beside,
        sends,
        arrivals,
        sends.shape[0] - 1,
        place_at("wide", 1),
    )
    own_rows = lambda ref: ref.at[
        pl.ds(pl.multiple_of(y * (ref.shape[0] // 2), 8), ref.shape[0] // 2), :
    ]
    own_columns = lambda ref: ref.at[
        :, pl.ds(pl.multiple_of(y * (ref.shape[1] // 2), LANES), ref.shape[1] // 2)
    ]
    loads = []
    own = attend_moment_any.shape[2]
    for j in range(3):
        pltpu.make_async_copy(
            attend_moment_any.at[j], attend_moment.at[:, pl.ds(j * own, own)], load_sems.at[1]
        ).start()
    for src, dst in (
        (attend_out_any, attend_out),
        (None, None),
        (own_rows(output_moment_any), output_moment),
        (expand_any, expand),
        (own_columns(expand_moment_any), expand_moment),
        (reduce_any, reduce),
        (own_rows(reduce_moment_any), reduce_moment),
    ):
        if src is None:
            loads.append(pltpu.make_async_copy(attend_moment, attend_moment, load_sems.at[1]))
            continue
        loads.append(pltpu.make_async_copy(src, dst, load_sems.at[len(loads)]))
        loads[-1].start()
    clip = jnp.minimum(1.0, 1.0 / (norm_ref[0:1, 0:1] + 1e-06))
    count = halves.shape[1] * sub
    start = z * count
    lines = lax.axis_size("wide") // 2
    band = halves.shape[2]

    def blend(k, moment, gradient):
        total = highs[k].shape[0]

        def one(i, carry):
            spot = slab_at(i)
            highs[k][spot, :], lows[k][spot, :] = split(
                muon_momentum * moment[spot, :] + clip * gradient[spot, :]
            )
            return carry

        lax.fori_loop(0, total // SLAB, one, 0, unroll=UNROLL)

    def multiply(k):
        columns = pl.ds(pl.multiple_of(start, LANES), count)
        high, low = highs[k][:, columns], lows[k][:, columns]
        values = dot_of(high, highs[k][...], 0, 0) + (
            dot_of(high, lows[k][...], 0, 0) + dot_of(low, highs[k][...], 0, 0)
        )
        twice[:, :size] = values
        twice[:, size:] = values[:, :band]
        for s in range(sub):
            for at in range(0, rows, LANES):
                extent = min(LANES, rows)
                first = s * rows + at
                lanes = pl.ds(pl.multiple_of(start + first // LANES * LANES, LANES), band)
                halves[k * sub + s, at : at + extent, :] = twice[first : first + extent, lanes]

    share = attend_out.shape[0] // lines
    first_rows, second_rows = 3 * share // 4, share // 4
    loads[0].wait()
    loads[1].wait()
    loads[2].wait()
    for at in range(0, 3 * own, LANES):
        attend_turned[pl.ds(at, LANES), :] = attend_moment[:, pl.ds(at, LANES)].T
    offset = y * (3 * own // 2)
    for b in range(lines):
        gradient = attend_out[b * share : (b + 1) * share, :]
        spot = pl.ds(pl.multiple_of(offset + b * first_rows, 8), first_rows)
        attend_blend[pl.ds(b * first_rows, first_rows), :] = (
            muon_momentum * attend_turned[spot, :] + clip * gradient[:first_rows]
        )
        spot = pl.ds(b * second_rows, second_rows)
        output_moment[spot, :] = (
            muon_momentum * output_moment[spot, :] + clip * gradient[first_rows:]
        )

    def cut(k, values):
        def one(i, carry):
            spot = slab_at(i)
            highs[k][spot, :], lows[k][spot, :] = split(values[spot, :])
            return carry

        lax.fori_loop(0, highs[k].shape[0] // SLAB, one, 0, unroll=UNROLL)

    cut(0, attend_blend)
    multiply(0)
    loads[3].wait()
    later_copy = pltpu.make_async_copy(expand.at[pl.ds(early, early), :], expand_later, load_sems.at[3])
    later_copy.start()
    cut(1, output_moment)
    multiply(1)
    loads[4].wait()
    for at in range(0, expand.shape[0], LANES):
        spot = pl.ds(at, LANES)
        highs[2][spot, :], lows[2][spot, :] = split(
            muon_momentum * expand_moment[:, spot].T + clip * expand[spot, :]
        )
    multiply(2)
    loads[5].wait()
    loads[6].wait()
    blend(3, reduce_moment, reduce)
    multiply(3)
    half = rows // 2
    row_half = lambda side: pl.ds(pl.multiple_of(side * half, 8), half)
    slot = iter(range(sends.shape[0]))
    copies = []

    def push(src, dst, place):
        copies.append(send(src, dst, sends, arrivals, next(slot), place))
        return copies[-1]

    at = 0
    for bit in narrow_bits:
        value = (n // bit) % 2
        last = 2 * bit == parts
        waits = []
        for j in range(parts // (2 * bit)):
            mine = n % bit + value * bit + j * 2 * bit
            theirs = n % bit + (1 - value) * bit + j * 2 * bit
            for side in (1 - y, y) if last else (None,):
                spot = slice(None) if side is None else row_half(side)
                copy = push(
                    halves.at[theirs] if side is None else halves.at[theirs, spot],
                    inbox.at[at + j] if side is None else inbox.at[at + j, spot],
                    place_at("narrow", bit),
                )
                waits.append((copy, mine, at + j, spot))
        at += parts // (2 * bit)
        for copy, mine, where, spot in waits:
            copy.wait_recv()
            halves[mine, spot] = halves[mine, spot] + inbox[where, spot]
            if last and copy is waits[0][0]:
                side_copy = push(halves.at[n, row_half(1 - y)], block.at[0], place_at("wide", 1))
    side_copy.wait_recv()
    block[1] = halves[n, row_half(y)] + block[0]

    def spot_of(item):
        big, small = w, n % sub
        for index, (axis, bit) in enumerate(hops):
            if (item >> index) % 2:
                if axis == "wide":
                    big = partner(big, bit)
                else:
                    small = partner(small, bit)
        first = ((big // 2) * (2 * sub) + small * 2 + big % 2) * half
        return band_ref.at[pl.ds(pl.multiple_of(first, 8), half), :]

    keep = pltpu.make_async_copy(block.at[1], spot_of(0), local.at[0])
    keep.start()
    gather = Gather(block.at[1], spot_of, hops, sends, arrivals, next(slot))
    for item in gather.order:
        gather.step(item)
    keep.wait()
    gather.finish()
    expand_copy.wait()
    later_copy.wait()
    for copy in copies:
        copy.wait_send()


def gram_whole(norm, lines, moments, number):
    narrow_bits = bits_of(lax.axis_size("narrow"))
    wide_bits = bits_of(lax.axis_size("wide"))
    size = lines[0].shape[1]
    sub = lax.axis_size("narrow") // MATRICES
    parts = lax.axis_size("narrow")
    count = 2 * size // lax.axis_size("wide")
    band = size // 2 + LANES
    halves = (parts, count // sub, band)
    line_rows = [lines[0].shape[0] * 3 // 4, lines[0].shape[0] // 4]
    line_rows += [lines[1].shape[0], lines[2].shape[0]]
    gathers = len(bits_of(sub)) + len(wide_bits)
    slots = parts + 3 + 2**gathers
    vmem = pl.BlockSpec(memory_space=pltpu.VMEM)
    anywhere = pl.BlockSpec(memory_space=pl.ANY)
    wide = lambda *shape: pltpu.VMEM(shape, jnp.float32)
    return pl.pallas_call(
        gram_kernel,
        out_shape=(
            jax.ShapeDtypeStruct((size, band), jnp.float32),
            jax.ShapeDtypeStruct((lines[1].shape[0] // 2, size), jnp.float32),
            jax.ShapeDtypeStruct((lines[1].shape[0] // 2, size), jnp.float32),
        ),
        in_specs=[vmem] + [anywhere] * 7,
        out_specs=(anywhere,) * 3,
        scratch_shapes=[
            wide(*lines[0].shape),
            wide(*lines[1].shape),
            wide(*lines[2].shape),
            wide(size, 2 * line_rows[0]),
            wide(line_rows[1], size),
            wide(size, line_rows[2]),
            wide(line_rows[3], size),
        ]
        + [pltpu.VMEM((rows, size), jnp.bfloat16) for rows in line_rows] * 2
        + [
            wide(2 * line_rows[0], size),
            wide(line_rows[0], size),
            wide(count, size + band),
            wide(*halves),
            wide(*halves),
            wide(2, halves[1] // 2, band),
            pltpu.SemaphoreType.DMA((7,)),
            pltpu.SemaphoreType.DMA((slots,)),
            pltpu.SemaphoreType.DMA((slots,)),
            pltpu.SemaphoreType.DMA((1,)),
        ],
        compiler_params=pltpu.CompilerParams(
            collective_id=number, has_side_effects=True, vmem_limit_bytes=48 * 2**20
        ),
        cost_estimate=pl.CostEstimate(
            flops=3 * size * size * size, bytes_accessed=80 * size * size, transcendentals=0
        ),
    )(norm, *lines, *moments)


def split(values):
    high = values.astype(jnp.bfloat16)
    return high, (values - high.astype(jnp.float32)).astype(jnp.bfloat16)


def product(left_high, left_low, right_high, right_low):
    dot = functools.partial(jnp.dot, preferred_element_type=jnp.float32)
    return dot(left_high, right_high) + (dot(left_high, right_low) + dot(left_low, right_high))


def polar_kernel(g_ref, band_ref, q_ref, gh, gl, ph, pw, th, tl):
    size = g_ref.shape[0]
    blocks = size // BLK
    first, second, third = newton_terms
    rows = lambda block: pl.ds(block * BLK, BLK)
    square = (BLK, BLK)
    unit = (
        lax.broadcasted_iota(jnp.int32, square, 0) == lax.broadcasted_iota(jnp.int32, square, 1)
    ).astype(jnp.float32)
    count = size // LANES
    lanes = lambda block: pl.ds((block % count) * LANES, LANES)
    trace = jnp.zeros((), jnp.float32)
    for i in range(count):
        trace = trace + jnp.sum(g_ref[lanes(i), lanes(0)] * unit[:LANES, :LANES])
    factor = 1.0 / (jnp.sqrt(trace) + 1e-07)
    for i in range(count):
        for j in range(count // 2 + 1):
            values = g_ref[lanes(i), lanes(j)] * (factor * factor)
            gh[lanes(i), lanes(i + j)], gl[lanes(i), lanes(i + j)] = split(values)
            if 0 < j < count // 2:
                values = values.T
                gh[lanes(i + j), lanes(i)], gl[lanes(i + j), lanes(i)] = split(values)

    def put(high, low, i, j, values):
        high[rows(i), rows(j)], low[rows(i), rows(j)] = split(values)
        if i != j:
            high[rows(j), rows(i)], low[rows(j), rows(i)] = split(values.T)

    def symmetric(left, right, emit):
        for i in range(blocks):
            columns = pl.ds(i * BLK, size - i * BLK)
            values = product(
                left[0][rows(i), :], left[1][rows(i), :], right[0][:, columns], right[1][:, columns]
            )
            for j in range(i, blocks):
                emit(i, j, values[:, (j - i) * BLK : (j - i + 1) * BLK])

    def emit_terms(i, j, values):
        gram = gh[rows(i), rows(j)].astype(jnp.float32) + gl[rows(i), rows(j)].astype(jnp.float32)
        terms = second * gram + third * values
        if i == j:
            terms = terms + first * unit
        put(ph, pw, i, j, terms)

    def emit_total(i, j, values):
        q_ref[rows(i), rows(j)] = values
        if i != j:
            q_ref[rows(j), rows(i)] = values.T

    symmetric((gh, gl), (gh, gl), emit_terms)
    for i in range(blocks):
        q_ref[rows(i), :] = (
            ph[rows(i), :].astype(jnp.float32) + pw[rows(i), :].astype(jnp.float32)
        ) * factor

    def one_step(step, carry):
        symmetric((ph, pw), (gh, gl), functools.partial(put, th, tl))
        symmetric((th, tl), (ph, pw), functools.partial(put, gh, gl))
        symmetric((gh, gl), (gh, gl), emit_terms)
        for i in range(blocks):
            th[rows(i), :], tl[rows(i), :] = split(q_ref[rows(i), :])
        symmetric((ph, pw), (th, tl), emit_total)
        return carry

    lax.fori_loop(0, NEWTON - 1, one_step, 0)
    for i in range(count):
        for j in range(count // 2 + 1):
            band_ref[lanes(i), lanes(j)] = q_ref[lanes(i), lanes(i + j)]


def polar_factor(gramian):
    size = gramian.shape[0]
    vmem = pl.BlockSpec(memory_space=pltpu.VMEM)
    return pl.pallas_call(
        polar_kernel,
        out_shape=jax.ShapeDtypeStruct(gramian.shape, jnp.float32),
        in_specs=[vmem],
        out_specs=vmem,
        scratch_shapes=[pltpu.VMEM((size, size), jnp.float32)]
        + [pltpu.VMEM((size, size), jnp.bfloat16)] * 6,
        compiler_params=pltpu.CompilerParams(vmem_limit_bytes=48 * 2**20),
        cost_estimate=pl.CostEstimate(
            flops=17 * 6 * size**3, bytes_accessed=8 * size * size, transcendentals=0
        ),
    )(gramian)


class Matrices:
    def __init__(self, own):
        self.own = own

    def move(self, outer, inner, sem, k, inward, rows=slice(None), columns=slice(None)):
        if k:
            pairs = [(outer.at[rows, columns], inner.at[rows, columns])]
        else:
            pairs = [
                (outer.at[j, rows], inner.at[rows, pl.ds(j * self.own, self.own)]) for j in range(3)
            ]
        for there, here in pairs:
            src, dst = (there, here) if inward else (here, there)
            pltpu.make_async_copy(src, dst, sem).start()


def whole_of(ref, sem):
    return pltpu.make_async_copy(ref, ref, sem)


def assemble(band, factor_high, factor_low):
    count = factor_high.shape[0] // LANES
    lanes = lambda block: pl.ds((block % count) * LANES, LANES)
    for i in range(count):
        for j in range(count // 2 + 1):
            part = band[lanes(i), lanes(j)]
            spot = (lanes(i), lanes(i + j))
            factor_high[spot], factor_low[spot] = split(part)
            if 0 < j < count // 2:
                spot = (lanes(i + j), lanes(i))
                factor_high[spot], factor_low[spot] = split(part.T)


def update(k, start, factor_high, factor_low, high, low, value):
    spot = pl.ds(pl.multiple_of(start, BLK), BLK)
    q_high, q_low = factor_high[spot, :], factor_low[spot, :]
    if k in COLUMNS:
        polar = dot_of(q_high, high[...], 1, 0) + (
            dot_of(q_high, low[...], 1, 0) + dot_of(q_low, high[...], 1, 0)
        )
        where = (spot, slice(None))
    else:
        polar = dot_of(high[...], q_high, 1, 1) + (
            dot_of(low[...], q_high, 1, 1) + dot_of(high[...], q_low, 1, 1)
        )
        where = (slice(None), spot)
    scale = muon_rate * 0.2 * math.sqrt((3 * D, D, FF, FF)[k])
    value[where] = value[where] * (1.0 - muon_rate * weight_decay) - scale * polar
    return where


def spread_kernel(sub, pieces, norm_ref, q_ref, *refs):
    lines, others, refs = refs[:3], refs[3:7], refs[7:]
    moments, weights, refs = refs[:4], refs[4:8], refs[8:]
    o_ref, carried, fresh, high_outs, low_outs = refs[0], refs[1:5], refs[5:9], refs[9:13], refs[13:17]
    refs = refs[17:]
    pair_bands, factor_high, factor_low = refs[:3]
    staged, values, highs, lows = refs[3:7], refs[7:11], refs[11:15], refs[15:19]
    load_sems, value_sems, out_sems, split_sems, band_sems, sends, arrivals = refs[19:]
    size = q_ref.shape[0]
    half = size // 2
    step = half // pieces
    w, n = lax.axis_index("wide"), lax.axis_index("narrow")
    own = n // sub
    across, near = partner(own, 2), partner(own, 1)
    far = own // 2
    near_place, far_place = place_at("narrow", sub), place_at("narrow", 2 * sub)
    side_place = place_at("wide", 1)
    greet([near_place, far_place, side_place])
    y = w % 2
    rows = lambda side, p: pl.ds(pl.multiple_of(side * half + p * step, 8), step)
    copies = []

    def push(src, dst, place):
        copies.append(send(src, dst, sends, arrivals, len(copies), place))
        return copies[-1]

    crossing = [
        push(q_ref.at[rows(y, p)], o_ref.at[own, rows(y, p)], far_place) for p in range(pieces)
    ]
    landing = [push(q_ref, o_ref.at[own], near_place)]
    keep = pltpu.make_async_copy(q_ref, o_ref.at[own], band_sems.at[0])
    keep.start()
    own_band = pltpu.make_async_copy(q_ref, pair_bands.at[own % 2], band_sems.at[1])
    own_band.start()
    matrices = Matrices(moments[0].shape[2])
    blocks = lax.axis_size("wide")
    for k in range(MATRICES):
        extent = staged[k].shape[0] // 2
        if k >= 2:
            pieces_of = [(y, 0, lines[k - 1])]
            if k == 2:
                pieces_of += [(1 - y, 0, others[1]), (1 - y, extent // 2, others[2])]
            else:
                pieces_of += [(1 - y, 0, others[3])]
            for side, at, source in pieces_of:
                to = pl.multiple_of(side * extent + at, 8)
                spot = staged[k].at[pl.ds(to, source.shape[0]), :]
                pltpu.make_async_copy(source, spot, load_sems.at[k]).start()
        for side, source in ((y, lines[0]), (1 - y, others[0])):
            if k >= 2:
                continue
            share = (staged[0].shape[0] // blocks, staged[1].shape[0] // blocks)
            for b in range(blocks // 2):
                start = b * (share[0] + share[1]) + k * share[0]
                to = pl.multiple_of(side * extent + b * share[k], 8)
                pltpu.make_async_copy(
                    source.at[pl.ds(start, share[k]), :],
                    staged[k].at[pl.ds(to, share[k]), :],
                    load_sems.at[k],
                ).start()
        matrices.move(moments[k], values[k], value_sems.at[k], k, True)
    clip = jnp.minimum(1.0, 1.0 / (norm_ref[0:1, 0:1] + 1e-06))

    def blend_rows(value, stage):
        def one(i, carry):
            spot = slab_at(i)
            value[spot, :] = muon_momentum * value[spot, :] + clip * stage[spot, :]
            return carry

        lax.fori_loop(0, value.shape[0] // SLAB, one, 0, unroll=UNROLL)

    def blend_columns(value, stage):
        def one(i, carry):
            spot = pl.ds(pl.multiple_of(i * LANES, LANES), LANES)
            value[:, spot] = muon_momentum * value[:, spot] + clip * stage[spot, :].T
            return carry

        lax.fori_loop(0, value.shape[1] // LANES, one, 0)

    aside = []

    def forward(p):
        crossing[p].wait_recv()
        spot = o_ref.at[across, rows(y, p)]
        aside.append(push(spot, spot, side_place))
        landing.append(push(spot, spot, near_place))

    def forward_side(p):
        aside[p].wait_recv()
        spot = o_ref.at[across, rows(1 - y, p)]
        landing.append(push(spot, spot, near_place))

    for k in range(MATRICES):
        whole_of(staged[k], load_sems.at[k]).wait()
        whole_of(values[k], value_sems.at[k]).wait()
        blend = blend_columns if k in COLUMNS else blend_rows
        blend(values[k], staged[k])
        matrices.move(carried[k], values[k], out_sems.at[k], k, False)

        def cut(i, carry, k=k):
            highs[k][slab_at(i), :], lows[k][slab_at(i), :] = split(values[k][slab_at(i), :])
            return carry

        lax.fori_loop(0, values[k].shape[0] // SLAB, cut, 0, unroll=UNROLL)

        @pl.when(far != k // 2)
        def _(k=k):
            pltpu.make_async_copy(highs[k], high_outs[k], split_sems.at[2 * k]).start()
            pltpu.make_async_copy(lows[k], low_outs[k], split_sems.at[2 * k + 1]).start()

        if k == 1:
            forward(0)
    for k in range(MATRICES):
        whole_of(values[k], out_sems.at[k]).wait()

        @pl.when(far == k // 2)
        def _(k=k):
            matrices.move(weights[k], values[k], value_sems.at[k], k, True)

    forward(1)
    landing[0].wait_recv()
    near_band = pltpu.make_async_copy(o_ref.at[near], pair_bands.at[1 - own % 2], band_sems.at[2])
    near_band.start()
    own_band.wait()
    near_band.wait()

    def pair(index):
        for side in range(2):

            @pl.when(far == side)
            def _(k=2 * side + index):
                assemble(pair_bands.at[index], factor_high, factor_low)
                whole_of(values[k], value_sems.at[k]).wait()

                def one(i, carry):
                    where = update(
                        k, i * BLK, factor_high, factor_low, highs[k], lows[k], values[k]
                    )
                    matrices.move(fresh[k], values[k], out_sems.at[k], k, False, *where)
                    return carry

                lax.fori_loop(0, size // BLK, one, 0)

    pair(0)
    forward(2)
    forward_side(0)
    pair(1)
    forward_side(1)
    for p in range(3, pieces):
        forward(p)
        forward_side(p - 1)
    forward_side(pieces - 1)
    keep.wait()
    for k in range(MATRICES):

        @pl.when(far == k // 2)
        def _(k=k):
            whole_of(values[k], out_sems.at[k]).wait()

        @pl.when(far != k // 2)
        def _(k=k):
            pltpu.make_async_copy(highs[k], high_outs[k], split_sems.at[2 * k]).wait()
            pltpu.make_async_copy(lows[k], low_outs[k], split_sems.at[2 * k + 1]).wait()

    for copy in landing[1:]:
        copy.wait_recv()
    for copy in copies:
        copy.wait_send()


def spread(norm, band, lines, others, moments, weights, number):
    pieces = 4
    size = band.shape[0]
    slots = 1 + 4 * pieces
    sub = lax.axis_size("narrow") // MATRICES
    vmem = pl.BlockSpec(memory_space=pltpu.VMEM)
    anywhere = pl.BlockSpec(memory_space=pl.ANY)
    operands = [*lines, *others]
    f32 = [jax.ShapeDtypeStruct(moment.shape, jnp.float32) for moment in moments]
    staged = [(moment.size // size, size) for moment in moments]
    flat = [(size, 3 * moments[0].shape[2])] + [moment.shape for moment in moments[1:]]
    low = [jax.ShapeDtypeStruct(shape, jnp.bfloat16) for shape in flat]
    outs = pl.pallas_call(
        functools.partial(spread_kernel, sub, pieces),
        out_shape=tuple(
            [jax.ShapeDtypeStruct((MATRICES,) + band.shape, jnp.float32)] + f32 + f32 + low + low
        ),
        in_specs=[vmem] * 2 + [anywhere] * (len(operands) + 8),
        out_specs=(anywhere,) * 17,
        scratch_shapes=[
            pltpu.VMEM((2,) + band.shape, jnp.float32),
            pltpu.VMEM((size, size), jnp.bfloat16),
            pltpu.VMEM((size, size), jnp.bfloat16),
        ]
        + [pltpu.VMEM(shape, jnp.float32) for shape in staged]
        + [pltpu.VMEM(shape, jnp.float32) for shape in flat]
        + [pltpu.VMEM(shape, jnp.bfloat16) for shape in flat] * 2
        + [pltpu.SemaphoreType.DMA((MATRICES,))] * 3
        + [
            pltpu.SemaphoreType.DMA((2 * MATRICES,)),
            pltpu.SemaphoreType.DMA((3,)),
            pltpu.SemaphoreType.DMA((slots,)),
            pltpu.SemaphoreType.DMA((slots,)),
        ],
        compiler_params=pltpu.CompilerParams(
            collective_id=number, has_side_effects=True, vmem_limit_bytes=58 * 2**20
        ),
        cost_estimate=pl.CostEstimate(
            flops=9 * size * size * size, bytes_accessed=80 * size * size, transcendentals=0
        ),
    )(norm, band, *operands, *moments, *weights)
    return outs[0], outs[1:5], outs[5:9], outs[9:13], outs[13:17]


def finish_kernel(sub, norm_ref, small_ref, hidden_sum_ref, *refs):
    adam_ins, passing, refs = refs[:9], refs[9:11], refs[11:]
    bands_any, refs = refs[0], refs[1:]
    ready, fresh, high_ins, low_ins, weights = (refs[4 * i : 4 * i + 4] for i in range(5))
    carried, results, refs = refs[20:24], refs[24:28], refs[28:]
    adam_outs, passed, refs = refs[:9], refs[9:11], refs[11:]
    held, pass_in, pass_out, refs = refs[:2], refs[2], refs[3], refs[4:]
    bands, factor_high, factor_low = refs[:3]
    news, values, highs, lows = refs[3:7], refs[7:11], refs[11:15], refs[15:19]
    news_sems, value_sems, split_sems, band_sems, carried_sems, out_sems = refs[19:]
    size = factor_high.shape[0]
    far = lax.axis_index("narrow") // sub // 2
    matrices = Matrices(weights[0].shape[2])
    for side in range(2):

        @pl.when(far == side)
        def _(side=side):
            for index in range(2):
                k = 2 * (1 - side) + index
                pltpu.make_async_copy(bands_any.at[k], bands.at[index], band_sems.at[index]).start()
                pltpu.make_async_copy(high_ins[k], highs[k], split_sems.at[2 * index]).start()
                pltpu.make_async_copy(low_ins[k], lows[k], split_sems.at[2 * index + 1]).start()
                matrices.move(weights[k], values[k], value_sems.at[k], k, True)
            for k in (2 * side, 2 * side + 1):
                matrices.move(fresh[k], values[k], value_sems.at[k], k, True)

    for k in range(MATRICES):
        matrices.move(ready[k], news[k], news_sems.at[k], k, True)
    enters = [
        pltpu.make_async_copy(passing[i], held[i], pass_in.at[i]) for i in range(2)
    ]
    leaves = [
        pltpu.make_async_copy(held[i], passed[i], pass_out.at[i]) for i in range(2)
    ]
    for copy in enters:
        copy.start()
    clip = jnp.minimum(1.0, 1.0 / (norm_ref[0:1, 0:1] + 1e-06))
    first, second = adam_ins[0].shape[0], adam_ins[3].shape[0]
    sums = (small_ref[0:first, :], small_ref[first : first + second, :], hidden_sum_ref[...])
    for i, gradient in enumerate(sums):
        news_of = adam_update(*(ref[...] for ref in adam_ins[3 * i : 3 * i + 3]), clip * gradient)
        for ref, value in zip(adam_outs[3 * i : 3 * i + 3], news_of):
            ref[...] = value
    for index in range(2):
        whole_of(bands.at[index], band_sems.at[index]).wait()
        if index:
            for enter_copy, leave_copy in zip(enters, leaves):
                enter_copy.wait()
                leave_copy.start()
            for k in range(MATRICES):
                whole_of(news[k], news_sems.at[k]).wait()
                matrices.move(carried[k], news[k], carried_sems.at[k], k, False)
        for side in range(2):

            @pl.when(far == side)
            def _(k=2 * (1 - side) + index, done=2 * side + index):
                if index:
                    for late in (done - 1, done):
                        whole_of(values[late], value_sems.at[late]).wait()
                        matrices.move(results[late], values[late], out_sems.at[late], late, False)
                assemble(bands.at[index], factor_high, factor_low)
                whole_of(highs[k], split_sems.at[2 * index]).wait()
                whole_of(lows[k], split_sems.at[2 * index + 1]).wait()
                whole_of(values[k], value_sems.at[k]).wait()

                def one(i, carry):
                    where = update(
                        k, i * BLK, factor_high, factor_low, highs[k], lows[k], values[k]
                    )
                    matrices.move(results[k], values[k], out_sems.at[k], k, False, *where)
                    return carry

                lax.fori_loop(0, size // BLK, one, 0)

    for copy in leaves:
        copy.wait()
    for k in range(MATRICES):
        whole_of(news[k], carried_sems.at[k]).wait()
        whole_of(values[k], out_sems.at[k]).wait()


def finish(norm, small, hidden_sum, adams, passing, bands, ready, fresh, highs, lows, weights):
    size = bands.shape[1]
    sub = lax.axis_size("narrow") // MATRICES
    anywhere = pl.BlockSpec(memory_space=pl.ANY)
    shapes = [jax.ShapeDtypeStruct(weight.shape, jnp.float32) for weight in weights]
    flat = [(size, 3 * weights[0].shape[2])] + [weight.shape for weight in weights[1:]]
    vmem = pl.BlockSpec(memory_space=pltpu.VMEM)
    others = [jax.ShapeDtypeStruct(array.shape, jnp.float32) for array in adams]
    others += [jax.ShapeDtypeStruct(array.shape, array.dtype) for array in passing]
    outs = pl.pallas_call(
        functools.partial(finish_kernel, sub),
        out_shape=tuple(shapes + shapes + others),
        in_specs=[vmem] * 12 + [anywhere] * 23,
        out_specs=(anywhere,) * 8 + (vmem,) * 9 + (anywhere,) * 2,
        scratch_shapes=[pltpu.VMEM(array.shape, array.dtype) for array in passing]
        + [pltpu.SemaphoreType.DMA((2,)), pltpu.SemaphoreType.DMA((2,))]
        + [
            pltpu.VMEM((2,) + bands.shape[1:], jnp.float32),
            pltpu.VMEM((size, size), jnp.bfloat16),
            pltpu.VMEM((size, size), jnp.bfloat16),
        ]
        + [pltpu.VMEM(shape, jnp.float32) for shape in flat] * 2
        + [pltpu.VMEM(shape, jnp.bfloat16) for shape in flat] * 2
        + [pltpu.SemaphoreType.DMA((MATRICES,))] * 6,
        compiler_params=pltpu.CompilerParams(vmem_limit_bytes=58 * 2**20),
        cost_estimate=pl.CostEstimate(
            flops=9 * size * size * size, bytes_accessed=60 * size * size, transcendentals=0
        ),
    )(norm, small, hidden_sum, *adams, *passing, bands, *ready, *fresh, *highs, *lows, *weights)
    return outs[:4], outs[4:8], outs[8:17], outs[17:]


def adam_update(weight, moment, square, gradient):
    moment_new = first_decay * moment + (1.0 - first_decay) * gradient
    square_new = second_decay * square + (1.0 - second_decay) * gradient * gradient
    moment_hat = moment_new / (1.0 - first_decay**STEP)
    square_hat = square_new / (1.0 - second_decay**STEP)
    weight_new = weight * (1.0 - adam_rate * weight_decay) - adam_rate * moment_hat / (
        jnp.sqrt(square_hat) + 1e-08
    )
    return (moment_new, square_new, weight_new)


def column_shifts(strip, column):
    rows = strip.shape[0]
    left = jnp.where(column == 0, 0.0, pltpu.roll(strip, 1, 0))
    right = jnp.where(column == rows - 1, 0.0, pltpu.roll(strip, rows - 1, 0))
    return (left, strip, right)


def tap_rows(shifts, taps):
    return [
        taps[3 * i] * shifts[0] + taps[3 * i + 1] * shifts[1] + taps[3 * i + 2] * shifts[2]
        for i in range(3)
    ]


def strip_at(index):
    return pl.ds(pl.multiple_of(index * GRID, GRID), GRID)


def convolve(load, taps, emit):
    shape = load(0).shape
    column = lax.broadcasted_iota(jnp.int32, shape, 0)

    def one(r, carry):
        above, here = carry
        upper, middle, lower = tap_rows(column_shifts(load(r), column), taps)
        emit(r - 1, here + lower)
        return (upper, above + middle)

    upper, middle, _ = tap_rows(column_shifts(load(0), column), taps)
    above, here = lax.fori_loop(1, GRID, one, (upper, middle))
    emit(GRID - 1, here)


def kernel_sums(load, weigh, width):
    column = lax.broadcasted_iota(jnp.int32, (GRID, width), 0)
    fold = lambda values: values.reshape(GRID // 8, 8, width).sum(axis=0)
    zero = jnp.zeros((8, width), jnp.float32)

    def one(r, carry):
        sums = carry
        shifts = column_shifts(load(r), column)
        later = weigh(jnp.minimum(r + 1, GRID - 1)) * jnp.where(r < GRID - 1, 1.0, 0.0)
        earlier = weigh(jnp.maximum(r - 1, 0)) * jnp.where(r > 0, 1.0, 0.0)
        terms = (later, weigh(r), earlier)
        return tuple(
            sums[3 * i + j] + fold(terms[i] * shifts[j]) for i in range(3) for j in range(3)
        )

    return lax.fori_loop(0, GRID, one, (zero,) * 9)


def middle_kernel(
    pieces,
    entry_ref,
    cotangent_ref,
    live_ref,
    gate_ref,
    expand_any,
    reduce_any,
    taps_ref,
    ffn_half_ref,
    grad_entry_any,
    reduce_share,
    expand_hold,
    expand_give,
    grad_taps_ref,
    expand_full,
    reduce_full,
    grad_ffn,
    upward,
    weight,
    active,
    grad_up,
    ffn,
    back,
    grad_reduce,
    grad_expand,
    ffn_inbox,
    near,
    far,
    held,
    local,
    reduce_held,
    reduce_beside,
    reduce_inbox,
    reduce_loads,
    expand_held,
    expand_beside,
    expand_inbox,
    expand_loads,
    give_sems,
    weight_sems,
    sends,
    arrivals,
):
    units = expand_any.shape[1]
    block = min(BLK, units // 2)
    steps = units // block
    groups = steps // 2
    y, z = wide_parts()
    count = lax.axis_size("wide") // 2
    far_bits = bits_of(lax.axis_size("narrow"))[1:]
    greet(
        [place_at("narrow", bit) for bit in [1] + far_bits]
        + [place_at("wide", bit) for bit in bits_of(lax.axis_size("wide"))]
    )

    def block_index(step):
        side = 1 - y if step < groups else y
        return side * groups + line_partner(z // (count // groups), groups - 1 - step % groups)

    fetches = []
    for step in range(steps):
        spot = pl.ds(pl.multiple_of(block_index(step) * block, LANES), block)
        pair = (
            pltpu.make_async_copy(
                expand_any.at[:, spot], expand_full.at[:, spot], weight_sems.at[step]
            ),
            pltpu.make_async_copy(
                reduce_any.at[spot, :], reduce_full.at[spot, :], weight_sems.at[steps + step]
            ),
        )
        for copy in pair:
            copy.start()
        fetches.append(pair)
    gate, live = gate_ref[...], live_ref[...]

    def gated(i, carry):
        spot = slab_at(i)
        result = cotangent_ref[spot, :].astype(jnp.float32) * live
        grad_ffn[spot, :] = (gate * result).astype(jnp.bfloat16)
        return carry

    lax.fori_loop(0, grad_ffn.shape[0] // SLAB, gated, 0, unroll=UNROLL)

    def work(spot, fresh):
        expand_low = expand_full[:, spot].astype(jnp.bfloat16)
        reduce_low = reduce_full[spot, :].astype(jnp.bfloat16)
        taps = [taps_ref[t : t + 1, spot] for t in range(9)]
        upward[...] = dot_of(entry_ref[...], expand_low, 1, 0)
        weight[...] = dot_of(grad_ffn[...], reduce_low, 1, 1)

        def emit_middle(r, values):
            inner = gelu_slope * (values + gelu_cubic * values * values * values)
            bent = jnp.tanh(inner)
            active[strip_at(r), :] = (0.5 * values * (1.0 + bent)).astype(jnp.bfloat16)
            turn = 0.5 * (1.0 + bent) + 0.5 * values * (1.0 - bent * bent) * (
                gelu_slope * (1.0 + 3.0 * gelu_cubic * values * values)
            )
            weight[strip_at(r), :] = weight[strip_at(r), :] * turn

        convolve(lambda r: upward[strip_at(r), :], taps, emit_middle)

        def emit_grad(r, values):
            grad_up[strip_at(r), :] = values.astype(jnp.bfloat16)

        convolve(lambda r: weight[strip_at(r), :], taps[::-1], emit_grad)
        sums = kernel_sums(
            lambda r: upward[strip_at(r), :], lambda r: weight[strip_at(r), :], block
        )
        for t in range(9):
            grad_taps_ref[t : t + 1, spot] = jnp.sum(sums[t], axis=0, keepdims=True)
        grad_reduce[spot, :] = dot_of(active[...], grad_ffn[...], 0, 0)
        grad_expand[spot, :] = dot_of(grad_up[...], entry_ref[...], 0, 0)
        if fresh:
            ffn[...] = dot_of(active[...], reduce_low, 1, 0)
            back[...] = dot_of(grad_up[...], expand_low, 1, 1)
        else:
            ffn[...] += dot_of(active[...], reduce_low, 1, 0)
            back[...] += dot_of(grad_up[...], expand_low, 1, 1)

    base = (len(far_bits) + 2) * pieces + 1
    reduce_sum = Scatter(
        grad_reduce, reduce_held, reduce_beside, reduce_inbox, sends, arrivals, reduce_loads, base
    )
    expand_sum = Scatter(
        grad_expand,
        expand_held,
        expand_beside,
        expand_inbox,
        sends,
        arrivals,
        expand_loads,
        base + Scatter.slots(),
    )
    for step in range(groups):
        for copy in fetches[step]:
            copy.wait()
        work(pl.ds(pl.multiple_of(block_index(step) * block, LANES), block), step == 0)
        size = count // groups
        ready = [(groups - 1 - step) * size + e for e in reversed(range(size))]
        for scatter in (reduce_sum, expand_sum):
            for e in ready:
                if scatter is reduce_sum or e >= count // 2:
                    scatter.give(e)
    for step in range(groups, steps):
        for copy in fetches[step]:
            copy.wait()

    def later(i, carry):
        side_block = line_partner_of(z // (count // groups), i, groups)
        work(pl.ds(pl.multiple_of((y * groups + side_block) * block, LANES), block), False)
        return carry

    lax.fori_loop(0, groups, later, 0)
    narrow = NarrowSum(
        far_bits, pieces, back, grad_entry_any, near, far, held, sends, arrivals, local, 0
    )
    narrow.start()
    core = lax.axis_index("narrow") % 2
    half = ffn.shape[0] // 2
    side_rows = lambda side: pl.ds(pl.multiple_of(side * half, 8), half)
    ffn_copy = send(
        ffn.at[side_rows(1 - core)], ffn_inbox, sends, arrivals, base - 1, place_at("narrow", 1)
    )
    for scatter in (reduce_sum, expand_sum):
        scatter.load()
    for p in range(pieces):
        narrow.begin(p)
    left = [list(reversed(range(count))), list(reversed(range(count // 2, count)))]
    gives = []
    for e in range(count // 2):
        gives.append(
            pltpu.make_async_copy(
                block_of(grad_expand, 1 - y, line_partner(z, e)), expand_give.at[e], give_sems.at[e]
            )
        )
        gives[e].start()
    scatters = (reduce_sum, expand_sum)
    scatters[0].step(left[0].pop(0))
    scatters[1].step(left[1].pop(0))
    ffn_copy.wait_recv()
    ffn_half_ref[...] = ffn[side_rows(core), :] + ffn_inbox[...]
    turns = [0, 1, 0]
    for b in range(len(far_bits)):
        for p in range(pieces):
            narrow.step(b, p)
            if turns and len(left[turns[0]]) > (turns[0] == 0):
                which = turns.pop(0)
                scatters[which].step(left[which].pop(0))
    for which in range(2):
        while left[which]:
            scatters[which].step(left[which].pop(0))
    for e in range(count // 2):
        expand_sum.loads[e].wait()
    expand_sum.copies[("z", count // 2)].wait_recv()
    expand_held[0] = expand_held[0] + expand_inbox[count // 2 - 1]
    outs = [
        pltpu.make_async_copy(reduce_held.at[0], reduce_share, reduce_loads.at[0]),
        pltpu.make_async_copy(
            expand_held.at[pl.ds(0, count // 2)], expand_hold, expand_loads.at[0]
        ),
    ]
    for out in outs:
        out.start()
    outs += gives
    narrow.finish()
    ffn_copy.wait_send()
    for scatter in scatters:
        scatter.finish()
    for out in outs:
        out.wait()


def line_partner_of(place, index, count):
    flipped = 0 * place
    for bit in bits_of(count):
        one, two = (place // bit) % 2, (index // bit) % 2
        flipped = flipped + (one + two - 2 * one * two) * bit
    return flipped


def middle(entry, cotangent, live, gate, expand, reduce, taps, number):
    tokens, width = entry.shape
    units = expand.shape[1]
    block = min(BLK, units // 2)
    steps = units // block
    pieces = 4
    narrow_bits = bits_of(lax.axis_size("narrow"))
    slots = (len(narrow_bits) + 1) * pieces + 1 + 2 * Scatter.slots()
    vmem = pl.BlockSpec(memory_space=pltpu.VMEM)
    anywhere = pl.BlockSpec(memory_space=pl.ANY)
    f32 = lambda *shape: jax.ShapeDtypeStruct(shape, jnp.float32)
    wide = lambda *shape: pltpu.VMEM(shape, jnp.float32)
    low = lambda *shape: pltpu.VMEM(shape, jnp.bfloat16)
    share = block_shape((units, width))
    line = lax.axis_size("wide") // 2
    return pl.pallas_call(
        functools.partial(middle_kernel, pieces),
        out_shape=(
            f32(tokens // 2, width),
            f32(tokens, width),
            f32(*share),
            f32(line // 2, *share),
            f32(line // 2, *share),
            f32(9, units),
        ),
        in_specs=[vmem, vmem, vmem, vmem, anywhere, anywhere, vmem],
        out_specs=(vmem,) + (anywhere,) * 4 + (vmem,),
        scratch_shapes=[
            wide(width, units),
            wide(units, width),
            low(tokens, width),
            wide(tokens, block),
            wide(tokens, block),
            low(tokens, block),
            low(tokens, block),
            wide(tokens, width),
            wide(tokens, width),
            wide(units, width),
            wide(units, width),
            wide(tokens // 2, width),
        ]
        + narrow_scratch((tokens, width), pieces)
        + scatter_scratch((units, width)) * 2
        + [
            pltpu.SemaphoreType.DMA((line // 2,)),
            pltpu.SemaphoreType.DMA((2 * steps,)),
            pltpu.SemaphoreType.DMA((slots,)),
            pltpu.SemaphoreType.DMA((slots,)),
        ],
        compiler_params=pltpu.CompilerParams(
            collective_id=number, has_side_effects=True, vmem_limit_bytes=60 * 2**20
        ),
        cost_estimate=pl.CostEstimate(
            flops=12 * tokens * width * units,
            bytes_accessed=200 * tokens * width,
            transcendentals=tokens * units,
        ),
    )(entry, cotangent, live, gate, expand, reduce, taps)


def norm_strip(values):
    average = jnp.mean(values, axis=-1, keepdims=True)
    centred = values - average
    spread_of = jnp.mean(centred * centred, axis=-1, keepdims=True)
    inverse = lax.rsqrt(spread_of + 1e-06)
    return centred * inverse, inverse


def slab_at(index):
    return pl.ds(pl.multiple_of(index * SLAB, SLAB), SLAB)


def fold_rows(values):
    return values.reshape(values.shape[0] // 8, 8, values.shape[1]).sum(axis=0)


def mixer_kernel_forward(tokens_ref, shift_ref, scale_ref, taps_ref, out_ref, entered):
    stretch = 1.0 + scale_ref[...]
    offset = shift_ref[...]

    def enter(r, carry):
        normed, _ = norm_strip(tokens_ref[slab_at(r), :].astype(jnp.float32))
        entered[slab_at(r), :] = normed * stretch + offset
        return carry

    rows, width = tokens_ref.shape
    lax.fori_loop(0, rows // SLAB, enter, 0, unroll=UNROLL)
    for start in range(0, width, BLK):
        lanes = pl.ds(start, BLK)

        def emit(r, values, lanes=lanes):
            out_ref[strip_at(r), lanes] = values.astype(jnp.bfloat16)

        taps = [taps_ref[t : t + 1, lanes] for t in range(9)]
        convolve(lambda r, lanes=lanes: entered[strip_at(r), lanes], taps, emit)


def mixer_forward(tokens, shift, scale, taps):
    rows, width = tokens.shape
    vmem = pl.BlockSpec(memory_space=pltpu.VMEM)
    return pl.pallas_call(
        mixer_kernel_forward,
        out_shape=jax.ShapeDtypeStruct((rows, width), jnp.bfloat16),
        in_specs=[vmem] * 4,
        out_specs=vmem,
        scratch_shapes=[pltpu.VMEM((rows, width), jnp.float32)],
        compiler_params=pltpu.CompilerParams(vmem_limit_bytes=40 * 2**20),
        cost_estimate=pl.CostEstimate(
            flops=40 * rows * width, bytes_accessed=4 * rows * width, transcendentals=0
        ),
    )(tokens, shift, scale, taps)


def mixer_kernel_backward(
    tokens_ref,
    shift_ref,
    scale_ref,
    taps_ref,
    grad_mixed_ref,
    grad_hidden_ref,
    out_ref,
    grad_taps_ref,
    grad_shift_ref,
    grad_scale_ref,
    normed_ref,
    back_ref,
    inverse_ref,
    wait_tokens,
    wait_mixed,
    wait_hidden,
):
    width = tokens_ref.shape[1]
    stretch = 1.0 + scale_ref[...]
    wait_tokens()

    def enter(r, carry):
        normed, inverse = norm_strip(tokens_ref[slab_at(r), :].astype(jnp.float32))
        normed_ref[slab_at(r), :] = normed
        inverse_ref[slab_at(r), :] = jnp.broadcast_to(inverse, (SLAB, LANES))
        return carry

    rows = tokens_ref.shape[0]
    lax.fori_loop(0, rows // SLAB, enter, 0, unroll=UNROLL)
    wait_mixed()
    for start in range(0, width, BLK):
        lanes = pl.ds(start, BLK)
        taps = [taps_ref[t : t + 1, lanes] for t in range(9)]
        stretch_part = 1.0 + scale_ref[:, lanes]
        offset_part = shift_ref[:, lanes]

        def emit(r, values, lanes=lanes):
            back_ref[strip_at(r), lanes] = values

        def entered(r, lanes=lanes, stretch_part=stretch_part, offset_part=offset_part):
            return normed_ref[strip_at(r), lanes] * stretch_part + offset_part

        weigh = lambda r, lanes=lanes: grad_mixed_ref[strip_at(r), lanes]
        convolve(weigh, taps[::-1], emit)
        sums = kernel_sums(entered, weigh, BLK)
        for t in range(9):
            grad_taps_ref[t : t + 1, lanes] = jnp.sum(sums[t], axis=0, keepdims=True)

    def leave(r, carry):
        shifts, scales = carry
        normed = normed_ref[slab_at(r), :]
        back = back_ref[slab_at(r), :]
        stretched = back * stretch
        first = jnp.mean(stretched, axis=-1, keepdims=True)
        second = jnp.mean(stretched * normed, axis=-1, keepdims=True)
        inverse = inverse_ref[slab_at(r), :][:, :1]
        out = grad_hidden_ref[slab_at(r), :] + (stretched - first - normed * second) * inverse
        out_ref[slab_at(r), :] = out.astype(jnp.bfloat16)
        return shifts + fold_rows(back), scales + fold_rows(back * normed)

    wait_hidden()
    zero = jnp.zeros((8, width), jnp.float32)
    shifts, scales = lax.fori_loop(0, rows // SLAB, leave, (zero, zero), unroll=UNROLL)
    grad_shift_ref[...] = jnp.sum(shifts, axis=0, keepdims=True)
    grad_scale_ref[...] = jnp.sum(scales, axis=0, keepdims=True)


def dot_of(left, right, left_axis, right_axis):
    return lax.dot_general(
        left,
        right,
        (((left_axis,), (right_axis,)), ((), ())),
        preferred_element_type=jnp.float32,
    )


def head_only(values, head):
    lane = lax.broadcasted_iota(jnp.int32, values.shape, 1)
    return jnp.where(lane // HEAD == head, values, jnp.zeros_like(values))


def attend_kernel(
    mixed_ref, attend_ref, triple_ref, context_ref, logsum_ref, low_ref, turned, values_t
):
    tokens = mixed_ref.shape[0]
    width = context_ref.shape[1]
    for j in range(3):
        columns = pl.ds(j * width, width)
        low_ref[:, columns] = attend_ref[j].astype(jnp.bfloat16)
        triple_ref[:, columns] = dot_of(mixed_ref[...], low_ref[:, columns], 1, 0).astype(
            jnp.bfloat16
        )
    values_t[...] = triple_ref[:, pl.ds(2 * width, width)].T
    scale = jnp.bfloat16(HEAD ** (-0.5))
    for head in range(width // HEAD):
        pair = head * HEAD // LANES * LANES
        inside = head % (LANES // HEAD)

        def one(block, carry, head=head, pair=pair, inside=inside):
            spot = pl.ds(pl.multiple_of(block * QUERIES, QUERIES), QUERIES)
            queries = head_only(triple_ref[spot, pl.ds(pair, LANES)], inside) * scale
            scores = dot_of(triple_ref[:, pl.ds(width + pair, LANES)], queries, 1, 1)
            peak = jnp.max(scores, axis=0, keepdims=True)
            weights = jnp.exp(scores - peak)
            total = jnp.sum(weights, axis=0, keepdims=True)
            soft_low = (weights * (1.0 / total)).astype(jnp.bfloat16)
            turned[pl.ds(head * HEAD, HEAD), spot] = dot_of(
                values_t[pl.ds(head * HEAD, HEAD), :], soft_low, 1, 0
            )
            logsum_ref[pl.ds(head, 1), spot] = peak + jnp.log(total)
            return carry

        lax.fori_loop(0, tokens // QUERIES, one, 0)
    context_ref[...] = turned[...].T.astype(jnp.bfloat16)


def attend(mixed, attend_weight):
    tokens, width = mixed.shape
    own = attend_weight.shape[2]
    vmem = pl.BlockSpec(memory_space=pltpu.VMEM)
    return pl.pallas_call(
        attend_kernel,
        out_shape=(
            jax.ShapeDtypeStruct((tokens, 3 * own), jnp.bfloat16),
            jax.ShapeDtypeStruct((tokens, own), jnp.bfloat16),
            jax.ShapeDtypeStruct((8, tokens), jnp.float32),
            jax.ShapeDtypeStruct((width, 3 * own), jnp.bfloat16),
        ),
        in_specs=[vmem] * 2,
        out_specs=(vmem,) * 4,
        scratch_shapes=[
            pltpu.VMEM((own, tokens), jnp.float32),
            pltpu.VMEM((own, tokens), jnp.bfloat16),
        ],
        compiler_params=pltpu.CompilerParams(vmem_limit_bytes=40 * 2**20),
        cost_estimate=pl.CostEstimate(
            flops=16 * tokens * tokens * own,
            bytes_accessed=12 * tokens * width,
            transcendentals=tokens * tokens * own // HEAD,
        ),
    )(mixed, attend_weight)


def narrow_hops():
    return [("narrow", bit) for bit in reversed(bits_of(lax.axis_size("narrow")))]


def narrow_position(item):
    n = lax.axis_index("narrow")
    position = 0
    for index, (_, bit) in enumerate(narrow_hops()):
        value = (n // bit) % 2
        if (item >> index) % 2:
            value = 1 - value
        position = position + value * 2**index
    return position


def entry_kernel(
    pieces,
    context_ref,
    tokens_ref,
    output_ref,
    gate_ref,
    shift_ref,
    scale_ref,
    branch_any,
    hidden_any,
    entry_ref,
    branch_ref,
    hidden_ref,
    out_sems,
    slots,
    output_low,
    output_inbox,
    sends,
    arrivals,
):
    rows, own = context_ref.shape
    step = rows // pieces
    hops = narrow_hops()
    count = 2 ** len(hops)
    greet([place_at(axis, bit) for axis, bit in hops])
    chunk = lambda p: pl.ds(p * step, step)
    slots[narrow_position(0)] = context_ref[...].astype(jnp.float32)
    output_copy = send(
        output_ref, output_inbox, sends, arrivals, pieces * (count - 1), place_at("narrow", 1)
    )
    gathers = []
    for p in range(pieces):
        spot_of = lambda item, p=p: slots.at[narrow_position(item), chunk(p)]
        gathers.append(Gather(spot_of(0), spot_of, hops, sends, arrivals, p * (count - 1)))
        gathers[p].step(0)
    core = lax.axis_index("narrow") % 2
    half = output_ref.shape[0]
    output_low[pl.ds(pl.multiple_of(core * half, SLAB), half), :] = output_ref[...].astype(
        jnp.bfloat16
    )
    output_copy.wait_recv()
    output_low[pl.ds(pl.multiple_of((1 - core) * half, SLAB), half), :] = output_inbox[...].astype(
        jnp.bfloat16
    )
    gate, offset, stretch = gate_ref[...], shift_ref[...], 1.0 + scale_ref[...]
    outs = []
    for p in range(pieces):
        for item in gathers[p].order[1:]:
            gathers[p].step(item)
        branch = jnp.zeros((step, output_ref.shape[1]), jnp.float32)
        for position in range(count):
            branch = branch + dot_of(
                slots[position, chunk(p)].astype(jnp.bfloat16),
                output_low[pl.ds(position * own, own), :],
                1,
                0,
            )
        branch_ref[chunk(p), :] = branch

        def one(i, carry, p=p):
            spot = pl.ds(pl.multiple_of(p * step + i * SLAB, SLAB), SLAB)
            hidden = tokens_ref[spot, :].astype(jnp.float32) + gate * branch_ref[spot, :]
            hidden_ref[spot, :] = hidden
            normed, _ = norm_strip(hidden)
            entry_ref[spot, :] = (normed * stretch + offset).astype(jnp.bfloat16)
            return carry

        lax.fori_loop(0, step // SLAB, one, 0, unroll=UNROLL)
        for index, (src, dst) in enumerate(((branch_ref, branch_any), (hidden_ref, hidden_any))):
            outs.append(
                pltpu.make_async_copy(
                    src.at[chunk(p), :], dst.at[chunk(p), :], out_sems.at[2 * p + index]
                )
            )
            outs[-1].start()
    for gather in gathers:
        gather.finish()
    output_copy.wait_send()
    for out in outs:
        out.wait()


def enter(context, tokens, output_rows, gate, shift, scale, number):
    pieces = 4
    rows, own = context.shape
    width = tokens.shape[1]
    count = lax.axis_size("narrow")
    vmem = pl.BlockSpec(memory_space=pltpu.VMEM)
    slots = pieces * (count - 1) + 1
    return pl.pallas_call(
        functools.partial(entry_kernel, pieces),
        out_shape=(
            jax.ShapeDtypeStruct((rows, width), jnp.float32),
            jax.ShapeDtypeStruct((rows, width), jnp.float32),
            jax.ShapeDtypeStruct((rows, width), jnp.bfloat16),
        ),
        in_specs=[vmem] * 6,
        out_specs=(pl.BlockSpec(memory_space=pl.ANY),) * 2 + (vmem,),
        scratch_shapes=[
            pltpu.VMEM((rows, width), jnp.float32),
            pltpu.VMEM((rows, width), jnp.float32),
            pltpu.SemaphoreType.DMA((2 * pieces,)),
            pltpu.VMEM((count, rows, own), jnp.float32),
            pltpu.VMEM((width, width), jnp.bfloat16),
            pltpu.VMEM(output_rows.shape, jnp.float32),
            pltpu.SemaphoreType.DMA((slots,)),
            pltpu.SemaphoreType.DMA((slots,)),
        ],
        compiler_params=pltpu.CompilerParams(
            collective_id=number, has_side_effects=True, vmem_limit_bytes=40 * 2**20
        ),
        cost_estimate=pl.CostEstimate(
            flops=2 * rows * width * width, bytes_accessed=100 * rows * width, transcendentals=0
        ),
    )(context, tokens, output_rows, gate, shift, scale)


def all_rows(values):
    for _, bit in narrow_hops()[:-1]:
        side = (lax.axis_index("narrow") // bit) % 2
        other = permute(values, "narrow", bit)
        values = jnp.where(
            side == 0,
            jnp.concatenate([values, other], axis=0),
            jnp.concatenate([other, values], axis=0),
        )
    return values


def back_kernel(
    pieces,
    hidden_any,
    branch_any,
    grad_entry_any,
    cotangent_any,
    live_ref,
    scale_ref,
    gate_ref,
    mixed_ref,
    attend_ref,
    output_ref,
    triple_ref,
    context_ref,
    logsum_ref,
    reduce_share_ref,
    expand_hold,
    expand_give,
    grad_hidden_ref,
    grad_shift_ref,
    grad_scale_ref,
    grad_gate_ref,
    grad_mixed_any,
    attend_out_share,
    reduce_line,
    expand_line,
    expand_share,
    hidden,
    branch,
    grad_entry,
    cotangent,
    grad_branch,
    output_low,
    grad_context,
    keys_t,
    grad_queries_t,
    grad_keys,
    grad_values,
    grad_triple,
    near,
    far,
    held,
    local,
    scatter_held,
    scatter_beside,
    scatter_inbox,
    scatter_loads,
    output_held,
    output_beside,
    output_inbox,
    output_loads,
    rest_held,
    rest_beside,
    rest_inbox,
    rest_loads,
    load_sems,
    keep_sems,
    sends,
    arrivals,
):
    tokens, width = hidden.shape
    own = output_ref.shape[0]
    _, z = wide_parts()
    far_bits = bits_of(lax.axis_size("narrow"))[1:]
    greet(
        [place_at("narrow", bit) for bit in [1] + far_bits]
        + [place_at("wide", bit) for bit in bits_of(lax.axis_size("wide"))]
    )
    hops = line_hops()
    base = (len(far_bits) + 2) * pieces + Scatter.slots()

    def spot_in(line):
        def spot_of(item):
            spot = z
            for index, (_, bit) in enumerate(hops):
                if (item >> index) % 2:
                    spot = partner(spot, bit // 2)
            return line_block(line, spot)

        return spot_of

    gathers, keeps = [], []
    rest_base = base + 2 * (2 ** len(hops) - 1)
    rest = Scatter(
        None, rest_held, rest_beside, rest_inbox, sends, arrivals, rest_loads, rest_base,
        (expand_hold, expand_give),
    )
    rest.start()
    for index, (share, line) in enumerate(
        ((reduce_share_ref, reduce_line), (rest_held.at[0], expand_line))
    ):
        start = base + index * (2 ** len(hops) - 1)
        gathers.append(Gather(share, spot_in(line), hops, sends, arrivals, start))
        keeps.append(pltpu.make_async_copy(share, spot_in(line)(0), keep_sems.at[index]))
    gathers[0].step(0)
    keeps[0].start()
    step = tokens // pieces
    loads = []
    for p in range(pieces):
        spot = pl.ds(p * step, step)
        pairs = (
            (hidden_any, hidden),
            (branch_any, branch),
            (grad_entry_any, grad_entry),
            (cotangent_any, cotangent),
        )
        loads.append(
            [
                pltpu.make_async_copy(src.at[spot, :], dst.at[spot, :], load_sems.at[4 * p + i])
                for i, (src, dst) in enumerate(pairs)
            ]
        )
        for load in loads[p]:
            load.start()
    output_low[...] = output_ref[...].astype(jnp.bfloat16)
    stretch, gate, live = 1.0 + scale_ref[...], gate_ref[...], live_ref[...]

    def one_slab(r, carry):
        shifts, scales, gates = carry
        spot = slab_at(r)
        normed, inverse = norm_strip(hidden[spot, :])
        back = grad_entry[spot, :]
        stretched = back * stretch
        first = jnp.mean(stretched, axis=-1, keepdims=True)
        second = jnp.mean(stretched * normed, axis=-1, keepdims=True)
        grad = cotangent[spot, :].astype(jnp.float32) * live + (
            stretched - first - normed * second
        ) * inverse
        grad_hidden_ref[spot, :] = grad
        grad_branch[spot, :] = (gate * grad).astype(jnp.bfloat16)
        return (
            shifts + fold_rows(back),
            scales + fold_rows(back * normed),
            gates + fold_rows(branch[spot, :] * grad),
        )

    sums = (jnp.zeros((8, width), jnp.float32),) * 3
    for p in range(pieces):
        for load in loads[p]:
            load.wait()
        first_slab = p * step // SLAB
        sums = lax.fori_loop(
            first_slab, first_slab + step // SLAB, one_slab, sums, unroll=UNROLL
        )
    for ref, total in zip((grad_shift_ref, grad_scale_ref, grad_gate_ref), sums):
        ref[...] = jnp.sum(total, axis=0, keepdims=True)
    output_grad = branch.at[pl.ds(3 * own, own), :]
    output_grad[...] = dot_of(context_ref[...], grad_branch[...], 0, 0)
    output_sum = Scatter(
        output_grad,
        output_held,
        output_beside,
        output_inbox,
        sends,
        arrivals,
        output_loads,
        rest_base + rest.count * 2 - 1,
    )
    output_sum.start()
    for e in reversed(range(1, rest.count)):
        rest.step(e)
    grad_context[...] = dot_of(grad_branch[...], output_low[...], 1, 1).astype(jnp.bfloat16)
    keys_t[...] = triple_ref[:, pl.ds(own, own)].T
    grad_keys[...] = jnp.zeros_like(grad_keys)
    grad_values[...] = jnp.zeros_like(grad_values)
    scale = HEAD ** (-0.5)
    low_scale = jnp.bfloat16(scale)
    heads = own // HEAD
    for head in range(heads):
        pair = head * HEAD // LANES * LANES
        inside = head % (LANES // HEAD)
        lanes = pl.ds(pair, LANES)

        def one(block, carry, head=head, pair=pair, inside=inside, lanes=lanes):
            spot = pl.ds(pl.multiple_of(block * QUERIES, QUERIES), QUERIES)
            queries = head_only(triple_ref[spot, lanes], inside)
            back = head_only(grad_context[spot, lanes], inside)
            scores = dot_of(triple_ref[:, pl.ds(own + pair, LANES)], queries * low_scale, 1, 1)
            weights = jnp.exp(scores - logsum_ref[pl.ds(head, 1), spot])
            grad_weights = dot_of(triple_ref[:, pl.ds(2 * own + pair, LANES)], back, 1, 1)
            grad_values[:, lanes] += dot_of(weights.astype(jnp.bfloat16), back, 1, 0)
            inner = jnp.sum(weights * grad_weights, axis=0, keepdims=True)
            grad_low = (weights * (grad_weights - inner)).astype(jnp.bfloat16)
            grad_keys[:, lanes] += dot_of(grad_low, queries, 1, 0)
            grad_queries_t[pl.ds(head * HEAD, HEAD), spot] = dot_of(
                keys_t[pl.ds(head * HEAD, HEAD), :], grad_low, 1, 0
            )
            return carry

        lax.fori_loop(0, tokens // QUERIES, one, 0)
        if head == max(heads - 2, 0):
            gathers[0].step(gathers[0].order[1])
            rest.step(0)
            gathers[1].step(0)
            keeps[1].start()
            keeps.append(pltpu.make_async_copy(rest_held.at[0], expand_share, keep_sems.at[2]))
            keeps[2].start()
    grad_triple[:, pl.ds(0, own)] = (grad_queries_t[...].T * scale).astype(jnp.bfloat16)
    grad_triple[:, pl.ds(own, own)] = (grad_keys[...] * scale).astype(jnp.bfloat16)
    grad_triple[:, pl.ds(2 * own, own)] = grad_values[...].astype(jnp.bfloat16)
    mixed_partial, attend_grad = grad_entry, branch.at[pl.ds(0, 3 * own), :]
    mixed_partial[...] = dot_of(grad_triple[...], attend_ref[...], 1, 1)
    narrow = NarrowSum(
        far_bits, pieces, mixed_partial, grad_mixed_any, near, far, held, sends, arrivals, local, 0
    )
    narrow.start()
    attend_grad[...] = dot_of(grad_triple[...], mixed_ref[...], 0, 0)
    blocks = lax.axis_size("wide")
    scatter = Scatter(
        attend_grad,
        scatter_held,
        scatter_beside,
        scatter_inbox,
        sends,
        arrivals,
        scatter_loads,
        (len(far_bits) + 2) * pieces,
    )
    for p in range(pieces):
        narrow.begin(p)
    scatter.start()
    for e in reversed(range(1, blocks // 2)):
        output_sum.step(e)
    left = list(reversed(range(blocks // 2)))
    forwards = [(0, item) for item in gathers[0].order[2:]] + [
        (1, item) for item in gathers[1].order[1:]
    ]
    urgent = [(1, gathers[1].order[1])]
    for b in range(len(far_bits)):
        for p in range(pieces):
            narrow.step(b, p)
            if urgent:
                index, item = urgent.pop(0)
                gathers[index].step(item)
            if len(left) > 1:
                scatter.step(left.pop(0))
    for index, item in forwards:
        if (index, item) != (1, gathers[1].order[1]):
            gathers[index].step(item)
    while left:
        scatter.step(left.pop(0))
    output_sum.step(0)
    first = 3 * own // blocks
    outs = [
        pltpu.make_async_copy(
            scatter.held.at[0], attend_out_share.at[pl.ds(0, first), :], scatter.local.at[0]
        ),
        pltpu.make_async_copy(
            output_sum.held.at[0],
            attend_out_share.at[pl.ds(first, own // blocks), :],
            output_sum.local.at[0],
        ),
    ]
    for out in outs:
        out.start()
    narrow.finish()
    scatter.finish()
    output_sum.finish()
    rest.finish()
    for gather in gathers:
        gather.finish()
    for keep in keeps:
        keep.wait()
    for out in outs:
        out.wait()


def back(
    hidden,
    branch,
    grad_entry,
    cotangent,
    live,
    scale,
    gate,
    mixed,
    attend_low,
    output_weight,
    triple,
    context,
    logsum,
    reduce_share,
    expand_hold,
    expand_give,
    number,
):
    tokens, width = hidden.shape
    own = output_weight.shape[0]
    pieces = 4
    line = lax.axis_size("wide") // 2
    narrow_bits = bits_of(lax.axis_size("narrow"))
    slots = (len(narrow_bits) + 1) * pieces + 2 * Scatter.slots() + 2 * (line - 1) + line - 1
    block = reduce_share.shape
    vmem = pl.BlockSpec(memory_space=pltpu.VMEM)
    anywhere = pl.BlockSpec(memory_space=pl.ANY)
    f32 = lambda *shape: jax.ShapeDtypeStruct(shape, jnp.float32)
    wide = lambda *shape: pltpu.VMEM(shape, jnp.float32)
    low = lambda *shape: pltpu.VMEM(shape, jnp.bfloat16)
    return pl.pallas_call(
        functools.partial(back_kernel, pieces),
        out_shape=(
            f32(tokens, width),
            f32(1, width),
            f32(1, width),
            f32(1, width),
            f32(tokens, width),
            f32(4 * own // (2 * line), width),
            f32(line * reduce_share.shape[0], width),
            f32(line * reduce_share.shape[0], width),
            f32(*block),
        ),
        in_specs=[anywhere] * 4 + [vmem] * 10 + [anywhere] * 2,
        out_specs=(vmem,) * 4 + (anywhere,) * 5,
        scratch_shapes=[
            wide(tokens, width),
            wide(max(tokens, 4 * own), width),
            wide(tokens, width),
            low(tokens, width),
            low(tokens, width),
            low(own, width),
            low(tokens, own),
            low(own, tokens),
            wide(own, tokens),
            wide(tokens, own),
            wide(tokens, own),
            low(tokens, 3 * own),
        ]
        + narrow_scratch((tokens, width), pieces)
        + scatter_scratch((3 * own, width))
        + scatter_scratch((own, width))
        + [
            wide(line // 2, *block),
            wide(line // 2, *block),
            wide(max(line // 2 - 1, 1), *block),
            pltpu.SemaphoreType.DMA((line // 2,)),
            pltpu.SemaphoreType.DMA((4 * pieces,)),
            pltpu.SemaphoreType.DMA((3,)),
            pltpu.SemaphoreType.DMA((slots,)),
            pltpu.SemaphoreType.DMA((slots,)),
        ],
        compiler_params=pltpu.CompilerParams(
            collective_id=number, has_side_effects=True, vmem_limit_bytes=60 * 2**20
        ),
        cost_estimate=pl.CostEstimate(
            flops=40 * tokens * tokens * own,
            bytes_accessed=150 * tokens * width,
            transcendentals=tokens * tokens * own // HEAD,
        ),
    )(
        hidden,
        branch,
        grad_entry,
        cotangent,
        live,
        scale,
        gate,
        mixed,
        attend_low,
        output_weight,
        triple,
        context,
        logsum,
        reduce_share,
        expand_hold,
        expand_give,
    )


def tail_kernel(
    tokens_any,
    shift_ref,
    scale_ref,
    taps_ref,
    grad_mixed_any,
    grad_hidden_any,
    hidden_any,
    ffn_half_any,
    ffn_across_any,
    cotangent_any,
    live_ref,
    gate_ref,
    rows_ref,
    split_ref,
    attend_out_ref,
    reduce_ref,
    expand_ref,
    reduce_line,
    tokens_grad_ref,
    block_out_ref,
    small_ref,
    norm_ref,
    line_ref,
    reduce_other,
    tokens_ref,
    grad_mixed_ref,
    grad_hidden_ref,
    hidden_ref,
    cotangent_ref,
    ffn_across_ref,
    ffn,
    normed_ref,
    back_ref,
    inverse_ref,
    grad_taps,
    grad_shift,
    grad_scale,
    slots,
    spare,
    spare_in,
    keep_sems,
    load_sems,
    sends,
    arrivals,
):
    width = tokens_ref.shape[1]
    core = lax.axis_index("narrow") % 2
    half = ffn.shape[0] // 2
    mine = pl.ds(pl.multiple_of(core * half, SLAB), half)
    loads = []
    for src, dst in (
        (ffn_half_any, ffn.at[mine, :]),
        (ffn_across_any, ffn_across_ref),
        (tokens_any, tokens_ref),
        (grad_mixed_any, grad_mixed_ref),
        (cotangent_any, cotangent_ref),
        (grad_hidden_any, grad_hidden_ref),
        (hidden_any, hidden_ref),
    ):
        loads.append(pltpu.make_async_copy(src, dst, load_sems.at[len(loads)]))
        loads[-1].start()
    wide_bits = bits_of(lax.axis_size("wide"))
    narrow_bits = bits_of(lax.axis_size("narrow"))
    greet(
        [place_at("wide", bit) for bit in wide_bits]
        + [place_at("narrow", bit) for bit in narrow_bits]
    )
    _, z = wide_parts()
    count = len(wide_bits)
    hops = line_hops()

    def spot_of(item):
        spot = z
        for index, (_, bit) in enumerate(hops):
            if (item >> index) % 2:
                spot = partner(spot, bit // 2)
        return line_block(line_ref, spot)

    gather = Gather(attend_out_ref, spot_of, hops, sends, arrivals, count + len(narrow_bits))
    gather.step(0)
    across = []

    def cross(part):
        extent = reduce_line.shape[0] // 2
        spot = pl.ds(part * extent, extent)
        slot = sends.shape[0] - 2 + part
        across.append(
            send(
                reduce_line.at[spot, :],
                reduce_other.at[spot, :],
                sends,
                arrivals,
                slot,
                place_at("wide", 1),
            )
        )

    cross(0)
    keep = pltpu.make_async_copy(attend_out_ref, spot_of(0), keep_sems.at[0])
    keep.start()
    loads[0].wait()
    loads[1].wait()
    ffn[mine, :] = ffn[mine, :] + ffn_across_ref[...]
    last = count + len(narrow_bits) + 2 ** len(hops) - 1
    ffn_copy = send(ffn.at[mine, :], ffn.at[mine, :], sends, arrivals, last, place_at("narrow", 1))
    mixer_kernel_backward(
        tokens_ref,
        shift_ref,
        scale_ref,
        taps_ref,
        grad_mixed_ref,
        grad_hidden_ref,
        tokens_grad_ref,
        grad_taps,
        grad_shift,
        grad_scale,
        normed_ref,
        back_ref,
        inverse_ref,
        loads[2].wait,
        loads[3].wait,
        loads[5].wait,
    )
    gather.step(gather.order[1])
    ffn_copy.wait_recv()
    loads[4].wait()
    gate, live = gate_ref[...], live_ref[...]

    def weigh(r, gates):
        spot = slab_at(r)
        return gates + fold_rows(ffn[spot, :] * (cotangent_ref[spot, :].astype(jnp.float32) * live))

    def leave(r, carry):
        spot = slab_at(r)
        block_out_ref[spot, :] = (live * (hidden_ref[spot, :] + gate * ffn[spot, :])).astype(
            jnp.bfloat16
        )
        return carry

    gates = lax.fori_loop(
        0, ffn.shape[0] // SLAB, weigh, jnp.zeros((8, width), jnp.float32), unroll=UNROLL
    )
    slots[0] = jnp.zeros(slots.shape[1:], jnp.float32)
    slots[0, 0:1, :] = grad_shift[...]
    slots[0, 1:2, :] = grad_scale[...]
    slots[0, 2:5, :] = rows_ref[...]
    slots[0, 5:6, :] = jnp.sum(gates, axis=0, keepdims=True)
    shared_rows = 6 + taps_ref.shape[0]
    slots[0, 6:shared_rows, :] = grad_taps[...]
    split_rows = split_ref.shape[0]
    slots[0, shared_rows : shared_rows + split_rows, :] = split_ref[...]
    squares = jnp.zeros((8, width), jnp.float32)
    for share in (attend_out_ref, reduce_ref, expand_ref):
        squares = squares + fold_rows(share[...] * share[...])
    end = shared_rows + split_rows
    slots[0, end : end + 1, :] = jnp.sum(squares, axis=0, keepdims=True)
    copies = []
    for b in range(count):
        copy = send(
            slots.at[b], slots.at[count + 1 + b], sends, arrivals, b, place_at("wide", wide_bits[b])
        )
        copies.append(copy)
        if b == 0:
            cross(1)
            loads[6].wait()
            lax.fori_loop(0, ffn.shape[0] // SLAB, leave, 0, unroll=UNROLL)
        copy.wait_recv()
        slots[b + 1] = slots[b] + slots[count + 1 + b]
    total = slots[count]
    small_ref[...] = total
    shared_part = total[:shared_rows]
    split_part = total[shared_rows:end]
    shared = jnp.sum(shared_part * shared_part)
    split_sum = jnp.sum(split_part * split_part) + jnp.sum(total[end : end + 1])
    spare[0] = jnp.full(spare.shape[1:], split_sum, jnp.float32)
    for b in range(len(narrow_bits)):
        copy = send(
            spare.at[b], spare_in.at[b], sends, arrivals, count + b, place_at("narrow", narrow_bits[b])
        )
        copies.append(copy)
        copy.wait_recv()
        spare[b + 1] = spare[b] + spare_in[b]
    norm_ref[...] = jnp.sqrt(spare[len(narrow_bits)] + shared)
    for item in gather.order[2:]:
        gather.step(item)
    keep.wait()
    gather.finish()
    ffn_copy.wait_send()
    for copy in across:
        copy.wait()
    for copy in copies:
        copy.wait_send()


def tail(
    tokens,
    shift,
    scale,
    taps,
    grad_mixed,
    grad_hidden,
    hidden,
    ffn_half,
    ffn_across,
    cotangent,
    live,
    gate,
    table_rows,
    split_rows,
    shares,
    reduce_line,
    number,
):
    rows, width = tokens.shape
    wide_bits = bits_of(lax.axis_size("wide"))
    narrow_bits = bits_of(lax.axis_size("narrow"))
    count = len(wide_bits)
    line = lax.axis_size("wide") // 2
    total = count + len(narrow_bits) + line + 2
    small = -(-(6 + taps.shape[0] + split_rows.shape[0] + 1) // 8) * 8
    vmem = pl.BlockSpec(memory_space=pltpu.VMEM)
    anywhere = pl.BlockSpec(memory_space=pl.ANY)
    f32 = lambda *shape: jax.ShapeDtypeStruct(shape, jnp.float32)
    low = lambda *shape: jax.ShapeDtypeStruct(shape, jnp.bfloat16)
    wide = lambda *shape: pltpu.VMEM(shape, jnp.float32)
    return pl.pallas_call(
        tail_kernel,
        out_shape=(
            low(rows, width),
            low(rows, width),
            f32(small, width),
            f32(8, LANES),
            f32(line * shares[0].shape[0], width),
            f32(*reduce_line.shape),
        ),
        in_specs=[anywhere] + [vmem] * 3 + [anywhere] * 6 + [vmem] * 7 + [anywhere],
        out_specs=(vmem,) * 4 + (anywhere,) * 2,
        scratch_shapes=[
            pltpu.VMEM((rows, width), jnp.bfloat16),
            wide(rows, width),
            wide(rows, width),
            wide(rows, width),
            pltpu.VMEM((rows, width), jnp.bfloat16),
            wide(rows // 2, width),
            wide(rows, width),
            wide(rows, width),
            wide(rows, width),
            wide(rows, LANES),
            wide(9, width),
            wide(1, width),
            wide(1, width),
            wide(2 * count + 1, small, width),
            wide(len(narrow_bits) + 1, 8, LANES),
            wide(len(narrow_bits), 8, LANES),
            pltpu.SemaphoreType.DMA((1,)),
            pltpu.SemaphoreType.DMA((7,)),
            pltpu.SemaphoreType.DMA((total,)),
            pltpu.SemaphoreType.DMA((total,)),
        ],
        compiler_params=pltpu.CompilerParams(
            collective_id=number, has_side_effects=True, vmem_limit_bytes=56 * 2**20
        ),
        cost_estimate=pl.CostEstimate(
            flops=100 * rows * width, bytes_accessed=60 * rows * width, transcendentals=0
        ),
    )(
        tokens,
        shift,
        scale,
        taps,
        grad_mixed,
        grad_hidden,
        hidden,
        ffn_half,
        ffn_across,
        cotangent,
        live,
        gate,
        table_rows,
        split_rows,
        *shares,
        reduce_line,
    )


def local(
    tokens,
    conditions,
    item_live,
    cotangent,
    modulation_table,
    mixer_kernel,
    hidden_kernel,
    attend_weight,
    output_weight,
    expand_weight,
    reduce_weight,
    attend_moment,
    output_moment,
    expand_moment,
    reduce_moment,
    table_first,
    table_second,
    mixer_first,
    mixer_second,
    hidden_first,
    hidden_second,
):
    live_mask = item_live.astype(jnp.float32)[:, None, None]
    modulation = modulation_table[None] + conditions
    shift_one = modulation[:, 0:1]
    scale_one = modulation[:, 1:2]
    gate_one = modulation[:, 2:3]
    shift_two = modulation[:, 3:4]
    scale_two = modulation[:, 4:5]
    gate_two = modulation[:, 5:6]
    width = tokens.shape[2]
    flat_tokens = tokens.reshape(-1, width)
    mixed_low = mixer_forward(flat_tokens, shift_one[0], scale_one[0], mixer_kernel)
    three = lambda matrix: jnp.transpose(matrix, (1, 0, 2))
    triple, context, logsum, attend_low = attend(mixed_low, three(attend_weight))
    output_rows, context = together(all_rows(output_weight), context)
    branch, hidden, entry_low = enter(
        context, flat_tokens, output_rows, gate_one[0], shift_two[0], scale_two[0], 1
    )
    flat_cotangent = cotangent.reshape(-1, width)
    live_row = jnp.broadcast_to(live_mask[0], (1, width))
    ffn_half, grad_entry, reduce_share, expand_hold, expand_give, grad_hidden_kernel = middle(
        entry_low,
        flat_cotangent,
        live_row,
        gate_two[0],
        expand_weight,
        reduce_weight,
        hidden_kernel,
        2,
    )
    grad_entry, reduce_share, expand_hold, ffn_half = together(
        grad_entry, reduce_share, expand_hold, ffn_half
    )
    for bit in bits_of(lax.axis_size("narrow"))[1:-1]:
        ffn_half = ffn_half + permute(ffn_half, "narrow", bit)
    ffn_across = permute(ffn_half, "narrow", lax.axis_size("narrow") // 2)
    (
        grad_hidden,
        grad_shift_two,
        grad_scale_two,
        grad_gate_one,
        grad_mixed,
        attend_out_share,
        reduce_line,
        expand_line,
        expand_share,
    ) = back(
        hidden,
        branch,
        grad_entry,
        flat_cotangent,
        live_row,
        scale_two[0],
        gate_one[0],
        mixed_low,
        attend_low,
        output_weight,
        triple,
        context,
        logsum,
        reduce_share,
        expand_hold,
        expand_give,
        3,
    )
    ffn_across, grad_mixed = together(ffn_across, grad_mixed)
    shared_rows = modulation_table.shape[0] + mixer_kernel.shape[0]
    hidden_rows = -(-grad_hidden_kernel.size // width)
    padding = hidden_rows * width - grad_hidden_kernel.size
    hidden_flat = jnp.pad(grad_hidden_kernel.reshape(-1), (0, padding))
    tokens_gradient, block_out, small, norm, attend_out_line, reduce_other = tail(
        flat_tokens,
        shift_one[0],
        scale_one[0],
        mixer_kernel,
        grad_mixed,
        grad_hidden,
        hidden,
        ffn_half,
        ffn_across,
        flat_cotangent,
        live_row,
        gate_two[0],
        jnp.concatenate([grad_gate_one, grad_shift_two, grad_scale_two], axis=0),
        hidden_flat.reshape(hidden_rows, width),
        [attend_out_share, reduce_share, expand_share],
        reduce_line,
        4,
    )
    summed_hidden = small[shared_rows : shared_rows + hidden_rows].reshape(-1)
    summed_hidden = summed_hidden[: hidden_kernel.size].reshape(hidden_kernel.shape)
    gradient_norm = norm[0, 0]
    gramian, expand_first, expand_later = gram_whole(
        norm,
        [attend_out_line, expand_line, reduce_line],
        [three(attend_moment), output_moment, expand_moment, reduce_moment],
        5,
    )
    gramian, expand_line, attend_out_line = together(gramian, expand_line, attend_out_line)
    expand_other = permute(expand_later, "wide", 1)
    attend_out_other = permute(attend_out_line, "wide", 1)
    factor = polar_factor(gramian)
    factor, expand_other, attend_out_other = together(factor, expand_other, attend_out_other)
    weights = [three(attend_weight), output_weight, expand_weight, reduce_weight]
    bands, ready, fresh, highs, lows = spread(
        norm,
        factor,
        [attend_out_line, expand_line, reduce_line],
        [attend_out_other, expand_first, expand_other, reduce_other],
        [three(attend_moment), output_moment, expand_moment, reduce_moment],
        weights,
        6,
    )
    adams = [modulation_table, table_first, table_second]
    adams += [mixer_kernel, mixer_first, mixer_second]
    adams += [hidden_kernel, hidden_first, hidden_second]
    carried, results, news, passed = finish(
        norm,
        small,
        summed_hidden,
        adams,
        [tokens_gradient, block_out],
        bands,
        ready,
        fresh,
        highs,
        lows,
        weights,
    )
    table_moment, table_square, table_result = news[:3]
    mixer_moment, mixer_square, mixer_result = news[3:6]
    hidden_moment, hidden_square, hidden_result = news[6:]
    tokens_gradient = passed[0].reshape(tokens.shape)
    block_out = passed[1].reshape(tokens.shape)
    attend_carried = jnp.transpose(carried[0], (1, 0, 2))
    attend_result = jnp.transpose(results[0], (1, 0, 2))
    return (
        block_out,
        tokens_gradient,
        gradient_norm,
        attend_carried,
        carried[1],
        carried[2],
        carried[3],
        attend_result,
        results[1],
        results[2],
        results[3],
        table_moment,
        table_square,
        table_result,
        mixer_moment,
        mixer_square,
        mixer_result,
        hidden_moment,
        hidden_square,
        hidden_result,
    )


def solution(mesh):
    placed = (
        P("wide", None, None),
        P("wide", None, None),
        P("wide"),
        P("wide", None, None),
        P(),
        P(),
        P(None, "narrow"),
        P(None, None, "narrow"),
        P("narrow", None),
        P(None, "narrow"),
        P("narrow", None),
        P(None, None, "narrow"),
        P("narrow", None),
        P(None, "narrow"),
        P("narrow", None),
        P(),
        P(),
        P(),
        P(),
        P(None, "narrow"),
        P(None, "narrow"),
    )
    return jax.shard_map(
        local,
        mesh=mesh,
        in_specs=placed,
        out_specs=(
            P("wide", None, None),
            P("wide", None, None),
            P(),
            P(None, None, "narrow"),
            P("narrow", None),
            P(None, "narrow"),
            P("narrow", None),
            P(None, None, "narrow"),
            P("narrow", None),
            P(None, "narrow"),
            P("narrow", None),
            P(),
            P(),
            P(),
            P(),
            P(),
            P(),
            P(None, "narrow"),
            P(None, "narrow"),
            P(None, "narrow"),
        ),
        check_vma=False,
    )
```

```python
import functools
import math

import jax
import jax.numpy as jnp
from jax import lax
from jax.experimental import pallas as pl
from jax.experimental.pallas import tpu as pltpu
from jax.sharding import PartitionSpec as P

D = 1024
HEAD = 64
FF = 4096
GRID = 32
NEWTON = 5
STEP = 10


first_decay = 0.9
second_decay = 0.999
adam_rate = 0.3
muon_rate = 0.15
muon_momentum = 0.5
weight_decay = 0.01
newton_terms = (3.4445, -4.775, 2.0315)
gelu_slope = 0.7978845608
gelu_cubic = 0.044715


MESH = pl.DeviceIdType.MESH
BLK = 256
LANES = 128
SLAB = 16
QUERIES = 512
UNROLL = 4
MATRICES = 4
COLUMNS = (0, 2)


def partner(index, bit):
    return index + (1 - 2 * ((index // bit) % 2)) * bit


def bits_of(count):
    found = []
    bit = 1
    while bit < count:
        found.append(bit)
        bit *= 2
    return found


def place_at(axis, bit):
    place = {"wide": lax.axis_index("wide"), "narrow": lax.axis_index("narrow")}
    place[axis] = partner(place[axis], bit)
    return (place["wide"], place["narrow"])


def greet(places):
    barrier = pltpu.get_barrier_semaphore()
    for place in places:
        pl.semaphore_signal(barrier, inc=1, device_id=place, device_id_type=MESH)
    pl.semaphore_wait(barrier, len(places))


def send(src, dst, sends, arrivals, slot, place):
    copy = pltpu.make_async_remote_copy(
        src_ref=src,
        dst_ref=dst,
        send_sem=sends.at[slot],
        recv_sem=arrivals.at[slot],
        device_id=place,
        device_id_type=MESH,
    )
    copy.start()
    return copy


def permute(values, axis, bit):
    size = lax.axis_size(axis)
    return lax.ppermute(values, axis, [(index, index ^ bit) for index in range(size)])


def together(*values):
    return lax.optimization_barrier(values)


def wide_parts():
    w = lax.axis_index("wide")
    return w % 2, w // 2


def line_partner(z, offset):
    for bit in bits_of(2 * offset):
        if (offset // bit) % 2:
            z = partner(z, bit)
    return z


def block_of(ref, y, z):
    count = lax.axis_size("wide") // 2
    rows = ref.shape[0] // (2 * count)
    return ref.at[pl.ds(pl.multiple_of((y * count + z) * rows, 8), rows), :]


def line_block(ref, z):
    rows = ref.shape[0] // (lax.axis_size("wide") // 2)
    return ref.at[pl.ds(pl.multiple_of(z * rows, 8), rows), :]


def block_shape(shape):
    return (shape[0] // lax.axis_size("wide"), shape[1])


class Scatter:
    def __init__(self, src, held, beside, inbox, sends, arrivals, local, base, blocks=None):
        self.src, self.held, self.beside, self.inbox = src, held, beside, inbox
        self.blocks = blocks
        self.sends, self.arrivals, self.local, self.base = sends, arrivals, local, base
        self.count = lax.axis_size("wide") // 2 if blocks is None else blocks[0].shape[0]
        self.copies = {}
        self.loads = {}

    @staticmethod
    def slots():
        return lax.axis_size("wide") - 1

    def load(self):
        y, z = wide_parts()
        for e in reversed(range(self.count)):
            own = self.blocks[0].at[e] if self.blocks else block_of(self.src, y, line_partner(z, e))
            self.loads[e] = pltpu.make_async_copy(own, self.held.at[e], self.local.at[e])
            self.loads[e].start()

    def give(self, e):
        y, z = wide_parts()
        self.copies[("y", e)] = send(
            self.blocks[1].at[e] if self.blocks else block_of(self.src, 1 - y, line_partner(z, e)),
            self.beside.at[e],
            self.sends,
            self.arrivals,
            self.base + e,
            place_at("wide", 1),
        )

    def start(self):
        self.load()
        for e in reversed(range(self.count)):
            self.give(e)

    def step(self, e):
        self.loads[e].wait()
        self.copies[("y", e)].wait_recv()
        self.held[e] = self.held[e] + self.beside[e]
        bit = 1
        while bit < self.count and e % (2 * bit) == 0:
            self.copies[("z", e + bit)].wait_recv()
            self.held[e] = self.held[e] + self.inbox[e + bit - 1]
            bit *= 2
        if e:
            low = e & -e
            self.copies[("z", e)] = send(
                self.held.at[e],
                self.inbox.at[e - 1],
                self.sends,
                self.arrivals,
                self.base + self.count + e - 1,
                place_at("wide", 2 * low),
            )

    def finish(self):
        for copy in self.copies.values():
            copy.wait_send()


def scatter_scratch(shape):
    count = lax.axis_size("wide") // 2
    block = block_shape(shape)
    return [
        pltpu.VMEM((count,) + block, jnp.float32),
        pltpu.VMEM((count,) + block, jnp.float32),
        pltpu.VMEM((max(count - 1, 1),) + block, jnp.float32),
        pltpu.SemaphoreType.DMA((count,)),
    ]


class Gather:
    def __init__(self, own, spot_of, hops, sends, arrivals, base):
        self.own, self.spot_of, self.hops = own, spot_of, hops
        self.sends, self.arrivals, self.base = sends, arrivals, base
        self.copies = {}
        last = 2 ** (len(hops) - 1)
        self.order = sorted(
            range(2 * last), key=lambda item: (item >= last, bin(item).count("1"), -item)
        )

    def step(self, item):
        if item:
            self.copies[item].wait_recv()
        for index in range(item.bit_length(), len(self.hops)):
            later = item + 2**index
            spot = self.spot_of(item)
            axis, bit = self.hops[index]
            self.copies[later] = send(
                spot if item else self.own,
                spot,
                self.sends,
                self.arrivals,
                self.base + later - 1,
                place_at(axis, bit),
            )

    def finish(self):
        for copy in self.copies.values():
            copy.wait_send()


def line_hops():
    return [("wide", bit) for bit in reversed(bits_of(lax.axis_size("wide"))) if bit > 1]


class NarrowSum:
    def __init__(self, far_bits, pieces, x, o, near, far, held, sends, arrivals, local, base):
        self.bits, self.pieces = far_bits, pieces
        self.x, self.o, self.near, self.far, self.held = x, o, near, far, held
        self.sends, self.arrivals, self.local, self.base = sends, arrivals, local, base
        self.rows = x.shape[0] // 2
        self.core = lax.axis_index("narrow") % 2
        self.copies = []
        self.cross = {}
        self.keeps = []

    def block(self, side, p):
        step = self.rows // self.pieces
        return pl.ds(pl.multiple_of(side * self.rows + p * step, 8), step)

    def push(self, src, dst, slot, bit):
        copy = send(
            src, dst, self.sends, self.arrivals, self.base + slot, place_at("narrow", bit)
        )
        self.copies.append(copy)
        return copy

    def start(self):
        self.first = [
            self.push(self.x.at[self.block(1 - self.core, p)], self.near.at[p], p, 1)
            for p in range(self.pieces)
        ]
        self.loads = [
            pltpu.make_async_copy(
                self.x.at[self.block(self.core, p)], self.held.at[0, p], self.local.at[p]
            )
            for p in range(self.pieces)
        ]
        for load in self.loads:
            load.start()

    def hop(self, b, p):
        slot = (b + 1) * self.pieces + p
        self.cross[(b, p)] = self.push(
            self.held.at[b, p], self.far.at[b, p], slot, self.bits[b]
        )

    def begin(self, p):
        self.loads[p].wait()
        self.first[p].wait_recv()
        self.held[0, p] = self.held[0, p] + self.near[p]
        self.hop(0, p)

    def step(self, b, p):
        self.cross[(b, p)].wait_recv()
        self.held[b + 1, p] = self.held[b, p] + self.far[b, p]
        if b + 1 < len(self.bits):
            self.hop(b + 1, p)
            return
        spot = self.o.at[self.block(self.core, p)]
        slot = (b + 2) * self.pieces + p
        self.keeps.append(self.push(self.held.at[b + 1, p], spot, slot, 1))
        keep = pltpu.make_async_copy(self.held.at[b + 1, p], spot, self.local.at[p])
        keep.start()
        self.loads[p] = keep

    def finish(self):
        for copy in self.keeps:
            copy.wait_recv()
        for keep in self.loads:
            keep.wait()
        for copy in self.copies:
            copy.wait_send()


def narrow_scratch(shape, pieces):
    count = len(bits_of(lax.axis_size("narrow"))) - 1
    step = shape[0] // (2 * pieces)
    return [
        pltpu.VMEM((pieces, step, shape[1]), jnp.float32),
        pltpu.VMEM((count, pieces, step, shape[1]), jnp.float32),
        pltpu.VMEM((count + 1, pieces, step, shape[1]), jnp.float32),
        pltpu.SemaphoreType.DMA((pieces,)),
    ]


def gram_kernel(
    norm_ref,
    attend_out_any,
    expand_any,
    reduce_any,
    attend_moment_any,
    output_moment_any,
    expand_moment_any,
    reduce_moment_any,
    band_ref,
    expand_beside,
    expand_later,
    attend_out,
    expand,
    reduce,
    attend_moment,
    output_moment,
    expand_moment,
    reduce_moment,
    *refs,
):
    highs, lows, refs = refs[:MATRICES], refs[MATRICES : 2 * MATRICES], refs[2 * MATRICES :]
    attend_turned, attend_blend, refs = refs[0], refs[1], refs[2:]
    twice, halves, inbox, block, load_sems, sends, arrivals, local = refs
    narrow_bits = bits_of(lax.axis_size("narrow"))
    wide_bits = bits_of(lax.axis_size("wide"))
    parts, rows = halves.shape[0], halves.shape[1]
    sub = parts // MATRICES
    size = attend_out.shape[1]
    hops = [("narrow", bit) for bit in bits_of(sub)]
    hops += [("wide", bit) for bit in reversed(wide_bits)]
    w, n = lax.axis_index("wide"), lax.axis_index("narrow")
    y, z = wide_parts()
    greet(
        [place_at("narrow", bit) for bit in narrow_bits]
        + [place_at("wide", bit) for bit in wide_bits]
    )
    early = expand_beside.shape[0]
    expand_copy = send(
        expand_any.at[pl.ds(0, early), :],
        expand_beside,
        sends,
        arrivals,
        sends.shape[0] - 1,
        place_at("wide", 1),
    )
    own_rows = lambda ref: ref.at[
        pl.ds(pl.multiple_of(y * (ref.shape[0] // 2), 8), ref.shape[0] // 2), :
    ]
    own_columns = lambda ref: ref.at[
        :, pl.ds(pl.multiple_of(y * (ref.shape[1] // 2), LANES), ref.shape[1] // 2)
    ]
    loads = []
    own = attend_moment_any.shape[2]
    for j in range(3):
        pltpu.make_async_copy(
            attend_moment_any.at[j], attend_moment.at[:, pl.ds(j * own, own)], load_sems.at[1]
        ).start()
    for src, dst in (
        (attend_out_any, attend_out),
        (None, None),
        (own_rows(output_moment_any), output_moment),
        (expand_any, expand),
        (own_columns(expand_moment_any), expand_moment),
        (reduce_any, reduce),
        (own_rows(reduce_moment_any), reduce_moment),
    ):
        if src is None:
            loads.append(pltpu.make_async_copy(attend_moment, attend_moment, load_sems.at[1]))
            continue
        loads.append(pltpu.make_async_copy(src, dst, load_sems.at[len(loads)]))
        loads[-1].start()
    clip = jnp.minimum(1.0, 1.0 / (norm_ref[0:1, 0:1] + 1e-06))
    count = halves.shape[1] * sub
    start = z * count
    lines = lax.axis_size("wide") // 2
    band = halves.shape[2]

    def blend(k, moment, gradient):
        total = highs[k].shape[0]

        def one(i, carry):
            spot = slab_at(i)
            highs[k][spot, :], lows[k][spot, :] = split(
                muon_momentum * moment[spot, :] + clip * gradient[spot, :]
            )
            return carry

        lax.fori_loop(0, total // SLAB, one, 0, unroll=UNROLL)

    def multiply(k):
        columns = pl.ds(pl.multiple_of(start, LANES), count)
        high, low = highs[k][:, columns], lows[k][:, columns]
        values = dot_of(high, highs[k][...], 0, 0) + (
            dot_of(high, lows[k][...], 0, 0) + dot_of(low, highs[k][...], 0, 0)
        )
        twice[:, :size] = values
        twice[:, size:] = values[:, :band]
        for s in range(sub):
            for at in range(0, rows, LANES):
                extent = min(LANES, rows)
                first = s * rows + at
                lanes = pl.ds(pl.multiple_of(start + first // LANES * LANES, LANES), band)
                halves[k * sub + s, at : at + extent, :] = twice[first : first + extent, lanes]

    share = attend_out.shape[0] // lines
    first_rows, second_rows = 3 * share // 4, share // 4
    loads[0].wait()
    loads[1].wait()
    loads[2].wait()
    for at in range(0, 3 * own, LANES):
        attend_turned[pl.ds(at, LANES), :] = attend_moment[:, pl.ds(at, LANES)].T
    offset = y * (3 * own // 2)
    for b in range(lines):
        gradient = attend_out[b * share : (b + 1) * share, :]
        spot = pl.ds(pl.multiple_of(offset + b * first_rows, 8), first_rows)
        attend_blend[pl.ds(b * first_rows, first_rows), :] = (
            muon_momentum * attend_turned[spot, :] + clip * gradient[:first_rows]
        )
        spot = pl.ds(b * second_rows, second_rows)
        output_moment[spot, :] = (
            muon_momentum * output_moment[spot, :] + clip * gradient[first_rows:]
        )

    def cut(k, values):
        def one(i, carry):
            spot = slab_at(i)
            highs[k][spot, :], lows[k][spot, :] = split(values[spot, :])
            return carry

        lax.fori_loop(0, highs[k].shape[0] // SLAB, one, 0, unroll=UNROLL)

    cut(0, attend_blend)
    multiply(0)
    loads[3].wait()
    later_copy = pltpu.make_async_copy(expand.at[pl.ds(early, early), :], expand_later, load_sems.at[3])
    later_copy.start()
    cut(1, output_moment)
    multiply(1)
    loads[4].wait()
    for at in range(0, expand.shape[0], LANES):
        spot = pl.ds(at, LANES)
        highs[2][spot, :], lows[2][spot, :] = split(
            muon_momentum * expand_moment[:, spot].T + clip * expand[spot, :]
        )
    multiply(2)
    loads[5].wait()
    loads[6].wait()
    blend(3, reduce_moment, reduce)
    multiply(3)
    half = rows // 2
    row_half = lambda side: pl.ds(pl.multiple_of(side * half, 8), half)
    slot = iter(range(sends.shape[0]))
    copies = []

    def push(src, dst, place):
        copies.append(send(src, dst, sends, arrivals, next(slot), place))
        return copies[-1]

    at = 0
    for bit in narrow_bits:
        value = (n // bit) % 2
        last = 2 * bit == parts
        waits = []
        for j in range(parts // (2 * bit)):
            mine = n % bit + value * bit + j * 2 * bit
            theirs = n % bit + (1 - value) * bit + j * 2 * bit
            for side in (1 - y, y) if last else (None,):
                spot = slice(None) if side is None else row_half(side)
                copy = push(
                    halves.at[theirs] if side is None else halves.at[theirs, spot],
                    inbox.at[at + j] if side is None else inbox.at[at + j, spot],
                    place_at("narrow", bit),
                )
                waits.append((copy, mine, at + j, spot))
        at += parts // (2 * bit)
        for copy, mine, where, spot in waits:
            copy.wait_recv()
            halves[mine, spot] = halves[mine, spot] + inbox[where, spot]
            if last and copy is waits[0][0]:
                side_copy = push(halves.at[n, row_half(1 - y)], block.at[0], place_at("wide", 1))
    side_copy.wait_recv()
    block[1] = halves[n, row_half(y)] + block[0]

    def spot_of(item):
        big, small = w, n % sub
        for index, (axis, bit) in enumerate(hops):
            if (item >> index) % 2:
                if axis == "wide":
                    big = partner(big, bit)
                else:
                    small = partner(small, bit)
        first = ((big // 2) * (2 * sub) + small * 2 + big % 2) * half
        return band_ref.at[pl.ds(pl.multiple_of(first, 8), half), :]

    keep = pltpu.make_async_copy(block.at[1], spot_of(0), local.at[0])
    keep.start()
    gather = Gather(block.at[1], spot_of, hops, sends, arrivals, next(slot))
    for item in gather.order:
        gather.step(item)
    keep.wait()
    gather.finish()
    expand_copy.wait()
    later_copy.wait()
    for copy in copies:
        copy.wait_send()


def gram_whole(norm, lines, moments, number):
    narrow_bits = bits_of(lax.axis_size("narrow"))
    wide_bits = bits_of(lax.axis_size("wide"))
    size = lines[0].shape[1]
    sub = lax.axis_size("narrow") // MATRICES
    parts = lax.axis_size("narrow")
    count = 2 * size // lax.axis_size("wide")
    band = size // 2 + LANES
    halves = (parts, count // sub, band)
    line_rows = [lines[0].shape[0] * 3 // 4, lines[0].shape[0] // 4]
    line_rows += [lines[1].shape[0], lines[2].shape[0]]
    gathers = len(bits_of(sub)) + len(wide_bits)
    slots = parts + 3 + 2**gathers
    vmem = pl.BlockSpec(memory_space=pltpu.VMEM)
    anywhere = pl.BlockSpec(memory_space=pl.ANY)
    wide = lambda *shape: pltpu.VMEM(shape, jnp.float32)
    return pl.pallas_call(
        gram_kernel,
        out_shape=(
            jax.ShapeDtypeStruct((size, band), jnp.float32),
            jax.ShapeDtypeStruct((lines[1].shape[0] // 2, size), jnp.float32),
            jax.ShapeDtypeStruct((lines[1].shape[0] // 2, size), jnp.float32),
        ),
        in_specs=[vmem] + [anywhere] * 7,
        out_specs=(anywhere,) * 3,
        scratch_shapes=[
            wide(*lines[0].shape),
            wide(*lines[1].shape),
            wide(*lines[2].shape),
            wide(size, 2 * line_rows[0]),
            wide(line_rows[1], size),
            wide(size, line_rows[2]),
            wide(line_rows[3], size),
        ]
        + [pltpu.VMEM((rows, size), jnp.bfloat16) for rows in line_rows] * 2
        + [
            wide(2 * line_rows[0], size),
            wide(line_rows[0], size),
            wide(count, size + band),
            wide(*halves),
            wide(*halves),
            wide(2, halves[1] // 2, band),
            pltpu.SemaphoreType.DMA((7,)),
            pltpu.SemaphoreType.DMA((slots,)),
            pltpu.SemaphoreType.DMA((slots,)),
            pltpu.SemaphoreType.DMA((1,)),
        ],
        compiler_params=pltpu.CompilerParams(
            collective_id=number, has_side_effects=True, vmem_limit_bytes=48 * 2**20
        ),
        cost_estimate=pl.CostEstimate(
            flops=3 * size * size * size, bytes_accessed=80 * size * size, transcendentals=0
        ),
    )(norm, *lines, *moments)


def split(values):
    high = values.astype(jnp.bfloat16)
    return high, (values - high.astype(jnp.float32)).astype(jnp.bfloat16)


def product(left_high, left_low, right_high, right_low):
    dot = functools.partial(jnp.dot, preferred_element_type=jnp.float32)
    return dot(left_high, right_high) + (dot(left_high, right_low) + dot(left_low, right_high))


def polar_kernel(g_ref, band_ref, q_ref, gh, gl, ph, pw, th, tl):
    size = g_ref.shape[0]
    blocks = size // BLK
    first, second, third = newton_terms
    rows = lambda block: pl.ds(block * BLK, BLK)
    square = (BLK, BLK)
    unit = (
        lax.broadcasted_iota(jnp.int32, square, 0) == lax.broadcasted_iota(jnp.int32, square, 1)
    ).astype(jnp.float32)
    count = size // LANES
    lanes = lambda block: pl.ds((block % count) * LANES, LANES)
    trace = jnp.zeros((), jnp.float32)
    for i in range(count):
        trace = trace + jnp.sum(g_ref[lanes(i), lanes(0)] * unit[:LANES, :LANES])
    factor = 1.0 / (jnp.sqrt(trace) + 1e-07)
    for i in range(count):
        for j in range(count // 2 + 1):
            values = g_ref[lanes(i), lanes(j)] * (factor * factor)
            gh[lanes(i), lanes(i + j)], gl[lanes(i), lanes(i + j)] = split(values)
            if 0 < j < count // 2:
                values = values.T
                gh[lanes(i + j), lanes(i)], gl[lanes(i + j), lanes(i)] = split(values)

    def put(high, low, i, j, values):
        high[rows(i), rows(j)], low[rows(i), rows(j)] = split(values)
        if i != j:
            high[rows(j), rows(i)], low[rows(j), rows(i)] = split(values.T)

    def symmetric(left, right, emit):
        for i in range(blocks):
            columns = pl.ds(i * BLK, size - i * BLK)
            values = product(
                left[0][rows(i), :], left[1][rows(i), :], right[0][:, columns], right[1][:, columns]
            )
            for j in range(i, blocks):
                emit(i, j, values[:, (j - i) * BLK : (j - i + 1) * BLK])

    def emit_terms(i, j, values):
        gram = gh[rows(i), rows(j)].astype(jnp.float32) + gl[rows(i), rows(j)].astype(jnp.float32)
        terms = second * gram + third * values
        if i == j:
            terms = terms + first * unit
        put(ph, pw, i, j, terms)

    def emit_total(i, j, values):
        q_ref[rows(i), rows(j)] = values
        if i != j:
            q_ref[rows(j), rows(i)] = values.T

    symmetric((gh, gl), (gh, gl), emit_terms)
    for i in range(blocks):
        q_ref[rows(i), :] = (
            ph[rows(i), :].astype(jnp.float32) + pw[rows(i), :].astype(jnp.float32)
        ) * factor

    def one_step(step, carry):
        symmetric((ph, pw), (gh, gl), functools.partial(put, th, tl))
        symmetric((th, tl), (ph, pw), functools.partial(put, gh, gl))
        symmetric((gh, gl), (gh, gl), emit_terms)
        for i in range(blocks):
            th[rows(i), :], tl[rows(i), :] = split(q_ref[rows(i), :])
        symmetric((ph, pw), (th, tl), emit_total)
        return carry

    lax.fori_loop(0, NEWTON - 1, one_step, 0)
    for i in range(count):
        for j in range(count // 2 + 1):
            band_ref[lanes(i), lanes(j)] = q_ref[lanes(i), lanes(i + j)]


def polar_factor(gramian):
    size = gramian.shape[0]
    vmem = pl.BlockSpec(memory_space=pltpu.VMEM)
    return pl.pallas_call(
        polar_kernel,
        out_shape=jax.ShapeDtypeStruct(gramian.shape, jnp.float32),
        in_specs=[vmem],
        out_specs=vmem,
        scratch_shapes=[pltpu.VMEM((size, size), jnp.float32)]
        + [pltpu.VMEM((size, size), jnp.bfloat16)] * 6,
        compiler_params=pltpu.CompilerParams(vmem_limit_bytes=48 * 2**20),
        cost_estimate=pl.CostEstimate(
            flops=17 * 6 * size**3, bytes_accessed=8 * size * size, transcendentals=0
        ),
    )(gramian)


class Matrices:
    def __init__(self, own):
        self.own = own

    def move(self, outer, inner, sem, k, inward, rows=slice(None), columns=slice(None)):
        if k:
            pairs = [(outer.at[rows, columns], inner.at[rows, columns])]
        else:
            pairs = [
                (outer.at[j, rows], inner.at[rows, pl.ds(j * self.own, self.own)]) for j in range(3)
            ]
        for there, here in pairs:
            src, dst = (there, here) if inward else (here, there)
            pltpu.make_async_copy(src, dst, sem).start()


def whole_of(ref, sem):
    return pltpu.make_async_copy(ref, ref, sem)


def assemble(band, factor_high, factor_low):
    count = factor_high.shape[0] // LANES
    lanes = lambda block: pl.ds((block % count) * LANES, LANES)
    for i in range(count):
        for j in range(count // 2 + 1):
            part = band[lanes(i), lanes(j)]
            spot = (lanes(i), lanes(i + j))
            factor_high[spot], factor_low[spot] = split(part)
            if 0 < j < count // 2:
                spot = (lanes(i + j), lanes(i))
                factor_high[spot], factor_low[spot] = split(part.T)


def update(k, start, factor_high, factor_low, high, low, value):
    spot = pl.ds(pl.multiple_of(start, BLK), BLK)
    q_high, q_low = factor_high[spot, :], factor_low[spot, :]
    if k in COLUMNS:
        polar = dot_of(q_high, high[...], 1, 0) + (
            dot_of(q_high, low[...], 1, 0) + dot_of(q_low, high[...], 1, 0)
        )
        where = (spot, slice(None))
    else:
        polar = dot_of(high[...], q_high, 1, 1) + (
            dot_of(low[...], q_high, 1, 1) + dot_of(high[...], q_low, 1, 1)
        )
        where = (slice(None), spot)
    scale = muon_rate * 0.2 * math.sqrt((3 * D, D, FF, FF)[k])
    value[where] = value[where] * (1.0 - muon_rate * weight_decay) - scale * polar
    return where


def spread_kernel(sub, pieces, norm_ref, q_ref, *refs):
    lines, others, refs = refs[:3], refs[3:7], refs[7:]
    moments, weights, refs = refs[:4], refs[4:8], refs[8:]
    o_ref, carried, fresh, high_outs, low_outs = refs[0], refs[1:5], refs[5:9], refs[9:13], refs[13:17]
    refs = refs[17:]
    pair_bands, factor_high, factor_low = refs[:3]
    staged, values, highs, lows = refs[3:7], refs[7:11], refs[11:15], refs[15:19]
    load_sems, value_sems, out_sems, split_sems, band_sems, sends, arrivals = refs[19:]
    size = q_ref.shape[0]
    half = size // 2
    step = half // pieces
    w, n = lax.axis_index("wide"), lax.axis_index("narrow")
    own = n // sub
    across, near = partner(own, 2), partner(own, 1)
    far = own // 2
    near_place, far_place = place_at("narrow", sub), place_at("narrow", 2 * sub)
    side_place = place_at("wide", 1)
    greet([near_place, far_place, side_place])
    y = w % 2
    rows = lambda side, p: pl.ds(pl.multiple_of(side * half + p * step, 8), step)
    copies = []

    def push(src, dst, place):
        copies.append(send(src, dst, sends, arrivals, len(copies), place))
        return copies[-1]

    crossing = [
        push(q_ref.at[rows(y, p)], o_ref.at[own, rows(y, p)], far_place) for p in range(pieces)
    ]
    landing = [push(q_ref, o_ref.at[own], near_place)]
    keep = pltpu.make_async_copy(q_ref, o_ref.at[own], band_sems.at[0])
    keep.start()
    own_band = pltpu.make_async_copy(q_ref, pair_bands.at[own % 2], band_sems.at[1])
    own_band.start()
    matrices = Matrices(moments[0].shape[2])
    blocks = lax.axis_size("wide")
    for k in range(MATRICES):
        extent = staged[k].shape[0] // 2
        if k >= 2:
            pieces_of = [(y, 0, lines[k - 1])]
            if k == 2:
                pieces_of += [(1 - y, 0, others[1]), (1 - y, extent // 2, others[2])]
            else:
                pieces_of += [(1 - y, 0, others[3])]
            for side, at, source in pieces_of:
                to = pl.multiple_of(side * extent + at, 8)
                spot = staged[k].at[pl.ds(to, source.shape[0]), :]
                pltpu.make_async_copy(source, spot, load_sems.at[k]).start()
        for side, source in ((y, lines[0]), (1 - y, others[0])):
            if k >= 2:
                continue
            share = (staged[0].shape[0] // blocks, staged[1].shape[0] // blocks)
            for b in range(blocks // 2):
                start = b * (share[0] + share[1]) + k * share[0]
                to = pl.multiple_of(side * extent + b * share[k], 8)
                pltpu.make_async_copy(
                    source.at[pl.ds(start, share[k]), :],
                    staged[k].at[pl.ds(to, share[k]), :],
                    load_sems.at[k],
                ).start()
        matrices.move(moments[k], values[k], value_sems.at[k], k, True)
    clip = jnp.minimum(1.0, 1.0 / (norm_ref[0:1, 0:1] + 1e-06))

    def blend_rows(value, stage):
        def one(i, carry):
            spot = slab_at(i)
            value[spot, :] = muon_momentum * value[spot, :] + clip * stage[spot, :]
            return carry

        lax.fori_loop(0, value.shape[0] // SLAB, one, 0, unroll=UNROLL)

    def blend_columns(value, stage):
        def one(i, carry):
            spot = pl.ds(pl.multiple_of(i * LANES, LANES), LANES)
            value[:, spot] = muon_momentum * value[:, spot] + clip * stage[spot, :].T
            return carry

        lax.fori_loop(0, value.shape[1] // LANES, one, 0)

    aside = []

    def forward(p):
        crossing[p].wait_recv()
        spot = o_ref.at[across, rows(y, p)]
        aside.append(push(spot, spot, side_place))
        landing.append(push(spot, spot, near_place))

    def forward_side(p):
        aside[p].wait_recv()
        spot = o_ref.at[across, rows(1 - y, p)]
        landing.append(push(spot, spot, near_place))

    for k in range(MATRICES):
        whole_of(staged[k], load_sems.at[k]).wait()
        whole_of(values[k], value_sems.at[k]).wait()
        blend = blend_columns if k in COLUMNS else blend_rows
        blend(values[k], staged[k])
        matrices.move(carried[k], values[k], out_sems.at[k], k, False)

        def cut(i, carry, k=k):
            highs[k][slab_at(i), :], lows[k][slab_at(i), :] = split(values[k][slab_at(i), :])
            return carry

        lax.fori_loop(0, values[k].shape[0] // SLAB, cut, 0, unroll=UNROLL)

        @pl.when(far != k // 2)
        def _(k=k):
            pltpu.make_async_copy(highs[k], high_outs[k], split_sems.at[2 * k]).start()
            pltpu.make_async_copy(lows[k], low_outs[k], split_sems.at[2 * k + 1]).start()

        if k == 1:
            forward(0)
    for k in range(MATRICES):
        whole_of(values[k], out_sems.at[k]).wait()

        @pl.when(far == k // 2)
        def _(k=k):
            matrices.move(weights[k], values[k], value_sems.at[k], k, True)

    forward(1)
    landing[0].wait_recv()
    near_band = pltpu.make_async_copy(o_ref.at[near], pair_bands.at[1 - own % 2], band_sems.at[2])
    near_band.start()
    own_band.wait()
    near_band.wait()

    def pair(index):
        for side in range(2):

            @pl.when(far == side)
            def _(k=2 * side + index):
                assemble(pair_bands.at[index], factor_high, factor_low)
                whole_of(values[k], value_sems.at[k]).wait()

                def one(i, carry):
                    where = update(
                        k, i * BLK, factor_high, factor_low, highs[k], lows[k], values[k]
                    )
                    matrices.move(fresh[k], values[k], out_sems.at[k], k, False, *where)
                    return carry

                lax.fori_loop(0, size // BLK, one, 0)

    pair(0)
    forward(2)
    forward_side(0)
    pair(1)
    forward_side(1)
    for p in range(3, pieces):
        forward(p)
        forward_side(p - 1)
    forward_side(pieces - 1)
    keep.wait()
    for k in range(MATRICES):

        @pl.when(far == k // 2)
        def _(k=k):
            whole_of(values[k], out_sems.at[k]).wait()

        @pl.when(far != k // 2)
        def _(k=k):
            pltpu.make_async_copy(highs[k], high_outs[k], split_sems.at[2 * k]).wait()
            pltpu.make_async_copy(lows[k], low_outs[k], split_sems.at[2 * k + 1]).wait()

    for copy in landing[1:]:
        copy.wait_recv()
    for copy in copies:
        copy.wait_send()


def spread(norm, band, lines, others, moments, weights, number):
    pieces = 4
    size = band.shape[0]
    slots = 1 + 4 * pieces
    sub = lax.axis_size("narrow") // MATRICES
    vmem = pl.BlockSpec(memory_space=pltpu.VMEM)
    anywhere = pl.BlockSpec(memory_space=pl.ANY)
    operands = [*lines, *others]
    f32 = [jax.ShapeDtypeStruct(moment.shape, jnp.float32) for moment in moments]
    staged = [(moment.size // size, size) for moment in moments]
    flat = [(size, 3 * moments[0].shape[2])] + [moment.shape for moment in moments[1:]]
    low = [jax.ShapeDtypeStruct(shape, jnp.bfloat16) for shape in flat]
    outs = pl.pallas_call(
        functools.partial(spread_kernel, sub, pieces),
        out_shape=tuple(
            [jax.ShapeDtypeStruct((MATRICES,) + band.shape, jnp.float32)] + f32 + f32 + low + low
        ),
        in_specs=[vmem] * 2 + [anywhere] * (len(operands) + 8),
        out_specs=(anywhere,) * 17,
        scratch_shapes=[
            pltpu.VMEM((2,) + band.shape, jnp.float32),
            pltpu.VMEM((size, size), jnp.bfloat16),
            pltpu.VMEM((size, size), jnp.bfloat16),
        ]
        + [pltpu.VMEM(shape, jnp.float32) for shape in staged]
        + [pltpu.VMEM(shape, jnp.float32) for shape in flat]
        + [pltpu.VMEM(shape, jnp.bfloat16) for shape in flat] * 2
        + [pltpu.SemaphoreType.DMA((MATRICES,))] * 3
        + [
            pltpu.SemaphoreType.DMA((2 * MATRICES,)),
            pltpu.SemaphoreType.DMA((3,)),
            pltpu.SemaphoreType.DMA((slots,)),
            pltpu.SemaphoreType.DMA((slots,)),
        ],
        compiler_params=pltpu.CompilerParams(
            collective_id=number, has_side_effects=True, vmem_limit_bytes=58 * 2**20
        ),
        cost_estimate=pl.CostEstimate(
            flops=9 * size * size * size, bytes_accessed=80 * size * size, transcendentals=0
        ),
    )(norm, band, *operands, *moments, *weights)
    return outs[0], outs[1:5], outs[5:9], outs[9:13], outs[13:17]


def finish_kernel(sub, norm_ref, small_ref, hidden_sum_ref, *refs):
    adam_ins, passing, refs = refs[:9], refs[9:11], refs[11:]
    bands_any, refs = refs[0], refs[1:]
    ready, fresh, high_ins, low_ins, weights = (refs[4 * i : 4 * i + 4] for i in range(5))
    carried, results, refs = refs[20:24], refs[24:28], refs[28:]
    adam_outs, passed, refs = refs[:9], refs[9:11], refs[11:]
    held, pass_in, pass_out, refs = refs[:2], refs[2], refs[3], refs[4:]
    bands, factor_high, factor_low = refs[:3]
    news, values, highs, lows = refs[3:7], refs[7:11], refs[11:15], refs[15:19]
    news_sems, value_sems, split_sems, band_sems, carried_sems, out_sems = refs[19:]
    size = factor_high.shape[0]
    far = lax.axis_index("narrow") // sub // 2
    matrices = Matrices(weights[0].shape[2])
    for side in range(2):

        @pl.when(far == side)
        def _(side=side):
            for index in range(2):
                k = 2 * (1 - side) + index
                pltpu.make_async_copy(bands_any.at[k], bands.at[index], band_sems.at[index]).start()
                pltpu.make_async_copy(high_ins[k], highs[k], split_sems.at[2 * index]).start()
                pltpu.make_async_copy(low_ins[k], lows[k], split_sems.at[2 * index + 1]).start()
                matrices.move(weights[k], values[k], value_sems.at[k], k, True)
            for k in (2 * side, 2 * side + 1):
                matrices.move(fresh[k], values[k], value_sems.at[k], k, True)

    for k in range(MATRICES):
        matrices.move(ready[k], news[k], news_sems.at[k], k, True)
    enters = [
        pltpu.make_async_copy(passing[i], held[i], pass_in.at[i]) for i in range(2)
    ]
    leaves = [
        pltpu.make_async_copy(held[i], passed[i], pass_out.at[i]) for i in range(2)
    ]
    for copy in enters:
        copy.start()
    clip = jnp.minimum(1.0, 1.0 / (norm_ref[0:1, 0:1] + 1e-06))
    first, second = adam_ins[0].shape[0], adam_ins[3].shape[0]
    sums = (small_ref[0:first, :], small_ref[first : first + second, :], hidden_sum_ref[...])
    for i, gradient in enumerate(sums):
        news_of = adam_update(*(ref[...] for ref in adam_ins[3 * i : 3 * i + 3]), clip * gradient)
        for ref, value in zip(adam_outs[3 * i : 3 * i + 3], news_of):
            ref[...] = value
    for index in range(2):
        whole_of(bands.at[index], band_sems.at[index]).wait()
        if index:
            for enter_copy, leave_copy in zip(enters, leaves):
                enter_copy.wait()
                leave_copy.start()
            for k in range(MATRICES):
                whole_of(news[k], news_sems.at[k]).wait()
                matrices.move(carried[k], news[k], carried_sems.at[k], k, False)
        for side in range(2):

            @pl.when(far == side)
            def _(k=2 * (1 - side) + index, done=2 * side + index):
                if index:
                    for late in (done - 1, done):
                        whole_of(values[late], value_sems.at[late]).wait()
                        matrices.move(results[late], values[late], out_sems.at[late], late, False)
                assemble(bands.at[index], factor_high, factor_low)
                whole_of(highs[k], split_sems.at[2 * index]).wait()
                whole_of(lows[k], split_sems.at[2 * index + 1]).wait()
                whole_of(values[k], value_sems.at[k]).wait()

                def one(i, carry):
                    where = update(
                        k, i * BLK, factor_high, factor_low, highs[k], lows[k], values[k]
                    )
                    matrices.move(results[k], values[k], out_sems.at[k], k, False, *where)
                    return carry

                lax.fori_loop(0, size // BLK, one, 0)

    for copy in leaves:
        copy.wait()
    for k in range(MATRICES):
        whole_of(news[k], carried_sems.at[k]).wait()
        whole_of(values[k], out_sems.at[k]).wait()


def finish(norm, small, hidden_sum, adams, passing, bands, ready, fresh, highs, lows, weights):
    size = bands.shape[1]
    sub = lax.axis_size("narrow") // MATRICES
    anywhere = pl.BlockSpec(memory_space=pl.ANY)
    shapes = [jax.ShapeDtypeStruct(weight.shape, jnp.float32) for weight in weights]
    flat = [(size, 3 * weights[0].shape[2])] + [weight.shape for weight in weights[1:]]
    vmem = pl.BlockSpec(memory_space=pltpu.VMEM)
    others = [jax.ShapeDtypeStruct(array.shape, jnp.float32) for array in adams]
    others += [jax.ShapeDtypeStruct(array.shape, array.dtype) for array in passing]
    outs = pl.pallas_call(
        functools.partial(finish_kernel, sub),
        out_shape=tuple(shapes + shapes + others),
        in_specs=[vmem] * 12 + [anywhere] * 23,
        out_specs=(anywhere,) * 8 + (vmem,) * 9 + (anywhere,) * 2,
        scratch_shapes=[pltpu.VMEM(array.shape, array.dtype) for array in passing]
        + [pltpu.SemaphoreType.DMA((2,)), pltpu.SemaphoreType.DMA((2,))]
        + [
            pltpu.VMEM((2,) + bands.shape[1:], jnp.float32),
            pltpu.VMEM((size, size), jnp.bfloat16),
            pltpu.VMEM((size, size), jnp.bfloat16),
        ]
        + [pltpu.VMEM(shape, jnp.float32) for shape in flat] * 2
        + [pltpu.VMEM(shape, jnp.bfloat16) for shape in flat] * 2
        + [pltpu.SemaphoreType.DMA((MATRICES,))] * 6,
        compiler_params=pltpu.CompilerParams(vmem_limit_bytes=58 * 2**20),
        cost_estimate=pl.CostEstimate(
            flops=9 * size * size * size, bytes_accessed=60 * size * size, transcendentals=0
        ),
    )(norm, small, hidden_sum, *adams, *passing, bands, *ready, *fresh, *highs, *lows, *weights)
    return outs[:4], outs[4:8], outs[8:17], outs[17:]


def adam_update(weight, moment, square, gradient):
    moment_new = first_decay * moment + (1.0 - first_decay) * gradient
    square_new = second_decay * square + (1.0 - second_decay) * gradient * gradient
    moment_hat = moment_new / (1.0 - first_decay**STEP)
    square_hat = square_new / (1.0 - second_decay**STEP)
    weight_new = weight * (1.0 - adam_rate * weight_decay) - adam_rate * moment_hat / (
        jnp.sqrt(square_hat) + 1e-08
    )
    return (moment_new, square_new, weight_new)


def column_shifts(strip, column):
    rows = strip.shape[0]
    left = jnp.where(column == 0, 0.0, pltpu.roll(strip, 1, 0))
    right = jnp.where(column == rows - 1, 0.0, pltpu.roll(strip, rows - 1, 0))
    return (left, strip, right)


def tap_rows(shifts, taps):
    return [
        taps[3 * i] * shifts[0] + taps[3 * i + 1] * shifts[1] + taps[3 * i + 2] * shifts[2]
        for i in range(3)
    ]


def strip_at(index):
    return pl.ds(pl.multiple_of(index * GRID, GRID), GRID)


def convolve(load, taps, emit):
    shape = load(0).shape
    column = lax.broadcasted_iota(jnp.int32, shape, 0)

    def one(r, carry):
        above, here = carry
        upper, middle, lower = tap_rows(column_shifts(load(r), column), taps)
        emit(r - 1, here + lower)
        return (upper, above + middle)

    upper, middle, _ = tap_rows(column_shifts(load(0), column), taps)
    above, here = lax.fori_loop(1, GRID, one, (upper, middle))
    emit(GRID - 1, here)


def kernel_sums(load, weigh, width):
    column = lax.broadcasted_iota(jnp.int32, (GRID, width), 0)
    fold = lambda values: values.reshape(GRID // 8, 8, width).sum(axis=0)
    zero = jnp.zeros((8, width), jnp.float32)

    def one(r, carry):
        sums = carry
        shifts = column_shifts(load(r), column)
        later = weigh(jnp.minimum(r + 1, GRID - 1)) * jnp.where(r < GRID - 1, 1.0, 0.0)
        earlier = weigh(jnp.maximum(r - 1, 0)) * jnp.where(r > 0, 1.0, 0.0)
        terms = (later, weigh(r), earlier)
        return tuple(
            sums[3 * i + j] + fold(terms[i] * shifts[j]) for i in range(3) for j in range(3)
        )

    return lax.fori_loop(0, GRID, one, (zero,) * 9)


def middle_kernel(
    pieces,
    entry_ref,
    cotangent_ref,
    live_ref,
    gate_ref,
    expand_any,
    reduce_any,
    taps_ref,
    ffn_half_ref,
    grad_entry_any,
    reduce_share,
    expand_hold,
    expand_give,
    grad_taps_ref,
    expand_full,
    reduce_full,
    grad_ffn,
    upward,
    weight,
    active,
    grad_up,
    ffn,
    back,
    grad_reduce,
    grad_expand,
    ffn_inbox,
    near,
    far,
    held,
    local,
    reduce_held,
    reduce_beside,
    reduce_inbox,
    reduce_loads,
    expand_held,
    expand_beside,
    expand_inbox,
    expand_loads,
    give_sems,
    weight_sems,
    sends,
    arrivals,
):
    units = expand_any.shape[1]
    block = min(BLK, units // 2)
    steps = units // block
    groups = steps // 2
    y, z = wide_parts()
    count = lax.axis_size("wide") // 2
    far_bits = bits_of(lax.axis_size("narrow"))[1:]
    greet(
        [place_at("narrow", bit) for bit in [1] + far_bits]
        + [place_at("wide", bit) for bit in bits_of(lax.axis_size("wide"))]
    )

    def block_index(step):
        side = 1 - y if step < groups else y
        return side * groups + line_partner(z // (count // groups), groups - 1 - step % groups)

    fetches = []
    for step in range(steps):
        spot = pl.ds(pl.multiple_of(block_index(step) * block, LANES), block)
        pair = (
            pltpu.make_async_copy(
                expand_any.at[:, spot], expand_full.at[:, spot], weight_sems.at[step]
            ),
            pltpu.make_async_copy(
                reduce_any.at[spot, :], reduce_full.at[spot, :], weight_sems.at[steps + step]
            ),
        )
        for copy in pair:
            copy.start()
        fetches.append(pair)
    gate, live = gate_ref[...], live_ref[...]

    def gated(i, carry):
        spot = slab_at(i)
        result = cotangent_ref[spot, :].astype(jnp.float32) * live
        grad_ffn[spot, :] = (gate * result).astype(jnp.bfloat16)
        return carry

    lax.fori_loop(0, grad_ffn.shape[0] // SLAB, gated, 0, unroll=UNROLL)

    def work(spot, fresh):
        expand_low = expand_full[:, spot].astype(jnp.bfloat16)
        reduce_low = reduce_full[spot, :].astype(jnp.bfloat16)
        taps = [taps_ref[t : t + 1, spot] for t in range(9)]
        upward[...] = dot_of(entry_ref[...], expand_low, 1, 0)
        weight[...] = dot_of(grad_ffn[...], reduce_low, 1, 1)

        def emit_middle(r, values):
            inner = gelu_slope * (values + gelu_cubic * values * values * values)
            bent = jnp.tanh(inner)
            active[strip_at(r), :] = (0.5 * values * (1.0 + bent)).astype(jnp.bfloat16)
            turn = 0.5 * (1.0 + bent) + 0.5 * values * (1.0 - bent * bent) * (
                gelu_slope * (1.0 + 3.0 * gelu_cubic * values * values)
            )
            weight[strip_at(r), :] = weight[strip_at(r), :] * turn

        convolve(lambda r: upward[strip_at(r), :], taps, emit_middle)

        def emit_grad(r, values):
            grad_up[strip_at(r), :] = values.astype(jnp.bfloat16)

        convolve(lambda r: weight[strip_at(r), :], taps[::-1], emit_grad)
        sums = kernel_sums(
            lambda r: upward[strip_at(r), :], lambda r: weight[strip_at(r), :], block
        )
        for t in range(9):
            grad_taps_ref[t : t + 1, spot] = jnp.sum(sums[t], axis=0, keepdims=True)
        grad_reduce[spot, :] = dot_of(active[...], grad_ffn[...], 0, 0)
        grad_expand[spot, :] = dot_of(grad_up[...], entry_ref[...], 0, 0)
        if fresh:
            ffn[...] = dot_of(active[...], reduce_low, 1, 0)
            back[...] = dot_of(grad_up[...], expand_low, 1, 1)
        else:
            ffn[...] += dot_of(active[...], reduce_low, 1, 0)
            back[...] += dot_of(grad_up[...], expand_low, 1, 1)

    base = (len(far_bits) + 2) * pieces + 1
    reduce_sum = Scatter(
        grad_reduce, reduce_held, reduce_beside, reduce_inbox, sends, arrivals, reduce_loads, base
    )
    expand_sum = Scatter(
        grad_expand,
        expand_held,
        expand_beside,
        expand_inbox,
        sends,
        arrivals,
        expand_loads,
        base + Scatter.slots(),
    )
    for step in range(groups):
        for copy in fetches[step]:
            copy.wait()
        work(pl.ds(pl.multiple_of(block_index(step) * block, LANES), block), step == 0)
        size = count // groups
        ready = [(groups - 1 - step) * size + e for e in reversed(range(size))]
        for scatter in (reduce_sum, expand_sum):
            for e in ready:
                if scatter is reduce_sum or e >= count // 2:
                    scatter.give(e)
    for step in range(groups, steps):
        for copy in fetches[step]:
            copy.wait()

    def later(i, carry):
        side_block = line_partner_of(z // (count // groups), i, groups)
        work(pl.ds(pl.multiple_of((y * groups + side_block) * block, LANES), block), False)
        return carry

    lax.fori_loop(0, groups, later, 0)
    narrow = NarrowSum(
        far_bits, pieces, back, grad_entry_any, near, far, held, sends, arrivals, local, 0
    )
    narrow.start()
    core = lax.axis_index("narrow") % 2
    half = ffn.shape[0] // 2
    side_rows = lambda side: pl.ds(pl.multiple_of(side * half, 8), half)
    ffn_copy = send(
        ffn.at[side_rows(1 - core)], ffn_inbox, sends, arrivals, base - 1, place_at("narrow", 1)
    )
    for scatter in (reduce_sum, expand_sum):
        scatter.load()
    for p in range(pieces):
        narrow.begin(p)
    left = [list(reversed(range(count))), list(reversed(range(count // 2, count)))]
    gives = []
    for e in range(count // 2):
        gives.append(
            pltpu.make_async_copy(
                block_of(grad_expand, 1 - y, line_partner(z, e)), expand_give.at[e], give_sems.at[e]
            )
        )
        gives[e].start()
    scatters = (reduce_sum, expand_sum)
    scatters[0].step(left[0].pop(0))
    scatters[1].step(left[1].pop(0))
    ffn_copy.wait_recv()
    ffn_half_ref[...] = ffn[side_rows(core), :] + ffn_inbox[...]
    turns = [0, 1, 0]
    for b in range(len(far_bits)):
        for p in range(pieces):
            narrow.step(b, p)
            if turns and len(left[turns[0]]) > (turns[0] == 0):
                which = turns.pop(0)
                scatters[which].step(left[which].pop(0))
    for which in range(2):
        while left[which]:
            scatters[which].step(left[which].pop(0))
    for e in range(count // 2):
        expand_sum.loads[e].wait()
    expand_sum.copies[("z", count // 2)].wait_recv()
    expand_held[0] = expand_held[0] + expand_inbox[count // 2 - 1]
    outs = [
        pltpu.make_async_copy(reduce_held.at[0], reduce_share, reduce_loads.at[0]),
        pltpu.make_async_copy(
            expand_held.at[pl.ds(0, count // 2)], expand_hold, expand_loads.at[0]
        ),
    ]
    for out in outs:
        out.start()
    outs += gives
    narrow.finish()
    ffn_copy.wait_send()
    for scatter in scatters:
        scatter.finish()
    for out in outs:
        out.wait()


def line_partner_of(place, index, count):
    flipped = 0 * place
    for bit in bits_of(count):
        one, two = (place // bit) % 2, (index // bit) % 2
        flipped = flipped + (one + two - 2 * one * two) * bit
    return flipped


def middle(entry, cotangent, live, gate, expand, reduce, taps, number):
    tokens, width = entry.shape
    units = expand.shape[1]
    block = min(BLK, units // 2)
    steps = units // block
    pieces = 4
    narrow_bits = bits_of(lax.axis_size("narrow"))
    slots = (len(narrow_bits) + 1) * pieces + 1 + 2 * Scatter.slots()
    vmem = pl.BlockSpec(memory_space=pltpu.VMEM)
    anywhere = pl.BlockSpec(memory_space=pl.ANY)
    f32 = lambda *shape: jax.ShapeDtypeStruct(shape, jnp.float32)
    wide = lambda *shape: pltpu.VMEM(shape, jnp.float32)
    low = lambda *shape: pltpu.VMEM(shape, jnp.bfloat16)
    share = block_shape((units, width))
    line = lax.axis_size("wide") // 2
    return pl.pallas_call(
        functools.partial(middle_kernel, pieces),
        out_shape=(
            f32(tokens // 2, width),
            f32(tokens, width),
            f32(*share),
            f32(line // 2, *share),
            f32(line // 2, *share),
            f32(9, units),
        ),
        in_specs=[vmem, vmem, vmem, vmem, anywhere, anywhere, vmem],
        out_specs=(vmem,) + (anywhere,) * 4 + (vmem,),
        scratch_shapes=[
            wide(width, units),
            wide(units, width),
            low(tokens, width),
            wide(tokens, block),
            wide(tokens, block),
            low(tokens, block),
            low(tokens, block),
            wide(tokens, width),
            wide(tokens, width),
            wide(units, width),
            wide(units, width),
            wide(tokens // 2, width),
        ]
        + narrow_scratch((tokens, width), pieces)
        + scatter_scratch((units, width)) * 2
        + [
            pltpu.SemaphoreType.DMA((line // 2,)),
            pltpu.SemaphoreType.DMA((2 * steps,)),
            pltpu.SemaphoreType.DMA((slots,)),
            pltpu.SemaphoreType.DMA((slots,)),
        ],
        compiler_params=pltpu.CompilerParams(
            collective_id=number, has_side_effects=True, vmem_limit_bytes=60 * 2**20
        ),
        cost_estimate=pl.CostEstimate(
            flops=12 * tokens * width * units,
            bytes_accessed=200 * tokens * width,
            transcendentals=tokens * units,
        ),
    )(entry, cotangent, live, gate, expand, reduce, taps)


def norm_strip(values):
    average = jnp.mean(values, axis=-1, keepdims=True)
    centred = values - average
    spread_of = jnp.mean(centred * centred, axis=-1, keepdims=True)
    inverse = lax.rsqrt(spread_of + 1e-06)
    return centred * inverse, inverse


def slab_at(index):
    return pl.ds(pl.multiple_of(index * SLAB, SLAB), SLAB)


def fold_rows(values):
    return values.reshape(values.shape[0] // 8, 8, values.shape[1]).sum(axis=0)


def mixer_kernel_forward(tokens_ref, shift_ref, scale_ref, taps_ref, out_ref, entered):
    stretch = 1.0 + scale_ref[...]
    offset = shift_ref[...]

    def enter(r, carry):
        normed, _ = norm_strip(tokens_ref[slab_at(r), :].astype(jnp.float32))
        entered[slab_at(r), :] = normed * stretch + offset
        return carry

    rows, width = tokens_ref.shape
    lax.fori_loop(0, rows // SLAB, enter, 0, unroll=UNROLL)
    for start in range(0, width, BLK):
        lanes = pl.ds(start, BLK)

        def emit(r, values, lanes=lanes):
            out_ref[strip_at(r), lanes] = values.astype(jnp.bfloat16)

        taps = [taps_ref[t : t + 1, lanes] for t in range(9)]
        convolve(lambda r, lanes=lanes: entered[strip_at(r), lanes], taps, emit)


def mixer_forward(tokens, shift, scale, taps):
    rows, width = tokens.shape
    vmem = pl.BlockSpec(memory_space=pltpu.VMEM)
    return pl.pallas_call(
        mixer_kernel_forward,
        out_shape=jax.ShapeDtypeStruct((rows, width), jnp.bfloat16),
        in_specs=[vmem] * 4,
        out_specs=vmem,
        scratch_shapes=[pltpu.VMEM((rows, width), jnp.float32)],
        compiler_params=pltpu.CompilerParams(vmem_limit_bytes=40 * 2**20),
        cost_estimate=pl.CostEstimate(
            flops=40 * rows * width, bytes_accessed=4 * rows * width, transcendentals=0
        ),
    )(tokens, shift, scale, taps)


def mixer_kernel_backward(
    tokens_ref,
    shift_ref,
    scale_ref,
    taps_ref,
    grad_mixed_ref,
    grad_hidden_ref,
    out_ref,
    grad_taps_ref,
    grad_shift_ref,
    grad_scale_ref,
    normed_ref,
    back_ref,
    inverse_ref,
    wait_tokens,
    wait_mixed,
    wait_hidden,
):
    width = tokens_ref.shape[1]
    stretch = 1.0 + scale_ref[...]
    wait_tokens()

    def enter(r, carry):
        normed, inverse = norm_strip(tokens_ref[slab_at(r), :].astype(jnp.float32))
        normed_ref[slab_at(r), :] = normed
        inverse_ref[slab_at(r), :] = jnp.broadcast_to(inverse, (SLAB, LANES))
        return carry

    rows = tokens_ref.shape[0]
    lax.fori_loop(0, rows // SLAB, enter, 0, unroll=UNROLL)
    wait_mixed()
    for start in range(0, width, BLK):
        lanes = pl.ds(start, BLK)
        taps = [taps_ref[t : t + 1, lanes] for t in range(9)]
        stretch_part = 1.0 + scale_ref[:, lanes]
        offset_part = shift_ref[:, lanes]

        def emit(r, values, lanes=lanes):
            back_ref[strip_at(r), lanes] = values

        def entered(r, lanes=lanes, stretch_part=stretch_part, offset_part=offset_part):
            return normed_ref[strip_at(r), lanes] * stretch_part + offset_part

        weigh = lambda r, lanes=lanes: grad_mixed_ref[strip_at(r), lanes]
        convolve(weigh, taps[::-1], emit)
        sums = kernel_sums(entered, weigh, BLK)
        for t in range(9):
            grad_taps_ref[t : t + 1, lanes] = jnp.sum(sums[t], axis=0, keepdims=True)

    def leave(r, carry):
        shifts, scales = carry
        normed = normed_ref[slab_at(r), :]
        back = back_ref[slab_at(r), :]
        stretched = back * stretch
        first = jnp.mean(stretched, axis=-1, keepdims=True)
        second = jnp.mean(stretched * normed, axis=-1, keepdims=True)
        inverse = inverse_ref[slab_at(r), :][:, :1]
        out = grad_hidden_ref[slab_at(r), :] + (stretched - first - normed * second) * inverse
        out_ref[slab_at(r), :] = out.astype(jnp.bfloat16)
        return shifts + fold_rows(back), scales + fold_rows(back * normed)

    wait_hidden()
    zero = jnp.zeros((8, width), jnp.float32)
    shifts, scales = lax.fori_loop(0, rows // SLAB, leave, (zero, zero), unroll=UNROLL)
    grad_shift_ref[...] = jnp.sum(shifts, axis=0, keepdims=True)
    grad_scale_ref[...] = jnp.sum(scales, axis=0, keepdims=True)


def dot_of(left, right, left_axis, right_axis):
    return lax.dot_general(
        left,
        right,
        (((left_axis,), (right_axis,)), ((), ())),
        preferred_element_type=jnp.float32,
    )


def head_only(values, head):
    lane = lax.broadcasted_iota(jnp.int32, values.shape, 1)
    return jnp.where(lane // HEAD == head, values, jnp.zeros_like(values))


def attend_kernel(
    mixed_ref, attend_ref, triple_ref, context_ref, logsum_ref, low_ref, turned, values_t
):
    tokens = mixed_ref.shape[0]
    width = context_ref.shape[1]
    for j in range(3):
        columns = pl.ds(j * width, width)
        low_ref[:, columns] = attend_ref[j].astype(jnp.bfloat16)
        triple_ref[:, columns] = dot_of(mixed_ref[...], low_ref[:, columns], 1, 0).astype(
            jnp.bfloat16
        )
    values_t[...] = triple_ref[:, pl.ds(2 * width, width)].T
    scale = jnp.bfloat16(HEAD ** (-0.5))
    for head in range(width // HEAD):
        pair = head * HEAD // LANES * LANES
        inside = head % (LANES // HEAD)

        def one(block, carry, head=head, pair=pair, inside=inside):
            spot = pl.ds(pl.multiple_of(block * QUERIES, QUERIES), QUERIES)
            queries = head_only(triple_ref[spot, pl.ds(pair, LANES)], inside) * scale
            scores = dot_of(triple_ref[:, pl.ds(width + pair, LANES)], queries, 1, 1)
            peak = jnp.max(scores, axis=0, keepdims=True)
            weights = jnp.exp(scores - peak)
            total = jnp.sum(weights, axis=0, keepdims=True)
            soft_low = (weights * (1.0 / total)).astype(jnp.bfloat16)
            turned[pl.ds(head * HEAD, HEAD), spot] = dot_of(
                values_t[pl.ds(head * HEAD, HEAD), :], soft_low, 1, 0
            )
            logsum_ref[pl.ds(head, 1), spot] = peak + jnp.log(total)
            return carry

        lax.fori_loop(0, tokens // QUERIES, one, 0)
    context_ref[...] = turned[...].T.astype(jnp.bfloat16)


def attend(mixed, attend_weight):
    tokens, width = mixed.shape
    own = attend_weight.shape[2]
    vmem = pl.BlockSpec(memory_space=pltpu.VMEM)
    return pl.pallas_call(
        attend_kernel,
        out_shape=(
            jax.ShapeDtypeStruct((tokens, 3 * own), jnp.bfloat16),
            jax.ShapeDtypeStruct((tokens, own), jnp.bfloat16),
            jax.ShapeDtypeStruct((8, tokens), jnp.float32),
            jax.ShapeDtypeStruct((width, 3 * own), jnp.bfloat16),
        ),
        in_specs=[vmem] * 2,
        out_specs=(vmem,) * 4,
        scratch_shapes=[
            pltpu.VMEM((own, tokens), jnp.float32),
            pltpu.VMEM((own, tokens), jnp.bfloat16),
        ],
        compiler_params=pltpu.CompilerParams(vmem_limit_bytes=40 * 2**20),
        cost_estimate=pl.CostEstimate(
            flops=16 * tokens * tokens * own,
            bytes_accessed=12 * tokens * width,
            transcendentals=tokens * tokens * own // HEAD,
        ),
    )(mixed, attend_weight)


def narrow_hops():
    return [("narrow", bit) for bit in reversed(bits_of(lax.axis_size("narrow")))]


def narrow_position(item):
    n = lax.axis_index("narrow")
    position = 0
    for index, (_, bit) in enumerate(narrow_hops()):
        value = (n // bit) % 2
        if (item >> index) % 2:
            value = 1 - value
        position = position + value * 2**index
    return position


def entry_kernel(
    pieces,
    context_ref,
    tokens_ref,
    output_ref,
    other_ref,
    gate_ref,
    shift_ref,
    scale_ref,
    branch_any,
    hidden_any,
    entry_ref,
    branch_ref,
    hidden_ref,
    out_sems,
    slots,
    output_low,
    output_inbox,
    sends,
    arrivals,
):
    rows, own = context_ref.shape
    step = rows // pieces
    hops = narrow_hops()
    count = 2 ** len(hops)
    greet([place_at(axis, bit) for axis, bit in hops])
    chunk = lambda p: pl.ds(p * step, step)
    slots[narrow_position(0)] = context_ref[...].astype(jnp.float32)
    part = output_ref.shape[0]
    side = (lax.axis_index("narrow") // hops[-2][1]) % 2
    output_copies = []
    for index, (ref, where) in enumerate(((output_ref, side), (other_ref, 1 - side))):
        output_copies.append(
            send(
                ref,
                output_inbox.at[pl.ds(pl.multiple_of(where * part, SLAB), part), :],
                sends,
                arrivals,
                pieces * (count - 1) + index,
                place_at("narrow", 1),
            )
        )
    gathers = []
    for p in range(pieces):
        spot_of = lambda item, p=p: slots.at[narrow_position(item), chunk(p)]
        gathers.append(Gather(spot_of(0), spot_of, hops, sends, arrivals, p * (count - 1)))
        gathers[p].step(0)
    core = lax.axis_index("narrow") % 2
    half = 2 * part
    for ref, where in ((output_ref, side), (other_ref, 1 - side)):
        start = pl.multiple_of(core * half + where * part, SLAB)
        output_low[pl.ds(start, part), :] = ref[...].astype(jnp.bfloat16)
    for copy in output_copies:
        copy.wait_recv()
    output_low[pl.ds(pl.multiple_of((1 - core) * half, SLAB), half), :] = output_inbox[...].astype(
        jnp.bfloat16
    )
    gate, offset, stretch = gate_ref[...], shift_ref[...], 1.0 + scale_ref[...]
    outs = []
    for p in range(pieces):
        for item in gathers[p].order[1:]:
            gathers[p].step(item)
        branch = jnp.zeros((step, output_ref.shape[1]), jnp.float32)
        for position in range(count):
            branch = branch + dot_of(
                slots[position, chunk(p)].astype(jnp.bfloat16),
                output_low[pl.ds(position * own, own), :],
                1,
                0,
            )
        branch_ref[chunk(p), :] = branch

        def one(i, carry, p=p):
            spot = pl.ds(pl.multiple_of(p * step + i * SLAB, SLAB), SLAB)
            hidden = tokens_ref[spot, :].astype(jnp.float32) + gate * branch_ref[spot, :]
            hidden_ref[spot, :] = hidden
            normed, _ = norm_strip(hidden)
            entry_ref[spot, :] = (normed * stretch + offset).astype(jnp.bfloat16)
            return carry

        lax.fori_loop(0, step // SLAB, one, 0, unroll=UNROLL)
        for index, (src, dst) in enumerate(((branch_ref, branch_any), (hidden_ref, hidden_any))):
            outs.append(
                pltpu.make_async_copy(
                    src.at[chunk(p), :], dst.at[chunk(p), :], out_sems.at[2 * p + index]
                )
            )
            outs[-1].start()
    for gather in gathers:
        gather.finish()
    for copy in output_copies:
        copy.wait_send()
    for out in outs:
        out.wait()


def enter(context, tokens, output_rows, other_rows, gate, shift, scale, number):
    pieces = 4
    rows, own = context.shape
    width = tokens.shape[1]
    count = lax.axis_size("narrow")
    vmem = pl.BlockSpec(memory_space=pltpu.VMEM)
    slots = pieces * (count - 1) + 2
    return pl.pallas_call(
        functools.partial(entry_kernel, pieces),
        out_shape=(
            jax.ShapeDtypeStruct((rows, width), jnp.float32),
            jax.ShapeDtypeStruct((rows, width), jnp.float32),
            jax.ShapeDtypeStruct((rows, width), jnp.bfloat16),
        ),
        in_specs=[vmem] * 7,
        out_specs=(pl.BlockSpec(memory_space=pl.ANY),) * 2 + (vmem,),
        scratch_shapes=[
            pltpu.VMEM((rows, width), jnp.float32),
            pltpu.VMEM((rows, width), jnp.float32),
            pltpu.SemaphoreType.DMA((2 * pieces,)),
            pltpu.VMEM((count, rows, own), jnp.float32),
            pltpu.VMEM((width, width), jnp.bfloat16),
            pltpu.VMEM((2 * output_rows.shape[0], width), jnp.float32),
            pltpu.SemaphoreType.DMA((slots,)),
            pltpu.SemaphoreType.DMA((slots,)),
        ],
        compiler_params=pltpu.CompilerParams(
            collective_id=number, has_side_effects=True, vmem_limit_bytes=40 * 2**20
        ),
        cost_estimate=pl.CostEstimate(
            flops=2 * rows * width * width, bytes_accessed=100 * rows * width, transcendentals=0
        ),
    )(context, tokens, output_rows, other_rows, gate, shift, scale)


def all_rows(values):
    *before, (_, last), _ = narrow_hops()
    for _, bit in before:
        side = (lax.axis_index("narrow") // bit) % 2
        other = permute(values, "narrow", bit)
        values = jnp.where(
            side == 0,
            jnp.concatenate([values, other], axis=0),
            jnp.concatenate([other, values], axis=0),
        )
    return values, permute(values, "narrow", last)


def back_kernel(
    pieces,
    hidden_any,
    branch_any,
    grad_entry_any,
    cotangent_any,
    live_ref,
    scale_ref,
    gate_ref,
    mixed_ref,
    attend_ref,
    output_ref,
    triple_ref,
    context_ref,
    logsum_ref,
    reduce_share_ref,
    expand_hold,
    expand_give,
    grad_hidden_ref,
    grad_shift_ref,
    grad_scale_ref,
    grad_gate_ref,
    grad_mixed_any,
    attend_out_share,
    reduce_line,
    expand_line,
    expand_share,
    hidden,
    branch,
    grad_entry,
    cotangent,
    grad_branch,
    output_low,
    grad_context,
    keys_t,
    grad_queries_t,
    grad_keys,
    grad_values,
    grad_triple,
    near,
    far,
    held,
    local,
    scatter_held,
    scatter_beside,
    scatter_inbox,
    scatter_loads,
    output_held,
    output_beside,
    output_inbox,
    output_loads,
    rest_held,
    rest_beside,
    rest_inbox,
    rest_loads,
    load_sems,
    keep_sems,
    sends,
    arrivals,
):
    tokens, width = hidden.shape
    own = output_ref.shape[0]
    _, z = wide_parts()
    far_bits = bits_of(lax.axis_size("narrow"))[1:]
    greet(
        [place_at("narrow", bit) for bit in [1] + far_bits]
        + [place_at("wide", bit) for bit in bits_of(lax.axis_size("wide"))]
    )
    hops = line_hops()
    base = (len(far_bits) + 2) * pieces + Scatter.slots()

    def spot_in(line):
        def spot_of(item):
            spot = z
            for index, (_, bit) in enumerate(hops):
                if (item >> index) % 2:
                    spot = partner(spot, bit // 2)
            return line_block(line, spot)

        return spot_of

    gathers, keeps = [], []
    rest_base = base + 2 * (2 ** len(hops) - 1)
    rest = Scatter(
        None, rest_held, rest_beside, rest_inbox, sends, arrivals, rest_loads, rest_base,
        (expand_hold, expand_give),
    )
    rest.start()
    for index, (share, line) in enumerate(
        ((reduce_share_ref, reduce_line), (rest_held.at[0], expand_line))
    ):
        start = base + index * (2 ** len(hops) - 1)
        gathers.append(Gather(share, spot_in(line), hops, sends, arrivals, start))
        keeps.append(pltpu.make_async_copy(share, spot_in(line)(0), keep_sems.at[index]))
    gathers[0].step(0)
    keeps[0].start()
    step = tokens // pieces
    loads = []
    for p in range(pieces):
        spot = pl.ds(p * step, step)
        pairs = (
            (hidden_any, hidden),
            (branch_any, branch),
            (grad_entry_any, grad_entry),
            (cotangent_any, cotangent),
        )
        loads.append(
            [
                pltpu.make_async_copy(src.at[spot, :], dst.at[spot, :], load_sems.at[4 * p + i])
                for i, (src, dst) in enumerate(pairs)
            ]
        )
        for load in loads[p]:
            load.start()
    output_low[...] = output_ref[...].astype(jnp.bfloat16)
    stretch, gate, live = 1.0 + scale_ref[...], gate_ref[...], live_ref[...]

    def one_slab(r, carry):
        shifts, scales, gates = carry
        spot = slab_at(r)
        normed, inverse = norm_strip(hidden[spot, :])
        back = grad_entry[spot, :]
        stretched = back * stretch
        first = jnp.mean(stretched, axis=-1, keepdims=True)
        second = jnp.mean(stretched * normed, axis=-1, keepdims=True)
        grad = cotangent[spot, :].astype(jnp.float32) * live + (
            stretched - first - normed * second
        ) * inverse
        grad_hidden_ref[spot, :] = grad
        grad_branch[spot, :] = (gate * grad).astype(jnp.bfloat16)
        return (
            shifts + fold_rows(back),
            scales + fold_rows(back * normed),
            gates + fold_rows(branch[spot, :] * grad),
        )

    sums = (jnp.zeros((8, width), jnp.float32),) * 3
    for p in range(pieces):
        for load in loads[p]:
            load.wait()
        first_slab = p * step // SLAB
        sums = lax.fori_loop(
            first_slab, first_slab + step // SLAB, one_slab, sums, unroll=UNROLL
        )
    for ref, total in zip((grad_shift_ref, grad_scale_ref, grad_gate_ref), sums):
        ref[...] = jnp.sum(total, axis=0, keepdims=True)
    output_grad = branch.at[pl.ds(3 * own, own), :]
    output_grad[...] = dot_of(context_ref[...], grad_branch[...], 0, 0)
    output_sum = Scatter(
        output_grad,
        output_held,
        output_beside,
        output_inbox,
        sends,
        arrivals,
        output_loads,
        rest_base + rest.count * 2 - 1,
    )
    output_sum.start()
    for e in reversed(range(1, rest.count)):
        rest.step(e)
    grad_context[...] = dot_of(grad_branch[...], output_low[...], 1, 1).astype(jnp.bfloat16)
    keys_t[...] = triple_ref[:, pl.ds(own, own)].T
    grad_keys[...] = jnp.zeros_like(grad_keys)
    grad_values[...] = jnp.zeros_like(grad_values)
    scale = HEAD ** (-0.5)
    low_scale = jnp.bfloat16(scale)
    heads = own // HEAD
    for head in range(heads):
        pair = head * HEAD // LANES * LANES
        inside = head % (LANES // HEAD)
        lanes = pl.ds(pair, LANES)

        def one(block, carry, head=head, pair=pair, inside=inside, lanes=lanes):
            spot = pl.ds(pl.multiple_of(block * QUERIES, QUERIES), QUERIES)
            queries = head_only(triple_ref[spot, lanes], inside)
            back = head_only(grad_context[spot, lanes], inside)
            scores = dot_of(triple_ref[:, pl.ds(own + pair, LANES)], queries * low_scale, 1, 1)
            weights = jnp.exp(scores - logsum_ref[pl.ds(head, 1), spot])
            grad_weights = dot_of(triple_ref[:, pl.ds(2 * own + pair, LANES)], back, 1, 1)
            grad_values[:, lanes] += dot_of(weights.astype(jnp.bfloat16), back, 1, 0)
            inner = jnp.sum(weights * grad_weights, axis=0, keepdims=True)
            grad_low = (weights * (grad_weights - inner)).astype(jnp.bfloat16)
            grad_keys[:, lanes] += dot_of(grad_low, queries, 1, 0)
            grad_queries_t[pl.ds(head * HEAD, HEAD), spot] = dot_of(
                keys_t[pl.ds(head * HEAD, HEAD), :], grad_low, 1, 0
            )
            return carry

        lax.fori_loop(0, tokens // QUERIES, one, 0)
        if head == max(heads - 2, 0):
            gathers[0].step(gathers[0].order[1])
            rest.step(0)
            gathers[1].step(0)
            keeps[1].start()
            keeps.append(pltpu.make_async_copy(rest_held.at[0], expand_share, keep_sems.at[2]))
            keeps[2].start()
    grad_triple[:, pl.ds(0, own)] = (grad_queries_t[...].T * scale).astype(jnp.bfloat16)
    grad_triple[:, pl.ds(own, own)] = (grad_keys[...] * scale).astype(jnp.bfloat16)
    grad_triple[:, pl.ds(2 * own, own)] = grad_values[...].astype(jnp.bfloat16)
    mixed_partial, attend_grad = grad_entry, branch.at[pl.ds(0, 3 * own), :]
    mixed_partial[...] = dot_of(grad_triple[...], attend_ref[...], 1, 1)
    narrow = NarrowSum(
        far_bits, pieces, mixed_partial, grad_mixed_any, near, far, held, sends, arrivals, local, 0
    )
    narrow.start()
    attend_grad[...] = dot_of(grad_triple[...], mixed_ref[...], 0, 0)
    blocks = lax.axis_size("wide")
    scatter = Scatter(
        attend_grad,
        scatter_held,
        scatter_beside,
        scatter_inbox,
        sends,
        arrivals,
        scatter_loads,
        (len(far_bits) + 2) * pieces,
    )
    for p in range(pieces):
        narrow.begin(p)
    scatter.start()
    for e in reversed(range(1, blocks // 2)):
        output_sum.step(e)
    left = list(reversed(range(blocks // 2)))
    forwards = [(0, item) for item in gathers[0].order[2:]] + [
        (1, item) for item in gathers[1].order[1:]
    ]
    urgent = [(1, gathers[1].order[1])]
    for b in range(len(far_bits)):
        for p in range(pieces):
            narrow.step(b, p)
            if urgent:
                index, item = urgent.pop(0)
                gathers[index].step(item)
            if len(left) > 1:
                scatter.step(left.pop(0))
    for index, item in forwards:
        if (index, item) != (1, gathers[1].order[1]):
            gathers[index].step(item)
    while left:
        scatter.step(left.pop(0))
    output_sum.step(0)
    first = 3 * own // blocks
    outs = [
        pltpu.make_async_copy(
            scatter.held.at[0], attend_out_share.at[pl.ds(0, first), :], scatter.local.at[0]
        ),
        pltpu.make_async_copy(
            output_sum.held.at[0],
            attend_out_share.at[pl.ds(first, own // blocks), :],
            output_sum.local.at[0],
        ),
    ]
    for out in outs:
        out.start()
    narrow.finish()
    scatter.finish()
    output_sum.finish()
    rest.finish()
    for gather in gathers:
        gather.finish()
    for keep in keeps:
        keep.wait()
    for out in outs:
        out.wait()


def back(
    hidden,
    branch,
    grad_entry,
    cotangent,
    live,
    scale,
    gate,
    mixed,
    attend_low,
    output_weight,
    triple,
    context,
    logsum,
    reduce_share,
    expand_hold,
    expand_give,
    number,
):
    tokens, width = hidden.shape
    own = output_weight.shape[0]
    pieces = 4
    line = lax.axis_size("wide") // 2
    narrow_bits = bits_of(lax.axis_size("narrow"))
    slots = (len(narrow_bits) + 1) * pieces + 2 * Scatter.slots() + 2 * (line - 1) + line - 1
    block = reduce_share.shape
    vmem = pl.BlockSpec(memory_space=pltpu.VMEM)
    anywhere = pl.BlockSpec(memory_space=pl.ANY)
    f32 = lambda *shape: jax.ShapeDtypeStruct(shape, jnp.float32)
    wide = lambda *shape: pltpu.VMEM(shape, jnp.float32)
    low = lambda *shape: pltpu.VMEM(shape, jnp.bfloat16)
    return pl.pallas_call(
        functools.partial(back_kernel, pieces),
        out_shape=(
            f32(tokens, width),
            f32(1, width),
            f32(1, width),
            f32(1, width),
            f32(tokens, width),
            f32(4 * own // (2 * line), width),
            f32(line * reduce_share.shape[0], width),
            f32(line * reduce_share.shape[0], width),
            f32(*block),
        ),
        in_specs=[anywhere] * 4 + [vmem] * 10 + [anywhere] * 2,
        out_specs=(vmem,) * 4 + (anywhere,) * 5,
        scratch_shapes=[
            wide(tokens, width),
            wide(max(tokens, 4 * own), width),
            wide(tokens, width),
            low(tokens, width),
            low(tokens, width),
            low(own, width),
            low(tokens, own),
            low(own, tokens),
            wide(own, tokens),
            wide(tokens, own),
            wide(tokens, own),
            low(tokens, 3 * own),
        ]
        + narrow_scratch((tokens, width), pieces)
        + scatter_scratch((3 * own, width))
        + scatter_scratch((own, width))
        + [
            wide(line // 2, *block),
            wide(line // 2, *block),
            wide(max(line // 2 - 1, 1), *block),
            pltpu.SemaphoreType.DMA((line // 2,)),
            pltpu.SemaphoreType.DMA((4 * pieces,)),
            pltpu.SemaphoreType.DMA((3,)),
            pltpu.SemaphoreType.DMA((slots,)),
            pltpu.SemaphoreType.DMA((slots,)),
        ],
        compiler_params=pltpu.CompilerParams(
            collective_id=number, has_side_effects=True, vmem_limit_bytes=60 * 2**20
        ),
        cost_estimate=pl.CostEstimate(
            flops=40 * tokens * tokens * own,
            bytes_accessed=150 * tokens * width,
            transcendentals=tokens * tokens * own // HEAD,
        ),
    )(
        hidden,
        branch,
        grad_entry,
        cotangent,
        live,
        scale,
        gate,
        mixed,
        attend_low,
        output_weight,
        triple,
        context,
        logsum,
        reduce_share,
        expand_hold,
        expand_give,
    )


def tail_kernel(
    tokens_any,
    shift_ref,
    scale_ref,
    taps_ref,
    grad_mixed_any,
    grad_hidden_any,
    hidden_any,
    ffn_half_any,
    ffn_across_any,
    cotangent_any,
    live_ref,
    gate_ref,
    rows_ref,
    split_ref,
    attend_out_ref,
    reduce_ref,
    expand_ref,
    reduce_line,
    tokens_grad_ref,
    block_out_ref,
    small_ref,
    norm_ref,
    line_ref,
    reduce_other,
    tokens_ref,
    grad_mixed_ref,
    grad_hidden_ref,
    hidden_ref,
    cotangent_ref,
    ffn_across_ref,
    ffn,
    normed_ref,
    back_ref,
    inverse_ref,
    grad_taps,
    grad_shift,
    grad_scale,
    slots,
    spare,
    spare_in,
    keep_sems,
    load_sems,
    sends,
    arrivals,
):
    width = tokens_ref.shape[1]
    core = lax.axis_index("narrow") % 2
    half = ffn.shape[0] // 2
    mine = pl.ds(pl.multiple_of(core * half, SLAB), half)
    loads = []
    for src, dst in (
        (ffn_half_any, ffn.at[mine, :]),
        (ffn_across_any, ffn_across_ref),
        (tokens_any, tokens_ref),
        (grad_mixed_any, grad_mixed_ref),
        (cotangent_any, cotangent_ref),
        (grad_hidden_any, grad_hidden_ref),
        (hidden_any, hidden_ref),
    ):
        loads.append(pltpu.make_async_copy(src, dst, load_sems.at[len(loads)]))
        loads[-1].start()
    wide_bits = bits_of(lax.axis_size("wide"))
    narrow_bits = bits_of(lax.axis_size("narrow"))
    greet(
        [place_at("wide", bit) for bit in wide_bits]
        + [place_at("narrow", bit) for bit in narrow_bits]
    )
    _, z = wide_parts()
    count = len(wide_bits)
    hops = line_hops()

    def spot_of(item):
        spot = z
        for index, (_, bit) in enumerate(hops):
            if (item >> index) % 2:
                spot = partner(spot, bit // 2)
        return line_block(line_ref, spot)

    gather = Gather(attend_out_ref, spot_of, hops, sends, arrivals, count + len(narrow_bits))
    gather.step(0)
    across = []

    def cross(part):
        extent = reduce_line.shape[0] // 2
        spot = pl.ds(part * extent, extent)
        slot = sends.shape[0] - 2 + part
        across.append(
            send(
                reduce_line.at[spot, :],
                reduce_other.at[spot, :],
                sends,
                arrivals,
                slot,
                place_at("wide", 1),
            )
        )

    cross(0)
    keep = pltpu.make_async_copy(attend_out_ref, spot_of(0), keep_sems.at[0])
    keep.start()
    loads[0].wait()
    loads[1].wait()
    ffn[mine, :] = ffn[mine, :] + ffn_across_ref[...]
    last = count + len(narrow_bits) + 2 ** len(hops) - 1
    ffn_copy = send(ffn.at[mine, :], ffn.at[mine, :], sends, arrivals, last, place_at("narrow", 1))
    mixer_kernel_backward(
        tokens_ref,
        shift_ref,
        scale_ref,
        taps_ref,
        grad_mixed_ref,
        grad_hidden_ref,
        tokens_grad_ref,
        grad_taps,
        grad_shift,
        grad_scale,
        normed_ref,
        back_ref,
        inverse_ref,
        loads[2].wait,
        loads[3].wait,
        loads[5].wait,
    )
    gather.step(gather.order[1])
    ffn_copy.wait_recv()
    loads[4].wait()
    gate, live = gate_ref[...], live_ref[...]

    def weigh(r, gates):
        spot = slab_at(r)
        return gates + fold_rows(ffn[spot, :] * (cotangent_ref[spot, :].astype(jnp.float32) * live))

    def leave(r, carry):
        spot = slab_at(r)
        block_out_ref[spot, :] = (live * (hidden_ref[spot, :] + gate * ffn[spot, :])).astype(
            jnp.bfloat16
        )
        return carry

    gates = lax.fori_loop(
        0, ffn.shape[0] // SLAB, weigh, jnp.zeros((8, width), jnp.float32), unroll=UNROLL
    )
    slots[0] = jnp.zeros(slots.shape[1:], jnp.float32)
    slots[0, 0:1, :] = grad_shift[...]
    slots[0, 1:2, :] = grad_scale[...]
    slots[0, 2:5, :] = rows_ref[...]
    slots[0, 5:6, :] = jnp.sum(gates, axis=0, keepdims=True)
    shared_rows = 6 + taps_ref.shape[0]
    slots[0, 6:shared_rows, :] = grad_taps[...]
    split_rows = split_ref.shape[0]
    slots[0, shared_rows : shared_rows + split_rows, :] = split_ref[...]
    squares = jnp.zeros((8, width), jnp.float32)
    for share in (attend_out_ref, reduce_ref, expand_ref):
        squares = squares + fold_rows(share[...] * share[...])
    end = shared_rows + split_rows
    slots[0, end : end + 1, :] = jnp.sum(squares, axis=0, keepdims=True)
    copies = []
    for b in range(count):
        copy = send(
            slots.at[b], slots.at[count + 1 + b], sends, arrivals, b, place_at("wide", wide_bits[b])
        )
        copies.append(copy)
        if b == 0:
            cross(1)
            loads[6].wait()
            lax.fori_loop(0, ffn.shape[0] // SLAB, leave, 0, unroll=UNROLL)
        copy.wait_recv()
        slots[b + 1] = slots[b] + slots[count + 1 + b]
    total = slots[count]
    small_ref[...] = total
    shared_part = total[:shared_rows]
    split_part = total[shared_rows:end]
    shared = jnp.sum(shared_part * shared_part)
    split_sum = jnp.sum(split_part * split_part) + jnp.sum(total[end : end + 1])
    spare[0] = jnp.full(spare.shape[1:], split_sum, jnp.float32)
    for b in range(len(narrow_bits)):
        copy = send(
            spare.at[b], spare_in.at[b], sends, arrivals, count + b, place_at("narrow", narrow_bits[b])
        )
        copies.append(copy)
        copy.wait_recv()
        spare[b + 1] = spare[b] + spare_in[b]
    norm_ref[...] = jnp.sqrt(spare[len(narrow_bits)] + shared)
    for item in gather.order[2:]:
        gather.step(item)
    keep.wait()
    gather.finish()
    ffn_copy.wait_send()
    for copy in across:
        copy.wait()
    for copy in copies:
        copy.wait_send()


def tail(
    tokens,
    shift,
    scale,
    taps,
    grad_mixed,
    grad_hidden,
    hidden,
    ffn_half,
    ffn_across,
    cotangent,
    live,
    gate,
    table_rows,
    split_rows,
    shares,
    reduce_line,
    number,
):
    rows, width = tokens.shape
    wide_bits = bits_of(lax.axis_size("wide"))
    narrow_bits = bits_of(lax.axis_size("narrow"))
    count = len(wide_bits)
    line = lax.axis_size("wide") // 2
    total = count + len(narrow_bits) + line + 2
    small = -(-(6 + taps.shape[0] + split_rows.shape[0] + 1) // 8) * 8
    vmem = pl.BlockSpec(memory_space=pltpu.VMEM)
    anywhere = pl.BlockSpec(memory_space=pl.ANY)
    f32 = lambda *shape: jax.ShapeDtypeStruct(shape, jnp.float32)
    low = lambda *shape: jax.ShapeDtypeStruct(shape, jnp.bfloat16)
    wide = lambda *shape: pltpu.VMEM(shape, jnp.float32)
    return pl.pallas_call(
        tail_kernel,
        out_shape=(
            low(rows, width),
            low(rows, width),
            f32(small, width),
            f32(8, LANES),
            f32(line * shares[0].shape[0], width),
            f32(*reduce_line.shape),
        ),
        in_specs=[anywhere] + [vmem] * 3 + [anywhere] * 6 + [vmem] * 7 + [anywhere],
        out_specs=(vmem,) * 4 + (anywhere,) * 2,
        scratch_shapes=[
            pltpu.VMEM((rows, width), jnp.bfloat16),
            wide(rows, width),
            wide(rows, width),
            wide(rows, width),
            pltpu.VMEM((rows, width), jnp.bfloat16),
            wide(rows // 2, width),
            wide(rows, width),
            wide(rows, width),
            wide(rows, width),
            wide(rows, LANES),
            wide(9, width),
            wide(1, width),
            wide(1, width),
            wide(2 * count + 1, small, width),
            wide(len(narrow_bits) + 1, 8, LANES),
            wide(len(narrow_bits), 8, LANES),
            pltpu.SemaphoreType.DMA((1,)),
            pltpu.SemaphoreType.DMA((7,)),
            pltpu.SemaphoreType.DMA((total,)),
            pltpu.SemaphoreType.DMA((total,)),
        ],
        compiler_params=pltpu.CompilerParams(
            collective_id=number, has_side_effects=True, vmem_limit_bytes=56 * 2**20
        ),
        cost_estimate=pl.CostEstimate(
            flops=100 * rows * width, bytes_accessed=60 * rows * width, transcendentals=0
        ),
    )(
        tokens,
        shift,
        scale,
        taps,
        grad_mixed,
        grad_hidden,
        hidden,
        ffn_half,
        ffn_across,
        cotangent,
        live,
        gate,
        table_rows,
        split_rows,
        *shares,
        reduce_line,
    )


def local(
    tokens,
    conditions,
    item_live,
    cotangent,
    modulation_table,
    mixer_kernel,
    hidden_kernel,
    attend_weight,
    output_weight,
    expand_weight,
    reduce_weight,
    attend_moment,
    output_moment,
    expand_moment,
    reduce_moment,
    table_first,
    table_second,
    mixer_first,
    mixer_second,
    hidden_first,
    hidden_second,
):
    live_mask = item_live.astype(jnp.float32)[:, None, None]
    modulation = modulation_table[None] + conditions
    shift_one = modulation[:, 0:1]
    scale_one = modulation[:, 1:2]
    gate_one = modulation[:, 2:3]
    shift_two = modulation[:, 3:4]
    scale_two = modulation[:, 4:5]
    gate_two = modulation[:, 5:6]
    width = tokens.shape[2]
    flat_tokens = tokens.reshape(-1, width)
    mixed_low = mixer_forward(flat_tokens, shift_one[0], scale_one[0], mixer_kernel)
    three = lambda matrix: jnp.transpose(matrix, (1, 0, 2))
    triple, context, logsum, attend_low = attend(mixed_low, three(attend_weight))
    output_rows, other_rows = all_rows(output_weight)
    other_rows, context = together(other_rows, context)
    branch, hidden, entry_low = enter(
        context, flat_tokens, output_rows, other_rows, gate_one[0], shift_two[0], scale_two[0], 1
    )
    flat_cotangent = cotangent.reshape(-1, width)
    live_row = jnp.broadcast_to(live_mask[0], (1, width))
    ffn_half, grad_entry, reduce_share, expand_hold, expand_give, grad_hidden_kernel = middle(
        entry_low,
        flat_cotangent,
        live_row,
        gate_two[0],
        expand_weight,
        reduce_weight,
        hidden_kernel,
        2,
    )
    grad_entry, reduce_share, expand_hold, ffn_half = together(
        grad_entry, reduce_share, expand_hold, ffn_half
    )
    for bit in bits_of(lax.axis_size("narrow"))[1:-1]:
        ffn_half = ffn_half + permute(ffn_half, "narrow", bit)
    ffn_across = permute(ffn_half, "narrow", lax.axis_size("narrow") // 2)
    (
        grad_hidden,
        grad_shift_two,
        grad_scale_two,
        grad_gate_one,
        grad_mixed,
        attend_out_share,
        reduce_line,
        expand_line,
        expand_share,
    ) = back(
        hidden,
        branch,
        grad_entry,
        flat_cotangent,
        live_row,
        scale_two[0],
        gate_one[0],
        mixed_low,
        attend_low,
        output_weight,
        triple,
        context,
        logsum,
        reduce_share,
        expand_hold,
        expand_give,
        3,
    )
    ffn_across, grad_mixed = together(ffn_across, grad_mixed)
    shared_rows = modulation_table.shape[0] + mixer_kernel.shape[0]
    hidden_rows = -(-grad_hidden_kernel.size // width)
    padding = hidden_rows * width - grad_hidden_kernel.size
    hidden_flat = jnp.pad(grad_hidden_kernel.reshape(-1), (0, padding))
    tokens_gradient, block_out, small, norm, attend_out_line, reduce_other = tail(
        flat_tokens,
        shift_one[0],
        scale_one[0],
        mixer_kernel,
        grad_mixed,
        grad_hidden,
        hidden,
        ffn_half,
        ffn_across,
        flat_cotangent,
        live_row,
        gate_two[0],
        jnp.concatenate([grad_gate_one, grad_shift_two, grad_scale_two], axis=0),
        hidden_flat.reshape(hidden_rows, width),
        [attend_out_share, reduce_share, expand_share],
        reduce_line,
        4,
    )
    summed_hidden = small[shared_rows : shared_rows + hidden_rows].reshape(-1)
    summed_hidden = summed_hidden[: hidden_kernel.size].reshape(hidden_kernel.shape)
    gradient_norm = norm[0, 0]
    gramian, expand_first, expand_later = gram_whole(
        norm,
        [attend_out_line, expand_line, reduce_line],
        [three(attend_moment), output_moment, expand_moment, reduce_moment],
        5,
    )
    gramian, expand_line, attend_out_line = together(gramian, expand_line, attend_out_line)
    expand_other = permute(expand_later, "wide", 1)
    attend_out_other = permute(attend_out_line, "wide", 1)
    factor = polar_factor(gramian)
    factor, expand_other, attend_out_other = together(factor, expand_other, attend_out_other)
    weights = [three(attend_weight), output_weight, expand_weight, reduce_weight]
    bands, ready, fresh, highs, lows = spread(
        norm,
        factor,
        [attend_out_line, expand_line, reduce_line],
        [attend_out_other, expand_first, expand_other, reduce_other],
        [three(attend_moment), output_moment, expand_moment, reduce_moment],
        weights,
        6,
    )
    adams = [modulation_table, table_first, table_second]
    adams += [mixer_kernel, mixer_first, mixer_second]
    adams += [hidden_kernel, hidden_first, hidden_second]
    carried, results, news, passed = finish(
        norm,
        small,
        summed_hidden,
        adams,
        [tokens_gradient, block_out],
        bands,
        ready,
        fresh,
        highs,
        lows,
        weights,
    )
    table_moment, table_square, table_result = news[:3]
    mixer_moment, mixer_square, mixer_result = news[3:6]
    hidden_moment, hidden_square, hidden_result = news[6:]
    tokens_gradient = passed[0].reshape(tokens.shape)
    block_out = passed[1].reshape(tokens.shape)
    attend_carried = jnp.transpose(carried[0], (1, 0, 2))
    attend_result = jnp.transpose(results[0], (1, 0, 2))
    return (
        block_out,
        tokens_gradient,
        gradient_norm,
        attend_carried,
        carried[1],
        carried[2],
        carried[3],
        attend_result,
        results[1],
        results[2],
        results[3],
        table_moment,
        table_square,
        table_result,
        mixer_moment,
        mixer_square,
        mixer_result,
        hidden_moment,
        hidden_square,
        hidden_result,
    )


def solution(mesh):
    placed = (
        P("wide", None, None),
        P("wide", None, None),
        P("wide"),
        P("wide", None, None),
        P(),
        P(),
        P(None, "narrow"),
        P(None, None, "narrow"),
        P("narrow", None),
        P(None, "narrow"),
        P("narrow", None),
        P(None, None, "narrow"),
        P("narrow", None),
        P(None, "narrow"),
        P("narrow", None),
        P(),
        P(),
        P(),
        P(),
        P(None, "narrow"),
        P(None, "narrow"),
    )
    return jax.shard_map(
        local,
        mesh=mesh,
        in_specs=placed,
        out_specs=(
            P("wide", None, None),
            P("wide", None, None),
            P(),
            P(None, None, "narrow"),
            P("narrow", None),
            P(None, "narrow"),
            P("narrow", None),
            P(None, None, "narrow"),
            P("narrow", None),
            P(None, "narrow"),
            P("narrow", None),
            P(),
            P(),
            P(),
            P(),
            P(),
            P(),
            P(None, "narrow"),
            P(None, "narrow"),
            P(None, "narrow"),
        ),
        check_vma=False,
    )
```
